32 devices in a mesh: groups: 2 (over x), morton: 16 (over z, y, core).
Axes of the slice: x: 2, y: 2, z: 4, core: 2. Of those that a mesh axis runs over, the one named last changes fastest.
Arguments:
- features: bfloat16 [32768, 256], P(('groups', 'morton')), parts along dimension 0, may hold values from -6 to 6
- norm_gain: float32 [256], replicated, may hold values from 0.1 to 1.9
- conv_weight: bfloat16 [6912, 256], replicated, may hold values from -0.078125 to 0.078125
- recv_slot: int32 [64, 26], P(('groups', 'morton')), parts along dimension 0, may hold values from -1 to 63, as said below
- send_face: int32 [32, 64], P(('groups', 'morton')), parts along dimension 0, may hold values from 0 to 11
- cotangent: bfloat16 [32768, 256], P(('groups', 'morton')), parts along dimension 0, may hold values from -6 to 6
Outputs:
- mixed: bfloat16 [32768, 256], P(('groups', 'morton')), parts along dimension 0
- grad_features: bfloat16 [32768, 256], P(('groups', 'morton')), parts along dimension 0
- grad_weight: float32 [13824, 256], P(('groups', 'morton')), parts along dimension 0
The draws below stay inside these ranges and needn't reach their ends.
There are 2 independent parts, one for each index of `groups`. The reference program is written for one: setup_inputs(seed, part) draws one part's arguments, and reference() takes and returns one part's arrays. A program takes and returns all parts, laid end to end along the dimension named above; an argument that names none is the same for every part. Nothing has to cross between parts.
Inputs may be any that keep to these rules, and one draw needn't show every extreme that they name: `recv_slot`: on a device no slot is named twice; -1 marks a missing neighbour; on every device all 4 slots from some device are named.
All inputs are finite; a program needn't handle non-finite values.
Results may differ from the reference program's by a relative error of at most 0.0033.
Values may be sent and summed in bfloat16 or wider, within the bound.
No kernel may reach another device: no remote copies, remote signals or barrier semaphores. Data moves between devices by JAX's collectives and lax.ppermute only.
A program may use at most 128 MiB of HBM per device.

```python
import math
import jax
import jax.numpy as jnp
import numpy as np
from jax import lax

C = 256
BRICKS = 2
SLOT = 4
VOXELS = 16384
N_MORTON = 16


def direction_sides():
    sides = []
    for i in (-1, 0, 1):
        for j in (-1, 0, 1):
            for l in (-1, 0, 1):
                if (i, j, l) != (0, 0, 0):
                    vector = (i, j, l)
                    main_axis = [t for t in range(3) if vector[t] != 0][0]
                    sides.append(2 * main_axis + (1 if vector[main_axis] == -1 else 0))
    return np.array(sides, np.int32)


def shared_faces(key):
    requests = BRICKS * 26
    slot_count = N_MORTON * SLOT
    side_table = jnp.asarray(direction_sides())

    def one_device(device_key, device):
        key_list = jax.random.split(device_key, 7)
        order_req = jax.random.permutation(key_list[0], requests).astype(jnp.int32)
        coin_flip = jax.random.randint(key_list[1], (requests,), 0, 32)
        rank_list = jnp.arange(requests, dtype=jnp.int32)
        occupied = (coin_flip < 31) | (rank_list < SLOT)
        peer_ids = jnp.arange(N_MORTON, dtype=jnp.int32)
        far_flag = jax.random.randint(key_list[2], (N_MORTON,), 0, 4) == 0
        far_score = jax.random.randint(key_list[3], (N_MORTON,), 0, N_MORTON)
        peer_score = jnp.where(far_flag, far_score, jnp.abs(peer_ids - device))
        peer_mixing = jax.random.permutation(key_list[4], N_MORTON).astype(jnp.int32)
        peer_rank = peer_score * N_MORTON + peer_mixing
        slot_ids = jnp.arange(slot_count, dtype=jnp.int32)
        scores = peer_rank[slot_ids // SLOT] * SLOT + slot_ids % SLOT
        slot_order = jnp.argsort(scores, stable=True).astype(jnp.int32)
        position = jnp.cumsum(occupied.astype(jnp.int32)) - 1
        chosen = jnp.where(occupied, slot_order[jnp.maximum(position, 0)], -1).astype(jnp.int32)
        slot_list = jnp.zeros((requests,), jnp.int32).at[order_req].set(chosen)
        sides = side_table[order_req % 26]
        sent_brick = jax.random.randint(key_list[5], (requests,), 0, BRICKS)
        base_codes = jax.random.randint(key_list[6], (slot_count,), 0, BRICKS * 6)
        landing = jnp.where(occupied, chosen, slot_count)
        codes = base_codes.at[landing].set((6 * sent_brick + sides).astype(jnp.int32), mode='drop')
        return (slot_list, codes.astype(jnp.int32))
    slot_table, code_table = jax.vmap(one_device)(jax.random.split(key, N_MORTON), jnp.arange(N_MORTON, dtype=jnp.int32))
    return (slot_table, code_table)


def draw_recv_slot(key, part):
    slot_table, _ = shared_faces(key)
    return slot_table.reshape(N_MORTON * BRICKS, 26).astype(jnp.int32)


def draw_send_face(key, part):
    _, code_table = shared_faces(key)
    moved = code_table.reshape(N_MORTON, N_MORTON, SLOT).transpose(1, 0, 2)
    return moved.reshape(N_MORTON, N_MORTON * SLOT).astype(jnp.int32)


def level_of(own_key, shape, cuts, low, high):
    def one(dim, parts):
        steps = jax.random.uniform(jax.random.fold_in(jax.random.fold_in(own_key, 6), dim), (parts,), jnp.float32, low / len(cuts), high / len(cuts))
        return jnp.repeat(jnp.exp(steps), shape[dim] // parts).reshape((-1,) + (1,) * (len(shape) - dim - 1))

    level = one(*cuts[0])
    for cut in cuts[1:]:
        level = level * one(*cut)
    return level


def noise(key, shape, scale, most, cuts=(), held_as=jnp.bfloat16):
    gain = level_of(key, shape, cuts, -0.22, 0.18) if cuts else 1.0
    values = jax.random.normal(key, shape, jnp.float32) * scale * gain
    return jnp.minimum(jnp.maximum(values, -most), most).astype(held_as)


def setup_inputs(seed: int = 0, part: int = 0) -> dict:
    streams_of = jax.random.split(jax.random.key(seed), 7)
    own_keys = jax.random.split(jax.random.fold_in(streams_of[6], part), 7)
    return {
        "features": noise(own_keys[0], (VOXELS, C), 1.0, 6.0, ((0, 16),)),
        "norm_gain": jnp.clip(1.0 + 0.18 * jax.random.normal(streams_of[1], (C,), jnp.float32), 0.1, 1.9),
        "conv_weight": noise(streams_of[2], (27 * C, C), (27 * C) ** -0.5, 0.078125),
        "recv_slot": draw_recv_slot(jax.random.fold_in(jax.random.fold_in(streams_of[6], part), 71), part),
        "send_face": draw_send_face(jax.random.fold_in(jax.random.fold_in(streams_of[6], part), 71), part),
        "cotangent": noise(own_keys[5], (VOXELS, C), 1.0, 6.0, ((0, 16),)),
    }


def direction_list():
    return [(i, j, l) for i in (-1, 0, 1) for j in (-1, 0, 1) for l in (-1, 0, 1) if (i, j, l) != (0, 0, 0)]

def tap_list():
    return [(i, j, l) for i in (-1, 0, 1) for j in (-1, 0, 1) for l in (-1, 0, 1)]

def brick_tables():
    directions = direction_list()
    face_cells = np.zeros((6, 64), np.int32)
    for face_side in range(6):
        main_axis = face_side // 2
        face_level = 0 if face_side % 2 == 0 else 7
        others = [t for t in range(3) if t != main_axis]
        for u in range(8):
            for w in range(8):
                coords = [0, 0, 0]
                coords[main_axis] = face_level
                coords[others[0]] = u
                coords[others[1]] = w
                face_cells[face_side, u * 8 + w] = (coords[0] * 8 + coords[1]) * 8 + coords[2]
    pad_source = np.zeros((1000,), np.int32)
    inverse = np.full((512 + 26 * 64,), 1000, np.int32)
    for first in range(10):
        for second in range(10):
            for third in range(10):
                coords = (first, second, third)
                place = (first * 10 + second) * 10 + third
                d = tuple((-1 if t == 0 else 1 if t == 9 else 0 for t in coords))
                if d == (0, 0, 0):
                    target = ((first - 1) * 8 + (second - 1)) * 8 + (third - 1)
                else:
                    main_axis = [t for t in range(3) if d[t] != 0][0]
                    others = [t for t in range(3) if t != main_axis]
                    spots = []
                    for t in others:
                        if d[t] == 0:
                            spots.append(coords[t] - 1)
                        elif d[t] == 1:
                            spots.append(0)
                        else:
                            spots.append(7)
                    target = 512 + directions.index(d) * 64 + spots[0] * 8 + spots[1]
                pad_source[place] = target
                inverse[target] = place
    return (face_cells, pad_source, inverse)

def activate(values, norm_gain):
    inverse_rms = lax.rsqrt(lax.optimization_barrier(jnp.mean(values * values, axis=-1, keepdims=True)) + 1e-06)
    return jax.nn.silu(values * inverse_rms * norm_gain)

def columns_of(padded):
    bricks = padded.shape[0]
    channels = padded.shape[-1]
    pieces = [padded[:, 1 + i:9 + i, 1 + j:9 + j, 1 + l:9 + l, :].reshape(bricks * 512, channels) for i, j, l in tap_list()]
    return jnp.concatenate(pieces, axis=1)

def tap_gradients(grad_out, conv_weight, bricks):
    channels = grad_out.shape[1]
    padded = jnp.zeros((bricks, 10, 10, 10, channels), jnp.float32)
    for number, (i, j, l) in enumerate(tap_list()):
        weight_tap = conv_weight[number * channels:(number + 1) * channels]
        tap_term = lax.dot_general(grad_out, weight_tap, (((1,), (1,)), ((), ())), preferred_element_type=jnp.float32)
        padded = padded.at[:, 1 + i:9 + i, 1 + j:9 + j, 1 + l:9 + l, :].add(tap_term.reshape(bricks, 8, 8, 8, channels))
    return padded

def reference(features, norm_gain, conv_weight, recv_slot, send_face, cotangent):
    face_cells, pad_source, inverse = brick_tables()
    face_table = jnp.asarray(face_cells)
    channels = features.shape[1]
    per_device = BRICKS * 512
    factor = 1.0 / math.sqrt(VOXELS)
    hidden = activate(features.astype(jnp.float32), norm_gain).astype(jnp.bfloat16)
    codes = send_face.reshape(N_MORTON, N_MORTON, SLOT)
    face_rows = (codes // 6)[..., None] * 512 + face_table[codes % 6]
    owners = jnp.arange(N_MORTON, dtype=jnp.int32)[:, None, None, None] * per_device
    global_rows = (face_rows + owners).astype(jnp.int32)
    slot_table = recv_slot.reshape(N_MORTON, BRICKS * 26)

    def one_device(carry, device):
        weight_sum, grad_hidden = carry
        rows_here = lax.dynamic_index_in_dim(global_rows, device, 1, keepdims=False).reshape(N_MORTON * SLOT, 64)
        arrived = hidden[rows_here.reshape(-1)].reshape(N_MORTON * SLOT, 64, channels)
        slots_here = lax.dynamic_index_in_dim(slot_table, device, 0, keepdims=False)
        valid = slots_here >= 0
        safe = jnp.maximum(slots_here, 0).astype(jnp.int32)
        near = jnp.where(valid[:, None, None], arrived[safe], jnp.zeros((), jnp.bfloat16))
        start = (device * per_device).astype(jnp.int32)
        own = lax.dynamic_slice_in_dim(hidden, start, per_device, 0)
        grad_out = lax.dynamic_slice_in_dim(cotangent, start, per_device, 0)
        source = jnp.concatenate([own.reshape(BRICKS, 512, channels), near.reshape(BRICKS, 26 * 64, channels)], axis=1)
        padded = source[:, pad_source].reshape(BRICKS, 10, 10, 10, channels)
        columns = columns_of(padded)
        conv_out = jnp.dot(columns, conv_weight, preferred_element_type=jnp.float32)
        weight_sum = weight_sum + factor * lax.dot_general(columns, grad_out, (((0,), (0,)), ((), ())), preferred_element_type=jnp.float32)
        grad_padded = tap_gradients(grad_out, conv_weight, BRICKS)
        grad_source = jnp.concatenate([grad_padded.reshape(BRICKS, 1000, channels), jnp.zeros((BRICKS, 1, channels), jnp.float32)], axis=1)[:, inverse]
        own_grad = grad_source[:, :512].reshape(per_device, channels)
        face_grad = grad_source[:, 512:].reshape(BRICKS * 26, 64, channels).astype(jnp.bfloat16)
        face_grad = lax.optimization_barrier(face_grad).astype(jnp.float32)
        face_grad = jnp.where(valid[:, None, None], face_grad, jnp.float32(0.0))
        targets = rows_here[safe]
        grad_hidden = grad_hidden.at[targets.reshape(-1)].add(face_grad.reshape(-1, channels))
        current = lax.dynamic_slice_in_dim(grad_hidden, start, per_device, 0)
        grad_hidden = lax.dynamic_update_slice_in_dim(grad_hidden, current + own_grad, start, 0)
        return ((weight_sum, grad_hidden), conv_out)
    initial = (jnp.zeros((27 * channels, channels), jnp.float32), jnp.zeros((VOXELS, channels), jnp.float32))
    (weight_sum, grad_hidden), conv_all = lax.scan(one_device, initial, jnp.arange(N_MORTON, dtype=jnp.int32))
    conv_all = conv_all.reshape(VOXELS, channels)
    mixed = (features.astype(jnp.float32) + conv_all).astype(jnp.bfloat16)
    _, pullback = jax.vjp(lambda v: activate(v, norm_gain), features.astype(jnp.float32))
    grad_norm = pullback(grad_hidden)[0]
    grad_features = (cotangent.astype(jnp.float32) + grad_norm).astype(jnp.bfloat16)
    return (mixed, grad_features, weight_sum)
```

```python
import functools
import math

import jax
import jax.numpy as jnp
import numpy as np
from jax import lax
from jax.experimental import pallas as pl
from jax.experimental.pallas import tpu as pltpu
from jax.sharding import PartitionSpec as P

F32 = jnp.float32
BF16 = jnp.bfloat16
C = 256
C_LINES = 128
B_LINES = 256
ROWS = 352
HB = 24
VMEM_LIMIT = 56 * 1024 * 1024
DIRECTIONS = [
    (i, j, l)
    for i in (-1, 0, 1)
    for j in (-1, 0, 1)
    for l in (-1, 0, 1)
    if (i, j, l) != (0, 0, 0)
]

VMEM = pl.BlockSpec(memory_space=pltpu.VMEM)
SMEM = pl.BlockSpec(memory_space=pltpu.SMEM)


def call(body, out_shape, in_specs, scratch=(), flops=0, nbytes=0, name=None):
    return pl.pallas_call(
        body,
        out_shape=out_shape,
        in_specs=in_specs,
        out_specs=jax.tree.map(lambda _: VMEM, out_shape),
        scratch_shapes=list(scratch),
        compiler_params=pltpu.CompilerParams(vmem_limit_bytes=VMEM_LIMIT),
        cost_estimate=pl.CostEstimate(flops=flops, bytes_accessed=nbytes, transcendentals=0),
        name=name,
    )


def put_boundary(rows, brick, a, out_ref, stage):
    wide = rows.astype(F32)
    for half in range(2):
        stage[half] = wide[:, half * 128 : half * 128 + 128]
    for edge, at in ((0, 0), (7, 64)):

        @pl.when(a == edge)
        def _():
            out_ref[brick, at : at + 64, :] = rows

    for half in range(2):
        lanes = slice(half * 128, half * 128 + 128)
        first = stage[half, pl.ds(0, 8, stride=8), :]
        last = stage[half, pl.ds(7, 8, stride=8), :]
        pair = jnp.concatenate([first, last], axis=0).astype(BF16)
        out_ref[brick, pl.ds(pl.multiple_of(C_LINES + 16 * a, 16), 16), lanes] = pair
    pair = jnp.concatenate([wide[:8], wide[56:]], axis=0).astype(BF16)

    @pl.when((a > 0) & (a < 7))
    def _():
        out_ref[brick, pl.ds(pl.multiple_of(B_LINES - 16 + 16 * a, 16), 16), :] = pair


def norm_body(x_ref, gain_ref, hidden_ref, out_ref, stage):
    bricks = out_ref.shape[0]
    gain = gain_ref[...]

    def step(k, _):
        at = pl.ds(pl.multiple_of(k * 64, 64), 64)
        x = x_ref[at, :].astype(F32)
        inverse = lax.rsqrt(jnp.mean(x * x, axis=-1, keepdims=True) + 1e-6)
        v = x * inverse * gain
        rows = (v / (1.0 + jnp.exp(-v))).astype(BF16)
        hidden_ref[at, :] = rows
        put_boundary(rows, k // 8, k % 8, out_ref, stage)
        return 0

    lax.fori_loop(0, bricks * 8, step, 0)


def extract_body(x_ref, out_ref, stage):
    bricks = out_ref.shape[0]

    def step(k, _):
        at = pl.ds(pl.multiple_of(k * 64, 64), 64)
        put_boundary(x_ref[at, :], k // 8, k % 8, out_ref, stage)
        return 0

    lax.fori_loop(0, bricks * 8, step, 0)


def start_padded(own_ref, cells, halo, bricks):
    zero = jnp.zeros((8, C), F32)

    def clear(k, _):
        for b in range(10):
            cells[k * 10 + b] = zero
        for side in range(2):
            for part in range(HB // 8):
                halo[side, k, part * 8 : part * 8 + 8, :] = zero
        return 0

    lax.fori_loop(0, bricks * 10, clear, 0)

    def fill(k, _):
        plane = (k // 8) * 10 + k % 8 + 1
        rows = own_ref[pl.ds(pl.multiple_of(k * 64, 64), 64), :].astype(F32)
        for b in range(8):
            cells[plane * 10 + b + 1] = rows[b * 8 : b * 8 + 8]
        return 0

    lax.fori_loop(0, bricks * 8, fill, 0)


def add_line(ref, index, line):
    ref[index] = ref[index] + line


def place(kind, e, keep, source, brick, share, cells, halo):
    flags = [t == -1 for t in e]
    pads = [jnp.where(f, 0, 9) for f in flags]
    take = [jnp.where(f, 1, 0) for f in flags]

    def rows(at, size):
        got = share[source, pl.ds(at, size), :].astype(F32)
        return got if keep is None else jnp.where(keep, got, 0.0)

    def half(pair, axis):
        return jnp.where(flags[axis], pair[8:], pair[:8])

    side = jnp.where(flags[2], 0, 1)
    base = brick * 10
    if kind == (1, 0, 0):
        got = rows(pl.multiple_of(take[0] * 64, 64), 64)
        first = (base + pads[0]) * 10 + 1
        for b in range(8):
            add_line(cells, first + b, got[b * 8 : b * 8 + 8])
    elif kind == (0, 1, 0):
        for a in range(8):
            if a in (0, 7):
                plane = rows(0 if a == 0 else 64, 64)
                line = jnp.where(flags[1], plane[56:], plane[:8])
            else:
                line = half(rows(B_LINES - 16 + 16 * a, 16), 1)
            add_line(cells, (base + a + 1) * 10 + pads[1], line)
    elif kind == (0, 0, 1):
        for a in range(8):
            line = half(rows(C_LINES + 16 * a, 16), 2)
            halo[side, base + a + 1, 8:16, :] = halo[side, base + a + 1, 8:16, :] + line
    elif kind == (1, 1, 0):
        plane = rows(pl.multiple_of(take[0] * 64, 64), 64)
        line = jnp.where(flags[1], plane[56:], plane[:8])
        add_line(cells, (base + pads[0]) * 10 + pads[1], line)
    elif kind == (1, 0, 1):
        line = half(rows(pl.multiple_of(C_LINES + 112 * take[0], 16), 16), 2)
        at = base + pads[0]
        halo[side, at, 8:16, :] = halo[side, at, 8:16, :] + line
    else:
        spot = pl.ds(jnp.where(flags[1], 7, 16), 1)
        planes = range(8) if kind == (0, 1, 1) else (None,)
        for a in planes:
            if a is None:
                line = half(rows(pl.multiple_of(C_LINES + 112 * take[0], 16), 16), 2)
                at = base + pads[0]
            else:
                line = half(rows(C_LINES + 16 * a, 16), 2)
                at = base + a + 1
            cell = jnp.where(flags[1], line[7:8], line[0:1])
            halo[side, at, spot, :] = halo[side, at, spot, :] + cell


def windows(cells, halo, cols, bricks):
    row = lax.broadcasted_iota(jnp.int32, (8, C), 0)

    def step(k, _):
        shifted = [[], [], []]
        for b in range(10):
            x = cells[k * 10 + b]
            before = halo[0, k, pl.ds(b + 7, 1), :]
            after = halo[1, k, pl.ds(b + 7, 1), :]
            shifted[0].append(jnp.where(row == 0, before, pltpu.roll(x, 1, 0)))
            shifted[1].append(x)
            shifted[2].append(jnp.where(row == 7, after, pltpu.roll(x, 7, 0)))
        for j in range(3):
            for l in range(3):
                block = jnp.concatenate(shifted[l][j : j + 8], axis=0).astype(BF16)
                at = (3 * j + l) * C
                cols[k, :, at : at + C] = block
        return 0

    lax.fori_loop(0, bricks * 10, step, 0)


def weight_grad_body(slots, factor, recv, codes, own_ref, share, cot_ref, gw_ref, cols, cells, halo):
    bricks = own_ref.shape[0] // 512
    start_padded(own_ref, cells, halo, bricks)
    for brick in range(bricks):
        for number, e in enumerate(DIRECTIONS):
            slot = recv[brick * 26 + number]
            safe = jnp.maximum(slot, 0)
            source = (safe // slots) * bricks + codes[safe] // 6
            kind = tuple(abs(t) for t in e)
            place(kind, e, slot >= 0, source, brick, share, cells, halo)
    windows(cells, halo, cols, bricks)

    def step(t, _):
        i = t // 9
        for jl in range(9):
            total = None
            for brick in range(bricks):
                left = cols[pl.ds(brick * 10 + t, 8), :, jl * C : jl * C + C].reshape(512, C)
                right = cot_ref[brick * 512 : brick * 512 + 512, :]
                term = lax.dot_general(
                    left, right, (((0,), (0,)), ((), ())), preferred_element_type=F32
                )
                total = term if total is None else total + term
            at = pl.multiple_of((t * 9 + jl) * C, C)
            gw_ref[pl.ds(at, C), :] = total * factor
        return 0

    lax.fori_loop(0, 3, step, 0)


def tap_sum(cols, weight_ref, brick):
    total = None
    for i in range(3):
        left = cols[brick * 10 + i : brick * 10 + i + 8].reshape(512, 9 * C)
        right = weight_ref[i * 9 * C : (i + 1) * 9 * C, :]
        term = jnp.dot(left, right, preferred_element_type=F32)
        total = term if total is None else total + term
    return total


def mix_body(cols, weight_ref, x_ref, out_ref):
    for brick in range(x_ref.shape[0] // 512):
        at = slice(brick * 512, brick * 512 + 512)
        out_ref[at, :] = (x_ref[at, :].astype(F32) + tap_sum(cols, weight_ref, brick)).astype(BF16)


def input_grad_body(
    slots, returned, code_here, cot_ref, share, weight_ref, x_ref, gain_ref, out_ref, cells, halo, cols
):
    bricks = cot_ref.shape[0] // 512
    start_padded(cot_ref, cells, halo, bricks)

    def one(k, _):
        info = returned[k]

        @pl.when(info > 0)
        def _():
            entry = info - 1
            brick = code_here[k] // 6
            source = (k // slots) * bricks + entry // 26
            number = 25 - entry % 26
            tap = jnp.where(number >= 13, number + 1, number)
            e = (tap // 9 - 1, (tap // 3) % 3 - 1, tap % 3 - 1)
            on = [t != 0 for t in e]
            for kind in ((1, 0, 0), (0, 1, 0), (0, 0, 1), (1, 1, 0), (1, 0, 1), (0, 1, 1), (1, 1, 1)):
                match = functools.reduce(
                    jnp.logical_and, [f if w else jnp.logical_not(f) for f, w in zip(on, kind)]
                )

                @pl.when(match)
                def _():
                    place(kind, e, None, source, brick, share, cells, halo)

        return 0

    lax.fori_loop(0, returned.shape[0], one, 0)
    windows(cells, halo, cols, bricks)
    gain = gain_ref[...]
    for brick in range(bricks):
        at = slice(brick * 512, brick * 512 + 512)
        grad = tap_sum(cols, weight_ref, brick)
        x = x_ref[at, :].astype(F32)
        inverse = lax.rsqrt(jnp.mean(x * x, axis=-1, keepdims=True) + 1e-6)
        unit = x * inverse
        v = unit * gain
        gate = 1.0 / (1.0 + jnp.exp(-v))
        grad = grad * (gate * (1.0 + v * (1.0 - gate))) * gain
        grad = inverse * (grad - unit * jnp.mean(grad * unit, axis=-1, keepdims=True))
        out_ref[at, :] = (cot_ref[at, :].astype(F32) + grad).astype(BF16)


def local(features, norm_gain, conv_weight, recv_slot, send_face, cotangent):
    channels = features.shape[1]
    per_device = features.shape[0]
    bricks = per_device // 512
    peers = lax.axis_size("morton")
    slots = send_face.shape[1] // peers
    factor = 1.0 / math.sqrt(peers * per_device)
    gain = norm_gain.reshape(1, channels)
    sds = jax.ShapeDtypeStruct
    stage = pltpu.VMEM((2, 64, 128), F32)
    padded = [
        pltpu.VMEM((bricks * 100, 8, channels), F32),
        pltpu.VMEM((2, bricks * 10, HB, channels), F32),
    ]
    cols_shape = (bricks * 10, 64, 9 * channels)
    conv_flops = 2 * per_device * 27 * channels * channels

    recv = recv_slot.reshape(-1)
    order = jnp.arange(peers * slots, dtype=jnp.int32)
    numbers = jnp.arange(1, bricks * 26 + 1, dtype=jnp.int32)
    served = jnp.sum(jnp.where(recv[:, None] == order[None, :], numbers[:, None], 0), axis=0)
    notes = jnp.concatenate(
        [send_face.reshape(peers, slots), served.astype(jnp.int32).reshape(peers, slots)], axis=1
    )
    notes = lax.all_to_all(notes, "morton", split_axis=0, concat_axis=0, tiled=True)
    codes = notes[:, :slots].reshape(-1)
    returned = notes[:, slots:].reshape(-1)

    hidden, share = call(
        norm_body,
        (sds((per_device, channels), BF16), sds((bricks, ROWS, channels), BF16)),
        [VMEM, VMEM],
        [stage],
        name="norm",
    )(features, gain)
    hidden_all = lax.all_gather(share, "morton", axis=0, tiled=True)

    cot_share = call(
        extract_body,
        sds((bricks, ROWS, channels), BF16),
        [VMEM],
        [stage],
        name="extract",
    )(cotangent)
    cot_all = lax.all_gather(cot_share, "morton", axis=0, tiled=True)

    whole_term, cols = call(
        functools.partial(weight_grad_body, slots, factor),
        (sds((27 * channels, channels), F32), sds(cols_shape, BF16)),
        [SMEM, SMEM, VMEM, VMEM, VMEM],
        padded,
        flops=conv_flops,
        nbytes=2**24,
        name="weight_grad",
    )(recv, codes, hidden, hidden_all, cotangent)
    grad_weight = lax.psum_scatter(whole_term, "morton", scatter_dimension=0, tiled=True)

    mixed = call(
        mix_body,
        sds((per_device, channels), BF16),
        [VMEM, VMEM, VMEM],
        flops=conv_flops,
        nbytes=2**23,
        name="mix",
    )(cols, conv_weight, features)

    turned = conv_weight.reshape(27, channels, channels)[::-1].transpose(0, 2, 1)
    grad_features = call(
        functools.partial(input_grad_body, slots),
        sds((per_device, channels), BF16),
        [SMEM, SMEM, VMEM, VMEM, VMEM, VMEM, VMEM],
        padded + [pltpu.VMEM(cols_shape, BF16)],
        flops=conv_flops,
        nbytes=2**24,
        name="input_grad",
    )(
        returned,
        send_face.reshape(-1),
        cotangent,
        cot_all,
        turned.reshape(27 * channels, channels),
        features,
        gain,
    )
    return (mixed, grad_features, grad_weight)


def solution(mesh):
    rows = P(("groups", "morton"), None)
    return jax.shard_map(
        local,
        mesh=mesh,
        in_specs=(rows, P(), P(), rows, rows, rows),
        out_specs=(rows, rows, rows),
        check_vma=False,
    )
```

```python
import functools
import math

import jax
import jax.numpy as jnp
import numpy as np
from jax import lax
from jax.experimental import pallas as pl
from jax.experimental.pallas import tpu as pltpu
from jax.sharding import PartitionSpec as P

F32 = jnp.float32
BF16 = jnp.bfloat16
C = 256
C_LINES = 128
B_LINES = 256
ROWS = 352
HB = 24
VMEM_LIMIT = 56 * 1024 * 1024
DIRECTIONS = [
    (i, j, l)
    for i in (-1, 0, 1)
    for j in (-1, 0, 1)
    for l in (-1, 0, 1)
    if (i, j, l) != (0, 0, 0)
]

VMEM = pl.BlockSpec(memory_space=pltpu.VMEM)
SMEM = pl.BlockSpec(memory_space=pltpu.SMEM)
ANY = pl.BlockSpec(memory_space=pl.ANY)


def ring_order(chips):
    if chips == 8:
        return [0, 2, 4, 6, 7, 5, 3, 1]
    return list(range(chips))


def ring_tables(peers):
    chips = peers // 2
    spot = np.argsort(np.array(ring_order(chips)))
    device = np.arange(peers)
    behind = (spot[device // 2][:, None] - spot[None, :]) % chips
    place_of = behind[:, device // 2] + chips * (device[:, None] % 2 != device[None, :] % 2)
    if chips > 8:
        place_of = np.broadcast_to(device, (peers, peers))
    return behind.astype(np.int32), place_of.astype(np.int32)


def ring_step(x, peers, step):
    order = ring_order(peers // 2)
    pairs = [
        (2 * order[i] + core, 2 * order[(i + step) % len(order)] + core)
        for i in range(len(order))
        for core in range(2)
    ]
    return lax.ppermute(x, "morton", pairs)


def swap_cores(x, peers):
    return lax.ppermute(x, "morton", [(m, m ^ 1) for m in range(peers)])


def gather_ring(x, peers):
    chips = peers // 2
    if chips > 8:
        return [lax.all_gather(x, "morton", axis=0, tiled=True)]
    ups, downs = [x], []
    for hop in range(chips // 2):
        ups.append(ring_step(ups[-1], peers, 1))
        if hop < (chips - 1) // 2:
            downs.append(ring_step((downs or [x])[-1], peers, -1))
    mine = ups + downs[::-1]
    return mine + [swap_cores(t, peers) for t in mine]


def scatter_ring(keep, give, peers):
    chips = peers // 2
    other = swap_cores(give, peers)

    def term(k):
        return keep[k] + other[k].astype(F32)

    ups, downs = chips // 2, (chips - 1) // 2
    total = term(0)
    for count, step in ((ups, 1), (downs, -1)):
        held = None
        for hop in range(count, 0, -1):
            part = term((-step * hop) % chips)
            if held is not None:
                part = part + held.astype(F32)
            held = ring_step(part.astype(BF16), peers, step)
        if held is not None:
            total = total + held.astype(F32)
    return total


def call(body, out_shape, in_specs, scratch=(), flops=0, nbytes=0, name=None, out_specs=None):
    return pl.pallas_call(
        body,
        out_shape=out_shape,
        in_specs=in_specs,
        out_specs=out_specs or jax.tree.map(lambda _: VMEM, out_shape),
        scratch_shapes=list(scratch),
        compiler_params=pltpu.CompilerParams(vmem_limit_bytes=VMEM_LIMIT),
        cost_estimate=pl.CostEstimate(flops=flops, bytes_accessed=nbytes, transcendentals=0),
        name=name,
    )


def put_boundary(rows, brick, a, out_ref, stage):
    wide = rows.astype(F32)
    for half in range(2):
        stage[half] = wide[:, half * 128 : half * 128 + 128]
    for edge, at in ((0, 0), (7, 64)):

        @pl.when(a == edge)
        def _():
            out_ref[brick, at : at + 64, :] = rows

    for half in range(2):
        lanes = slice(half * 128, half * 128 + 128)
        first = stage[half, pl.ds(0, 8, stride=8), :]
        last = stage[half, pl.ds(7, 8, stride=8), :]
        pair = jnp.concatenate([first, last], axis=0).astype(BF16)
        out_ref[brick, pl.ds(pl.multiple_of(C_LINES + 16 * a, 16), 16), lanes] = pair
    pair = jnp.concatenate([wide[:8], wide[56:]], axis=0).astype(BF16)

    @pl.when((a > 0) & (a < 7))
    def _():
        out_ref[brick, pl.ds(pl.multiple_of(B_LINES - 16 + 16 * a, 16), 16), :] = pair


def norm_body(x_ref, gain_ref, hidden_ref, out_ref, stage):
    bricks = out_ref.shape[0]
    gain = gain_ref[...]

    def step(k, _):
        at = pl.ds(pl.multiple_of(k * 64, 64), 64)
        x = x_ref[at, :].astype(F32)
        inverse = lax.rsqrt(jnp.mean(x * x, axis=-1, keepdims=True) + 1e-6)
        v = x * inverse * gain
        rows = (v / (1.0 + jnp.exp(-v))).astype(BF16)
        hidden_ref[at, :] = rows
        put_boundary(rows, k // 8, k % 8, out_ref, stage)
        return 0

    lax.fori_loop(0, bricks * 8, step, 0)


def extract_body(x_ref, out_ref, stage):
    bricks = out_ref.shape[0]

    def step(k, _):
        at = pl.ds(pl.multiple_of(k * 64, 64), 64)
        put_boundary(x_ref[at, :], k // 8, k % 8, out_ref, stage)
        return 0

    lax.fori_loop(0, bricks * 8, step, 0)


def start_padded(own_ref, cells, halo, bricks):
    zero = jnp.zeros((8, C), F32)

    def clear(k, _):
        for b in range(10):
            cells[k * 10 + b] = zero
        for side in range(2):
            for part in range(HB // 8):
                halo[side, k, part * 8 : part * 8 + 8, :] = zero
        return 0

    lax.fori_loop(0, bricks * 10, clear, 0)

    def fill(k, _):
        plane = (k // 8) * 10 + k % 8 + 1
        rows = own_ref[pl.ds(pl.multiple_of(k * 64, 64), 64), :].astype(F32)
        for b in range(8):
            cells[plane * 10 + b + 1] = rows[b * 8 : b * 8 + 8]
        return 0

    lax.fori_loop(0, bricks * 8, fill, 0)


def add_line(ref, index, line):
    ref[index] = ref[index] + line


def place(kind, e, keep, source, brick, share, cells, halo):
    flags = [t == -1 for t in e]
    pads = [jnp.where(f, 0, 9) for f in flags]
    take = [jnp.where(f, 1, 0) for f in flags]

    def rows(at, size):
        got = share[source, pl.ds(at, size), :].astype(F32)
        return got if keep is None else jnp.where(keep, got, 0.0)

    def half(pair, axis):
        return jnp.where(flags[axis], pair[8:], pair[:8])

    side = jnp.where(flags[2], 0, 1)
    base = brick * 10
    if kind == (1, 0, 0):
        got = rows(pl.multiple_of(take[0] * 64, 64), 64)
        first = (base + pads[0]) * 10 + 1
        for b in range(8):
            add_line(cells, first + b, got[b * 8 : b * 8 + 8])
    elif kind == (0, 1, 0):
        for a in range(8):
            if a in (0, 7):
                plane = rows(0 if a == 0 else 64, 64)
                line = jnp.where(flags[1], plane[56:], plane[:8])
            else:
                line = half(rows(B_LINES - 16 + 16 * a, 16), 1)
            add_line(cells, (base + a + 1) * 10 + pads[1], line)
    elif kind == (0, 0, 1):
        for a in range(8):
            line = half(rows(C_LINES + 16 * a, 16), 2)
            halo[side, base + a + 1, 8:16, :] = halo[side, base + a + 1, 8:16, :] + line
    elif kind == (1, 1, 0):
        plane = rows(pl.multiple_of(take[0] * 64, 64), 64)
        line = jnp.where(flags[1], plane[56:], plane[:8])
        add_line(cells, (base + pads[0]) * 10 + pads[1], line)
    elif kind == (1, 0, 1):
        line = half(rows(pl.multiple_of(C_LINES + 112 * take[0], 16), 16), 2)
        at = base + pads[0]
        halo[side, at, 8:16, :] = halo[side, at, 8:16, :] + line
    else:
        spot = pl.ds(jnp.where(flags[1], 7, 16), 1)
        planes = range(8) if kind == (0, 1, 1) else (None,)
        for a in planes:
            if a is None:
                line = half(rows(pl.multiple_of(C_LINES + 112 * take[0], 16), 16), 2)
                at = base + pads[0]
            else:
                line = half(rows(C_LINES + 16 * a, 16), 2)
                at = base + a + 1
            cell = jnp.where(flags[1], line[7:8], line[0:1])
            halo[side, at, spot, :] = halo[side, at, spot, :] + cell


def windows(cells, halo, cols, bricks):
    row = lax.broadcasted_iota(jnp.int32, (8, C), 0)

    def step(k, _):
        shifted = [[], [], []]
        for b in range(10):
            x = cells[k * 10 + b]
            before = halo[0, k, pl.ds(b + 7, 1), :]
            after = halo[1, k, pl.ds(b + 7, 1), :]
            shifted[0].append(jnp.where(row == 0, before, pltpu.roll(x, 1, 0)))
            shifted[1].append(x)
            shifted[2].append(jnp.where(row == 7, after, pltpu.roll(x, 7, 0)))
        for j in range(3):
            for l in range(3):
                block = jnp.concatenate(shifted[l][j : j + 8], axis=0).astype(BF16)
                at = (3 * j + l) * C
                cols[k, :, at : at + C] = block
        return 0

    lax.fori_loop(0, bricks * 10, step, 0)


def fetch(parts, share, sems):
    size = parts[0].shape[0]
    copies = [
        pltpu.make_async_copy(part, share.at[pl.ds(k * size, size)], sems.at[k])
        for k, part in enumerate(parts)
    ]
    for copy in copies:
        copy.start()
    return copies


def weight_grad_body(slots, factor, peers, count, *refs):
    recv, codes, place_of, behind, core, own_ref, cot_ref = refs[:7]
    parts = refs[7 : 7 + count]
    keep_ref, give_ref, cols, cells, halo, share, sums, sems, out_sems = refs[7 + count :]
    bricks = own_ref.shape[0] // 512
    copies = fetch(parts, share, sems)
    start_padded(own_ref, cells, halo, bricks)
    for copy in copies:
        copy.wait()
    for brick in range(bricks):
        for number, e in enumerate(DIRECTIONS):
            slot = recv[brick * 26 + number]
            safe = jnp.maximum(slot, 0)
            source = place_of[safe // slots] * bricks + codes[safe] // 6
            kind = tuple(abs(t) for t in e)
            place(kind, e, slot >= 0, source, brick, share, cells, halo)
    windows(cells, halo, cols, bricks)

    rows = 27 * C // peers
    mine = core[0]
    for tap in range(27):
        i, jl = divmod(tap, 9)
        total = None
        for brick in range(bricks):
            left = cols[brick * 10 + i : brick * 10 + i + 8, :, jl * C : jl * C + C].reshape(512, C)
            right = cot_ref[brick * 512 : brick * 512 + 512, :]
            term = lax.dot_general(left, right, (((0,), (0,)), ((), ())), preferred_element_type=F32)
            total = term if total is None else total + term
        total = total * factor
        start = tap * C
        while start < (tap + 1) * C:
            owner = start // rows
            stop = min((tap + 1) * C, (owner + 1) * rows)
            piece = total[start - tap * C : stop - tap * C]
            bucket = jnp.bitwise_xor(mine, owner % 2)
            where = slice(start - owner * rows, stop - owner * rows)
            sums[bucket, behind[owner // 2], where, :] = piece
            start = stop
    keep_copy = pltpu.make_async_copy(sums.at[0], keep_ref, out_sems.at[0])
    keep_copy.start()
    half = sums.shape[1]

    def narrow(k, _):
        give_ref[k] = sums[1, k].astype(BF16)
        return 0

    lax.fori_loop(0, half, narrow, 0)
    keep_copy.wait()


def tap_sum(cols, weight_ref, brick):
    total = None
    for i in range(3):
        left = cols[brick * 10 + i : brick * 10 + i + 8].reshape(512, 9 * C)
        right = weight_ref[i * 9 * C : (i + 1) * 9 * C, :]
        term = jnp.dot(left, right, preferred_element_type=F32)
        total = term if total is None else total + term
    return total


def mix_body(cols, weight_ref, x_ref, out_ref):
    for brick in range(x_ref.shape[0] // 512):
        at = slice(brick * 512, brick * 512 + 512)
        out_ref[at, :] = (x_ref[at, :].astype(F32) + tap_sum(cols, weight_ref, brick)).astype(BF16)


def input_grad_body(slots, count, *refs):
    returned, code_here, place_of, cot_ref, weight_ref, x_ref, gain_ref = refs[:7]
    parts = refs[7 : 7 + count]
    out_ref, cells, halo, cols, share, sems = refs[7 + count :]
    bricks = cot_ref.shape[0] // 512
    copies = fetch(parts, share, sems)
    start_padded(cot_ref, cells, halo, bricks)
    for copy in copies:
        copy.wait()

    def one(k, _):
        info = returned[k]

        @pl.when(info > 0)
        def _():
            entry = info - 1
            brick = code_here[k] // 6
            source = place_of[k // slots] * bricks + entry // 26
            number = 25 - entry % 26
            tap = jnp.where(number >= 13, number + 1, number)
            e = (tap // 9 - 1, (tap // 3) % 3 - 1, tap % 3 - 1)
            on = [t != 0 for t in e]
            for kind in ((1, 0, 0), (0, 1, 0), (0, 0, 1), (1, 1, 0), (1, 0, 1), (0, 1, 1), (1, 1, 1)):
                match = functools.reduce(
                    jnp.logical_and, [f if w else jnp.logical_not(f) for f, w in zip(on, kind)]
                )

                @pl.when(match)
                def _():
                    place(kind, e, None, source, brick, share, cells, halo)

        return 0

    lax.fori_loop(0, returned.shape[0], one, 0)
    windows(cells, halo, cols, bricks)
    gain = gain_ref[...]
    for brick in range(bricks):
        at = slice(brick * 512, brick * 512 + 512)
        grad = tap_sum(cols, weight_ref, brick)
        x = x_ref[at, :].astype(F32)
        inverse = lax.rsqrt(jnp.mean(x * x, axis=-1, keepdims=True) + 1e-6)
        unit = x * inverse
        v = unit * gain
        gate = 1.0 / (1.0 + jnp.exp(-v))
        grad = grad * (gate * (1.0 + v * (1.0 - gate))) * gain
        grad = inverse * (grad - unit * jnp.mean(grad * unit, axis=-1, keepdims=True))
        out_ref[at, :] = (cot_ref[at, :].astype(F32) + grad).astype(BF16)


def local(features, norm_gain, conv_weight, recv_slot, send_face, cotangent):
    channels = features.shape[1]
    per_device = features.shape[0]
    bricks = per_device // 512
    peers = lax.axis_size("morton")
    slots = send_face.shape[1] // peers
    factor = 1.0 / math.sqrt(peers * per_device)
    gain = norm_gain.reshape(1, channels)
    sds = jax.ShapeDtypeStruct
    stage = pltpu.VMEM((2, 64, 128), F32)
    padded = [
        pltpu.VMEM((bricks * 100, 8, channels), F32),
        pltpu.VMEM((2, bricks * 10, HB, channels), F32),
    ]
    cols_shape = (bricks * 10, 64, 9 * channels)
    conv_flops = 2 * per_device * 27 * channels * channels

    me = lax.axis_index("morton")
    behind_all, place_all = ring_tables(peers)
    behind = jnp.asarray(behind_all)[me]
    place_of = jnp.asarray(place_all)[me]
    core = (me % 2).astype(jnp.int32).reshape(1)

    recv = recv_slot.reshape(-1)
    order = jnp.arange(peers * slots, dtype=jnp.int32)
    numbers = jnp.arange(1, bricks * 26 + 1, dtype=jnp.int32)
    served = jnp.sum(jnp.where(recv[:, None] == order[None, :], numbers[:, None], 0), axis=0)
    notes = jnp.concatenate([send_face, served.astype(jnp.int32)[None]], axis=0)
    notes = lax.all_gather(notes, "morton", axis=0, tiled=False)
    notes = lax.dynamic_slice_in_dim(notes, me * slots, slots, 2)
    codes = notes[:, 0].reshape(-1)
    returned = notes[:, 1].reshape(-1)

    hidden, share = call(
        norm_body,
        (sds((per_device, channels), BF16), sds((bricks, ROWS, channels), BF16)),
        [VMEM, VMEM],
        [stage],
        name="norm",
    )(features, gain)
    hidden_parts = gather_ring(share, peers)

    cot_share = call(
        extract_body,
        sds((bricks, ROWS, channels), BF16),
        [VMEM],
        [stage],
        name="extract",
    )(cotangent)
    cot_share, _ = lax.optimization_barrier((cot_share, hidden_parts[len(hidden_parts) // 4]))
    cot_parts = gather_ring(cot_share, peers)

    gathered = [
        pltpu.VMEM((peers * bricks, ROWS, channels), BF16),
        pltpu.SemaphoreType.DMA((len(hidden_parts),)),
    ]
    rows = 27 * channels // peers
    keep, give, cols = call(
        functools.partial(weight_grad_body, slots, factor, peers, len(hidden_parts)),
        (
            sds((peers // 2, rows, channels), F32),
            sds((peers // 2, rows, channels), BF16),
            sds(cols_shape, BF16),
        ),
        [SMEM] * 5 + [VMEM] * 2 + [ANY] * len(hidden_parts),
        padded
        + gathered[:1]
        + [pltpu.VMEM((2, peers // 2, rows, channels), F32)]
        + gathered[1:]
        + [pltpu.SemaphoreType.DMA((1,))],
        flops=conv_flops,
        nbytes=2**24,
        name="weight_grad",
        out_specs=(ANY, VMEM, VMEM),
    )(recv, codes, place_of, behind, core, hidden, cotangent, *hidden_parts)
    grad_weight = scatter_ring(keep, give, peers)

    mixed = call(
        mix_body,
        sds((per_device, channels), BF16),
        [VMEM, VMEM, VMEM],
        flops=conv_flops,
        nbytes=2**23,
        name="mix",
    )(cols, conv_weight, features)

    turned = conv_weight.reshape(27, channels, channels)[::-1].transpose(0, 2, 1)
    grad_features = call(
        functools.partial(input_grad_body, slots, len(cot_parts)),
        sds((per_device, channels), BF16),
        [SMEM] * 3 + [VMEM] * 4 + [ANY] * len(cot_parts),
        padded + [pltpu.VMEM(cols_shape, BF16)] + gathered,
        flops=conv_flops,
        nbytes=2**24,
        name="input_grad",
    )(
        returned,
        send_face.reshape(-1),
        place_of,
        cotangent,
        turned.reshape(27 * channels, channels),
        features,
        gain,
        *cot_parts,
    )
    return (mixed, grad_features, grad_weight)


def solution(mesh):
    rows = P(("groups", "morton"), None)
    return jax.shard_map(
        local,
        mesh=mesh,
        in_specs=(rows, P(), P(), rows, rows, rows),
        out_specs=(rows, rows, rows),
        check_vma=False,
    )
```

```python
import functools
import math

import jax
import jax.numpy as jnp
import numpy as np
from jax import lax
from jax.experimental import pallas as pl
from jax.experimental.pallas import tpu as pltpu
from jax.sharding import PartitionSpec as P

F32 = jnp.float32
BF16 = jnp.bfloat16
C = 256
C_LINES = 128
B_LINES = 224
ROWS = 320
NOTES = 16
HB = 24
VMEM_LIMIT = 40 * 1024 * 1024
DIRECTIONS = [
    (i, j, l)
    for i in (-1, 0, 1)
    for j in (-1, 0, 1)
    for l in (-1, 0, 1)
    if (i, j, l) != (0, 0, 0)
]

VMEM = pl.BlockSpec(memory_space=pltpu.VMEM)
SMEM = pl.BlockSpec(memory_space=pltpu.SMEM)
ANY = pl.BlockSpec(memory_space=pl.ANY)


def ring_order(chips):
    if chips == 8:
        return [0, 2, 4, 6, 7, 5, 3, 1]
    return list(range(chips))


def ring_tables(peers):
    chips = peers // 2
    spot = np.argsort(np.array(ring_order(chips)))
    device = np.arange(peers)
    behind = (spot[device // 2][:, None] - spot[None, :]) % chips
    place_of = behind[:, device // 2] + chips * (device[:, None] % 2 != device[None, :] % 2)
    if chips > 8:
        place_of = np.broadcast_to(device, (peers, peers))
    return np.concatenate([place_of, behind, device[:, None]], axis=1).astype(np.int32)


def ring_step(x, peers, step):
    order = ring_order(peers // 2)
    pairs = [
        (2 * order[i] + core, 2 * order[(i + step) % len(order)] + core)
        for i in range(len(order))
        for core in range(2)
    ]
    return lax.ppermute(x, "morton", pairs)


def swap_cores(x, peers):
    return lax.ppermute(x, "morton", [(m, m ^ 1) for m in range(peers)])


def gather_ring(x, peers, step, after):
    chips = peers // 2
    if chips > 8:
        got = lax.all_gather(x[None], "morton", axis=0, tiled=True)
        return [got], ([got] * 4, [got] * 4)
    got = {0: x}
    hops = []
    for way, count, gate in ((step, chips // 2, after[0]), (-step, (chips - 1) // 2, after[1])):
        held = x if gate is None else lax.optimization_barrier((x, gate))[0]
        hops.append([])
        for hop in range(1, count + 1):
            held = ring_step(held, peers, way)
            hops[-1].append(held)
            got[(way * hop) % chips] = held
    mine = [got[k] for k in range(chips)]
    return [t[None] for t in mine + [swap_cores(t, peers) for t in mine]], hops


def scatter_ring(keep, give, peers):
    chips = peers // 2
    other = swap_cores(give, peers)

    def term(k):
        return keep[k] + other[k].astype(F32)

    ups, downs = chips // 2, (chips - 1) // 2
    total = term(0)
    for count, step in ((ups, 1), (downs, -1)):
        held = None
        for hop in range(count, 0, -1):
            part = term((-step * hop) % chips)
            if held is not None:
                part = part + held.astype(F32)
            held = ring_step(part.astype(BF16), peers, step)
        if held is not None:
            total = total + held.astype(F32)
    return total


def call(body, out_shape, in_specs, scratch=(), flops=0, nbytes=0, name=None, out_specs=None):
    return pl.pallas_call(
        body,
        out_shape=out_shape,
        in_specs=in_specs,
        out_specs=out_specs or jax.tree.map(lambda _: VMEM, out_shape),
        scratch_shapes=list(scratch),
        compiler_params=pltpu.CompilerParams(vmem_limit_bytes=VMEM_LIMIT),
        cost_estimate=pl.CostEstimate(flops=flops, bytes_accessed=nbytes, transcendentals=0),
        name=name,
    )


def put_boundary(rows, brick, a, out_ref, stage):
    wide = rows.astype(F32)
    base = brick * ROWS

    def put(at, value, lanes=slice(None)):
        out_ref[pl.ds(pl.multiple_of(base + at, 16), value.shape[0]), lanes] = value

    for edge, at in ((0, 0), (7, 64)):

        @pl.when(a == edge)
        def _():
            put(at, rows)

    @pl.when((a > 0) & (a < 7))
    def _():
        for half in range(2):
            lanes = slice(half * 128, half * 128 + 128)
            stage[half] = wide[:, lanes]
            first = stage[half, pl.ds(0, 8, stride=8), :]
            last = stage[half, pl.ds(7, 8, stride=8), :]
            put(C_LINES - 16 + 16 * a, jnp.concatenate([first, last], axis=0).astype(BF16), lanes)
        pair = jnp.concatenate([wide[:8], wide[56:]], axis=0).astype(BF16)
        put(B_LINES - 16 + 16 * a, pair)


def norm_body(recv, send, x_ref, gain_ref, hidden_ref, out_ref, stage):
    bricks, directions = recv.shape
    gain = gain_ref[...]
    row = lax.broadcasted_iota(jnp.int32, (NOTES, C), 0)
    lane = lax.broadcasted_iota(jnp.int32, (NOTES, C), 1)
    notes = jnp.zeros((NOTES, C), jnp.int32)
    for k in range(send.shape[1]):
        notes = jnp.where((row == 0) & (lane == k), send[0, k], notes)
    for brick in range(bricks):
        for number in range(directions):
            serves = (row == 1) & (lane == recv[brick, number])
            notes = jnp.where(serves, brick * directions + number + 1, notes)
    out_ref[bricks * ROWS :, :] = notes.astype(F32).astype(BF16)

    def step(k, _):
        at = pl.ds(pl.multiple_of(k * 64, 64), 64)
        x = x_ref[at, :].astype(F32)
        inverse = lax.rsqrt(jnp.mean(x * x, axis=-1, keepdims=True) + 1e-6)
        v = x * inverse * gain
        rows = (v / (1.0 + jnp.exp(-v))).astype(BF16)
        hidden_ref[at, :] = rows
        put_boundary(rows, k // 8, k % 8, out_ref, stage)
        return 0

    lax.fori_loop(0, bricks * 8, step, 0)


def extract_body(x_ref, out_ref, stage):
    def step(k, _):
        at = pl.ds(pl.multiple_of(k * 64, 64), 64)
        put_boundary(x_ref[at, :], k // 8, k % 8, out_ref, stage)
        return 0

    lax.fori_loop(0, x_ref.shape[0] // 64, step, 0)


def start_padded(own_ref, cells, halo, bricks):
    zero = jnp.zeros((8, C), F32)

    def clear(k, _):
        for b in range(10):
            cells[k * 10 + b] = zero
        for side in range(2):
            for part in range(HB // 8):
                halo[side, k, part * 8 : part * 8 + 8, :] = zero
        return 0

    lax.fori_loop(0, bricks * 10, clear, 0)

    def fill(k, _):
        plane = (k // 8) * 10 + k % 8 + 1
        rows = own_ref[pl.ds(pl.multiple_of(k * 64, 64), 64), :].astype(F32)
        for b in range(8):
            cells[plane * 10 + b + 1] = rows[b * 8 : b * 8 + 8]
        return 0

    lax.fori_loop(0, bricks * 8, fill, 0)


def add_line(ref, index, line):
    ref[index] = ref[index] + line


def pick(flag, yes, no):
    if isinstance(flag, bool):
        return yes if flag else no
    return jnp.where(flag, yes, no)


def place(kind, e, keep, place_at, source_brick, brick, share, cells, halo):
    flags = [t == -1 for t in e]
    pads = [pick(f, 0, 9) for f in flags]
    facing = pick(flags[0], 64, 0)
    start = source_brick * ROWS

    def rows(at, size):
        got = share[place_at, pl.ds(pl.multiple_of(start + at, 16), size), :].astype(F32)
        return got if keep is None else jnp.where(keep, got, 0.0)

    def half(pair, axis):
        return pick(flags[axis], pair[8:], pair[:8])

    def line_b(at):
        plane = rows(at, 64)
        return pick(flags[1], plane[56:], plane[:8])

    def line_c(at):
        plane = rows(at, 64)
        ends = [
            pick(flags[2], plane[8 * b + 7 : 8 * b + 8], plane[8 * b : 8 * b + 1]) for b in range(8)
        ]
        return jnp.concatenate(ends, axis=0)

    def cell(at):
        line = line_b(at)
        return pick(flags[2], line[7:8], line[0:1])

    side = pick(flags[2], 0, 1)
    base = brick * 10

    def add_halo(at, line):
        halo[side, base + at, 8:16, :] = halo[side, base + at, 8:16, :] + line

    def add_cell(at, value):
        spot = pl.ds(pick(flags[1], 7, 16), 1)
        halo[side, base + at, spot, :] = halo[side, base + at, spot, :] + value

    if kind == (1, 0, 0):
        got = rows(facing, 64)
        first = (base + pads[0]) * 10 + 1
        for b in range(8):
            add_line(cells, first + b, got[b * 8 : b * 8 + 8])
    elif kind == (0, 1, 0):
        for a in range(8):
            if a in (0, 7):
                line = line_b(0 if a == 0 else 64)
            else:
                line = half(rows(B_LINES - 16 + 16 * a, 16), 1)
            add_line(cells, (base + a + 1) * 10 + pads[1], line)
    elif kind == (0, 0, 1):
        for a in range(8):
            if a in (0, 7):
                line = line_c(0 if a == 0 else 64)
            else:
                line = half(rows(C_LINES - 16 + 16 * a, 16), 2)
            add_halo(a + 1, line)
    elif kind == (1, 1, 0):
        add_line(cells, (base + pads[0]) * 10 + pads[1], line_b(facing))
    elif kind == (1, 0, 1):
        add_halo(pads[0], line_c(facing))
    elif kind == (0, 1, 1):
        for a in range(8):
            if a in (0, 7):
                value = cell(0 if a == 0 else 64)
            else:
                line = half(rows(C_LINES - 16 + 16 * a, 16), 2)
                value = pick(flags[1], line[7:8], line[0:1])
            add_cell(a + 1, value)
    else:
        add_cell(pads[0], cell(facing))


def windows(cells, halo, cols, bricks):
    row = lax.broadcasted_iota(jnp.int32, (8, C), 0)

    def step(k, _):
        shifted = [[], [], []]
        for b in range(10):
            x = cells[k * 10 + b]
            before = halo[0, k, pl.ds(b + 7, 1), :]
            after = halo[1, k, pl.ds(b + 7, 1), :]
            shifted[0].append(jnp.where(row == 0, before, pltpu.roll(x, 1, 0)))
            shifted[1].append(x)
            shifted[2].append(jnp.where(row == 7, after, pltpu.roll(x, 7, 0)))
        for j in range(3):
            for l in range(3):
                block = jnp.concatenate(shifted[l][j : j + 8], axis=0).astype(BF16)
                at = (3 * j + l) * C
                cols[k, :, at : at + C] = block
        return 0

    lax.fori_loop(0, bricks * 10, step, 0)


def fetch(parts, share, sems):
    size = parts[0].shape[0]
    copies = [
        pltpu.make_async_copy(part, share.at[pl.ds(k * size, size)], sems.at[k])
        for k, part in enumerate(parts)
    ]
    for copy in copies:
        copy.start()
    return copies


def pad_body(slots, peers, count, *refs):
    recv, table, own_ref = refs[:3]
    parts = refs[3 : 3 + count]
    cols, codes_ref, served_ref = refs[-9:-6]
    cells, halo, share, codes, sems, codes_sem = refs[-6:]
    bricks = own_ref.shape[0] // 512
    me = table[peers + peers // 2]
    copies = fetch(parts, share, sems)
    start_padded(own_ref, cells, halo, bricks)
    for copy in copies:
        copy.wait()
    for k in range(peers):
        notes = share[k, bricks * ROWS :, :].astype(F32).astype(jnp.int32)
        codes_ref[k : k + 1, :] = notes[0:1]
        served_ref[k : k + 1, :] = notes[1:2]
    codes_copy = pltpu.make_async_copy(codes_ref, codes, codes_sem.at[0])
    codes_copy.start()
    codes_copy.wait()
    for brick in range(bricks):
        for number, e in enumerate(DIRECTIONS):
            slot = recv[brick, number]
            safe = jnp.maximum(slot, 0)
            sender = safe // slots
            at = table[sender]
            code = codes[at, me * slots + safe - sender * slots]
            kind = tuple(abs(t) for t in e)
            place(kind, e, slot >= 0, at, code // 6, brick, share, cells, halo)
    windows(cells, halo, cols, bricks)


def weight_grad_body(factor, peers, *refs):
    table, cols, cot_ref = refs[:3]
    keep_ref, give_ref, sums, turned, sem = refs[-5:]
    bricks = cot_ref.shape[0] // 512
    rows = 27 * C // peers
    mine = table[peers + peers // 2] % 2
    for part in range(bricks * 2):
        at = slice(part * 256, part * 256 + 256)
        turned[:, at] = cot_ref[at, :].astype(F32).T.astype(BF16)
    for tap in range(27):
        i, jl = divmod(tap, 9)
        total = None
        for brick in range(bricks):
            right = cols[brick * 10 + i : brick * 10 + i + 8, :, jl * C : jl * C + C].reshape(512, C)
            left = turned[:, brick * 512 : brick * 512 + 512]
            term = jnp.dot(left, right, preferred_element_type=F32)
            total = term if total is None else total + term
        total = (total * factor).T
        start = tap * C
        while start < (tap + 1) * C:
            owner = start // rows
            stop = min((tap + 1) * C, (owner + 1) * rows)
            piece = total[start - tap * C : stop - tap * C]
            bucket = jnp.bitwise_xor(mine, owner % 2)
            where = slice(start - owner * rows, stop - owner * rows)
            sums[bucket, table[peers + owner // 2], where, :] = piece
            start = stop
    keep_copy = pltpu.make_async_copy(sums.at[0], keep_ref, sem.at[0])
    keep_copy.start()

    def narrow(k, _):
        give_ref[k] = sums[1, k].astype(BF16)
        return 0

    lax.fori_loop(0, sums.shape[1], narrow, 0)
    keep_copy.wait()


def tap_sum(cols, weight_ref, brick):
    total = None
    for i in range(3):
        left = cols[brick * 10 + i : brick * 10 + i + 8].reshape(512, 9 * C)
        right = weight_ref[i * 9 * C : (i + 1) * 9 * C, :]
        term = jnp.dot(left, right, preferred_element_type=F32)
        total = term if total is None else total + term
    return total


def mix_body(cols, weight_ref, x_ref, out_ref):
    for brick in range(x_ref.shape[0] // 512):
        at = slice(brick * 512, brick * 512 + 512)
        out_ref[at, :] = (x_ref[at, :].astype(F32) + tap_sum(cols, weight_ref, brick)).astype(BF16)


def input_grad_body(slots, peers, here, count, *refs):
    served, send, table, cot_ref, weight_ref, x_ref, gain_ref = refs[:7]
    parts = refs[7 : 7 + count]
    out_ref, cells, halo, cols, share, sems = refs[7 + count :]
    me = table[peers + peers // 2]
    copies = fetch(parts, share, sems)
    start_padded(cot_ref, cells, halo, 1)
    for copy in copies:
        copy.wait()

    def one(k, _):
        receiver = k // slots
        at = table[receiver]
        info = served[at, me * slots + k - receiver * slots]

        @pl.when((info > 0) & (send[0, k] // 6 == here))
        def _():
            entry = info - 1
            number = 25 - entry % 26
            tap = jnp.where(number >= 13, number + 1, number)
            e = (tap // 9 - 1, (tap // 3) % 3 - 1, tap % 3 - 1)
            on = [t != 0 for t in e]
            for kind in ((1, 0, 0), (0, 1, 0), (0, 0, 1), (1, 1, 0), (1, 0, 1), (0, 1, 1), (1, 1, 1)):
                match = functools.reduce(
                    jnp.logical_and, [f if w else jnp.logical_not(f) for f, w in zip(on, kind)]
                )

                @pl.when(match)
                def _():
                    place(kind, e, None, at, entry // 26, 0, share, cells, halo)

        return 0

    lax.fori_loop(0, send.shape[1], one, 0)
    windows(cells, halo, cols, 1)
    grad = tap_sum(cols, weight_ref, 0)
    x = x_ref[...].astype(F32)
    gain = gain_ref[...]
    inverse = lax.rsqrt(jnp.mean(x * x, axis=-1, keepdims=True) + 1e-6)
    unit = x * inverse
    v = unit * gain
    gate = 1.0 / (1.0 + jnp.exp(-v))
    grad = grad * (gate * (1.0 + v * (1.0 - gate))) * gain
    grad = inverse * (grad - unit * jnp.mean(grad * unit, axis=-1, keepdims=True))
    out_ref[...] = (cot_ref[...].astype(F32) + grad).astype(BF16)


def local(features, norm_gain, conv_weight, recv_slot, send_face, cotangent):
    channels = features.shape[1]
    per_device = features.shape[0]
    bricks = per_device // 512
    peers = lax.axis_size("morton")
    slots = send_face.shape[1] // peers
    factor = 1.0 / math.sqrt(peers * per_device)
    gain = norm_gain.reshape(1, channels)
    sds = jax.ShapeDtypeStruct
    stage = pltpu.VMEM((2, 64, 128), F32)

    def padded(n):
        return [
            pltpu.VMEM((n * 100, 8, channels), F32),
            pltpu.VMEM((2, n * 10, HB, channels), F32),
        ]

    def cols_shape(n):
        return (n * 10, 64, 9 * channels)

    conv_flops = 2 * per_device * 27 * channels * channels

    table = jnp.asarray(ring_tables(peers))[lax.axis_index("morton")]

    hidden, share = call(
        norm_body,
        (sds((per_device, channels), BF16), sds((bricks * ROWS + NOTES, channels), BF16)),
        [SMEM, SMEM, VMEM, VMEM],
        [stage],
        name="norm",
    )(recv_slot, send_face, features, gain)
    hidden_parts, hidden_hops = gather_ring(share, peers, 1, (None, None))

    cot_share = call(
        extract_body,
        sds((bricks * ROWS, channels), BF16),
        [VMEM],
        [stage],
        name="extract",
    )(cotangent)
    gates = (hidden_hops[1][-1], hidden_hops[0][-1])
    cot_parts, (far, near) = gather_ring(cot_share, peers, -1, gates)
    turned = conv_weight.reshape(27, channels, channels)[::-1].transpose(0, 2, 1)
    turned = turned.reshape(27 * channels, channels)
    hidden, turned = lax.optimization_barrier((hidden, turned))

    count = len(hidden_parts)
    rows = 27 * channels // peers
    cols, _, served = call(
        functools.partial(pad_body, slots, peers, count),
        (
            sds(cols_shape(bricks), BF16),
            sds((peers, channels), jnp.int32),
            sds((peers, channels), jnp.int32),
        ),
        [SMEM] * 2 + [VMEM] + [ANY] * (count + 1),
        padded(bricks)
        + [
            pltpu.VMEM((peers, bricks * ROWS + NOTES, channels), BF16),
            pltpu.SMEM((peers, channels), jnp.int32),
            pltpu.SemaphoreType.DMA((count,)),
            pltpu.SemaphoreType.DMA((1,)),
        ],
        flops=conv_flops,
        nbytes=2**24,
        name="pad",
    )(recv_slot, table, hidden, *hidden_parts, far[0])
    keep, give = call(
        functools.partial(weight_grad_body, factor, peers),
        (
            sds((peers // 2, rows, channels), F32),
            sds((peers // 2, rows, channels), BF16),
        ),
        [SMEM] + [VMEM] * 2,
        [
            pltpu.VMEM((2, peers // 2, rows, channels), F32),
            pltpu.VMEM((channels, per_device), BF16),
            pltpu.SemaphoreType.DMA((1,)),
        ],
        flops=conv_flops,
        nbytes=2**24,
        name="weight_grad",
        out_specs=(ANY, VMEM),
    )(table, cols, cotangent)
    give = lax.optimization_barrier((give, far[2], near[1]))[0]
    grad_weight = scatter_ring(keep, give, peers)

    mixed = call(
        mix_body,
        sds((per_device, channels), BF16),
        [VMEM, VMEM, VMEM],
        flops=conv_flops,
        nbytes=2**23,
        name="mix",
    )(cols, conv_weight, features)

    grads = []
    for brick in range(bricks):
        at = slice(brick * 512, brick * 512 + 512)
        grads.append(
            call(
                functools.partial(input_grad_body, slots, peers, brick, count),
                sds((512, channels), BF16),
                [SMEM] * 3 + [VMEM] * 4 + [ANY] * count,
                padded(1)
                + [
                    pltpu.VMEM(cols_shape(1), BF16),
                    pltpu.VMEM((peers, bricks * ROWS, channels), BF16),
                    pltpu.SemaphoreType.DMA((count,)),
                ],
                flops=conv_flops // bricks,
                nbytes=2**24,
                name="input_grad_" + str(brick),
            )(served, send_face, table, cotangent[at], turned, features[at], gain, *cot_parts)
        )
    return (mixed, jnp.concatenate(grads, axis=0), grad_weight)


def solution(mesh):
    rows = P(("groups", "morton"), None)
    return jax.shard_map(
        local,
        mesh=mesh,
        in_specs=(rows, P(), P(), rows, rows, rows),
        out_specs=(rows, rows, rows),
        check_vma=False,
    )
```

```python
import functools
import math

import jax
import jax.numpy as jnp
import numpy as np
from jax import lax
from jax.experimental import pallas as pl
from jax.experimental.pallas import tpu as pltpu
from jax.sharding import PartitionSpec as P

F32 = jnp.float32
BF16 = jnp.bfloat16
C = 256
C_LINES = 128
B_LINES = 224
ROWS = 320
NOTES = 16
HB = 24
VMEM_LIMIT = 56 * 1024 * 1024
DIRECTIONS = [
    (i, j, l)
    for i in (-1, 0, 1)
    for j in (-1, 0, 1)
    for l in (-1, 0, 1)
    if (i, j, l) != (0, 0, 0)
]

VMEM = pl.BlockSpec(memory_space=pltpu.VMEM)
SMEM = pl.BlockSpec(memory_space=pltpu.SMEM)
ANY = pl.BlockSpec(memory_space=pl.ANY)
HBM = pl.BlockSpec(memory_space=pltpu.HBM)


def ring_order(chips):
    if chips == 8:
        return [0, 2, 4, 6, 7, 5, 3, 1]
    return list(range(chips))


def ring_tables(peers):
    chips = peers // 2
    spot = np.argsort(np.array(ring_order(chips)))
    device = np.arange(peers)
    behind = (spot[device // 2][:, None] - spot[None, :]) % chips
    place_of = behind[:, device // 2] + chips * (device[:, None] % 2 != device[None, :] % 2)
    if chips > 8:
        place_of = np.broadcast_to(device, (peers, peers))
    return np.concatenate([place_of, behind, device[:, None]], axis=1).astype(np.int32)


def ring_step(x, peers, step):
    order = ring_order(peers // 2)
    pairs = [
        (2 * order[i] + core, 2 * order[(i + step) % len(order)] + core)
        for i in range(len(order))
        for core in range(2)
    ]
    return lax.ppermute(x, "morton", pairs)


def swap_cores(x, peers):
    return lax.ppermute(x, "morton", [(m, m ^ 1) for m in range(peers)])


class RingGather:
    def __init__(self, x, peers, step):
        self.x, self.peers, self.chips = x, peers, peers // 2
        self.whole = None
        if self.chips > 8:
            self.whole = lax.all_gather(x[None], "morton", axis=0, tiled=True)
        self.steps = (step, -step)
        self.counts = (self.chips // 2, (self.chips - 1) // 2)
        self.hops = ([], [])

    def go(self, way, gate=None):
        hops = self.hops[way]
        if self.whole is not None or len(hops) == self.counts[way]:
            return
        held = hops[-1] if hops else self.x
        if gate is not None:
            held = lax.optimization_barrier((held, gate))[0]
        hops.append(ring_step(held, self.peers, self.steps[way]))

    def last(self, way):
        return self.x if self.whole is not None else self.hops[way][-1]

    def places(self, gate=None):
        if self.whole is not None:
            return [self.whole]
        got = {0: self.x}
        for hops, step in zip(self.hops, self.steps):
            for number, held in enumerate(hops):
                got[(step * (number + 1)) % self.chips] = held
        mine = [got[k] for k in range(self.chips)]
        held = mine
        if gate is not None:
            held = [lax.optimization_barrier((t, gate))[0] for t in mine]
        return [t[None] for t in mine + [swap_cores(t, self.peers) for t in held]]


def scatter_ring(keep, give, peers):
    chips = peers // 2
    other = swap_cores(give, peers)

    def term(k):
        return keep[k] + other[k].astype(F32)

    ups, downs = chips // 2, (chips - 1) // 2
    total = term(0)
    for count, step in ((ups, 1), (downs, -1)):
        held = None
        for hop in range(count, 0, -1):
            part = term((-step * hop) % chips)
            if held is not None:
                part = part + held.astype(F32)
            held = ring_step(part.astype(BF16), peers, step)
        if held is not None:
            total = total + held.astype(F32)
    return total


def call(body, out_shape, in_specs, scratch=(), cost=2, name=None, out_specs=None):
    return pl.pallas_call(
        body,
        out_shape=out_shape,
        in_specs=in_specs,
        out_specs=out_specs or jax.tree.map(lambda _: VMEM, out_shape),
        scratch_shapes=list(scratch),
        compiler_params=pltpu.CompilerParams(vmem_limit_bytes=VMEM_LIMIT),
        cost_estimate=pl.CostEstimate(flops=cost * 10**9, bytes_accessed=0, transcendentals=0),
        name=name,
    )


def put_boundary(rows, brick, a, out_ref, stage):
    wide = rows.astype(F32)
    base = brick * ROWS

    def put(at, value, lanes=slice(None)):
        out_ref[pl.ds(pl.multiple_of(base + at, 16), value.shape[0]), lanes] = value

    for edge, at in ((0, 0), (7, 64)):

        @pl.when(a == edge)
        def _():
            put(at, rows)

    @pl.when((a > 0) & (a < 7))
    def _():
        for half in range(2):
            lanes = slice(half * 128, half * 128 + 128)
            stage[half] = wide[:, lanes]
            first = stage[half, pl.ds(0, 8, stride=8), :]
            last = stage[half, pl.ds(7, 8, stride=8), :]
            put(C_LINES - 16 + 16 * a, jnp.concatenate([first, last], axis=0).astype(BF16), lanes)
        pair = jnp.concatenate([wide[:8], wide[56:]], axis=0).astype(BF16)
        put(B_LINES - 16 + 16 * a, pair)


def norm_body(recv, send, x_ref, gain_ref, hidden_ref, out_ref, stage):
    bricks, directions = recv.shape
    gain = gain_ref[...]
    row = lax.broadcasted_iota(jnp.int32, (NOTES, C), 0)
    lane = lax.broadcasted_iota(jnp.int32, (NOTES, C), 1)
    notes = jnp.zeros((NOTES, C), jnp.int32)
    for k in range(send.shape[1]):
        notes = jnp.where((row == 0) & (lane == k), send[0, k], notes)
    for brick in range(bricks):
        for number in range(directions):
            serves = (row == 1) & (lane == recv[brick, number])
            notes = jnp.where(serves, brick * directions + number + 1, notes)
    out_ref[bricks * ROWS :, :] = notes.astype(F32).astype(BF16)

    def step(k, _):
        at = pl.ds(pl.multiple_of(k * 64, 64), 64)
        x = x_ref[at, :].astype(F32)
        inverse = lax.rsqrt(jnp.mean(x * x, axis=-1, keepdims=True) + 1e-6)
        v = x * inverse * gain
        rows = (v / (1.0 + jnp.exp(-v))).astype(BF16)
        hidden_ref[at, :] = rows
        put_boundary(rows, k // 8, k % 8, out_ref, stage)
        return 0

    lax.fori_loop(0, bricks * 8, step, 0)


def extract_body(x_ref, out_ref, stage):
    def step(k, _):
        at = pl.ds(pl.multiple_of(k * 64, 64), 64)
        put_boundary(x_ref[at, :], k // 8, k % 8, out_ref, stage)
        return 0

    lax.fori_loop(0, x_ref.shape[0] // 64, step, 0)


def start_padded(own_ref, cells, halo, bricks):
    zero = jnp.zeros((8, C), F32)

    def clear(k, _):
        for b in range(10):
            cells[k * 10 + b] = zero
        for side in range(2):
            for part in range(HB // 8):
                halo[side, k, part * 8 : part * 8 + 8, :] = zero
        return 0

    lax.fori_loop(0, bricks * 10, clear, 0)

    def fill(k, _):
        plane = (k // 8) * 10 + k % 8 + 1
        rows = own_ref[pl.ds(pl.multiple_of(k * 64, 64), 64), :].astype(F32)
        for b in range(8):
            cells[plane * 10 + b + 1] = rows[b * 8 : b * 8 + 8]
        return 0

    lax.fori_loop(0, bricks * 8, fill, 0)


def add_line(ref, index, line):
    ref[index] = ref[index] + line


def pick(flag, yes, no):
    if isinstance(flag, bool):
        return yes if flag else no
    return jnp.where(flag, yes, no)


def place(kind, e, keep, place_at, source_brick, brick, share, cells, halo):
    flags = [t == -1 for t in e]
    pads = [pick(f, 0, 9) for f in flags]
    facing = pick(flags[0], 64, 0)
    start = source_brick * ROWS

    def rows(at, size):
        got = share[place_at, pl.ds(pl.multiple_of(start + at, 16), size), :].astype(F32)
        return got if keep is None else jnp.where(keep, got, 0.0)

    def half(pair, axis):
        return pick(flags[axis], pair[8:], pair[:8])

    def line_b(at):
        plane = rows(at, 64)
        return pick(flags[1], plane[56:], plane[:8])

    def line_c(at):
        plane = rows(at, 64)
        ends = [
            pick(flags[2], plane[8 * b + 7 : 8 * b + 8], plane[8 * b : 8 * b + 1]) for b in range(8)
        ]
        return jnp.concatenate(ends, axis=0)

    def cell(at):
        line = line_b(at)
        return pick(flags[2], line[7:8], line[0:1])

    side = pick(flags[2], 0, 1)
    base = brick * 10

    def add_halo(at, line):
        halo[side, base + at, 8:16, :] = halo[side, base + at, 8:16, :] + line

    def add_cell(at, value):
        spot = pl.ds(pick(flags[1], 7, 16), 1)
        halo[side, base + at, spot, :] = halo[side, base + at, spot, :] + value

    if kind == (1, 0, 0):
        got = rows(facing, 64)
        first = (base + pads[0]) * 10 + 1
        for b in range(8):
            add_line(cells, first + b, got[b * 8 : b * 8 + 8])
    elif kind == (0, 1, 0):
        for a in range(8):
            if a in (0, 7):
                line = line_b(0 if a == 0 else 64)
            else:
                line = half(rows(B_LINES - 16 + 16 * a, 16), 1)
            add_line(cells, (base + a + 1) * 10 + pads[1], line)
    elif kind == (0, 0, 1):
        for a in range(8):
            if a in (0, 7):
                line = line_c(0 if a == 0 else 64)
            else:
                line = half(rows(C_LINES - 16 + 16 * a, 16), 2)
            add_halo(a + 1, line)
    elif kind == (1, 1, 0):
        add_line(cells, (base + pads[0]) * 10 + pads[1], line_b(facing))
    elif kind == (1, 0, 1):
        add_halo(pads[0], line_c(facing))
    elif kind == (0, 1, 1):
        for a in range(8):
            if a in (0, 7):
                value = cell(0 if a == 0 else 64)
            else:
                line = half(rows(C_LINES - 16 + 16 * a, 16), 2)
                value = pick(flags[1], line[7:8], line[0:1])
            add_cell(a + 1, value)
    else:
        add_cell(pads[0], cell(facing))


def windows(cells, halo, cols, bricks):
    row = lax.broadcasted_iota(jnp.int32, (8, C), 0)

    def step(k, _):
        shifted = [[], [], []]
        for b in range(10):
            x = cells[k * 10 + b]
            before = halo[0, k, pl.ds(b + 7, 1), :]
            after = halo[1, k, pl.ds(b + 7, 1), :]
            shifted[0].append(jnp.where(row == 0, before, pltpu.roll(x, 1, 0)))
            shifted[1].append(x)
            shifted[2].append(jnp.where(row == 7, after, pltpu.roll(x, 7, 0)))
        for j in range(3):
            for l in range(3):
                block = jnp.concatenate(shifted[l][j : j + 8], axis=0).astype(BF16)
                at = (3 * j + l) * C
                cols[k, :, at : at + C] = block
        return 0

    lax.fori_loop(0, bricks * 10, step, 0)


def fetch(parts, share, sems):
    size = parts[0].shape[0]
    copies = [
        pltpu.make_async_copy(part, share.at[pl.ds(k * size, size)], sems.at[k])
        for k, part in enumerate(parts)
    ]
    for copy in copies:
        copy.start()
    return copies


def pad_body(slots, peers, count, *refs):
    recv, table, own_ref = refs[:3]
    parts = refs[3 : 3 + count]
    cols, codes_ref, served_ref = refs[-9:-6]
    cells, halo, share, codes, sems, codes_sem = refs[-6:]
    bricks = own_ref.shape[0] // 512
    me = table[peers + peers // 2]
    copies = fetch(parts, share, sems)
    start_padded(own_ref, cells, halo, bricks)
    for copy in copies:
        copy.wait()
    for k in range(peers):
        notes = share[k, bricks * ROWS :, :].astype(F32).astype(jnp.int32)
        codes_ref[k : k + 1, :] = notes[0:1]
        served_ref[k : k + 1, :] = notes[1:2]
    codes_copy = pltpu.make_async_copy(codes_ref, codes, codes_sem.at[0])
    codes_copy.start()
    codes_copy.wait()
    for brick in range(bricks):
        for number, e in enumerate(DIRECTIONS):
            slot = recv[brick, number]
            safe = jnp.maximum(slot, 0)
            sender = safe // slots
            at = table[sender]
            code = codes[at, me * slots + safe - sender * slots]
            kind = tuple(abs(t) for t in e)
            place(kind, e, slot >= 0, at, code // 6, brick, share, cells, halo)
    windows(cells, halo, cols, bricks)


def weight_grad_body(factor, peers, *refs):
    table, cols, cot_ref = refs[:3]
    keep_ref, give_ref, sums, turned, sem = refs[-5:]
    bricks = cot_ref.shape[0] // 512
    rows = 27 * C // peers
    mine = table[peers + peers // 2] % 2
    for part in range(bricks * 2):
        at = slice(part * 256, part * 256 + 256)
        turned[:, at] = cot_ref[at, :].astype(F32).T.astype(BF16)
    for tap in range(27):
        i, jl = divmod(tap, 9)
        total = None
        for brick in range(bricks):
            right = cols[brick * 10 + i : brick * 10 + i + 8, :, jl * C : jl * C + C].reshape(512, C)
            left = turned[:, brick * 512 : brick * 512 + 512]
            term = jnp.dot(left, right, preferred_element_type=F32)
            total = term if total is None else total + term
        total = (total * factor).T
        start = tap * C
        while start < (tap + 1) * C:
            owner = start // rows
            stop = min((tap + 1) * C, (owner + 1) * rows)
            piece = total[start - tap * C : stop - tap * C]
            bucket = jnp.bitwise_xor(mine, owner % 2)
            where = slice(start - owner * rows, stop - owner * rows)
            sums[bucket, table[peers + owner // 2], where, :] = piece
            start = stop
    keep_copy = pltpu.make_async_copy(sums.at[0], keep_ref, sem.at[0])
    keep_copy.start()

    def narrow(k, _):
        give_ref[k] = sums[1, k].astype(BF16)
        return 0

    lax.fori_loop(0, sums.shape[1], narrow, 0)
    keep_copy.wait()


def tap_sum(cols, weight_ref, brick):
    total = None
    for i in range(3):
        left = cols[brick * 10 + i : brick * 10 + i + 8].reshape(512, 9 * C)
        right = weight_ref[i * 9 * C : (i + 1) * 9 * C, :]
        term = jnp.dot(left, right, preferred_element_type=F32)
        total = term if total is None else total + term
    return total


def mix_body(cols, weight_ref, x_ref, out_ref):
    for brick in range(x_ref.shape[0] // 512):
        at = slice(brick * 512, brick * 512 + 512)
        out_ref[at, :] = (x_ref[at, :].astype(F32) + tap_sum(cols, weight_ref, brick)).astype(BF16)


def input_grad_body(slots, peers, here, count, *refs):
    served, send, table, cot_ref, weight_ref, x_ref, gain_ref = refs[:7]
    parts = refs[7 : 7 + count]
    out_ref, cells, halo, cols, share, sems = refs[7 + count :]
    me = table[peers + peers // 2]
    copies = fetch(parts, share, sems)
    start_padded(cot_ref, cells, halo, 1)
    for copy in copies:
        copy.wait()

    def one(k, _):
        receiver = k // slots
        at = table[receiver]
        info = served[at, me * slots + k - receiver * slots]

        @pl.when((info > 0) & (send[0, k] // 6 == here))
        def _():
            entry = info - 1
            number = 25 - entry % 26
            tap = jnp.where(number >= 13, number + 1, number)
            e = (tap // 9 - 1, (tap // 3) % 3 - 1, tap % 3 - 1)
            on = [t != 0 for t in e]
            for kind in ((1, 0, 0), (0, 1, 0), (0, 0, 1), (1, 1, 0), (1, 0, 1), (0, 1, 1), (1, 1, 1)):
                match = functools.reduce(
                    jnp.logical_and, [f if w else jnp.logical_not(f) for f, w in zip(on, kind)]
                )

                @pl.when(match)
                def _():
                    place(kind, e, None, at, entry // 26, 0, share, cells, halo)

        return 0

    lax.fori_loop(0, send.shape[1], one, 0)
    windows(cells, halo, cols, 1)
    grad = tap_sum(cols, weight_ref, 0)
    x = x_ref[...].astype(F32)
    gain = gain_ref[...]
    inverse = lax.rsqrt(jnp.mean(x * x, axis=-1, keepdims=True) + 1e-6)
    unit = x * inverse
    v = unit * gain
    gate = 1.0 / (1.0 + jnp.exp(-v))
    grad = grad * (gate * (1.0 + v * (1.0 - gate))) * gain
    grad = inverse * (grad - unit * jnp.mean(grad * unit, axis=-1, keepdims=True))
    out_ref[...] = (cot_ref[...].astype(F32) + grad).astype(BF16)


def local(features, norm_gain, conv_weight, recv_slot, send_face, cotangent):
    channels = features.shape[1]
    per_device = features.shape[0]
    bricks = per_device // 512
    peers = lax.axis_size("morton")
    slots = send_face.shape[1] // peers
    factor = 1.0 / math.sqrt(peers * per_device)
    gain = norm_gain.reshape(1, channels)
    sds = jax.ShapeDtypeStruct
    stage = pltpu.VMEM((2, 64, 128), F32)

    def padded(n):
        return [
            pltpu.VMEM((n * 100, 8, channels), F32),
            pltpu.VMEM((2, n * 10, HB, channels), F32),
        ]

    def cols_shape(n):
        return (n * 10, 64, 9 * channels)


    table = jnp.asarray(ring_tables(peers))[lax.axis_index("morton")]

    hidden, share = call(
        norm_body,
        (sds((per_device, channels), BF16), sds((bricks * ROWS + NOTES, channels), BF16)),
        [SMEM, SMEM, VMEM, VMEM],
        [stage],
        name="norm",
    )(recv_slot, send_face, features, gain)
    hidden_ring = RingGather(share, peers, 1)
    for way in (0, 0, 0, 0, 1, 1, 1):
        hidden_ring.go(way)
    hidden_parts = hidden_ring.places()

    cot_share = call(
        extract_body,
        sds((bricks * ROWS, channels), BF16),
        [VMEM],
        [stage],
        name="extract",
    )(cotangent)
    turned = conv_weight.reshape(27, channels, channels)[::-1].transpose(0, 2, 1)
    turned = turned.reshape(27 * channels, channels)
    cot_share, turned = lax.optimization_barrier((cot_share, turned))
    cot_ring = RingGather(cot_share, peers, -1)
    cot_ring.go(0, hidden_ring.last(1))
    first = cot_ring.last(0)
    cot_ring.go(1, hidden_ring.last(0))
    cot_ring.go(0)

    count = len(hidden_parts)
    rows = 27 * channels // peers
    cols, _, served = call(
        functools.partial(pad_body, slots, peers, count),
        (
            sds(cols_shape(bricks), BF16),
            sds((peers, channels), jnp.int32),
            sds((peers, channels), jnp.int32),
        ),
        [SMEM] * 2 + [VMEM] + [HBM] * (count + 1),
        padded(bricks)
        + [
            pltpu.VMEM((peers, bricks * ROWS + NOTES, channels), BF16),
            pltpu.SMEM((peers, channels), jnp.int32),
            pltpu.SemaphoreType.DMA((count,)),
            pltpu.SemaphoreType.DMA((1,)),
        ],
        cost=6,
        name="pad",
    )(recv_slot, table, hidden, *hidden_parts, first)
    cot_ring.go(1, cols)
    cot_ring.go(0, cols)
    keep, give = call(
        functools.partial(weight_grad_body, factor, peers),
        (
            sds((peers // 2, rows, channels), F32),
            sds((peers // 2, rows, channels), BF16),
        ),
        [SMEM] + [VMEM] * 2,
        [
            pltpu.VMEM((2, peers // 2, rows, channels), F32),
            pltpu.VMEM((channels, per_device), BF16),
            pltpu.SemaphoreType.DMA((1,)),
        ],
        cost=6,
        name="weight_grad",
        out_specs=(ANY, VMEM),
    )(table, cols, cotangent)
    mixed = call(
        mix_body,
        sds((per_device, channels), BF16),
        [VMEM, VMEM, VMEM],
        cost=5,
        name="mix",
    )(cols, conv_weight, features)

    cot_ring.go(1, give)
    cot_ring.go(0, give)
    cot_parts = cot_ring.places(cols)
    give = lax.optimization_barrier((give, mixed, *cot_parts))[0]
    grad_weight = scatter_ring(keep, give, peers)

    grads = []
    for brick in range(bricks):
        at = slice(brick * 512, brick * 512 + 512)
        grads.append(
            call(
                functools.partial(input_grad_body, slots, peers, brick, count),
                sds((512, channels), BF16),
                [SMEM] * 3 + [VMEM] * 4 + [HBM] * count,
                padded(1)
                + [
                    pltpu.VMEM(cols_shape(1), BF16),
                    pltpu.VMEM((peers, bricks * ROWS, channels), BF16),
                    pltpu.SemaphoreType.DMA((count,)),
                ],
                cost=8,
                name="input_grad_" + str(brick),
            )(served, send_face, table, cotangent[at], turned, features[at], gain, *cot_parts)
        )
    return (mixed, jnp.concatenate(grads, axis=0), grad_weight)


def solution(mesh):
    rows = P(("groups", "morton"), None)
    return jax.shard_map(
        local,
        mesh=mesh,
        in_specs=(rows, P(), P(), rows, rows, rows),
        out_specs=(rows, rows, rows),
        check_vma=False,
    )
```

```python
import functools
import math

import jax
import jax.numpy as jnp
import numpy as np
from jax import lax
from jax.experimental import pallas as pl
from jax.experimental.pallas import tpu as pltpu
from jax.sharding import PartitionSpec as P

F32 = jnp.float32
BF16 = jnp.bfloat16
C = 256
C_LINES = 128
B_LINES = 224
ROWS = 320
NOTES = 16
HB = 24
VMEM_LIMIT = 56 * 1024 * 1024
DIRECTIONS = [
    (i, j, l)
    for i in (-1, 0, 1)
    for j in (-1, 0, 1)
    for l in (-1, 0, 1)
    if (i, j, l) != (0, 0, 0)
]

VMEM = pl.BlockSpec(memory_space=pltpu.VMEM)
SMEM = pl.BlockSpec(memory_space=pltpu.SMEM)
ANY = pl.BlockSpec(memory_space=pl.ANY)
HBM = pl.BlockSpec(memory_space=pltpu.HBM)


def ring_order(chips):
    if chips == 8:
        return [0, 2, 4, 6, 7, 5, 3, 1]
    return list(range(chips))


def ring_tables(peers):
    chips = peers // 2
    spot = np.argsort(np.array(ring_order(chips)))
    device = np.arange(peers)
    behind = (spot[device // 2][:, None] - spot[None, :]) % chips
    place_of = behind[:, device // 2] + chips * (device[:, None] % 2 != device[None, :] % 2)
    if chips > 8:
        place_of = np.broadcast_to(device, (peers, peers))
    half = chips // 2
    turn = np.where(behind >= half, 2 * (behind - half), 2 * (half - 1 - behind) + 1)
    return np.concatenate([place_of, behind, turn, device[:, None]], axis=1).astype(np.int32)


def ring_step(x, peers, step):
    order = ring_order(peers // 2)
    pairs = [
        (2 * order[i] + core, 2 * order[(i + step) % len(order)] + core)
        for i in range(len(order))
        for core in range(2)
    ]
    return lax.ppermute(x, "morton", pairs)


def swap_cores(x, peers):
    return lax.ppermute(x, "morton", [(m, m ^ 1) for m in range(peers)])


class RingGather:
    def __init__(self, x, peers, step):
        self.x, self.peers, self.chips = x, peers, peers // 2
        self.whole = None
        if self.chips > 8:
            self.whole = lax.all_gather(x[None], "morton", axis=0, tiled=True)
        self.steps = (step, -step)
        self.counts = (self.chips // 2, (self.chips - 1) // 2)
        self.hops = ([], [])

    def go(self, way, gate=None):
        hops = self.hops[way]
        if self.whole is not None or len(hops) == self.counts[way]:
            return
        held = hops[-1] if hops else self.x
        if gate is not None:
            held = lax.optimization_barrier((held, gate))[0]
        hops.append(ring_step(held, self.peers, self.steps[way]))

    def last(self, way):
        return self.x if self.whole is not None else self.hops[way][-1]

    def places(self, gate=None):
        if self.whole is not None:
            return [self.whole]
        got = {0: self.x}
        for hops, step in zip(self.hops, self.steps):
            for number, held in enumerate(hops):
                got[(step * (number + 1)) % self.chips] = held
        mine = [got[k] for k in range(self.chips)]
        held = mine
        if gate is not None:
            held = [lax.optimization_barrier((t, gate))[0] for t in mine]
        return [t[None] for t in mine + [swap_cores(t, self.peers) for t in held]]


def scatter_ring(keep, give, peers, gates):
    chips = peers // 2
    half = chips // 2
    other = [swap_cores(t, peers) for t in give]

    def term(k):
        pair = other[k - half][0] if k >= half else other[half - 1 - k][1]
        return keep[k] + pair.astype(F32)

    ups, downs = chips // 2, (chips - 1) // 2
    total = term(0)
    for count, step in ((ups, 1), (downs, -1)):
        held = None
        for hop in range(count, 0, -1):
            part = term((-step * hop) % chips)
            if held is not None:
                part = part + held.astype(F32)
            part = part.astype(BF16)
            if count - hop < len(gates) and gates[count - hop] is not None:
                part = lax.optimization_barrier((part, gates[count - hop]))[0]
            held = ring_step(part, peers, step)
        if held is not None:
            total = total + held.astype(F32)
    return total


def call(body, out_shape, in_specs, scratch=(), cost=2, name=None, out_specs=None, aliases=None):
    return pl.pallas_call(
        body,
        out_shape=out_shape,
        in_specs=in_specs,
        out_specs=out_specs or jax.tree.map(lambda _: VMEM, out_shape),
        scratch_shapes=list(scratch),
        input_output_aliases=aliases or {},
        compiler_params=pltpu.CompilerParams(vmem_limit_bytes=VMEM_LIMIT),
        cost_estimate=pl.CostEstimate(flops=cost * 10**9, bytes_accessed=0, transcendentals=0),
        name=name,
    )


def put_boundary(rows, brick, a, out_ref, stage):
    wide = rows.astype(F32)
    base = brick * ROWS

    def put(at, value, lanes=slice(None)):
        out_ref[pl.ds(pl.multiple_of(base + at, 16), value.shape[0]), lanes] = value

    for edge, at in ((0, 0), (7, 64)):

        @pl.when(a == edge)
        def _():
            put(at, rows)

    @pl.when((a > 0) & (a < 7))
    def _():
        for half in range(2):
            lanes = slice(half * 128, half * 128 + 128)
            stage[half] = wide[:, lanes]
            first = stage[half, pl.ds(0, 8, stride=8), :]
            last = stage[half, pl.ds(7, 8, stride=8), :]
            put(C_LINES - 16 + 16 * a, jnp.concatenate([first, last], axis=0).astype(BF16), lanes)
        pair = jnp.concatenate([wide[:8], wide[56:]], axis=0).astype(BF16)
        put(B_LINES - 16 + 16 * a, pair)


def norm_body(recv, send, x_ref, gain_ref, hidden_ref, out_ref, stage):
    bricks, directions = recv.shape
    gain = gain_ref[...]
    row = lax.broadcasted_iota(jnp.int32, (NOTES, C), 0)
    lane = lax.broadcasted_iota(jnp.int32, (NOTES, C), 1)
    notes = jnp.zeros((NOTES, C), jnp.int32)
    for k in range(send.shape[1]):
        notes = jnp.where((row == 0) & (lane == k), send[0, k], notes)
    for brick in range(bricks):
        for number in range(directions):
            serves = (row == 1) & (lane == recv[brick, number])
            notes = jnp.where(serves, brick * directions + number + 1, notes)
    out_ref[bricks * ROWS :, :] = notes.astype(F32).astype(BF16)

    def step(k, _):
        at = pl.ds(pl.multiple_of(k * 64, 64), 64)
        x = x_ref[at, :].astype(F32)
        inverse = lax.rsqrt(jnp.mean(x * x, axis=-1, keepdims=True) + 1e-6)
        v = x * inverse * gain
        rows = (v / (1.0 + jnp.exp(-v))).astype(BF16)
        hidden_ref[at, :] = rows
        put_boundary(rows, k // 8, k % 8, out_ref, stage)
        return 0

    lax.fori_loop(0, bricks * 8, step, 0)


def extract_body(x_ref, out_ref, stage):
    def step(k, _):
        at = pl.ds(pl.multiple_of(k * 64, 64), 64)
        put_boundary(x_ref[at, :], k // 8, k % 8, out_ref, stage)
        return 0

    lax.fori_loop(0, x_ref.shape[0] // 64, step, 0)


def start_padded(own_ref, cells, halo, bricks):
    zero = jnp.zeros((8, C), F32)

    def clear(k, _):
        for b in range(10):
            cells[k * 10 + b] = zero
        for side in range(2):
            for part in range(HB // 8):
                halo[side, k, part * 8 : part * 8 + 8, :] = zero
        return 0

    lax.fori_loop(0, bricks * 10, clear, 0)

    def fill(k, _):
        plane = (k // 8) * 10 + k % 8 + 1
        rows = own_ref[pl.ds(pl.multiple_of(k * 64, 64), 64), :].astype(F32)
        for b in range(8):
            cells[plane * 10 + b + 1] = rows[b * 8 : b * 8 + 8]
        return 0

    lax.fori_loop(0, bricks * 8, fill, 0)


def add_line(ref, index, line):
    ref[index] = ref[index] + line


def pick(flag, yes, no):
    if isinstance(flag, bool):
        return yes if flag else no
    return jnp.where(flag, yes, no)


def place(kind, e, keep, place_at, source_brick, brick, share, cells, halo):
    flags = [t == -1 for t in e]
    pads = [pick(f, 0, 9) for f in flags]
    facing = pick(flags[0], 64, 0)
    start = source_brick * ROWS

    def rows(at, size):
        got = share[place_at, pl.ds(pl.multiple_of(start + at, 16), size), :].astype(F32)
        return got if keep is None else jnp.where(keep, got, 0.0)

    def half(pair, axis):
        return pick(flags[axis], pair[8:], pair[:8])

    def line_b(at):
        plane = rows(at, 64)
        return pick(flags[1], plane[56:], plane[:8])

    def line_c(at):
        plane = rows(at, 64)
        ends = [
            pick(flags[2], plane[8 * b + 7 : 8 * b + 8], plane[8 * b : 8 * b + 1]) for b in range(8)
        ]
        return jnp.concatenate(ends, axis=0)

    def cell(at):
        line = line_b(at)
        return pick(flags[2], line[7:8], line[0:1])

    side = pick(flags[2], 0, 1)
    base = brick * 10

    def add_halo(at, line):
        halo[side, base + at, 8:16, :] = halo[side, base + at, 8:16, :] + line

    def add_cell(at, value):
        spot = pl.ds(pick(flags[1], 7, 16), 1)
        halo[side, base + at, spot, :] = halo[side, base + at, spot, :] + value

    if kind == (1, 0, 0):
        got = rows(facing, 64)
        first = (base + pads[0]) * 10 + 1
        for b in range(8):
            add_line(cells, first + b, got[b * 8 : b * 8 + 8])
    elif kind == (0, 1, 0):
        for a in range(8):
            if a in (0, 7):
                line = line_b(0 if a == 0 else 64)
            else:
                line = half(rows(B_LINES - 16 + 16 * a, 16), 1)
            add_line(cells, (base + a + 1) * 10 + pads[1], line)
    elif kind == (0, 0, 1):
        for a in range(8):
            if a in (0, 7):
                line = line_c(0 if a == 0 else 64)
            else:
                line = half(rows(C_LINES - 16 + 16 * a, 16), 2)
            add_halo(a + 1, line)
    elif kind == (1, 1, 0):
        add_line(cells, (base + pads[0]) * 10 + pads[1], line_b(facing))
    elif kind == (1, 0, 1):
        add_halo(pads[0], line_c(facing))
    elif kind == (0, 1, 1):
        for a in range(8):
            if a in (0, 7):
                value = cell(0 if a == 0 else 64)
            else:
                line = half(rows(C_LINES - 16 + 16 * a, 16), 2)
                value = pick(flags[1], line[7:8], line[0:1])
            add_cell(a + 1, value)
    else:
        add_cell(pads[0], cell(facing))


def windows(cells, halo, cols, out, sems, bricks):
    row = lax.broadcasted_iota(jnp.int32, (8, C), 0)

    def step(k, _):
        shifted = [[], [], []]
        for b in range(10):
            x = cells[k * 10 + b]
            before = halo[0, k, pl.ds(b + 7, 1), :]
            after = halo[1, k, pl.ds(b + 7, 1), :]
            shifted[0].append(jnp.where(row == 0, before, pltpu.roll(x, 1, 0)))
            shifted[1].append(x)
            shifted[2].append(jnp.where(row == 7, after, pltpu.roll(x, 7, 0)))
        for j in range(3):
            for l in range(3):
                block = jnp.concatenate(shifted[l][j : j + 8], axis=0).astype(BF16)
                at = (3 * j + l) * C
                cols[k, :, at : at + C] = block
        pltpu.make_async_copy(cols.at[k], out.at[k], sems.at[k]).start()
        return 0

    lax.fori_loop(0, bricks * 10, step, 0)


def wait_windows(cols, out, sems, bricks):
    def step(k, _):
        pltpu.make_async_copy(cols.at[k], out.at[k], sems.at[k]).wait()
        return 0

    lax.fori_loop(0, bricks * 10, step, 0)


def fetch(parts, share, sems):
    size = parts[0].shape[0]
    copies = [
        pltpu.make_async_copy(part, share.at[pl.ds(k * size, size)], sems.at[k])
        for k, part in enumerate(parts)
    ]
    for copy in copies:
        copy.start()
    return copies


def weight_grad_body(slots, factor, peers, count, *refs):
    recv, table, own_ref, cot_ref = refs[:4]
    parts = refs[4 : 4 + count]
    keep_ref = refs[5 + count]
    give_refs = refs[6 + count : 6 + count + peers // 4]
    out_cols, codes_ref, served_ref = refs[-15:-12]
    cells, halo, share, cols, sums, narrow, turned, codes = refs[-12:-4]
    sems, cols_sems, codes_sem, out_sems = refs[-4:]
    bricks = own_ref.shape[0] // 512
    me = table[2 * peers]
    copies = fetch(parts, share, sems)
    start_padded(own_ref, cells, halo, bricks)
    for part in range(bricks * 2):
        at = slice(part * 256, part * 256 + 256)
        turned[:, at] = cot_ref[at, :].astype(F32).T.astype(BF16)
    for copy in copies:
        copy.wait()
    for k in range(peers):
        notes = share[k, bricks * ROWS :, :].astype(F32).astype(jnp.int32)
        codes_ref[k : k + 1, :] = notes[0:1]
        served_ref[k : k + 1, :] = notes[1:2]
    codes_copy = pltpu.make_async_copy(codes_ref, codes, codes_sem.at[0])
    codes_copy.start()
    codes_copy.wait()
    for brick in range(bricks):
        for number, e in enumerate(DIRECTIONS):
            slot = recv[brick, number]
            safe = jnp.maximum(slot, 0)
            sender = safe // slots
            at = table[sender]
            code = codes[at, me * slots + safe - sender * slots]
            kind = tuple(abs(t) for t in e)
            place(kind, e, slot >= 0, at, code // 6, brick, share, cells, halo)
    windows(cells, halo, cols, out_cols, cols_sems, bricks)

    rows = 27 * C // peers
    for tap in range(27):
        i, jl = divmod(tap, 9)
        total = None
        for brick in range(bricks):
            right = cols[brick * 10 + i : brick * 10 + i + 8, :, jl * C : jl * C + C].reshape(512, C)
            left = turned[:, brick * 512 : brick * 512 + 512]
            term = jnp.dot(left, right, preferred_element_type=F32)
            total = term if total is None else total + term
        total = (total * factor).T
        start = tap * C
        while start < (tap + 1) * C:
            owner = start // rows
            stop = min((tap + 1) * C, (owner + 1) * rows)
            piece = total[start - tap * C : stop - tap * C]
            bucket = jnp.bitwise_xor(me % 2, owner % 2)
            behind = table[peers + owner // 2]
            where = slice(start - owner * rows, stop - owner * rows)
            sums[bucket, behind, where, :] = piece
            narrow[bucket, behind, where, :] = piece.astype(BF16)
            start = stop
            if stop == (owner + 1) * rows:

                @pl.when(bucket == 0)
                def _():
                    pltpu.make_async_copy(
                        sums.at[0, behind], keep_ref.at[behind], out_sems.at[0, behind]
                    ).start()

                turn = table[peers + peers // 2 + owner // 2]
                for hop, give_ref in enumerate(give_refs):

                    @pl.when((bucket == 1) & (turn // 2 == hop))
                    def _():
                        pltpu.make_async_copy(
                            narrow.at[1, behind], give_ref.at[turn % 2], out_sems.at[1, turn]
                        ).start()

    for k in range(peers // 2):
        pltpu.make_async_copy(sums.at[0, k], keep_ref.at[k], out_sems.at[0, k]).wait()
        pltpu.make_async_copy(narrow.at[1, k], give_refs[k // 2].at[k % 2], out_sems.at[1, k]).wait()
    wait_windows(cols, out_cols, cols_sems, bricks)


GROUP = 3 * C


def start_stream(cols_ref, first, cols, weight_ref, weight, sems):
    copies = []
    planes = cols.shape[0]
    for g in range(3):
        lanes = pl.ds(g * GROUP, GROUP)
        group = [
            pltpu.make_async_copy(
                cols_ref.at[pl.ds(first, planes), :, lanes], cols.at[:, :, lanes], sems.at[g, 3]
            )
        ]
        for i in range(3):
            at = pl.ds((i * 3 + g) * GROUP, GROUP)
            group.append(pltpu.make_async_copy(weight_ref.at[at], weight.at[at], sems.at[g, i]))
        copies.append(group)
    for group in copies:
        for copy in group:
            copy.start()
    return copies


def tap_sum(copies, cols, weight):
    bricks = cols.shape[0] // 10
    totals = [None] * bricks
    for g in range(3):
        for copy in copies[g]:
            copy.wait()
        for brick in range(bricks):
            for i in range(3):
                at = brick * 10 + i
                left = cols[at : at + 8, :, g * GROUP : g * GROUP + GROUP].reshape(512, GROUP)
                right = weight[(i * 3 + g) * GROUP : (i * 3 + g + 1) * GROUP, :]
                term = jnp.dot(left, right, preferred_element_type=F32)
                totals[brick] = term if totals[brick] is None else totals[brick] + term
    return totals


def mix_body(cols_ref, weight_ref, x_ref, out_ref, cols, weight, sems):
    copies = start_stream(cols_ref, 0, cols, weight_ref, weight, sems)
    for brick, total in enumerate(tap_sum(copies, cols, weight)):
        at = slice(brick * 512, brick * 512 + 512)
        out_ref[at, :] = (x_ref[at, :].astype(F32) + total).astype(BF16)


def cot_pad_body(slots, peers, count, *refs):
    served, send, table, cot_ref = refs[:4]
    parts = refs[4 : 4 + count]
    out_cols, cells, halo, cols, share, sems, cols_sems = refs[4 + count :]
    bricks = cot_ref.shape[0] // 512
    me = table[2 * peers]
    copies = fetch(parts, share, sems)
    start_padded(cot_ref, cells, halo, bricks)
    for copy in copies:
        copy.wait()

    def one(k, _):
        receiver = k // slots
        at = table[receiver]
        info = served[at, me * slots + k - receiver * slots]

        @pl.when(info > 0)
        def _():
            entry = info - 1
            brick = send[0, k] // 6
            number = 25 - entry % 26
            tap = jnp.where(number >= 13, number + 1, number)
            e = (tap // 9 - 1, (tap // 3) % 3 - 1, tap % 3 - 1)
            on = [t != 0 for t in e]
            for kind in ((1, 0, 0), (0, 1, 0), (0, 0, 1), (1, 1, 0), (1, 0, 1), (0, 1, 1), (1, 1, 1)):
                match = functools.reduce(
                    jnp.logical_and, [f if w else jnp.logical_not(f) for f, w in zip(on, kind)]
                )

                @pl.when(match)
                def _():
                    place(kind, e, None, at, entry // 26, brick, share, cells, halo)

        return 0

    lax.fori_loop(0, send.shape[1], one, 0)
    windows(cells, halo, cols, out_cols, cols_sems, bricks)
    wait_windows(cols, out_cols, cols_sems, bricks)


def input_grad_body(here, *refs):
    cols_ref, weight_ref, cot_ref, x_ref, gain_ref = refs[:5]
    out_ref, cols, weight, rows, sems, row_sem = refs[-6:]
    copies = start_stream(cols_ref, here * 10, cols, weight_ref, weight, sems)
    at = slice(here * 512, here * 512 + 512)
    x = x_ref[at, :].astype(F32)
    gain = gain_ref[...]
    inverse = lax.rsqrt(jnp.mean(x * x, axis=-1, keepdims=True) + 1e-6)
    (grad,) = tap_sum(copies, cols, weight)
    unit = x * inverse
    v = unit * gain
    gate = 1.0 / (1.0 + jnp.exp(-v))
    grad = grad * (gate * (1.0 + v * (1.0 - gate))) * gain
    grad = inverse * (grad - unit * jnp.mean(grad * unit, axis=-1, keepdims=True))
    rows[...] = (cot_ref[at, :].astype(F32) + grad).astype(BF16)
    copy = pltpu.make_async_copy(rows, out_ref.at[pl.ds(here * 512, 512)], row_sem.at[0])
    copy.start()
    copy.wait()


def local(features, norm_gain, conv_weight, recv_slot, send_face, cotangent):
    channels = features.shape[1]
    per_device = features.shape[0]
    bricks = per_device // 512
    peers = lax.axis_size("morton")
    slots = send_face.shape[1] // peers
    factor = 1.0 / math.sqrt(peers * per_device)
    gain = norm_gain.reshape(1, channels)
    sds = jax.ShapeDtypeStruct
    stage = pltpu.VMEM((2, 64, 128), F32)

    def padded(n):
        return [
            pltpu.VMEM((n * 100, 8, channels), F32),
            pltpu.VMEM((2, n * 10, HB, channels), F32),
        ]

    def cols_shape(n):
        return (n * 10, 64, 9 * channels)


    table = jnp.asarray(ring_tables(peers))[lax.axis_index("morton")]

    hidden, share = call(
        norm_body,
        (sds((per_device, channels), BF16), sds((bricks * ROWS + NOTES, channels), BF16)),
        [SMEM, SMEM, VMEM, VMEM],
        [stage],
        name="norm",
    )(recv_slot, send_face, features, gain)
    cot_share = call(
        extract_body,
        sds((bricks * ROWS, channels), BF16),
        [VMEM],
        [stage],
        name="extract",
    )(cotangent)
    turned = conv_weight.reshape(27, channels, channels)[::-1].transpose(0, 2, 1)
    turned = turned.reshape(27 * channels, channels)

    hidden_ring = RingGather(share, peers, 1)
    hidden_ring.go(0)
    hidden_ring.go(1)
    hidden_ring.go(0, (cot_share, turned))
    hidden_ring.go(1, (cot_share, turned))
    for way in (0, 1, 0):
        hidden_ring.go(way)
    hidden_parts = hidden_ring.places()

    cot_ring = RingGather(cot_share, peers, -1)
    cot_ring.go(0, hidden_ring.last(1))
    first = cot_ring.last(0)
    cot_ring.go(1, hidden_ring.last(0))
    cot_ring.go(0)

    count = len(hidden_parts)
    rows = 27 * channels // peers
    chips = peers // 2
    keep, *give, cols, _, served = call(
        functools.partial(weight_grad_body, slots, factor, peers, count),
        (
            sds((chips, rows, channels), F32),
            *[sds((2, rows, channels), BF16)] * (chips // 2),
            sds(cols_shape(bricks), BF16),
            sds((peers, channels), jnp.int32),
            sds((peers, channels), jnp.int32),
        ),
        [SMEM] * 2 + [VMEM] * 2 + [HBM] * (count + 1),
        padded(bricks)
        + [
            pltpu.VMEM((peers, bricks * ROWS + NOTES, channels), BF16),
            pltpu.VMEM(cols_shape(bricks), BF16),
            pltpu.VMEM((2, chips, rows, channels), F32),
            pltpu.VMEM((2, chips, rows, channels), BF16),
            pltpu.VMEM((channels, per_device), BF16),
            pltpu.SMEM((peers, channels), jnp.int32),
            pltpu.SemaphoreType.DMA((count,)),
            pltpu.SemaphoreType.DMA((bricks * 10,)),
            pltpu.SemaphoreType.DMA((1,)),
            pltpu.SemaphoreType.DMA((2, chips)),
        ],
        cost=9,
        name="weight_grad",
        out_specs=(*[HBM] * (2 + chips // 2), VMEM, VMEM),
    )(recv_slot, table, hidden, cotangent, *hidden_parts, first)

    cot_ring.go(1, cols)
    cot_ring.go(0, cols)
    third = (cot_ring.last(0), cot_ring.last(1))
    weight_scratch = [
        pltpu.VMEM((27 * channels, channels), BF16),
        pltpu.SemaphoreType.DMA((3, 4)),
    ]
    mixed = call(
        mix_body,
        sds((per_device, channels), BF16),
        [HBM, HBM, VMEM],
        [pltpu.VMEM(cols_shape(bricks), BF16)] + weight_scratch,
        cost=6,
        name="mix",
    )(cols, conv_weight, features)
    cot_ring.go(1)
    cot_ring.go(0)
    fourth = (cot_ring.last(0), cot_ring.last(1))
    cot_parts = cot_ring.places(cols)

    cot_cols = call(
        functools.partial(cot_pad_body, slots, peers, count),
        sds(cols_shape(bricks), BF16),
        [SMEM] * 3 + [VMEM] + [HBM] * count,
        padded(bricks)
        + [
            pltpu.VMEM(cols_shape(bricks), BF16),
            pltpu.VMEM((peers, bricks * ROWS, channels), BF16),
            pltpu.SemaphoreType.DMA((count,)),
            pltpu.SemaphoreType.DMA((bricks * 10,)),
        ],
        cost=7,
        name="cot_pad",
        out_specs=HBM,
    )(served, send_face, table, cotangent, *cot_parts)

    grads = []
    for brick in range(bricks):
        grads.append(
            call(
                functools.partial(input_grad_body, brick),
                sds((per_device, channels), BF16),
                [HBM, HBM, VMEM, VMEM, VMEM] + [HBM] * len(grads[-1:]),
                [pltpu.VMEM(cols_shape(1), BF16)]
                + weight_scratch[:1]
                + [pltpu.VMEM((512, channels), BF16)]
                + weight_scratch[1:]
                + [pltpu.SemaphoreType.DMA((1,))],
                cost=5,
                name="input_grad_" + str(brick),
                out_specs=HBM,
                aliases={5: 0} if grads else None,
            )(cot_cols, turned, cotangent, features, gain, *grads[-1:])
        )
    gates = (None, fourth, cot_cols, grads[0])
    give = [lax.optimization_barrier((t, third, mixed))[0] for t in give]
    grad_weight = scatter_ring(keep, give, peers, gates)
    return (mixed, grads[-1], grad_weight)


def solution(mesh):
    rows = P(("groups", "morton"), None)
    return jax.shard_map(
        local,
        mesh=mesh,
        in_specs=(rows, P(), P(), rows, rows, rows),
        out_specs=(rows, rows, rows),
        check_vma=False,
    )
```

```python
import functools
import math

import jax
import jax.numpy as jnp
import numpy as np
from jax import lax
from jax.experimental import pallas as pl
from jax.experimental.pallas import tpu as pltpu
from jax.sharding import PartitionSpec as P

F32 = jnp.float32
BF16 = jnp.bfloat16
C = 256
C_LINES = 128
B_LINES = 224
ROWS = 320
NOTES = 16
HB = 24
VMEM_LIMIT = 56 * 1024 * 1024
DIRECTIONS = [
    (i, j, l)
    for i in (-1, 0, 1)
    for j in (-1, 0, 1)
    for l in (-1, 0, 1)
    if (i, j, l) != (0, 0, 0)
]

VMEM = pl.BlockSpec(memory_space=pltpu.VMEM)
SMEM = pl.BlockSpec(memory_space=pltpu.SMEM)
ANY = pl.BlockSpec(memory_space=pl.ANY)
HBM = pl.BlockSpec(memory_space=pltpu.HBM)


def ring_order(chips):
    if chips == 8:
        return [0, 2, 4, 6, 7, 5, 3, 1]
    return list(range(chips))


def ring_tables(peers):
    chips = peers // 2
    spot = np.argsort(np.array(ring_order(chips)))
    device = np.arange(peers)
    behind = (spot[device // 2][:, None] - spot[None, :]) % chips
    half = chips // 2
    turn = np.where(behind >= half, 2 * (behind - half), 2 * (half - 1 - behind) + 1)
    place_of = np.broadcast_to(device, (peers, peers)).copy()
    if chips <= 8:
        for me in range(peers):
            for other in range(peers):
                away = behind[me, other // 2] if me % 2 == 0 else -behind[me, other // 2] % chips
                same = me % 2 == other % 2
                if away == 0:
                    place = 0 if same else 1
                elif away < half or (away == half and same):
                    place = 1 + away if same else 1 + half + away
                else:
                    away = chips - away
                    place = half + (away if not same else half + away) + half
                place_of[me, other] = place
    return np.concatenate([place_of, behind, turn, device[:, None]], axis=1).astype(np.int32)


def ring_step(x, peers, step):
    order = ring_order(peers // 2)
    pairs = [
        (2 * order[i] + core, 2 * order[(i + (step or 1 - 2 * core)) % len(order)] + core)
        for i in range(len(order))
        for core in range(2)
    ]
    return lax.ppermute(x, "morton", pairs)


def swap_cores(x, peers):
    return lax.ppermute(x, "morton", [(m, m ^ 1) for m in range(peers)])


class RingGather:
    def __init__(self, x, peers, gate=None):
        self.x, self.peers, self.chips = x, peers, peers // 2
        self.whole = None
        if self.chips > 8:
            self.whole = lax.all_gather(x[None], "morton", axis=0, tiled=True)
            return
        if gate is not None:
            x = lax.optimization_barrier((x, gate))[0]
        self.chains = ([x], [swap_cores(x, peers)])

    def go(self, chain, gate=None):
        if self.whole is not None or len(self.chains[chain]) > self.chips // 2 - chain:
            return
        held = self.chains[chain][-1]
        if gate is not None:
            held = lax.optimization_barrier((held, gate))[0]
        self.chains[chain].append(ring_step(held, self.peers, 0))

    def last(self, chain):
        return self.x if self.whole is not None else self.chains[chain][-1]

    def places(self, gate=None):
        if self.whole is not None:
            return [self.whole]
        mine = self.chains[0][1:] + self.chains[1][1:]
        held = mine
        if gate is not None:
            held = [lax.optimization_barrier((t, gate))[0] for t in mine]
        others = [swap_cores(t, self.peers) for t in held]
        return [t[None] for t in [self.x, self.chains[1][0]] + mine + others]


def scatter_ring(keep, give, peers, gates):
    chips = peers // 2
    half = chips // 2
    other = [swap_cores(t, peers) for t in give]

    def term(k):
        pair = other[k - half][0] if k >= half else other[half - 1 - k][1]
        return keep[k] + pair.astype(F32)

    ups, downs = chips // 2, (chips - 1) // 2
    total = term(0)
    for count, step in ((ups, 1), (downs, -1)):
        held = None
        for hop in range(count, 0, -1):
            part = term((-step * hop) % chips)
            if held is not None:
                part = part + held.astype(F32)
            part = part.astype(BF16)
            if count - hop < len(gates) and gates[count - hop] is not None:
                part = lax.optimization_barrier((part, gates[count - hop]))[0]
            held = ring_step(part, peers, step)
        if held is not None:
            total = total + held.astype(F32)
    return total


def call(body, out_shape, in_specs, scratch=(), cost=2, name=None, out_specs=None, aliases=None):
    return pl.pallas_call(
        body,
        out_shape=out_shape,
        in_specs=in_specs,
        out_specs=out_specs or jax.tree.map(lambda _: VMEM, out_shape),
        scratch_shapes=list(scratch),
        input_output_aliases=aliases or {},
        compiler_params=pltpu.CompilerParams(vmem_limit_bytes=VMEM_LIMIT),
        cost_estimate=pl.CostEstimate(flops=cost * 10**9, bytes_accessed=0, transcendentals=0),
        name=name,
    )


def put_boundary(rows, brick, a, out_ref, stage):
    wide = rows.astype(F32)
    base = brick * ROWS

    def put(at, value, lanes=slice(None)):
        out_ref[pl.ds(pl.multiple_of(base + at, 16), value.shape[0]), lanes] = value

    for edge, at in ((0, 0), (7, 64)):

        @pl.when(a == edge)
        def _():
            put(at, rows)

    @pl.when((a > 0) & (a < 7))
    def _():
        for half in range(2):
            lanes = slice(half * 128, half * 128 + 128)
            stage[half] = wide[:, lanes]
            first = stage[half, pl.ds(0, 8, stride=8), :]
            last = stage[half, pl.ds(7, 8, stride=8), :]
            put(C_LINES - 16 + 16 * a, jnp.concatenate([first, last], axis=0).astype(BF16), lanes)
        pair = jnp.concatenate([wide[:8], wide[56:]], axis=0).astype(BF16)
        put(B_LINES - 16 + 16 * a, pair)


def norm_body(recv, send, x_ref, gain_ref, hidden_ref, out_ref, stage):
    bricks, directions = recv.shape
    gain = gain_ref[...]
    row = lax.broadcasted_iota(jnp.int32, (NOTES, C), 0)
    lane = lax.broadcasted_iota(jnp.int32, (NOTES, C), 1)
    notes = jnp.zeros((NOTES, C), jnp.int32)
    for k in range(send.shape[1]):
        notes = jnp.where((row == 0) & (lane == k), send[0, k], notes)
    for brick in range(bricks):
        for number in range(directions):
            serves = (row == 1) & (lane == recv[brick, number])
            notes = jnp.where(serves, brick * directions + number + 1, notes)
    out_ref[bricks * ROWS :, :] = notes.astype(F32).astype(BF16)

    def step(k, _):
        at = pl.ds(pl.multiple_of(k * 64, 64), 64)
        x = x_ref[at, :].astype(F32)
        inverse = lax.rsqrt(jnp.mean(x * x, axis=-1, keepdims=True) + 1e-6)
        v = x * inverse * gain
        rows = (v / (1.0 + jnp.exp(-v))).astype(BF16)
        hidden_ref[at, :] = rows
        put_boundary(rows, k // 8, k % 8, out_ref, stage)
        return 0

    lax.fori_loop(0, bricks * 8, step, 0)


def extract_body(x_ref, out_ref, stage):
    def step(k, _):
        at = pl.ds(pl.multiple_of(k * 64, 64), 64)
        put_boundary(x_ref[at, :], k // 8, k % 8, out_ref, stage)
        return 0

    lax.fori_loop(0, x_ref.shape[0] // 64, step, 0)


def start_padded(own_ref, cells, halo, bricks):
    zero = jnp.zeros((8, C), F32)

    def clear(k, _):
        for b in range(10):
            cells[k * 10 + b] = zero
        for side in range(2):
            for part in range(HB // 8):
                halo[side, k, part * 8 : part * 8 + 8, :] = zero
        return 0

    lax.fori_loop(0, bricks * 10, clear, 0)

    def fill(k, _):
        plane = (k // 8) * 10 + k % 8 + 1
        rows = own_ref[pl.ds(pl.multiple_of(k * 64, 64), 64), :].astype(F32)
        for b in range(8):
            cells[plane * 10 + b + 1] = rows[b * 8 : b * 8 + 8]
        return 0

    lax.fori_loop(0, bricks * 8, fill, 0)


def add_line(ref, index, line):
    ref[index] = ref[index] + line


def pick(flag, yes, no):
    if isinstance(flag, bool):
        return yes if flag else no
    return jnp.where(flag, yes, no)


def place(kind, e, keep, place_at, source_brick, brick, share, cells, halo):
    flags = [t == -1 for t in e]
    pads = [pick(f, 0, 9) for f in flags]
    facing = pick(flags[0], 64, 0)
    start = source_brick * ROWS

    def rows(at, size):
        got = share[place_at, pl.ds(pl.multiple_of(start + at, 16), size), :].astype(F32)
        return got if keep is None else jnp.where(keep, got, 0.0)

    def half(pair, axis):
        return pick(flags[axis], pair[8:], pair[:8])

    def line_b(at):
        plane = rows(at, 64)
        return pick(flags[1], plane[56:], plane[:8])

    def line_c(at):
        plane = rows(at, 64)
        ends = [
            pick(flags[2], plane[8 * b + 7 : 8 * b + 8], plane[8 * b : 8 * b + 1]) for b in range(8)
        ]
        return jnp.concatenate(ends, axis=0)

    def cell(at):
        line = line_b(at)
        return pick(flags[2], line[7:8], line[0:1])

    side = pick(flags[2], 0, 1)
    base = brick * 10

    def add_halo(at, line):
        halo[side, base + at, 8:16, :] = halo[side, base + at, 8:16, :] + line

    def add_cell(at, value):
        spot = pl.ds(pick(flags[1], 7, 16), 1)
        halo[side, base + at, spot, :] = halo[side, base + at, spot, :] + value

    if kind == (1, 0, 0):
        got = rows(facing, 64)
        first = (base + pads[0]) * 10 + 1
        for b in range(8):
            add_line(cells, first + b, got[b * 8 : b * 8 + 8])
    elif kind == (0, 1, 0):
        for a in range(8):
            if a in (0, 7):
                line = line_b(0 if a == 0 else 64)
            else:
                line = half(rows(B_LINES - 16 + 16 * a, 16), 1)
            add_line(cells, (base + a + 1) * 10 + pads[1], line)
    elif kind == (0, 0, 1):
        for a in range(8):
            if a in (0, 7):
                line = line_c(0 if a == 0 else 64)
            else:
                line = half(rows(C_LINES - 16 + 16 * a, 16), 2)
            add_halo(a + 1, line)
    elif kind == (1, 1, 0):
        add_line(cells, (base + pads[0]) * 10 + pads[1], line_b(facing))
    elif kind == (1, 0, 1):
        add_halo(pads[0], line_c(facing))
    elif kind == (0, 1, 1):
        for a in range(8):
            if a in (0, 7):
                value = cell(0 if a == 0 else 64)
            else:
                line = half(rows(C_LINES - 16 + 16 * a, 16), 2)
                value = pick(flags[1], line[7:8], line[0:1])
            add_cell(a + 1, value)
    else:
        add_cell(pads[0], cell(facing))


def windows(cells, halo, cols, bricks, out=None, sems=None):
    row = lax.broadcasted_iota(jnp.int32, (8, C), 0)

    def step(k, _):
        shifted = [[], [], []]
        for b in range(10):
            x = cells[k * 10 + b]
            before = halo[0, k, pl.ds(b + 7, 1), :]
            after = halo[1, k, pl.ds(b + 7, 1), :]
            shifted[0].append(jnp.where(row == 0, before, pltpu.roll(x, 1, 0)))
            shifted[1].append(x)
            shifted[2].append(jnp.where(row == 7, after, pltpu.roll(x, 7, 0)))
        for j in range(3):
            for l in range(3):
                block = jnp.concatenate(shifted[l][j : j + 8], axis=0).astype(BF16)
                at = (3 * j + l) * C
                cols[k, :, at : at + C] = block
        if out is not None:
            pltpu.make_async_copy(cols.at[k], out.at[k], sems.at[k]).start()
        return 0

    lax.fori_loop(0, bricks * 10, step, 0)


def wait_windows(cols, out, sems, bricks):
    def step(k, _):
        pltpu.make_async_copy(cols.at[k], out.at[k], sems.at[k]).wait()
        return 0

    lax.fori_loop(0, bricks * 10, step, 0)


def fetch(parts, share, sems):
    size = parts[0].shape[0]
    copies = [
        pltpu.make_async_copy(part, share.at[pl.ds(k * size, size)], sems.at[k])
        for k, part in enumerate(parts)
    ]
    for copy in copies:
        copy.start()
    return copies


def weight_grad_body(slots, factor, peers, count, *refs):
    recv, table, own_ref, cot_ref = refs[:4]
    parts = refs[4 : 4 + count]
    keep_ref = refs[4 + count]
    give_refs = refs[5 + count : 5 + count + peers // 4]
    out_cols, codes_ref, served_ref = refs[-15:-12]
    cells, halo, share, cols, sums, narrow, turned, codes = refs[-12:-4]
    sems, cols_sems, codes_sem, out_sems = refs[-4:]
    bricks = own_ref.shape[0] // 512
    me = table[2 * peers]
    copies = fetch(parts, share, sems)
    start_padded(own_ref, cells, halo, bricks)
    for part in range(bricks * 2):
        at = slice(part * 256, part * 256 + 256)
        turned[:, at] = cot_ref[at, :].astype(F32).T.astype(BF16)
    for copy in copies:
        copy.wait()
    for k in range(peers):
        notes = share[k, bricks * ROWS :, :].astype(F32).astype(jnp.int32)
        codes_ref[k : k + 1, :] = notes[0:1]
        served_ref[k : k + 1, :] = notes[1:2]
    codes_copy = pltpu.make_async_copy(codes_ref, codes, codes_sem.at[0])
    codes_copy.start()
    codes_copy.wait()
    for brick in range(bricks):
        for number, e in enumerate(DIRECTIONS):
            slot = recv[brick, number]
            safe = jnp.maximum(slot, 0)
            sender = safe // slots
            at = table[sender]
            code = codes[at, me * slots + safe - sender * slots]
            kind = tuple(abs(t) for t in e)
            place(kind, e, slot >= 0, at, code // 6, brick, share, cells, halo)
    windows(cells, halo, cols, bricks, out_cols, cols_sems)

    rows = 27 * C // peers
    for tap in range(27):
        i, jl = divmod(tap, 9)
        total = None
        for brick in range(bricks):
            right = cols[brick * 10 + i : brick * 10 + i + 8, :, jl * C : jl * C + C].reshape(512, C)
            left = turned[:, brick * 512 : brick * 512 + 512]
            term = jnp.dot(left, right, preferred_element_type=F32)
            total = term if total is None else total + term
        total = (total * factor).T
        start = tap * C
        while start < (tap + 1) * C:
            owner = start // rows
            stop = min((tap + 1) * C, (owner + 1) * rows)
            piece = total[start - tap * C : stop - tap * C]
            bucket = jnp.bitwise_xor(me % 2, owner % 2)
            behind = table[peers + owner // 2]
            where = slice(start - owner * rows, stop - owner * rows)
            sums[bucket, behind, where, :] = piece
            narrow[bucket, behind, where, :] = piece.astype(BF16)
            start = stop
            if stop == (owner + 1) * rows:

                @pl.when(bucket == 0)
                def _():
                    pltpu.make_async_copy(
                        sums.at[0, behind], keep_ref.at[behind], out_sems.at[0, behind]
                    ).start()

                turn = table[peers + peers // 2 + owner // 2]
                for hop, give_ref in enumerate(give_refs):

                    @pl.when((bucket == 1) & (turn // 2 == hop))
                    def _():
                        pltpu.make_async_copy(
                            narrow.at[1, behind], give_ref.at[turn % 2], out_sems.at[1, turn]
                        ).start()

    for k in range(peers // 2):
        pltpu.make_async_copy(sums.at[0, k], keep_ref.at[k], out_sems.at[0, k]).wait()
        pltpu.make_async_copy(narrow.at[1, k], give_refs[k // 2].at[k % 2], out_sems.at[1, k]).wait()
    wait_windows(cols, out_cols, cols_sems, bricks)


GROUP = 3 * C


def start_stream(cols_ref, first, cols, weight_ref, weight, sems):
    copies = []
    planes = cols.shape[0]
    for g in range(3):
        lanes = pl.ds(g * GROUP, GROUP)
        group = [
            pltpu.make_async_copy(
                cols_ref.at[pl.ds(first, planes), :, lanes], cols.at[:, :, lanes], sems.at[g, 3]
            )
        ]
        for i in range(3):
            at = pl.ds((i * 3 + g) * GROUP, GROUP)
            group.append(pltpu.make_async_copy(weight_ref.at[at], weight.at[at], sems.at[g, i]))
        copies.append(group)
    for group in copies:
        for copy in group:
            copy.start()
    return copies


def tap_sum(copies, cols, weight):
    bricks = cols.shape[0] // 10
    totals = [None] * bricks
    for g in range(3):
        for copy in copies[g]:
            copy.wait()
        for brick in range(bricks):
            for i in range(3):
                at = brick * 10 + i
                left = cols[at : at + 8, :, g * GROUP : g * GROUP + GROUP].reshape(512, GROUP)
                right = weight[(i * 3 + g) * GROUP : (i * 3 + g + 1) * GROUP, :]
                term = jnp.dot(left, right, preferred_element_type=F32)
                totals[brick] = term if totals[brick] is None else totals[brick] + term
    return totals


def mix_body(cols_ref, weight_ref, x_ref, out_ref, cols, weight, sems):
    copies = start_stream(cols_ref, 0, cols, weight_ref, weight, sems)
    for brick, total in enumerate(tap_sum(copies, cols, weight)):
        at = slice(brick * 512, brick * 512 + 512)
        out_ref[at, :] = (x_ref[at, :].astype(F32) + total).astype(BF16)


def input_grad_body(slots, peers, count, *refs):
    served, send, table, cot_ref, x_ref, gain_ref, weight_ref = refs[:7]
    parts = refs[7 : 7 + count]
    out_ref, cells, halo, cols, share, weight, heads, more, sems, weight_sem = refs[7 + count :]
    bricks = cot_ref.shape[0] // 512
    me = table[2 * peers]
    copies = fetch(parts, share, sems)
    weight_copy = pltpu.make_async_copy(weight_ref, weight, weight_sem.at[0])
    weight_copy.start()

    def no_head(k, _):
        heads[k] = -1
        return 0

    lax.fori_loop(0, bricks * 26, no_head, 0)

    def source_of(k):
        receiver = k // slots
        at = table[receiver]
        return at, served[at, me * slots + k - receiver * slots] - 1

    def sort(k, found):
        _, entry = source_of(k)
        asked = entry >= 0
        key = send[0, k] // 6 * 26 + 25 - jnp.maximum(entry, 0) % 26
        first = asked & (heads[key] < 0)
        extra = asked & jnp.logical_not(first)

        @pl.when(first)
        def _():
            heads[key] = k

        @pl.when(extra)
        def _():
            more[found] = k

        return found + jnp.where(extra, 1, 0)

    found = lax.fori_loop(0, send.shape[1], sort, 0)
    start_padded(cot_ref, cells, halo, bricks)
    for copy in copies:
        copy.wait()
    for brick in range(bricks):
        for number, e in enumerate(DIRECTIONS):
            head = heads[brick * 26 + number]
            at, entry = source_of(jnp.maximum(head, 0))
            kind = tuple(abs(t) for t in e)
            source = jnp.maximum(entry, 0) // 26
            place(kind, e, head >= 0, at, source, brick, share, cells, halo)

    def one(n, _):
        k = more[n]
        at, entry = source_of(k)
        number = 25 - entry % 26
        tap = jnp.where(number >= 13, number + 1, number)
        e = (tap // 9 - 1, (tap // 3) % 3 - 1, tap % 3 - 1)
        on = [t != 0 for t in e]
        for kind in ((1, 0, 0), (0, 1, 0), (0, 0, 1), (1, 1, 0), (1, 0, 1), (0, 1, 1), (1, 1, 1)):
            match = functools.reduce(
                jnp.logical_and, [f if w else jnp.logical_not(f) for f, w in zip(on, kind)]
            )

            @pl.when(match)
            def _():
                place(kind, e, None, at, entry // 26, send[0, k] // 6, share, cells, halo)

        return 0

    lax.fori_loop(0, found, one, 0)
    windows(cells, halo, cols, bricks)
    weight_copy.wait()
    gain = gain_ref[...]
    for brick in range(bricks):
        rows = slice(brick * 512, brick * 512 + 512)
        grad = None
        for i in range(3):
            left = cols[brick * 10 + i : brick * 10 + i + 8].reshape(512, 9 * C)
            right = weight[i * 9 * C : (i + 1) * 9 * C, :]
            term = jnp.dot(left, right, preferred_element_type=F32)
            grad = term if grad is None else grad + term
        x = x_ref[rows, :].astype(F32)
        inverse = lax.rsqrt(jnp.mean(x * x, axis=-1, keepdims=True) + 1e-6)
        unit = x * inverse
        v = unit * gain
        gate = 1.0 / (1.0 + jnp.exp(-v))
        grad = grad * (gate * (1.0 + v * (1.0 - gate))) * gain
        grad = inverse * (grad - unit * jnp.mean(grad * unit, axis=-1, keepdims=True))
        out_ref[rows, :] = (cot_ref[rows, :].astype(F32) + grad).astype(BF16)


def local(features, norm_gain, conv_weight, recv_slot, send_face, cotangent):
    channels = features.shape[1]
    per_device = features.shape[0]
    bricks = per_device // 512
    peers = lax.axis_size("morton")
    slots = send_face.shape[1] // peers
    factor = 1.0 / math.sqrt(peers * per_device)
    gain = norm_gain.reshape(1, channels)
    sds = jax.ShapeDtypeStruct
    stage = pltpu.VMEM((2, 64, 128), F32)

    def padded(n):
        return [
            pltpu.VMEM((n * 100, 8, channels), F32),
            pltpu.VMEM((2, n * 10, HB, channels), F32),
        ]

    def cols_shape(n):
        return (n * 10, 64, 9 * channels)


    table = jnp.asarray(ring_tables(peers))[lax.axis_index("morton")]

    hidden, share = call(
        norm_body,
        (sds((per_device, channels), BF16), sds((bricks * ROWS + NOTES, channels), BF16)),
        [SMEM, SMEM, VMEM, VMEM],
        [stage],
        name="norm",
    )(recv_slot, send_face, features, gain)
    cot_share = call(
        extract_body,
        sds((bricks * ROWS, channels), BF16),
        [VMEM],
        [stage],
        name="extract",
    )(cotangent)
    turned = conv_weight.reshape(27, channels, channels)[::-1].transpose(0, 2, 1)
    turned = turned.reshape(27 * channels, channels)

    hidden_ring = RingGather(share, peers)
    hidden_ring.go(0)
    hidden_ring.go(1)
    hidden_ring.go(0, cot_share)
    hidden_ring.go(1)
    hidden_ring.go(0, turned)
    hidden_ring.go(1)
    hidden_ring.go(0)
    hidden_parts = hidden_ring.places()

    cot_ring = RingGather(cot_share, peers, hidden_ring.last(1))
    cot_ring.go(0, hidden_ring.last(0))
    cot_ring.go(1, hidden_ring.last(0))

    count = len(hidden_parts)
    rows = 27 * channels // peers
    chips = peers // 2
    keep, *give, cols, _, served = call(
        functools.partial(weight_grad_body, slots, factor, peers, count),
        (
            sds((chips, rows, channels), F32),
            *[sds((2, rows, channels), BF16)] * (chips // 2),
            sds(cols_shape(bricks), BF16),
            sds((peers, channels), jnp.int32),
            sds((peers, channels), jnp.int32),
        ),
        [SMEM] * 2 + [VMEM] * 2 + [HBM] * count,
        padded(bricks)
        + [
            pltpu.VMEM((peers, bricks * ROWS + NOTES, channels), BF16),
            pltpu.VMEM(cols_shape(bricks), BF16),
            pltpu.VMEM((2, chips, rows, channels), F32),
            pltpu.VMEM((2, chips, rows, channels), BF16),
            pltpu.VMEM((channels, per_device), BF16),
            pltpu.SMEM((peers, channels), jnp.int32),
            pltpu.SemaphoreType.DMA((count,)),
            pltpu.SemaphoreType.DMA((bricks * 10,)),
            pltpu.SemaphoreType.DMA((1,)),
            pltpu.SemaphoreType.DMA((2, chips)),
        ],
        cost=9,
        name="weight_grad",
        out_specs=(*[HBM] * (2 + chips // 2), VMEM, VMEM),
    )(recv_slot, table, hidden, cotangent, *hidden_parts)

    cot_ring.go(0, cols)
    cot_ring.go(1, cols)
    weight_scratch = [
        pltpu.VMEM((27 * channels, channels), BF16),
        pltpu.SemaphoreType.DMA((3, 4)),
    ]
    mixed = call(
        mix_body,
        sds((per_device, channels), BF16),
        [HBM, HBM, VMEM],
        [pltpu.VMEM(cols_shape(bricks), BF16)] + weight_scratch,
        cost=6,
        name="mix",
    )(cols, conv_weight, features)
    cot_ring.go(0)
    cot_ring.go(1)
    third = (cot_ring.last(0), cot_ring.last(1))
    cot_ring.go(0)
    fourth = cot_ring.last(0)
    cot_parts = cot_ring.places(cols)

    grad_features = call(
        functools.partial(input_grad_body, slots, peers, count),
        sds((per_device, channels), BF16),
        [SMEM] * 3 + [VMEM] * 3 + [HBM] * (1 + count),
        padded(bricks)
        + [
            pltpu.VMEM(cols_shape(bricks), BF16),
            pltpu.VMEM((peers, bricks * ROWS, channels), BF16),
            weight_scratch[0],
            pltpu.SMEM((bricks * 26,), jnp.int32),
            pltpu.SMEM((peers * slots,), jnp.int32),
            pltpu.SemaphoreType.DMA((count,)),
            pltpu.SemaphoreType.DMA((1,)),
        ],
        cost=13,
        name="input_grad",
    )(served, send_face, table, cotangent, features, gain, turned, *cot_parts)
    gates = (mixed, third, fourth)
    grad_weight = scatter_ring(keep, give, peers, gates)
    return (mixed, grad_features, grad_weight)


def solution(mesh):
    rows = P(("groups", "morton"), None)
    return jax.shard_map(
        local,
        mesh=mesh,
        in_specs=(rows, P(), P(), rows, rows, rows),
        out_specs=(rows, rows, rows),
        check_vma=False,
    )
```

```python
import functools
import math

import jax
import jax.numpy as jnp
import numpy as np
from jax import lax
from jax.experimental import pallas as pl
from jax.experimental.pallas import tpu as pltpu
from jax.sharding import PartitionSpec as P

F32 = jnp.float32
BF16 = jnp.bfloat16
C = 256
C_LINES = 128
B_LINES = 224
ROWS = 320
NOTES = 16
HB = 24
VMEM_LIMIT = 56 * 1024 * 1024
DIRECTIONS = [
    (i, j, l)
    for i in (-1, 0, 1)
    for j in (-1, 0, 1)
    for l in (-1, 0, 1)
    if (i, j, l) != (0, 0, 0)
]

VMEM = pl.BlockSpec(memory_space=pltpu.VMEM)
SMEM = pl.BlockSpec(memory_space=pltpu.SMEM)
ANY = pl.BlockSpec(memory_space=pl.ANY)
HBM = pl.BlockSpec(memory_space=pltpu.HBM)


def ring_order(chips):
    if chips == 8:
        return [0, 2, 4, 6, 7, 5, 3, 1]
    return list(range(chips))


def ring_tables(peers):
    chips = peers // 2
    spot = np.argsort(np.array(ring_order(chips)))
    device = np.arange(peers)
    behind = (spot[device // 2][:, None] - spot[None, :]) % chips
    half = chips // 2
    turn = np.where(behind >= half, 2 * (behind - half), 2 * (half - 1 - behind) + 1)
    place_of = np.broadcast_to(device, (peers, peers)).copy()
    if chips <= 8:
        for me in range(peers):
            for other in range(peers):
                away = behind[me, other // 2] if me % 2 == 0 else -behind[me, other // 2] % chips
                same = me % 2 == other % 2
                if away == 0:
                    place = 0 if same else 1
                elif away < half or (away == half and same):
                    place = 1 + away if same else 1 + half + away
                else:
                    away = chips - away
                    place = half + (away if not same else half + away) + half
                place_of[me, other] = place
    return np.concatenate([place_of, behind, turn, device[:, None]], axis=1).astype(np.int32)


def ring_step(x, peers, step, cross=0):
    order = ring_order(peers // 2)
    pairs = [
        (2 * order[i] + (core ^ cross), 2 * order[(i + (step or 1 - 2 * core)) % len(order)] + core)
        for i in range(len(order))
        for core in range(2)
    ]
    return lax.ppermute(x, "morton", pairs)


def swap_cores(x, peers):
    return lax.ppermute(x, "morton", [(m, m ^ 1) for m in range(peers)])


class RingGather:
    def __init__(self, x, peers):
        self.x, self.peers, self.chips = x, peers, peers // 2
        self.whole = None
        if self.chips > 8:
            self.whole = lax.all_gather(x[None], "morton", axis=0, tiled=True)
            return
        self.chains = ([x], [x])

    def go(self, chain, gate=None):
        if self.whole is not None or len(self.chains[chain]) > self.chips // 2 - chain:
            return
        held = self.chains[chain][-1]
        if gate is not None:
            held = lax.optimization_barrier((held, gate))[0]
        cross = int(chain == 1 and len(self.chains[chain]) == 1)
        self.chains[chain].append(ring_step(held, self.peers, 0, cross))

    def last(self, chain):
        return self.x if self.whole is not None else self.chains[chain][-1]

    def places(self, gate=None):
        if self.whole is not None:
            return [self.whole]
        mine = self.chains[0][1:] + self.chains[1][1:]
        held = mine
        if gate is not None:
            held = [lax.optimization_barrier((t, gate))[0] for t in mine]
        others = [swap_cores(t, self.peers) for t in [self.x] + held]
        return [t[None] for t in [self.x] + others[:1] + mine + others[1:]]


class RingScatter:
    def __init__(self, keep, give, peers):
        self.keep, self.peers, self.chips = keep, peers, peers // 2
        self.other = [swap_cores(t, peers) for t in give]
        self.held = [None, None]
        self.hop = 0

    def term(self, k):
        half = self.chips // 2
        pair = self.other[k - half][0] if k >= half else self.other[half - 1 - k][1]
        return self.keep[k] + pair.astype(F32)

    def go(self, gate=None):
        sent = []
        for way, step, count in ((0, 1, self.chips // 2), (1, -1, (self.chips - 1) // 2)):
            left = count - self.hop
            if left <= 0:
                continue
            part = self.term((-step * left) % self.chips)
            if self.held[way] is not None:
                part = part + self.held[way].astype(F32)
            part = part.astype(BF16)
            if gate is not None:
                part = lax.optimization_barrier((part, gate))[0]
            sent.append(part)
            self.held[way] = ring_step(part, self.peers, step)
        self.hop += 1
        return sent

    def total(self):
        return sum((t.astype(F32) for t in self.held if t is not None), self.term(0))


def call(body, out_shape, in_specs, scratch=(), cost=2, name=None, out_specs=None, aliases=None):
    return pl.pallas_call(
        body,
        out_shape=out_shape,
        in_specs=in_specs,
        out_specs=out_specs or jax.tree.map(lambda _: VMEM, out_shape),
        scratch_shapes=list(scratch),
        input_output_aliases=aliases or {},
        compiler_params=pltpu.CompilerParams(vmem_limit_bytes=VMEM_LIMIT),
        cost_estimate=pl.CostEstimate(flops=cost * 10**9, bytes_accessed=0, transcendentals=0),
        name=name,
    )


def put_boundary(rows, brick, a, out_ref, stage):
    wide = rows.astype(F32)
    base = brick * ROWS

    def put(at, value, lanes=slice(None)):
        out_ref[pl.ds(pl.multiple_of(base + at, 16), value.shape[0]), lanes] = value

    for edge, at in ((0, 0), (7, 64)):

        @pl.when(a == edge)
        def _():
            put(at, rows)

    @pl.when((a > 0) & (a < 7))
    def _():
        for half in range(2):
            lanes = slice(half * 128, half * 128 + 128)
            stage[half] = wide[:, lanes]
            first = stage[half, pl.ds(0, 8, stride=8), :]
            last = stage[half, pl.ds(7, 8, stride=8), :]
            put(C_LINES - 16 + 16 * a, jnp.concatenate([first, last], axis=0).astype(BF16), lanes)
        pair = jnp.concatenate([wide[:8], wide[56:]], axis=0).astype(BF16)
        put(B_LINES - 16 + 16 * a, pair)


def norm_body(recv, send, x_ref, gain_ref, hidden_ref, out_ref, stage):
    bricks, directions = recv.shape
    gain = gain_ref[...]
    lane = lax.broadcasted_iota(jnp.int32, (1, C), 1)
    codes = jnp.zeros((1, C), jnp.int32)
    for k in range(send.shape[1]):
        codes = jnp.where(lane == k, send[0, k], codes)
    served = jnp.zeros((1, C), jnp.int32)
    for brick in range(bricks):
        for number in range(directions):
            served = jnp.where(lane == recv[brick, number], brick * directions + number + 1, served)
    row = lax.broadcasted_iota(jnp.int32, (NOTES, C), 0)
    notes = jnp.where(row == 0, codes, jnp.where(row == 1, served, 0))
    out_ref[bricks * ROWS :, :] = notes.astype(F32).astype(BF16)

    def step(k, _):
        at = pl.ds(pl.multiple_of(k * 64, 64), 64)
        x = x_ref[at, :].astype(F32)
        inverse = lax.rsqrt(jnp.mean(x * x, axis=-1, keepdims=True) + 1e-6)
        v = x * inverse * gain
        rows = (v / (1.0 + jnp.exp(-v))).astype(BF16)
        hidden_ref[at, :] = rows
        put_boundary(rows, k // 8, k % 8, out_ref, stage)
        return 0

    lax.fori_loop(0, bricks * 8, step, 0)


def extract_body(x_ref, out_ref, stage):
    def step(k, _):
        at = pl.ds(pl.multiple_of(k * 64, 64), 64)
        put_boundary(x_ref[at, :], k // 8, k % 8, out_ref, stage)
        return 0

    lax.fori_loop(0, x_ref.shape[0] // 64, step, 0)


def start_padded(own_ref, cells, halo, bricks):
    zero = jnp.zeros((8, C), F32)

    def clear(k, _):
        for b in range(10):
            cells[k * 10 + b] = zero
        for side in range(2):
            for part in range(HB // 8):
                halo[side, k, part * 8 : part * 8 + 8, :] = zero
        return 0

    lax.fori_loop(0, bricks * 10, clear, 0)

    def fill(k, _):
        plane = (k // 8) * 10 + k % 8 + 1
        rows = own_ref[pl.ds(pl.multiple_of(k * 64, 64), 64), :].astype(F32)
        for b in range(8):
            cells[plane * 10 + b + 1] = rows[b * 8 : b * 8 + 8]
        return 0

    lax.fori_loop(0, bricks * 8, fill, 0)


def add_line(ref, index, line):
    ref[index] = ref[index] + line


def pick(flag, yes, no):
    if isinstance(flag, bool):
        return yes if flag else no
    return jnp.where(flag, yes, no)


def place(kind, e, keep, place_at, source_brick, brick, share, cells, halo):
    flags = [t == -1 for t in e]
    pads = [pick(f, 0, 9) for f in flags]
    facing = pick(flags[0], 64, 0)
    start = source_brick * ROWS

    def rows(at, size):
        got = share[place_at, pl.ds(pl.multiple_of(start + at, 16), size), :].astype(F32)
        return got if keep is None else jnp.where(keep, got, 0.0)

    def half(pair, axis):
        return pick(flags[axis], pair[8:], pair[:8])

    def line_b(at):
        plane = rows(at, 64)
        return pick(flags[1], plane[56:], plane[:8])

    def line_c(at):
        plane = rows(at, 64)
        ends = [
            pick(flags[2], plane[8 * b + 7 : 8 * b + 8], plane[8 * b : 8 * b + 1]) for b in range(8)
        ]
        return jnp.concatenate(ends, axis=0)

    def cell(at):
        line = line_b(at)
        return pick(flags[2], line[7:8], line[0:1])

    side = pick(flags[2], 0, 1)
    base = brick * 10

    def add_halo(at, line):
        halo[side, base + at, 8:16, :] = halo[side, base + at, 8:16, :] + line

    def add_cell(at, value):
        spot = pl.ds(pick(flags[1], 7, 16), 1)
        halo[side, base + at, spot, :] = halo[side, base + at, spot, :] + value

    if kind == (1, 0, 0):
        got = rows(facing, 64)
        first = (base + pads[0]) * 10 + 1
        for b in range(8):
            add_line(cells, first + b, got[b * 8 : b * 8 + 8])
    elif kind == (0, 1, 0):
        for a in range(8):
            if a in (0, 7):
                line = line_b(0 if a == 0 else 64)
            else:
                line = half(rows(B_LINES - 16 + 16 * a, 16), 1)
            add_line(cells, (base + a + 1) * 10 + pads[1], line)
    elif kind == (0, 0, 1):
        for a in range(8):
            if a in (0, 7):
                line = line_c(0 if a == 0 else 64)
            else:
                line = half(rows(C_LINES - 16 + 16 * a, 16), 2)
            add_halo(a + 1, line)
    elif kind == (1, 1, 0):
        add_line(cells, (base + pads[0]) * 10 + pads[1], line_b(facing))
    elif kind == (1, 0, 1):
        add_halo(pads[0], line_c(facing))
    elif kind == (0, 1, 1):
        for a in range(8):
            if a in (0, 7):
                value = cell(0 if a == 0 else 64)
            else:
                line = half(rows(C_LINES - 16 + 16 * a, 16), 2)
                value = pick(flags[1], line[7:8], line[0:1])
            add_cell(a + 1, value)
    else:
        add_cell(pads[0], cell(facing))


def windows(cells, halo, cols, bricks, out=None, sems=None):
    row = lax.broadcasted_iota(jnp.int32, (8, C), 0)

    def step(k, _):
        shifted = [[], [], []]
        for b in range(10):
            x = cells[k * 10 + b]
            before = halo[0, k, pl.ds(b + 7, 1), :]
            after = halo[1, k, pl.ds(b + 7, 1), :]
            shifted[0].append(jnp.where(row == 0, before, pltpu.roll(x, 1, 0)))
            shifted[1].append(x)
            shifted[2].append(jnp.where(row == 7, after, pltpu.roll(x, 7, 0)))
        for j in range(3):
            for l in range(3):
                block = jnp.concatenate(shifted[l][j : j + 8], axis=0).astype(BF16)
                at = (3 * j + l) * C
                cols[k, :, at : at + C] = block
        if out is not None:
            pltpu.make_async_copy(cols.at[k], out.at[k], sems.at[k]).start()
        return 0

    lax.fori_loop(0, bricks * 10, step, 0)


def wait_windows(cols, out, sems, bricks):
    def step(k, _):
        pltpu.make_async_copy(cols.at[k], out.at[k], sems.at[k]).wait()
        return 0

    lax.fori_loop(0, bricks * 10, step, 0)


def fetch(parts, share, sems):
    size = parts[0].shape[0]
    copies = [
        pltpu.make_async_copy(part, share.at[pl.ds(k * size, size)], sems.at[k])
        for k, part in enumerate(parts)
    ]
    for copy in copies:
        copy.start()
    return copies


def weight_grad_body(slots, factor, peers, count, *refs):
    recv, table, own_ref, cot_ref = refs[:4]
    parts = refs[4 : 4 + count]
    keep_ref = refs[4 + count]
    give_refs = refs[5 + count : 5 + count + peers // 4]
    out_cols, codes_ref, served_ref = refs[-15:-12]
    cells, halo, share, cols, sums, narrow, turned, codes = refs[-12:-4]
    sems, cols_sems, codes_sem, out_sems = refs[-4:]
    bricks = own_ref.shape[0] // 512
    me = table[2 * peers]
    copies = fetch(parts, share, sems)
    start_padded(own_ref, cells, halo, bricks)
    for part in range(bricks * 2):
        at = slice(part * 256, part * 256 + 256)
        turned[:, at] = cot_ref[at, :].astype(F32).T.astype(BF16)
    for copy in copies:
        copy.wait()
    for k in range(peers):
        notes = share[k, bricks * ROWS :, :].astype(F32).astype(jnp.int32)
        codes_ref[k : k + 1, :] = notes[0:1]
        served_ref[k : k + 1, :] = notes[1:2]
    codes_copy = pltpu.make_async_copy(codes_ref, codes, codes_sem.at[0])
    codes_copy.start()
    codes_copy.wait()
    for brick in range(bricks):
        for number, e in enumerate(DIRECTIONS):
            slot = recv[brick, number]
            safe = jnp.maximum(slot, 0)
            sender = safe // slots
            at = table[sender]
            code = codes[at, me * slots + safe - sender * slots]
            kind = tuple(abs(t) for t in e)
            place(kind, e, slot >= 0, at, code // 6, brick, share, cells, halo)
    windows(cells, halo, cols, bricks, out_cols, cols_sems)

    rows = 27 * C // peers
    for tap in range(27):
        i, jl = divmod(tap, 9)
        total = None
        for brick in range(bricks):
            right = cols[brick * 10 + i : brick * 10 + i + 8, :, jl * C : jl * C + C].reshape(512, C)
            left = turned[:, brick * 512 : brick * 512 + 512]
            term = jnp.dot(left, right, preferred_element_type=F32)
            total = term if total is None else total + term
        total = (total * factor).T
        start = tap * C
        while start < (tap + 1) * C:
            owner = start // rows
            stop = min((tap + 1) * C, (owner + 1) * rows)
            piece = total[start - tap * C : stop - tap * C]
            bucket = jnp.bitwise_xor(me % 2, owner % 2)
            behind = table[peers + owner // 2]
            where = slice(start - owner * rows, stop - owner * rows)
            sums[bucket, behind, where, :] = piece
            narrow[bucket, behind, where, :] = piece.astype(BF16)
            start = stop
            if stop == (owner + 1) * rows:

                @pl.when(bucket == 0)
                def _():
                    pltpu.make_async_copy(
                        sums.at[0, behind], keep_ref.at[behind], out_sems.at[0, behind]
                    ).start()

                turn = table[peers + peers // 2 + owner // 2]
                for hop, give_ref in enumerate(give_refs):

                    @pl.when((bucket == 1) & (turn // 2 == hop))
                    def _():
                        pltpu.make_async_copy(
                            narrow.at[1, behind], give_ref.at[turn % 2], out_sems.at[1, turn]
                        ).start()

    for k in range(peers // 2):
        pltpu.make_async_copy(sums.at[0, k], keep_ref.at[k], out_sems.at[0, k]).wait()
        pltpu.make_async_copy(narrow.at[1, k], give_refs[k // 2].at[k % 2], out_sems.at[1, k]).wait()
    wait_windows(cols, out_cols, cols_sems, bricks)


GROUP = 3 * C


def start_stream(cols_ref, first, cols, weight_ref, weight, sems):
    copies = []
    planes = cols.shape[0]
    for g in range(3):
        lanes = pl.ds(g * GROUP, GROUP)
        group = [
            pltpu.make_async_copy(
                cols_ref.at[pl.ds(first, planes), :, lanes], cols.at[:, :, lanes], sems.at[g, 3]
            )
        ]
        for i in range(3):
            at = pl.ds((i * 3 + g) * GROUP, GROUP)
            group.append(pltpu.make_async_copy(weight_ref.at[at], weight.at[at], sems.at[g, i]))
        copies.append(group)
    for group in copies:
        for copy in group:
            copy.start()
    return copies


def tap_sum(copies, cols, weight):
    bricks = cols.shape[0] // 10
    totals = [None] * bricks
    for g in range(3):
        for copy in copies[g]:
            copy.wait()
        for brick in range(bricks):
            for i in range(3):
                at = brick * 10 + i
                left = cols[at : at + 8, :, g * GROUP : g * GROUP + GROUP].reshape(512, GROUP)
                right = weight[(i * 3 + g) * GROUP : (i * 3 + g + 1) * GROUP, :]
                term = jnp.dot(left, right, preferred_element_type=F32)
                totals[brick] = term if totals[brick] is None else totals[brick] + term
    return totals


def mix_body(cols_ref, weight_ref, x_ref, out_ref, cols, weight, sems):
    copies = start_stream(cols_ref, 0, cols, weight_ref, weight, sems)
    for brick, total in enumerate(tap_sum(copies, cols, weight)):
        at = slice(brick * 512, brick * 512 + 512)
        out_ref[at, :] = (x_ref[at, :].astype(F32) + total).astype(BF16)


def input_grad_body(slots, peers, count, *refs):
    served, send, table, cot_ref, x_ref, gain_ref, weight_ref = refs[:7]
    parts = refs[7 : 7 + count]
    out_ref, cells, halo, cols, share, weight, heads, more, sems, weight_sem = refs[7 + count :]
    bricks = cot_ref.shape[0] // 512
    me = table[2 * peers]
    copies = fetch(parts, share, sems)
    weight_copy = pltpu.make_async_copy(weight_ref, weight, weight_sem.at[0])
    weight_copy.start()

    def no_head(k, _):
        heads[k] = -1
        return 0

    lax.fori_loop(0, bricks * 26, no_head, 0)

    def source_of(k):
        receiver = k // slots
        at = table[receiver]
        return at, served[at, me * slots + k - receiver * slots] - 1

    def sort(k, found):
        _, entry = source_of(k)
        asked = entry >= 0
        key = send[0, k] // 6 * 26 + 25 - jnp.maximum(entry, 0) % 26
        first = asked & (heads[key] < 0)
        extra = asked & jnp.logical_not(first)

        @pl.when(first)
        def _():
            heads[key] = k

        @pl.when(extra)
        def _():
            more[found] = k

        return found + jnp.where(extra, 1, 0)

    found = lax.fori_loop(0, send.shape[1], sort, 0)
    start_padded(cot_ref, cells, halo, bricks)
    for copy in copies:
        copy.wait()
    for brick in range(bricks):
        for number, e in enumerate(DIRECTIONS):
            head = heads[brick * 26 + number]
            at, entry = source_of(jnp.maximum(head, 0))
            kind = tuple(abs(t) for t in e)
            source = jnp.maximum(entry, 0) // 26
            place(kind, e, head >= 0, at, source, brick, share, cells, halo)

    def one(n, _):
        k = more[n]
        at, entry = source_of(k)
        number = 25 - entry % 26
        tap = jnp.where(number >= 13, number + 1, number)
        e = (tap // 9 - 1, (tap // 3) % 3 - 1, tap % 3 - 1)
        on = [t != 0 for t in e]
        for kind in ((1, 0, 0), (0, 1, 0), (0, 0, 1), (1, 1, 0), (1, 0, 1), (0, 1, 1), (1, 1, 1)):
            match = functools.reduce(
                jnp.logical_and, [f if w else jnp.logical_not(f) for f, w in zip(on, kind)]
            )

            @pl.when(match)
            def _():
                place(kind, e, None, at, entry // 26, send[0, k] // 6, share, cells, halo)

        return 0

    lax.fori_loop(0, found, one, 0)
    windows(cells, halo, cols, bricks)
    weight_copy.wait()
    gain = gain_ref[...]
    for brick in range(bricks):
        rows = slice(brick * 512, brick * 512 + 512)
        grad = None
        for i in range(3):
            left = cols[brick * 10 + i : brick * 10 + i + 8].reshape(512, 9 * C)
            right = weight[i * 9 * C : (i + 1) * 9 * C, :]
            term = jnp.dot(left, right, preferred_element_type=F32)
            grad = term if grad is None else grad + term
        x = x_ref[rows, :].astype(F32)
        inverse = lax.rsqrt(jnp.mean(x * x, axis=-1, keepdims=True) + 1e-6)
        unit = x * inverse
        v = unit * gain
        gate = 1.0 / (1.0 + jnp.exp(-v))
        grad = grad * (gate * (1.0 + v * (1.0 - gate))) * gain
        grad = inverse * (grad - unit * jnp.mean(grad * unit, axis=-1, keepdims=True))
        out_ref[rows, :] = (cot_ref[rows, :].astype(F32) + grad).astype(BF16)


def local(features, norm_gain, conv_weight, recv_slot, send_face, cotangent):
    channels = features.shape[1]
    per_device = features.shape[0]
    bricks = per_device // 512
    peers = lax.axis_size("morton")
    slots = send_face.shape[1] // peers
    factor = 1.0 / math.sqrt(peers * per_device)
    gain = norm_gain.reshape(1, channels)
    sds = jax.ShapeDtypeStruct
    stage = pltpu.VMEM((2, 64, 128), F32)

    def padded(n):
        return [
            pltpu.VMEM((n * 100, 8, channels), F32),
            pltpu.VMEM((2, n * 10, HB, channels), F32),
        ]

    def cols_shape(n):
        return (n * 10, 64, 9 * channels)


    table = jnp.asarray(ring_tables(peers))[lax.axis_index("morton")]

    hidden, share = call(
        norm_body,
        (sds((per_device, channels), BF16), sds((bricks * ROWS + NOTES, channels), BF16)),
        [SMEM, SMEM, VMEM, VMEM],
        [stage],
        name="norm",
    )(recv_slot, send_face, features, gain)
    hidden_ring = RingGather(share, peers)
    cot_share = call(
        extract_body,
        sds((bricks * ROWS, channels), BF16),
        [VMEM],
        [stage],
        name="extract",
    )(cotangent)
    hidden_ring.go(0)
    hidden_ring.go(1)
    hidden_ring.go(0, cot_share)
    hidden_ring.go(1)
    hidden_ring.go(0, table)
    hidden_ring.go(1)
    hidden_ring.go(0)
    hidden_parts = hidden_ring.places()

    cot_ring = RingGather(cot_share, peers)
    cot_ring.go(0, hidden_ring.last(1))
    cot_ring.go(1, hidden_ring.last(0))

    count = len(hidden_parts)
    rows = 27 * channels // peers
    chips = peers // 2
    keep, *give, cols, _, served = call(
        functools.partial(weight_grad_body, slots, factor, peers, count),
        (
            sds((chips, rows, channels), F32),
            *[sds((2, rows, channels), BF16)] * (chips // 2),
            sds(cols_shape(bricks), BF16),
            sds((peers, channels), jnp.int32),
            sds((peers, channels), jnp.int32),
        ),
        [SMEM] * 2 + [VMEM] * 2 + [HBM] * count,
        padded(bricks)
        + [
            pltpu.VMEM((peers, bricks * ROWS + NOTES, channels), BF16),
            pltpu.VMEM(cols_shape(bricks), BF16),
            pltpu.VMEM((2, chips, rows, channels), F32),
            pltpu.VMEM((2, chips, rows, channels), BF16),
            pltpu.VMEM((channels, per_device), BF16),
            pltpu.SMEM((peers, channels), jnp.int32),
            pltpu.SemaphoreType.DMA((count,)),
            pltpu.SemaphoreType.DMA((bricks * 10,)),
            pltpu.SemaphoreType.DMA((1,)),
            pltpu.SemaphoreType.DMA((2, chips)),
        ],
        cost=9,
        name="weight_grad",
        out_specs=(*[HBM] * (2 + chips // 2), VMEM, VMEM),
    )(recv_slot, table, hidden, cotangent, *hidden_parts)

    first = (cot_ring.last(0), cot_ring.last(1))
    give = [lax.optimization_barrier((t, first))[0] for t in give]
    sums_ring = RingScatter(keep, give, peers)
    sent = sums_ring.go()
    cot_ring.go(0, cols)
    cot_ring.go(1, cols)
    second = (cot_ring.last(0), cot_ring.last(1))
    mix_cols = lax.optimization_barrier((cols, sent))[0]
    weight_scratch = [
        pltpu.VMEM((27 * channels, channels), BF16),
        pltpu.SemaphoreType.DMA((3, 4)),
    ]
    mixed = call(
        mix_body,
        sds((per_device, channels), BF16),
        [HBM, HBM, VMEM],
        [pltpu.VMEM(cols_shape(bricks), BF16)] + weight_scratch,
        cost=6,
        name="mix",
    )(mix_cols, conv_weight, features)
    sent = sums_ring.go((second, mixed))
    cot_ring.go(0)
    cot_ring.go(1)
    third = (cot_ring.last(0), cot_ring.last(1))
    turned = lax.optimization_barrier((conv_weight, sent))[0]
    turned = turned.reshape(27, channels, channels)[::-1].transpose(0, 2, 1)
    turned = turned.reshape(27 * channels, channels)
    sums_ring.go((third, turned))
    cot_ring.go(0)
    sent = sums_ring.go(cot_ring.last(0))
    cot_parts = cot_ring.places(cols)
    turned = lax.optimization_barrier((turned, sent))[0]

    grad_features = call(
        functools.partial(input_grad_body, slots, peers, count),
        sds((per_device, channels), BF16),
        [SMEM] * 3 + [VMEM] * 3 + [HBM] * (1 + count),
        padded(bricks)
        + [
            pltpu.VMEM(cols_shape(bricks), BF16),
            pltpu.VMEM((peers, bricks * ROWS, channels), BF16),
            weight_scratch[0],
            pltpu.SMEM((bricks * 26,), jnp.int32),
            pltpu.SMEM((peers * slots,), jnp.int32),
            pltpu.SemaphoreType.DMA((count,)),
            pltpu.SemaphoreType.DMA((1,)),
        ],
        cost=13,
        name="input_grad",
    )(served, send_face, table, cotangent, features, gain, turned, *cot_parts)
    for _ in range(chips // 2 - 4):
        sums_ring.go()
    return (mixed, grad_features, sums_ring.total())


def solution(mesh):
    rows = P(("groups", "morton"), None)
    return jax.shard_map(
        local,
        mesh=mesh,
        in_specs=(rows, P(), P(), rows, rows, rows),
        out_specs=(rows, rows, rows),
        check_vma=False,
    )
```

```python
import functools
import math

import jax
import jax.numpy as jnp
import numpy as np
from jax import lax
from jax.experimental import pallas as pl
from jax.experimental.pallas import tpu as pltpu
from jax.sharding import PartitionSpec as P

F32 = jnp.float32
BF16 = jnp.bfloat16
C = 256
C_LINES = 128
B_LINES = 224
ROWS = 320
NOTES = 16
HB = 24
VMEM_LIMIT = 56 * 1024 * 1024
DIRECTIONS = [
    (i, j, l)
    for i in (-1, 0, 1)
    for j in (-1, 0, 1)
    for l in (-1, 0, 1)
    if (i, j, l) != (0, 0, 0)
]

VMEM = pl.BlockSpec(memory_space=pltpu.VMEM)
SMEM = pl.BlockSpec(memory_space=pltpu.SMEM)
ANY = pl.BlockSpec(memory_space=pl.ANY)
HBM = pl.BlockSpec(memory_space=pltpu.HBM)


def ring_order(chips):
    if chips == 8:
        return [0, 2, 4, 6, 7, 5, 3, 1]
    return list(range(chips))


def ring_tables(peers):
    chips = peers // 2
    spot = np.argsort(np.array(ring_order(chips)))
    device = np.arange(peers)
    behind = (spot[device // 2][:, None] - spot[None, :]) % chips
    half = chips // 2
    turn = np.where(behind >= half, 2 * (behind - half), 2 * (half - 1 - behind) + 1)
    place_of = np.broadcast_to(device, (peers, peers)).copy()
    if chips <= 8:
        for me in range(peers):
            for other in range(peers):
                away = behind[me, other // 2] if me % 2 == 0 else -behind[me, other // 2] % chips
                same = me % 2 == other % 2
                if away == 0:
                    place = 0 if same else 1
                elif away < half or (away == half and same):
                    place = 1 + away if same else 1 + half + away
                else:
                    away = chips - away
                    place = half + (away if not same else half + away) + half
                place_of[me, other] = place
    return np.concatenate([place_of, behind, turn, device[:, None]], axis=1).astype(np.int32)


def ring_step(x, peers, step, cross=0):
    order = ring_order(peers // 2)
    pairs = [
        (2 * order[i] + (core ^ cross), 2 * order[(i + (step or 1 - 2 * core)) % len(order)] + core)
        for i in range(len(order))
        for core in range(2)
    ]
    return lax.ppermute(x, "morton", pairs)


def swap_cores(x, peers):
    return lax.ppermute(x, "morton", [(m, m ^ 1) for m in range(peers)])


class RingGather:
    def __init__(self, x, peers):
        self.x, self.peers, self.chips = x, peers, peers // 2
        self.whole = None
        if self.chips > 8:
            self.whole = lax.all_gather(x[None], "morton", axis=0, tiled=True)
            return
        self.chains = ([x], [x])

    def go(self, chain, gate=None):
        if self.whole is not None or len(self.chains[chain]) > self.chips // 2 - chain:
            return
        held = self.chains[chain][-1]
        if gate is not None:
            held = lax.optimization_barrier((held, gate))[0]
        cross = int(chain == 1 and len(self.chains[chain]) == 1)
        self.chains[chain].append(ring_step(held, self.peers, 0, cross))

    def last(self, chain):
        return self.x if self.whole is not None else self.chains[chain][-1]

    def places(self, gate=None):
        if self.whole is not None:
            return [self.whole]
        mine = self.chains[0][1:] + self.chains[1][1:]
        held = mine
        if gate is not None:
            held = [lax.optimization_barrier((t, gate))[0] for t in mine]
        others = [swap_cores(t, self.peers) for t in [self.x] + held]
        return [t[None] for t in [self.x] + others[:1] + mine + others[1:]]


class RingScatter:
    def __init__(self, keep, give, peers):
        self.keep, self.peers, self.chips = keep, peers, peers // 2
        self.other = [swap_cores(t, peers) for t in give]
        self.held = [None, None]
        self.hop = 0

    def term(self, k):
        half = self.chips // 2
        pair = self.other[k - half][0] if k >= half else self.other[half - 1 - k][1]
        return self.keep[k] + pair.astype(F32)

    def go(self, gate=None):
        sent = []
        for way, step, count in ((0, 1, self.chips // 2), (1, -1, (self.chips - 1) // 2)):
            left = count - self.hop
            if left <= 0:
                continue
            part = self.term((-step * left) % self.chips)
            if self.held[way] is not None:
                part = part + self.held[way].astype(F32)
            part = part.astype(BF16)
            if gate is not None:
                part = lax.optimization_barrier((part, gate))[0]
            sent.append(part)
            self.held[way] = ring_step(part, self.peers, step)
        self.hop += 1
        return sent

    def total(self):
        return sum((t.astype(F32) for t in self.held if t is not None), self.term(0))


def call(body, out_shape, in_specs, scratch=(), cost=2, name=None, out_specs=None, aliases=None):
    return pl.pallas_call(
        body,
        out_shape=out_shape,
        in_specs=in_specs,
        out_specs=out_specs or jax.tree.map(lambda _: VMEM, out_shape),
        scratch_shapes=list(scratch),
        input_output_aliases=aliases or {},
        compiler_params=pltpu.CompilerParams(vmem_limit_bytes=VMEM_LIMIT),
        cost_estimate=pl.CostEstimate(flops=cost * 10**9, bytes_accessed=0, transcendentals=0),
        name=name,
    )


def put_boundary(rows, brick, a, out_ref, stage):
    wide = rows.astype(F32)
    base = brick * ROWS

    def put(at, value, lanes=slice(None)):
        out_ref[pl.ds(pl.multiple_of(base + at, 16), value.shape[0]), lanes] = value

    for edge, at in ((0, 0), (7, 64)):

        @pl.when(a == edge)
        def _():
            put(at, rows)

    @pl.when((a > 0) & (a < 7))
    def _():
        for half in range(2):
            lanes = slice(half * 128, half * 128 + 128)
            stage[half] = wide[:, lanes]
            first = stage[half, pl.ds(0, 8, stride=8), :]
            last = stage[half, pl.ds(7, 8, stride=8), :]
            put(C_LINES - 16 + 16 * a, jnp.concatenate([first, last], axis=0).astype(BF16), lanes)
        pair = jnp.concatenate([wide[:8], wide[56:]], axis=0).astype(BF16)
        put(B_LINES - 16 + 16 * a, pair)


def norm_body(recv, send, x_ref, gain_ref, hidden_ref, out_ref, stage):
    bricks, directions = recv.shape
    gain = gain_ref[...]
    lane = lax.broadcasted_iota(jnp.int32, (1, C), 1)
    codes = jnp.zeros((1, C), jnp.int32)
    for k in range(send.shape[1]):
        codes = jnp.where(lane == k, send[0, k], codes)
    served = jnp.zeros((1, C), jnp.int32)
    for brick in range(bricks):
        for number in range(directions):
            served = jnp.where(lane == recv[brick, number], brick * directions + number + 1, served)
    row = lax.broadcasted_iota(jnp.int32, (NOTES, C), 0)
    notes = jnp.where(row == 0, codes, jnp.where(row == 1, served, 0))
    out_ref[bricks * ROWS :, :] = notes.astype(F32).astype(BF16)

    def step(k, _):
        at = pl.ds(pl.multiple_of(k * 64, 64), 64)
        x = x_ref[at, :].astype(F32)
        inverse = lax.rsqrt(jnp.mean(x * x, axis=-1, keepdims=True) + 1e-6)
        v = x * inverse * gain
        rows = (v / (1.0 + jnp.exp(-v))).astype(BF16)
        hidden_ref[at, :] = rows
        put_boundary(rows, k // 8, k % 8, out_ref, stage)
        return 0

    lax.fori_loop(0, bricks * 8, step, 0)


def extract_body(x_ref, out_ref, stage):
    def step(k, _):
        at = pl.ds(pl.multiple_of(k * 64, 64), 64)
        put_boundary(x_ref[at, :], k // 8, k % 8, out_ref, stage)
        return 0

    lax.fori_loop(0, x_ref.shape[0] // 64, step, 0)


def start_padded(own_ref, cells, halo, bricks):
    zero = jnp.zeros((8, C), F32)

    def clear(k, _):
        for b in range(10):
            cells[k * 10 + b] = zero
        for side in range(2):
            for part in range(HB // 8):
                halo[side, k, part * 8 : part * 8 + 8, :] = zero
        return 0

    lax.fori_loop(0, bricks * 10, clear, 0)

    def fill(k, _):
        plane = (k // 8) * 10 + k % 8 + 1
        rows = own_ref[pl.ds(pl.multiple_of(k * 64, 64), 64), :].astype(F32)
        for b in range(8):
            cells[plane * 10 + b + 1] = rows[b * 8 : b * 8 + 8]
        return 0

    lax.fori_loop(0, bricks * 8, fill, 0)


def add_line(ref, index, line):
    ref[index] = ref[index] + line


def pick(flag, yes, no):
    if isinstance(flag, bool):
        return yes if flag else no
    return jnp.where(flag, yes, no)


def place(kind, e, keep, place_at, source_brick, brick, share, cells, halo):
    flags = [t == -1 for t in e]
    pads = [pick(f, 0, 9) for f in flags]
    facing = pick(flags[0], 64, 0)
    start = source_brick * ROWS

    def rows(at, size):
        got = share[place_at, pl.ds(pl.multiple_of(start + at, 16), size), :].astype(F32)
        return got if keep is None else jnp.where(keep, got, 0.0)

    def half(pair, axis):
        return pick(flags[axis], pair[8:], pair[:8])

    def line_b(at):
        plane = rows(at, 64)
        return pick(flags[1], plane[56:], plane[:8])

    def line_c(at):
        plane = rows(at, 64)
        ends = [
            pick(flags[2], plane[8 * b + 7 : 8 * b + 8], plane[8 * b : 8 * b + 1]) for b in range(8)
        ]
        return jnp.concatenate(ends, axis=0)

    def cell(at):
        line = line_b(at)
        return pick(flags[2], line[7:8], line[0:1])

    side = pick(flags[2], 0, 1)
    base = brick * 10

    def add_halo(at, line):
        halo[side, base + at, 8:16, :] = halo[side, base + at, 8:16, :] + line

    def add_cell(at, value):
        spot = pl.ds(pick(flags[1], 7, 16), 1)
        halo[side, base + at, spot, :] = halo[side, base + at, spot, :] + value

    if kind == (1, 0, 0):
        got = rows(facing, 64)
        first = (base + pads[0]) * 10 + 1
        for b in range(8):
            add_line(cells, first + b, got[b * 8 : b * 8 + 8])
    elif kind == (0, 1, 0):
        for a in range(8):
            if a in (0, 7):
                line = line_b(0 if a == 0 else 64)
            else:
                line = half(rows(B_LINES - 16 + 16 * a, 16), 1)
            add_line(cells, (base + a + 1) * 10 + pads[1], line)
    elif kind == (0, 0, 1):
        for a in range(8):
            if a in (0, 7):
                line = line_c(0 if a == 0 else 64)
            else:
                line = half(rows(C_LINES - 16 + 16 * a, 16), 2)
            add_halo(a + 1, line)
    elif kind == (1, 1, 0):
        add_line(cells, (base + pads[0]) * 10 + pads[1], line_b(facing))
    elif kind == (1, 0, 1):
        add_halo(pads[0], line_c(facing))
    elif kind == (0, 1, 1):
        for a in range(8):
            if a in (0, 7):
                value = cell(0 if a == 0 else 64)
            else:
                line = half(rows(C_LINES - 16 + 16 * a, 16), 2)
                value = pick(flags[1], line[7:8], line[0:1])
            add_cell(a + 1, value)
    else:
        add_cell(pads[0], cell(facing))


def windows(cells, halo, cols, bricks, out=None, sems=None):
    row = lax.broadcasted_iota(jnp.int32, (8, C), 0)

    def step(k, _):
        shifted = [[], [], []]
        for b in range(10):
            x = cells[k * 10 + b]
            before = halo[0, k, pl.ds(b + 7, 1), :]
            after = halo[1, k, pl.ds(b + 7, 1), :]
            shifted[0].append(jnp.where(row == 0, before, pltpu.roll(x, 1, 0)))
            shifted[1].append(x)
            shifted[2].append(jnp.where(row == 7, after, pltpu.roll(x, 7, 0)))
        for j in range(3):
            for l in range(3):
                block = jnp.concatenate(shifted[l][j : j + 8], axis=0).astype(BF16)
                at = (3 * j + l) * C
                cols[k, :, at : at + C] = block
        if out is not None:
            pltpu.make_async_copy(cols.at[k], out.at[k], sems.at[k]).start()
        return 0

    lax.fori_loop(0, bricks * 10, step, 0)


def wait_windows(cols, out, sems, bricks):
    def step(k, _):
        pltpu.make_async_copy(cols.at[k], out.at[k], sems.at[k]).wait()
        return 0

    lax.fori_loop(0, bricks * 10, step, 0)


def fetch(parts, share, sems):
    size = parts[0].shape[0]
    copies = [
        pltpu.make_async_copy(part, share.at[pl.ds(k * size, size)], sems.at[k])
        for k, part in enumerate(parts)
    ]
    for copy in copies:
        copy.start()
    return copies


def weight_grad_body(slots, factor, peers, count, *refs):
    recv, table, own_ref, cot_ref = refs[:4]
    parts = refs[4 : 4 + count]
    keep_ref = refs[4 + count]
    give_refs = refs[5 + count : 5 + count + peers // 4]
    out_cols, codes_ref, served_ref = refs[-15:-12]
    cells, halo, share, cols, sums, narrow, turned, codes = refs[-12:-4]
    sems, cols_sems, codes_sem, out_sems = refs[-4:]
    bricks = own_ref.shape[0] // 512
    me = table[2 * peers]
    copies = fetch(parts, share, sems)
    start_padded(own_ref, cells, halo, bricks)
    for part in range(bricks * 2):
        at = slice(part * 256, part * 256 + 256)
        turned[:, at] = cot_ref[at, :].astype(F32).T.astype(BF16)
    for copy in copies:
        copy.wait()
    for k in range(peers):
        notes = share[k, bricks * ROWS :, :].astype(F32).astype(jnp.int32)
        codes_ref[k : k + 1, :] = notes[0:1]
        served_ref[k : k + 1, :] = notes[1:2]
    codes_copy = pltpu.make_async_copy(codes_ref, codes, codes_sem.at[0])
    codes_copy.start()
    codes_copy.wait()
    for brick in range(bricks):
        for number, e in enumerate(DIRECTIONS):
            slot = recv[brick, number]
            safe = jnp.maximum(slot, 0)
            sender = safe // slots
            at = table[sender]
            code = codes[at, me * slots + safe - sender * slots]
            kind = tuple(abs(t) for t in e)
            place(kind, e, slot >= 0, at, code // 6, brick, share, cells, halo)
    windows(cells, halo, cols, bricks, out_cols, cols_sems)

    rows = 27 * C // peers
    for tap in range(27):
        i, jl = divmod(tap, 9)
        total = None
        for brick in range(bricks):
            right = cols[brick * 10 + i : brick * 10 + i + 8, :, jl * C : jl * C + C].reshape(512, C)
            left = turned[:, brick * 512 : brick * 512 + 512]
            term = jnp.dot(left, right, preferred_element_type=F32)
            total = term if total is None else total + term
        total = (total * factor).T
        start = tap * C
        while start < (tap + 1) * C:
            owner = start // rows
            stop = min((tap + 1) * C, (owner + 1) * rows)
            piece = total[start - tap * C : stop - tap * C]
            bucket = jnp.bitwise_xor(me % 2, owner % 2)
            behind = table[peers + owner // 2]
            where = slice(start - owner * rows, stop - owner * rows)
            sums[bucket, behind, where, :] = piece
            narrow[bucket, behind, where, :] = piece.astype(BF16)
            start = stop
            if stop == (owner + 1) * rows:

                @pl.when(bucket == 0)
                def _():
                    pltpu.make_async_copy(
                        sums.at[0, behind], keep_ref.at[behind], out_sems.at[0, behind]
                    ).start()

                turn = table[peers + peers // 2 + owner // 2]
                for hop, give_ref in enumerate(give_refs):

                    @pl.when((bucket == 1) & (turn // 2 == hop))
                    def _():
                        pltpu.make_async_copy(
                            narrow.at[1, behind], give_ref.at[turn % 2], out_sems.at[1, turn]
                        ).start()

    for k in range(peers // 2):
        pltpu.make_async_copy(sums.at[0, k], keep_ref.at[k], out_sems.at[0, k]).wait()
        pltpu.make_async_copy(narrow.at[1, k], give_refs[k // 2].at[k % 2], out_sems.at[1, k]).wait()
    wait_windows(cols, out_cols, cols_sems, bricks)


GROUP = 3 * C


def start_stream(cols_ref, first, cols, weight_ref, weight, sems):
    copies = []
    planes = cols.shape[0]
    for g in range(3):
        lanes = pl.ds(g * GROUP, GROUP)
        group = [
            pltpu.make_async_copy(
                cols_ref.at[pl.ds(first, planes), :, lanes], cols.at[:, :, lanes], sems.at[g, 3]
            )
        ]
        for i in range(3):
            at = pl.ds((i * 3 + g) * GROUP, GROUP)
            group.append(pltpu.make_async_copy(weight_ref.at[at], weight.at[at], sems.at[g, i]))
        copies.append(group)
    for group in copies:
        for copy in group:
            copy.start()
    return copies


def tap_sum(copies, cols, weight):
    bricks = cols.shape[0] // 10
    totals = [None] * bricks
    for g in range(3):
        for copy in copies[g]:
            copy.wait()
        for brick in range(bricks):
            for i in range(3):
                at = brick * 10 + i
                left = cols[at : at + 8, :, g * GROUP : g * GROUP + GROUP].reshape(512, GROUP)
                right = weight[(i * 3 + g) * GROUP : (i * 3 + g + 1) * GROUP, :]
                term = jnp.dot(left, right, preferred_element_type=F32)
                totals[brick] = term if totals[brick] is None else totals[brick] + term
    return totals


def mix_body(cols_ref, weight_ref, x_ref, out_ref, cols, weight, sems):
    copies = start_stream(cols_ref, 0, cols, weight_ref, weight, sems)
    for brick, total in enumerate(tap_sum(copies, cols, weight)):
        at = slice(brick * 512, brick * 512 + 512)
        out_ref[at, :] = (x_ref[at, :].astype(F32) + total).astype(BF16)


def input_grad_body(slots, peers, count, *refs):
    served, send, table, cot_ref, x_ref, gain_ref, weight_ref = refs[:7]
    parts = refs[7 : 7 + count]
    out_ref, cells, halo, cols, share, weight, heads, more, sems, weight_sem = refs[7 + count :]
    bricks = cot_ref.shape[0] // 512
    me = table[2 * peers]
    copies = fetch(parts, share, sems)
    weight_copy = pltpu.make_async_copy(weight_ref, weight, weight_sem.at[0])
    weight_copy.start()

    def no_head(k, _):
        heads[k] = -1
        return 0

    lax.fori_loop(0, bricks * 26, no_head, 0)

    def source_of(k):
        receiver = k // slots
        at = table[receiver]
        return at, served[at, me * slots + k - receiver * slots] - 1

    def sort(k, found):
        _, entry = source_of(k)
        asked = entry >= 0
        key = send[0, k] // 6 * 26 + 25 - jnp.maximum(entry, 0) % 26
        first = asked & (heads[key] < 0)
        extra = asked & jnp.logical_not(first)

        @pl.when(first)
        def _():
            heads[key] = k

        @pl.when(extra)
        def _():
            more[found] = k

        return found + jnp.where(extra, 1, 0)

    found = lax.fori_loop(0, send.shape[1], sort, 0)
    start_padded(cot_ref, cells, halo, bricks)
    for copy in copies:
        copy.wait()
    for brick in range(bricks):
        for number, e in enumerate(DIRECTIONS):
            head = heads[brick * 26 + number]
            at, entry = source_of(jnp.maximum(head, 0))
            kind = tuple(abs(t) for t in e)
            source = jnp.maximum(entry, 0) // 26
            place(kind, e, head >= 0, at, source, brick, share, cells, halo)

    def one(n, _):
        k = more[n]
        at, entry = source_of(k)
        number = 25 - entry % 26
        tap = jnp.where(number >= 13, number + 1, number)
        e = (tap // 9 - 1, (tap // 3) % 3 - 1, tap % 3 - 1)
        on = [t != 0 for t in e]
        for kind in ((1, 0, 0), (0, 1, 0), (0, 0, 1), (1, 1, 0), (1, 0, 1), (0, 1, 1), (1, 1, 1)):
            match = functools.reduce(
                jnp.logical_and, [f if w else jnp.logical_not(f) for f, w in zip(on, kind)]
            )

            @pl.when(match)
            def _():
                place(kind, e, None, at, entry // 26, send[0, k] // 6, share, cells, halo)

        return 0

    lax.fori_loop(0, found, one, 0)
    windows(cells, halo, cols, bricks)
    weight_copy.wait()
    gain = gain_ref[...]
    for brick in range(bricks):
        rows = slice(brick * 512, brick * 512 + 512)
        grad = None
        for i in range(3):
            left = cols[brick * 10 + i : brick * 10 + i + 8].reshape(512, 9 * C)
            right = weight[i * 9 * C : (i + 1) * 9 * C, :]
            term = jnp.dot(left, right, preferred_element_type=F32)
            grad = term if grad is None else grad + term
        x = x_ref[rows, :].astype(F32)
        inverse = lax.rsqrt(jnp.mean(x * x, axis=-1, keepdims=True) + 1e-6)
        unit = x * inverse
        v = unit * gain
        gate = 1.0 / (1.0 + jnp.exp(-v))
        grad = grad * (gate * (1.0 + v * (1.0 - gate))) * gain
        grad = inverse * (grad - unit * jnp.mean(grad * unit, axis=-1, keepdims=True))
        out_ref[rows, :] = (cot_ref[rows, :].astype(F32) + grad).astype(BF16)


def local(features, norm_gain, conv_weight, recv_slot, send_face, cotangent):
    channels = features.shape[1]
    per_device = features.shape[0]
    bricks = per_device // 512
    peers = lax.axis_size("morton")
    slots = send_face.shape[1] // peers
    factor = 1.0 / math.sqrt(peers * per_device)
    gain = norm_gain.reshape(1, channels)
    sds = jax.ShapeDtypeStruct
    stage = pltpu.VMEM((2, 64, 128), F32)

    def padded(n):
        return [
            pltpu.VMEM((n * 100, 8, channels), F32),
            pltpu.VMEM((2, n * 10, HB, channels), F32),
        ]

    def cols_shape(n):
        return (n * 10, 64, 9 * channels)


    table = jnp.asarray(ring_tables(peers))[lax.axis_index("morton")]

    hidden, share = call(
        norm_body,
        (sds((per_device, channels), BF16), sds((bricks * ROWS + NOTES, channels), BF16)),
        [SMEM, SMEM, VMEM, VMEM],
        [stage],
        name="norm",
    )(recv_slot, send_face, features, gain)
    hidden_ring = RingGather(share, peers)
    cot_share = call(
        extract_body,
        sds((bricks * ROWS, channels), BF16),
        [VMEM],
        [stage],
        name="extract",
    )(cotangent)
    hidden_ring.go(0)
    hidden_ring.go(1)
    hidden_ring.go(0, cot_share)
    hidden_ring.go(1)
    cot_ring = RingGather(cot_share, peers)
    cot_ring.go(0, hidden_ring.last(0))
    cot_ring.go(1, hidden_ring.last(1))
    hidden_ring.go(0, table)
    hidden_ring.go(1)
    hidden_ring.go(0)
    hidden_parts = hidden_ring.places()
    cot_ring.go(0, hidden_ring.last(1))
    cot_ring.go(1, hidden_ring.last(0))

    count = len(hidden_parts)
    rows = 27 * channels // peers
    chips = peers // 2
    keep, *give, cols, _, served = call(
        functools.partial(weight_grad_body, slots, factor, peers, count),
        (
            sds((chips, rows, channels), F32),
            *[sds((2, rows, channels), BF16)] * (chips // 2),
            sds(cols_shape(bricks), BF16),
            sds((peers, channels), jnp.int32),
            sds((peers, channels), jnp.int32),
        ),
        [SMEM] * 2 + [VMEM] * 2 + [HBM] * count,
        padded(bricks)
        + [
            pltpu.VMEM((peers, bricks * ROWS + NOTES, channels), BF16),
            pltpu.VMEM(cols_shape(bricks), BF16),
            pltpu.VMEM((2, chips, rows, channels), F32),
            pltpu.VMEM((2, chips, rows, channels), BF16),
            pltpu.VMEM((channels, per_device), BF16),
            pltpu.SMEM((peers, channels), jnp.int32),
            pltpu.SemaphoreType.DMA((count,)),
            pltpu.SemaphoreType.DMA((bricks * 10,)),
            pltpu.SemaphoreType.DMA((1,)),
            pltpu.SemaphoreType.DMA((2, chips)),
        ],
        cost=9,
        name="weight_grad",
        out_specs=(*[HBM] * (2 + chips // 2), VMEM, VMEM),
    )(recv_slot, table, hidden, cotangent, *hidden_parts)

    first = (cot_ring.last(0), cot_ring.last(1))
    give = [lax.optimization_barrier((t, first))[0] for t in give]
    sums_ring = RingScatter(keep, give, peers)
    sent = sums_ring.go()
    cot_ring.go(0, cols)
    cot_ring.go(1, cols)
    second = (cot_ring.last(0), cot_ring.last(1))
    mix_cols = lax.optimization_barrier((cols, sent))[0]
    weight_scratch = pltpu.VMEM((27 * channels, channels), BF16)
    mixed = call(
        mix_body,
        sds((per_device, channels), BF16),
        [HBM, HBM, VMEM],
        [pltpu.VMEM(cols_shape(bricks), BF16), weight_scratch, pltpu.SemaphoreType.DMA((3, 4))],
        cost=6,
        name="mix",
    )(mix_cols, conv_weight, features)
    sent = sums_ring.go((second, mixed))
    cot_ring.go(0)
    turned = lax.optimization_barrier((conv_weight, sent))[0]
    turned = turned.reshape(27, channels, channels)[::-1].transpose(0, 2, 1)
    turned = turned.reshape(27 * channels, channels)
    sums_ring.go((cot_ring.last(0), turned))
    cot_parts = cot_ring.places(cols)
    sent = sums_ring.go()
    turned = lax.optimization_barrier((turned, sent))[0]

    grad_features = call(
        functools.partial(input_grad_body, slots, peers, count),
        sds((per_device, channels), BF16),
        [SMEM] * 3 + [VMEM] * 3 + [HBM] * (1 + count),
        padded(bricks)
        + [
            pltpu.VMEM(cols_shape(bricks), BF16),
            pltpu.VMEM((peers, bricks * ROWS, channels), BF16),
            weight_scratch,
            pltpu.SMEM((bricks * 26,), jnp.int32),
            pltpu.SMEM((peers * slots,), jnp.int32),
            pltpu.SemaphoreType.DMA((count,)),
            pltpu.SemaphoreType.DMA((1,)),
        ],
        cost=13,
        name="input_grad",
    )(served, send_face, table, cotangent, features, gain, turned, *cot_parts)
    for _ in range(chips // 2 - 4):
        sums_ring.go()
    return (mixed, grad_features, sums_ring.total())


def solution(mesh):
    rows = P(("groups", "morton"), None)
    return jax.shard_map(
        local,
        mesh=mesh,
        in_specs=(rows, P(), P(), rows, rows, rows),
        out_specs=(rows, rows, rows),
        check_vma=False,
    )
```

```python
import functools
import math

import jax
import jax.numpy as jnp
import numpy as np
from jax import lax
from jax.experimental import pallas as pl
from jax.experimental.pallas import tpu as pltpu
from jax.sharding import PartitionSpec as P

F32 = jnp.float32
BF16 = jnp.bfloat16
C = 256
C_LINES = 128
B_LINES = 224
ROWS = 320
NOTES = 16
HB = 24
VMEM_LIMIT = 56 * 1024 * 1024
DIRECTIONS = [
    (i, j, l)
    for i in (-1, 0, 1)
    for j in (-1, 0, 1)
    for l in (-1, 0, 1)
    if (i, j, l) != (0, 0, 0)
]

VMEM = pl.BlockSpec(memory_space=pltpu.VMEM)
SMEM = pl.BlockSpec(memory_space=pltpu.SMEM)
ANY = pl.BlockSpec(memory_space=pl.ANY)
HBM = pl.BlockSpec(memory_space=pltpu.HBM)


def ring_order(chips):
    if chips == 8:
        return [0, 2, 4, 6, 7, 5, 3, 1]
    return list(range(chips))


def ring_tables(peers):
    chips = peers // 2
    spot = np.argsort(np.array(ring_order(chips)))
    device = np.arange(peers)
    behind = (spot[device // 2][:, None] - spot[None, :]) % chips
    half = chips // 2
    turn = np.where(behind >= half, 2 * (behind - half), 2 * (half - 1 - behind) + 1)
    place_of = np.broadcast_to(device, (peers, peers)).copy()
    if chips <= 8:
        for me in range(peers):
            for other in range(peers):
                away = behind[me, other // 2] if me % 2 == 0 else -behind[me, other // 2] % chips
                same = me % 2 == other % 2
                if away == 0:
                    place = 0 if same else 1
                elif away < half or (away == half and same):
                    place = 1 + away if same else 1 + half + away
                else:
                    away = chips - away
                    place = half + (away if not same else half + away) + half
                place_of[me, other] = place
    return np.concatenate([place_of, behind, turn, device[:, None]], axis=1).astype(np.int32)


def ring_step(x, peers, step, cross=0):
    order = ring_order(peers // 2)
    pairs = [
        (2 * order[i] + (core ^ cross), 2 * order[(i + (step or 1 - 2 * core)) % len(order)] + core)
        for i in range(len(order))
        for core in range(2)
    ]
    return lax.ppermute(x, "morton", pairs)


def swap_cores(x, peers):
    return lax.ppermute(x, "morton", [(m, m ^ 1) for m in range(peers)])


class RingGather:
    def __init__(self, x, peers):
        self.x, self.peers, self.chips = x, peers, peers // 2
        self.whole = None
        if self.chips > 8:
            self.whole = lax.all_gather(x[None], "morton", axis=0, tiled=True)
            return
        self.chains = ([x], [x])

    def go(self, chain, gate=None):
        if self.whole is not None or len(self.chains[chain]) > self.chips // 2 - chain:
            return
        held = self.chains[chain][-1]
        if gate is not None:
            held = lax.optimization_barrier((held, gate))[0]
        cross = int(chain == 1 and len(self.chains[chain]) == 1)
        self.chains[chain].append(ring_step(held, self.peers, 0, cross))

    def last(self, chain):
        return self.x if self.whole is not None else self.chains[chain][-1]

    def places(self, gate=None):
        if self.whole is not None:
            return [self.whole]
        mine = self.chains[0][1:] + self.chains[1][1:]
        held = mine
        if gate is not None:
            held = [lax.optimization_barrier((t, gate))[0] for t in mine]
        others = [swap_cores(t, self.peers) for t in [self.x] + held]
        return [t[None] for t in [self.x] + others[:1] + mine + others[1:]]


class RingScatter:
    def __init__(self, keep, give, peers):
        self.keep, self.peers, self.chips = keep, peers, peers // 2
        self.other = [swap_cores(t, peers) for t in give]
        self.held = [None, None]
        self.hop = 0

    def term(self, k):
        half = self.chips // 2
        pair = self.other[k - half][0] if k >= half else self.other[half - 1 - k][1]
        return self.keep[k] + pair.astype(F32)

    def go(self, gate=None):
        sent = []
        for way, step, count in ((0, 1, self.chips // 2), (1, -1, (self.chips - 1) // 2)):
            left = count - self.hop
            if left <= 0:
                continue
            part = self.term((-step * left) % self.chips)
            if self.held[way] is not None:
                part = part + self.held[way].astype(F32)
            part = part.astype(BF16)
            if gate is not None:
                part = lax.optimization_barrier((part, gate))[0]
            sent.append(part)
            self.held[way] = ring_step(part, self.peers, step)
        self.hop += 1
        return sent

    def total(self):
        return sum((t.astype(F32) for t in self.held if t is not None), self.term(0))


def call(body, out_shape, in_specs, scratch=(), cost=2, name=None, out_specs=None, aliases=None):
    return pl.pallas_call(
        body,
        out_shape=out_shape,
        in_specs=in_specs,
        out_specs=out_specs or jax.tree.map(lambda _: VMEM, out_shape),
        scratch_shapes=list(scratch),
        input_output_aliases=aliases or {},
        compiler_params=pltpu.CompilerParams(vmem_limit_bytes=VMEM_LIMIT),
        cost_estimate=pl.CostEstimate(flops=cost * 10**9, bytes_accessed=0, transcendentals=0),
        name=name,
    )


def put_boundary(rows, brick, a, out_ref, stage):
    wide = rows.astype(F32)
    base = brick * ROWS

    def put(at, value, lanes=slice(None)):
        out_ref[pl.ds(pl.multiple_of(base + at, 16), value.shape[0]), lanes] = value

    for edge, at in ((0, 0), (7, 64)):

        @pl.when(a == edge)
        def _():
            put(at, rows)

    @pl.when((a > 0) & (a < 7))
    def _():
        for half in range(2):
            lanes = slice(half * 128, half * 128 + 128)
            stage[half] = wide[:, lanes]
            first = stage[half, pl.ds(0, 8, stride=8), :]
            last = stage[half, pl.ds(7, 8, stride=8), :]
            put(C_LINES - 16 + 16 * a, jnp.concatenate([first, last], axis=0).astype(BF16), lanes)
        pair = jnp.concatenate([wide[:8], wide[56:]], axis=0).astype(BF16)
        put(B_LINES - 16 + 16 * a, pair)


def norm_body(recv, send, x_ref, gain_ref, hidden_ref, out_ref, stage):
    bricks, directions = recv.shape
    gain = gain_ref[...]
    lane = lax.broadcasted_iota(jnp.int32, (1, C), 1)
    codes = jnp.zeros((1, C), jnp.int32)
    for k in range(send.shape[1]):
        codes = jnp.where(lane == k, send[0, k], codes)
    served = jnp.zeros((1, C), jnp.int32)
    for brick in range(bricks):
        for number in range(directions):
            served = jnp.where(lane == recv[brick, number], brick * directions + number + 1, served)
    row = lax.broadcasted_iota(jnp.int32, (NOTES, C), 0)
    notes = jnp.where(row == 0, codes, jnp.where(row == 1, served, 0))
    out_ref[bricks * ROWS :, :] = notes.astype(F32).astype(BF16)

    def step(k, _):
        at = pl.ds(pl.multiple_of(k * 64, 64), 64)
        x = x_ref[at, :].astype(F32)
        inverse = lax.rsqrt(jnp.mean(x * x, axis=-1, keepdims=True) + 1e-6)
        v = x * inverse * gain
        rows = (v / (1.0 + jnp.exp(-v))).astype(BF16)
        hidden_ref[at, :] = rows
        put_boundary(rows, k // 8, k % 8, out_ref, stage)
        return 0

    lax.fori_loop(0, bricks * 8, step, 0)


def extract_body(x_ref, out_ref, stage):
    def step(k, _):
        at = pl.ds(pl.multiple_of(k * 64, 64), 64)
        put_boundary(x_ref[at, :], k // 8, k % 8, out_ref, stage)
        return 0

    lax.fori_loop(0, x_ref.shape[0] // 64, step, 0)


def start_padded(own_ref, cells, halo, bricks):
    zero = jnp.zeros((8, C), F32)

    def clear(k, _):
        for b in range(10):
            cells[k * 10 + b] = zero
        for side in range(2):
            for part in range(HB // 8):
                halo[side, k, part * 8 : part * 8 + 8, :] = zero
        return 0

    lax.fori_loop(0, bricks * 10, clear, 0)

    def fill(k, _):
        plane = (k // 8) * 10 + k % 8 + 1
        rows = own_ref[pl.ds(pl.multiple_of(k * 64, 64), 64), :].astype(F32)
        for b in range(8):
            cells[plane * 10 + b + 1] = rows[b * 8 : b * 8 + 8]
        return 0

    lax.fori_loop(0, bricks * 8, fill, 0)


def add_line(ref, index, line):
    ref[index] = ref[index] + line


def pick(flag, yes, no):
    if isinstance(flag, bool):
        return yes if flag else no
    return jnp.where(flag, yes, no)


def place(kind, e, keep, place_at, source_brick, brick, share, cells, halo):
    flags = [t == -1 for t in e]
    pads = [pick(f, 0, 9) for f in flags]
    facing = pick(flags[0], 64, 0)
    start = source_brick * ROWS

    def rows(at, size):
        got = share[place_at, pl.ds(pl.multiple_of(start + at, 16), size), :].astype(F32)
        return got if keep is None else jnp.where(keep, got, 0.0)

    def half(pair, axis):
        return pick(flags[axis], pair[8:], pair[:8])

    def line_b(at):
        plane = rows(at, 64)
        return pick(flags[1], plane[56:], plane[:8])

    def line_c(at):
        plane = rows(at, 64)
        ends = [
            pick(flags[2], plane[8 * b + 7 : 8 * b + 8], plane[8 * b : 8 * b + 1]) for b in range(8)
        ]
        return jnp.concatenate(ends, axis=0)

    def cell(at):
        line = line_b(at)
        return pick(flags[2], line[7:8], line[0:1])

    side = pick(flags[2], 0, 1)
    base = brick * 10

    def add_halo(at, line):
        halo[side, base + at, 8:16, :] = halo[side, base + at, 8:16, :] + line

    def add_cell(at, value):
        spot = pl.ds(pick(flags[1], 7, 16), 1)
        halo[side, base + at, spot, :] = halo[side, base + at, spot, :] + value

    if kind == (1, 0, 0):
        got = rows(facing, 64)
        first = (base + pads[0]) * 10 + 1
        for b in range(8):
            add_line(cells, first + b, got[b * 8 : b * 8 + 8])
    elif kind == (0, 1, 0):
        for a in range(8):
            if a in (0, 7):
                line = line_b(0 if a == 0 else 64)
            else:
                line = half(rows(B_LINES - 16 + 16 * a, 16), 1)
            add_line(cells, (base + a + 1) * 10 + pads[1], line)
    elif kind == (0, 0, 1):
        for a in range(8):
            if a in (0, 7):
                line = line_c(0 if a == 0 else 64)
            else:
                line = half(rows(C_LINES - 16 + 16 * a, 16), 2)
            add_halo(a + 1, line)
    elif kind == (1, 1, 0):
        add_line(cells, (base + pads[0]) * 10 + pads[1], line_b(facing))
    elif kind == (1, 0, 1):
        add_halo(pads[0], line_c(facing))
    elif kind == (0, 1, 1):
        for a in range(8):
            if a in (0, 7):
                value = cell(0 if a == 0 else 64)
            else:
                line = half(rows(C_LINES - 16 + 16 * a, 16), 2)
                value = pick(flags[1], line[7:8], line[0:1])
            add_cell(a + 1, value)
    else:
        add_cell(pads[0], cell(facing))


def windows(cells, halo, cols, bricks, out=None, sems=None):
    row = lax.broadcasted_iota(jnp.int32, (8, C), 0)

    def step(k, _):
        shifted = [[], [], []]
        for b in range(10):
            x = cells[k * 10 + b]
            before = halo[0, k, pl.ds(b + 7, 1), :]
            after = halo[1, k, pl.ds(b + 7, 1), :]
            shifted[0].append(jnp.where(row == 0, before, pltpu.roll(x, 1, 0)))
            shifted[1].append(x)
            shifted[2].append(jnp.where(row == 7, after, pltpu.roll(x, 7, 0)))
        for j in range(3):
            for l in range(3):
                block = jnp.concatenate(shifted[l][j : j + 8], axis=0).astype(BF16)
                at = (3 * j + l) * C
                cols[k, :, at : at + C] = block
        if out is not None:
            pltpu.make_async_copy(cols.at[k], out.at[k], sems.at[k]).start()
        return 0

    lax.fori_loop(0, bricks * 10, step, 0)


def wait_windows(cols, out, sems, bricks):
    def step(k, _):
        pltpu.make_async_copy(cols.at[k], out.at[k], sems.at[k]).wait()
        return 0

    lax.fori_loop(0, bricks * 10, step, 0)


def fetch(parts, share, sems):
    size = parts[0].shape[0]
    copies = [
        pltpu.make_async_copy(part, share.at[pl.ds(k * size, size)], sems.at[k])
        for k, part in enumerate(parts)
    ]
    for copy in copies:
        copy.start()
    return copies


def weight_grad_body(slots, factor, peers, count, *refs):
    recv, table, own_ref, cot_ref = refs[:4]
    parts = refs[4 : 4 + count]
    keep_ref = refs[4 + count]
    give_refs = refs[5 + count : 5 + count + peers // 4]
    out_cols, codes_ref, served_ref = refs[-15:-12]
    cells, halo, share, cols, sums, narrow, turned, codes = refs[-12:-4]
    sems, cols_sems, codes_sem, out_sems = refs[-4:]
    bricks = own_ref.shape[0] // 512
    me = table[2 * peers]
    copies = fetch(parts, share, sems)
    start_padded(own_ref, cells, halo, bricks)
    for part in range(bricks * 2):
        at = slice(part * 256, part * 256 + 256)
        turned[:, at] = cot_ref[at, :].astype(F32).T.astype(BF16)
    for copy in copies:
        copy.wait()
    for k in range(peers):
        notes = share[k, bricks * ROWS :, :].astype(F32).astype(jnp.int32)
        codes_ref[k : k + 1, :] = notes[0:1]
        served_ref[k : k + 1, :] = notes[1:2]
    codes_copy = pltpu.make_async_copy(codes_ref, codes, codes_sem.at[0])
    codes_copy.start()
    codes_copy.wait()
    for brick in range(bricks):
        for number, e in enumerate(DIRECTIONS):
            slot = recv[brick, number]
            safe = jnp.maximum(slot, 0)
            sender = safe // slots
            at = table[sender]
            code = codes[at, me * slots + safe - sender * slots]
            kind = tuple(abs(t) for t in e)
            place(kind, e, slot >= 0, at, code // 6, brick, share, cells, halo)
    windows(cells, halo, cols, bricks, out_cols, cols_sems)

    rows = 27 * C // peers
    for tap in range(27):
        i, jl = divmod(tap, 9)
        total = None
        for brick in range(bricks):
            right = cols[brick * 10 + i : brick * 10 + i + 8, :, jl * C : jl * C + C].reshape(512, C)
            left = turned[:, brick * 512 : brick * 512 + 512]
            term = jnp.dot(left, right, preferred_element_type=F32)
            total = term if total is None else total + term
        total = (total * factor).T
        start = tap * C
        while start < (tap + 1) * C:
            owner = start // rows
            stop = min((tap + 1) * C, (owner + 1) * rows)
            piece = total[start - tap * C : stop - tap * C]
            bucket = jnp.bitwise_xor(me % 2, owner % 2)
            behind = table[peers + owner // 2]
            where = slice(start - owner * rows, stop - owner * rows)
            sums[bucket, behind, where, :] = piece
            narrow[bucket, behind, where, :] = piece.astype(BF16)
            start = stop
            if stop == (owner + 1) * rows:

                @pl.when(bucket == 0)
                def _():
                    pltpu.make_async_copy(
                        sums.at[0, behind], keep_ref.at[behind], out_sems.at[0, behind]
                    ).start()

                turn = table[peers + peers // 2 + owner // 2]
                for hop, give_ref in enumerate(give_refs):

                    @pl.when((bucket == 1) & (turn // 2 == hop))
                    def _():
                        pltpu.make_async_copy(
                            narrow.at[1, behind], give_ref.at[turn % 2], out_sems.at[1, turn]
                        ).start()

    for k in range(peers // 2):
        pltpu.make_async_copy(sums.at[0, k], keep_ref.at[k], out_sems.at[0, k]).wait()
        pltpu.make_async_copy(narrow.at[1, k], give_refs[k // 2].at[k % 2], out_sems.at[1, k]).wait()
    wait_windows(cols, out_cols, cols_sems, bricks)


GROUP = 3 * C


def start_stream(cols_ref, first, cols, weight_ref, weight, sems):
    copies = []
    planes = cols.shape[0]
    for g in range(3):
        lanes = pl.ds(g * GROUP, GROUP)
        group = [
            pltpu.make_async_copy(
                cols_ref.at[pl.ds(first, planes), :, lanes], cols.at[:, :, lanes], sems.at[g, 3]
            )
        ]
        for i in range(3):
            at = pl.ds((i * 3 + g) * GROUP, GROUP)
            group.append(pltpu.make_async_copy(weight_ref.at[at], weight.at[at], sems.at[g, i]))
        copies.append(group)
    for group in copies:
        for copy in group:
            copy.start()
    return copies


def tap_sum(copies, cols, weight):
    bricks = cols.shape[0] // 10
    totals = [None] * bricks
    for g in range(3):
        for copy in copies[g]:
            copy.wait()
        for brick in range(bricks):
            for i in range(3):
                at = brick * 10 + i
                left = cols[at : at + 8, :, g * GROUP : g * GROUP + GROUP].reshape(512, GROUP)
                right = weight[(i * 3 + g) * GROUP : (i * 3 + g + 1) * GROUP, :]
                term = jnp.dot(left, right, preferred_element_type=F32)
                totals[brick] = term if totals[brick] is None else totals[brick] + term
    return totals


def mix_body(cols_ref, weight_ref, x_ref, out_ref, cols, weight, sems):
    copies = start_stream(cols_ref, 0, cols, weight_ref, weight, sems)
    for brick, total in enumerate(tap_sum(copies, cols, weight)):
        at = slice(brick * 512, brick * 512 + 512)
        out_ref[at, :] = (x_ref[at, :].astype(F32) + total).astype(BF16)


def input_grad_body(slots, peers, *refs):
    served, send, table, cot_ref, x_ref, gain_ref, weight_ref, all_ref = refs[:8]
    out_ref, cells, halo, cols, share, weight, heads, more, sems = refs[8:]
    bricks = cot_ref.shape[0] // 512
    me = table[2 * peers]
    share_copy = pltpu.make_async_copy(all_ref, share, sems.at[0])
    share_copy.start()
    weight_copy = pltpu.make_async_copy(weight_ref, weight, sems.at[1])
    weight_copy.start()

    def no_head(k, _):
        heads[k] = -1
        return 0

    lax.fori_loop(0, bricks * 26, no_head, 0)

    def source_of(k):
        receiver = k // slots
        return receiver, served[table[receiver], me * slots + k - receiver * slots] - 1

    def sort(k, found):
        _, entry = source_of(k)
        asked = entry >= 0
        key = send[0, k] // 6 * 26 + 25 - jnp.maximum(entry, 0) % 26
        first = asked & (heads[key] < 0)
        extra = asked & jnp.logical_not(first)

        @pl.when(first)
        def _():
            heads[key] = k

        @pl.when(extra)
        def _():
            more[found] = k

        return found + jnp.where(extra, 1, 0)

    found = lax.fori_loop(0, send.shape[1], sort, 0)
    start_padded(cot_ref, cells, halo, bricks)
    share_copy.wait()
    for brick in range(bricks):
        for number, e in enumerate(DIRECTIONS):
            head = heads[brick * 26 + number]
            at, entry = source_of(jnp.maximum(head, 0))
            kind = tuple(abs(t) for t in e)
            source = jnp.maximum(entry, 0) // 26
            place(kind, e, head >= 0, at, source, brick, share, cells, halo)

    def one(n, _):
        k = more[n]
        at, entry = source_of(k)
        number = 25 - entry % 26
        tap = jnp.where(number >= 13, number + 1, number)
        e = (tap // 9 - 1, (tap // 3) % 3 - 1, tap % 3 - 1)
        on = [t != 0 for t in e]
        for kind in ((1, 0, 0), (0, 1, 0), (0, 0, 1), (1, 1, 0), (1, 0, 1), (0, 1, 1), (1, 1, 1)):
            match = functools.reduce(
                jnp.logical_and, [f if w else jnp.logical_not(f) for f, w in zip(on, kind)]
            )

            @pl.when(match)
            def _():
                place(kind, e, None, at, entry // 26, send[0, k] // 6, share, cells, halo)

        return 0

    lax.fori_loop(0, found, one, 0)
    windows(cells, halo, cols, bricks)
    weight_copy.wait()
    gain = gain_ref[...]
    for brick in range(bricks):
        rows = slice(brick * 512, brick * 512 + 512)
        grad = None
        for tap in range(27):
            i, jl = divmod(tap, 9)
            first = brick * 10 + i
            left = cols[first : first + 8, :, jl * C : jl * C + C].reshape(512, C)
            right = weight[(26 - tap) * C : (27 - tap) * C, :]
            term = lax.dot_general(left, right, (((1,), (1,)), ((), ())), preferred_element_type=F32)
            grad = term if grad is None else grad + term
        x = x_ref[rows, :].astype(F32)
        inverse = lax.rsqrt(jnp.mean(x * x, axis=-1, keepdims=True) + 1e-6)
        unit = x * inverse
        v = unit * gain
        gate = 1.0 / (1.0 + jnp.exp(-v))
        grad = grad * (gate * (1.0 + v * (1.0 - gate))) * gain
        grad = inverse * (grad - unit * jnp.mean(grad * unit, axis=-1, keepdims=True))
        out_ref[rows, :] = (cot_ref[rows, :].astype(F32) + grad).astype(BF16)


def local(features, norm_gain, conv_weight, recv_slot, send_face, cotangent):
    channels = features.shape[1]
    per_device = features.shape[0]
    bricks = per_device // 512
    peers = lax.axis_size("morton")
    slots = send_face.shape[1] // peers
    factor = 1.0 / math.sqrt(peers * per_device)
    gain = norm_gain.reshape(1, channels)
    sds = jax.ShapeDtypeStruct
    stage = pltpu.VMEM((2, 64, 128), F32)

    def padded(n):
        return [
            pltpu.VMEM((n * 100, 8, channels), F32),
            pltpu.VMEM((2, n * 10, HB, channels), F32),
        ]

    def cols_shape(n):
        return (n * 10, 64, 9 * channels)


    table = jnp.asarray(ring_tables(peers))[lax.axis_index("morton")]

    hidden, share = call(
        norm_body,
        (sds((per_device, channels), BF16), sds((bricks * ROWS + NOTES, channels), BF16)),
        [SMEM, SMEM, VMEM, VMEM],
        [stage],
        name="norm",
    )(recv_slot, send_face, features, gain)
    hidden_ring = RingGather(share, peers)
    cot_share = call(
        extract_body,
        sds((bricks * ROWS, channels), BF16),
        [VMEM],
        [stage],
        name="extract",
    )(cotangent)
    hidden_ring.go(0)
    hidden_ring.go(1)
    hidden_ring.go(0, cot_share)
    hidden_ring.go(1)
    hidden_ring.go(0, table)
    hidden_ring.go(1)
    hidden_ring.go(0)
    hidden_parts = hidden_ring.places()
    cot_all = lax.all_gather(cot_share[None], "morton", axis=0, tiled=True)

    count = len(hidden_parts)
    rows = 27 * channels // peers
    chips = peers // 2
    keep, *give, cols, _, served = call(
        functools.partial(weight_grad_body, slots, factor, peers, count),
        (
            sds((chips, rows, channels), F32),
            *[sds((2, rows, channels), BF16)] * (chips // 2),
            sds(cols_shape(bricks), BF16),
            sds((peers, channels), jnp.int32),
            sds((peers, channels), jnp.int32),
        ),
        [SMEM] * 2 + [VMEM] * 2 + [HBM] * count,
        padded(bricks)
        + [
            pltpu.VMEM((peers, bricks * ROWS + NOTES, channels), BF16),
            pltpu.VMEM(cols_shape(bricks), BF16),
            pltpu.VMEM((2, chips, rows, channels), F32),
            pltpu.VMEM((2, chips, rows, channels), BF16),
            pltpu.VMEM((channels, per_device), BF16),
            pltpu.SMEM((peers, channels), jnp.int32),
            pltpu.SemaphoreType.DMA((count,)),
            pltpu.SemaphoreType.DMA((bricks * 10,)),
            pltpu.SemaphoreType.DMA((1,)),
            pltpu.SemaphoreType.DMA((2, chips)),
        ],
        cost=9,
        name="weight_grad",
        out_specs=(*[HBM] * (2 + chips // 2), VMEM, VMEM),
    )(recv_slot, table, hidden, cotangent, *hidden_parts)

    sums_ring = RingScatter(keep, give, peers)
    sent = sums_ring.go()
    mix_cols = lax.optimization_barrier((cols, sent))[0]
    weight_scratch = [
        pltpu.VMEM((27 * channels, channels), BF16),
        pltpu.SemaphoreType.DMA((3, 4)),
    ]
    mixed = call(
        mix_body,
        sds((per_device, channels), BF16),
        [HBM, HBM, VMEM],
        [pltpu.VMEM(cols_shape(bricks), BF16)] + weight_scratch,
        cost=6,
        name="mix",
    )(mix_cols, conv_weight, features)
    sums_ring.go(mixed)
    sums_ring.go()
    sent = sums_ring.go()
    served = lax.optimization_barrier((served, sent))[0]

    grad_features = call(
        functools.partial(input_grad_body, slots, peers),
        sds((per_device, channels), BF16),
        [SMEM] * 3 + [VMEM] * 3 + [HBM] * 2,
        padded(bricks)
        + [
            pltpu.VMEM(cols_shape(bricks), BF16),
            pltpu.VMEM((peers, bricks * ROWS, channels), BF16),
            weight_scratch[0],
            pltpu.SMEM((bricks * 26,), jnp.int32),
            pltpu.SMEM((peers * slots,), jnp.int32),
            pltpu.SemaphoreType.DMA((2,)),
        ],
        cost=13,
        name="input_grad",
    )(served, send_face, table, cotangent, features, gain, conv_weight, cot_all)
    for _ in range(chips // 2 - 4):
        sums_ring.go()
    return (mixed, grad_features, sums_ring.total())


def solution(mesh):
    rows = P(("groups", "morton"), None)
    return jax.shard_map(
        local,
        mesh=mesh,
        in_specs=(rows, P(), P(), rows, rows, rows),
        out_specs=(rows, rows, rows),
        check_vma=False,
    )
```

```python
import functools
import math

import jax
import jax.numpy as jnp
import numpy as np
from jax import lax
from jax.experimental import pallas as pl
from jax.experimental.pallas import tpu as pltpu
from jax.sharding import PartitionSpec as P

F32 = jnp.float32
BF16 = jnp.bfloat16
C = 256
C_LINES = 128
B_LINES = 224
ROWS = 320
NOTES = 16
HB = 24
VMEM_LIMIT = 56 * 1024 * 1024
DIRECTIONS = [
    (i, j, l)
    for i in (-1, 0, 1)
    for j in (-1, 0, 1)
    for l in (-1, 0, 1)
    if (i, j, l) != (0, 0, 0)
]

VMEM = pl.BlockSpec(memory_space=pltpu.VMEM)
SMEM = pl.BlockSpec(memory_space=pltpu.SMEM)
ANY = pl.BlockSpec(memory_space=pl.ANY)
HBM = pl.BlockSpec(memory_space=pltpu.HBM)


def ring_order(chips):
    if chips == 8:
        return [0, 2, 4, 6, 7, 5, 3, 1]
    return list(range(chips))


def ring_tables(peers):
    chips = peers // 2
    spot = np.argsort(np.array(ring_order(chips)))
    device = np.arange(peers)
    behind = (spot[device // 2][:, None] - spot[None, :]) % chips
    half = chips // 2
    turn = np.where(behind >= half, 2 * (behind - half), 2 * (half - 1 - behind) + 1)
    place_of = np.broadcast_to(device, (peers, peers)).copy()
    if chips <= 8:
        for me in range(peers):
            for other in range(peers):
                away = behind[me, other // 2] if me % 2 == 0 else -behind[me, other // 2] % chips
                same = me % 2 == other % 2
                if away == 0:
                    place = 0 if same else 1
                elif away < half or (away == half and same):
                    place = 1 + away if same else 1 + half + away
                else:
                    away = chips - away
                    place = half + (away if not same else half + away) + half
                place_of[me, other] = place
    return np.concatenate([place_of, behind, turn, device[:, None]], axis=1).astype(np.int32)


def ring_step(x, peers, step, cross=0):
    order = ring_order(peers // 2)
    pairs = [
        (2 * order[i] + (core ^ cross), 2 * order[(i + (step or 1 - 2 * core)) % len(order)] + core)
        for i in range(len(order))
        for core in range(2)
    ]
    return lax.ppermute(x, "morton", pairs)


def swap_cores(x, peers):
    return lax.ppermute(x, "morton", [(m, m ^ 1) for m in range(peers)])


class RingGather:
    def __init__(self, x, peers):
        self.x, self.peers, self.chips = x, peers, peers // 2
        self.whole = None
        if self.chips > 8:
            self.whole = lax.all_gather(x[None], "morton", axis=0, tiled=True)
            return
        self.chains = ([x], [x])

    def go(self, chain, gate=None):
        if self.whole is not None or len(self.chains[chain]) > self.chips // 2 - chain:
            return
        held = self.chains[chain][-1]
        if gate is not None:
            held = lax.optimization_barrier((held, gate))[0]
        cross = int(chain == 1 and len(self.chains[chain]) == 1)
        self.chains[chain].append(ring_step(held, self.peers, 0, cross))

    def last(self, chain):
        return self.x if self.whole is not None else self.chains[chain][-1]

    def places(self, gate=None):
        if self.whole is not None:
            return [self.whole]
        mine = self.chains[0][1:] + self.chains[1][1:]
        held = mine
        if gate is not None:
            held = [lax.optimization_barrier((t, gate))[0] for t in mine]
        others = [swap_cores(t, self.peers) for t in [self.x] + held]
        return [t[None] for t in [self.x] + others[:1] + mine + others[1:]]


class RingScatter:
    def __init__(self, keep, give, peers):
        self.keep, self.peers, self.chips = keep, peers, peers // 2
        self.other = [swap_cores(t, peers) for t in give]
        self.held = [None, None]
        self.hop = 0

    def term(self, k):
        half = self.chips // 2
        pair = self.other[k - half][0] if k >= half else self.other[half - 1 - k][1]
        return self.keep[k] + pair.astype(F32)

    def go(self, gate=None):
        sent = []
        for way, step, count in ((0, 1, self.chips // 2), (1, -1, (self.chips - 1) // 2)):
            left = count - self.hop
            if left <= 0:
                continue
            part = self.term((-step * left) % self.chips)
            if self.held[way] is not None:
                part = part + self.held[way].astype(F32)
            part = part.astype(BF16)
            if gate is not None:
                part = lax.optimization_barrier((part, gate))[0]
            sent.append(part)
            self.held[way] = ring_step(part, self.peers, step)
        self.hop += 1
        return sent

    def total(self):
        return sum((t.astype(F32) for t in self.held if t is not None), self.term(0))


def call(body, out_shape, in_specs, scratch=(), cost=2, name=None, out_specs=None, aliases=None):
    return pl.pallas_call(
        body,
        out_shape=out_shape,
        in_specs=in_specs,
        out_specs=out_specs or jax.tree.map(lambda _: VMEM, out_shape),
        scratch_shapes=list(scratch),
        input_output_aliases=aliases or {},
        compiler_params=pltpu.CompilerParams(vmem_limit_bytes=VMEM_LIMIT),
        cost_estimate=pl.CostEstimate(flops=cost * 10**9, bytes_accessed=0, transcendentals=0),
        name=name,
    )


PLANES = 4


def put_boundary(rows, base, a, out_ref, stage):
    wide = rows.astype(F32)

    def put(at, value, lanes=slice(None)):
        out_ref[pl.ds(pl.multiple_of(base + at, 16), value.shape[0]), lanes] = value

    if a in (0, 7):
        put(0 if a == 0 else 64, rows)
        return
    for half in range(2):
        lanes = slice(half * 128, half * 128 + 128)
        stage[half] = wide[:, lanes]
        first = stage[half, pl.ds(0, 8, stride=8), :]
        last = stage[half, pl.ds(7, 8, stride=8), :]
        put(C_LINES - 16 + 16 * a, jnp.concatenate([first, last], axis=0).astype(BF16), lanes)
    pair = jnp.concatenate([wide[:8], wide[56:]], axis=0).astype(BF16)
    put(B_LINES - 16 + 16 * a, pair)


def each_brick(rows_of, bricks, out_ref, stage):
    def step(brick, _):
        for first in range(0, 8, PLANES):
            at = pl.multiple_of(brick * 512 + first * 64, 64)
            rows = rows_of(pl.ds(at, PLANES * 64))
            for t in range(PLANES):
                plane = rows[t * 64 : t * 64 + 64]
                put_boundary(plane, brick * ROWS, first + t, out_ref, stage.at[first + t])
        return 0

    lax.fori_loop(0, bricks, step, 0)


def norm_body(recv, send, x_ref, gain_ref, hidden_ref, out_ref, stage):
    bricks, directions = recv.shape
    gain = gain_ref[...]
    lane = lax.broadcasted_iota(jnp.int32, (1, C), 1)
    codes = jnp.zeros((1, C), jnp.int32)
    for k in range(send.shape[1]):
        codes = jnp.where(lane == k, send[0, k], codes)
    served = jnp.zeros((1, C), jnp.int32)
    for brick in range(bricks):
        for number in range(directions):
            served = jnp.where(lane == recv[brick, number], brick * directions + number + 1, served)
    row = lax.broadcasted_iota(jnp.int32, (NOTES, C), 0)
    notes = jnp.where(row == 0, codes, jnp.where(row == 1, served, 0))
    out_ref[bricks * ROWS :, :] = notes.astype(F32).astype(BF16)

    def rows_of(at):
        x = x_ref[at, :].astype(F32)
        inverse = lax.rsqrt(jnp.mean(x * x, axis=-1, keepdims=True) + 1e-6)
        v = x * inverse * gain
        rows = (v / (1.0 + jnp.exp(-v))).astype(BF16)
        hidden_ref[at, :] = rows
        return rows

    each_brick(rows_of, bricks, out_ref, stage)


def extract_body(x_ref, out_ref, stage):
    each_brick(lambda at: x_ref[at, :], x_ref.shape[0] // 512, out_ref, stage)


def start_padded(own_ref, cells, halo, bricks):
    zero = jnp.zeros((8, C), F32)

    def clear(k, _):
        for b in range(10):
            cells[k * 10 + b] = zero
        for side in range(2):
            for part in range(HB // 8):
                halo[side, k, part * 8 : part * 8 + 8, :] = zero
        return 0

    lax.fori_loop(0, bricks * 10, clear, 0)

    def fill(k, _):
        plane = (k // 8) * 10 + k % 8 + 1
        rows = own_ref[pl.ds(pl.multiple_of(k * 64, 64), 64), :].astype(F32)
        for b in range(8):
            cells[plane * 10 + b + 1] = rows[b * 8 : b * 8 + 8]
        return 0

    lax.fori_loop(0, bricks * 8, fill, 0)


def add_line(ref, index, line):
    ref[index] = ref[index] + line


def pick(flag, yes, no):
    if isinstance(flag, bool):
        return yes if flag else no
    return jnp.where(flag, yes, no)


def place(kind, e, keep, place_at, source_brick, brick, share, cells, halo):
    flags = [t == -1 for t in e]
    pads = [pick(f, 0, 9) for f in flags]
    facing = pick(flags[0], 64, 0)
    start = source_brick * ROWS

    def rows(at, size):
        got = share[place_at, pl.ds(pl.multiple_of(start + at, 16), size), :].astype(F32)
        return got if keep is None else jnp.where(keep, got, 0.0)

    def half(pair, axis):
        return pick(flags[axis], pair[8:], pair[:8])

    def line_b(at):
        plane = rows(at, 64)
        return pick(flags[1], plane[56:], plane[:8])

    def line_c(at):
        plane = rows(at, 64)
        ends = [
            pick(flags[2], plane[8 * b + 7 : 8 * b + 8], plane[8 * b : 8 * b + 1]) for b in range(8)
        ]
        return jnp.concatenate(ends, axis=0)

    def cell(at):
        line = line_b(at)
        return pick(flags[2], line[7:8], line[0:1])

    side = pick(flags[2], 0, 1)
    base = brick * 10

    def add_halo(at, line):
        halo[side, base + at, 8:16, :] = halo[side, base + at, 8:16, :] + line

    def add_cell(at, value):
        spot = pl.ds(pick(flags[1], 7, 16), 1)
        halo[side, base + at, spot, :] = halo[side, base + at, spot, :] + value

    if kind == (1, 0, 0):
        got = rows(facing, 64)
        first = (base + pads[0]) * 10 + 1
        for b in range(8):
            add_line(cells, first + b, got[b * 8 : b * 8 + 8])
    elif kind == (0, 1, 0):
        for a in range(8):
            if a in (0, 7):
                line = line_b(0 if a == 0 else 64)
            else:
                line = half(rows(B_LINES - 16 + 16 * a, 16), 1)
            add_line(cells, (base + a + 1) * 10 + pads[1], line)
    elif kind == (0, 0, 1):
        for a in range(8):
            if a in (0, 7):
                line = line_c(0 if a == 0 else 64)
            else:
                line = half(rows(C_LINES - 16 + 16 * a, 16), 2)
            add_halo(a + 1, line)
    elif kind == (1, 1, 0):
        add_line(cells, (base + pads[0]) * 10 + pads[1], line_b(facing))
    elif kind == (1, 0, 1):
        add_halo(pads[0], line_c(facing))
    elif kind == (0, 1, 1):
        for a in range(8):
            if a in (0, 7):
                value = cell(0 if a == 0 else 64)
            else:
                line = half(rows(C_LINES - 16 + 16 * a, 16), 2)
                value = pick(flags[1], line[7:8], line[0:1])
            add_cell(a + 1, value)
    else:
        add_cell(pads[0], cell(facing))


def windows(cells, halo, cols, bricks, out=None, sems=None):
    row = lax.broadcasted_iota(jnp.int32, (8, C), 0)

    def step(k, _):
        shifted = [[], [], []]
        for b in range(10):
            x = cells[k * 10 + b]
            before = halo[0, k, pl.ds(b + 7, 1), :]
            after = halo[1, k, pl.ds(b + 7, 1), :]
            shifted[0].append(jnp.where(row == 0, before, pltpu.roll(x, 1, 0)))
            shifted[1].append(x)
            shifted[2].append(jnp.where(row == 7, after, pltpu.roll(x, 7, 0)))
        for j in range(3):
            for l in range(3):
                block = jnp.concatenate(shifted[l][j : j + 8], axis=0).astype(BF16)
                at = (3 * j + l) * C
                cols[k, :, at : at + C] = block
        if out is not None:
            pltpu.make_async_copy(cols.at[k], out.at[k], sems.at[k]).start()
        return 0

    lax.fori_loop(0, bricks * 10, step, 0)


def wait_windows(cols, out, sems, bricks):
    def step(k, _):
        pltpu.make_async_copy(cols.at[k], out.at[k], sems.at[k]).wait()
        return 0

    lax.fori_loop(0, bricks * 10, step, 0)


def fetch(parts, share, sems, first=0, rows=None):
    size = parts[0].shape[0]
    lines = pl.ds(first, rows or parts[0].shape[1])
    copies = [
        pltpu.make_async_copy(part.at[:, lines], share.at[pl.ds(k * size, size), lines], sems.at[k])
        for k, part in enumerate(parts)
    ]
    for copy in copies:
        copy.start()
    return copies


def weight_grad_body(slots, factor, peers, count, *refs):
    recv, table, own_ref, cot_ref = refs[:4]
    parts = refs[4 : 4 + count]
    keep_ref = refs[4 + count]
    give_refs = refs[5 + count : 5 + count + peers // 4]
    out_cols, codes_ref, served_ref = refs[-16:-13]
    cells, halo, share, cols, sums, narrow, turned, codes = refs[-13:-5]
    sems, cols_sems, codes_sem, out_sems, notes_sems = refs[-5:]
    bricks = own_ref.shape[0] // 512
    me = table[2 * peers]
    notes_copies = fetch(parts, share, notes_sems, bricks * ROWS, NOTES)
    copies = fetch(parts, share, sems, 0, bricks * ROWS)
    for part in range(bricks * 2):
        at = slice(part * 256, part * 256 + 256)
        turned[:, at] = cot_ref[at, :].astype(F32).T.astype(BF16)
    for copy in notes_copies:
        copy.wait()
    for k in range(peers):
        notes = share[k, bricks * ROWS :, :].astype(F32).astype(jnp.int32)
        codes_ref[k : k + 1, :] = notes[0:1]
        served_ref[k : k + 1, :] = notes[1:2]
    codes_copy = pltpu.make_async_copy(codes_ref, codes, codes_sem.at[0])
    codes_copy.start()
    start_padded(own_ref, cells, halo, bricks)
    codes_copy.wait()
    for copy in copies:
        copy.wait()
    for brick in range(bricks):
        for number, e in enumerate(DIRECTIONS):
            slot = recv[brick, number]
            safe = jnp.maximum(slot, 0)
            sender = safe // slots
            at = table[sender]
            code = codes[at, me * slots + safe - sender * slots]
            kind = tuple(abs(t) for t in e)
            place(kind, e, slot >= 0, at, code // 6, brick, share, cells, halo)
    windows(cells, halo, cols, bricks, out_cols, cols_sems)

    rows = 27 * C // peers
    for tap in range(27):
        i, jl = divmod(tap, 9)
        total = None
        for brick in range(bricks):
            right = cols[brick * 10 + i : brick * 10 + i + 8, :, jl * C : jl * C + C].reshape(512, C)
            left = turned[:, brick * 512 : brick * 512 + 512]
            term = jnp.dot(left, right, preferred_element_type=F32)
            total = term if total is None else total + term
        total = (total * factor).T
        start = tap * C
        while start < (tap + 1) * C:
            owner = start // rows
            stop = min((tap + 1) * C, (owner + 1) * rows)
            piece = total[start - tap * C : stop - tap * C]
            bucket = jnp.bitwise_xor(me % 2, owner % 2)
            behind = table[peers + owner // 2]
            where = slice(start - owner * rows, stop - owner * rows)
            sums[bucket, behind, where, :] = piece
            narrow[bucket, behind, where, :] = piece.astype(BF16)
            start = stop
            if stop == (owner + 1) * rows:

                @pl.when(bucket == 0)
                def _():
                    pltpu.make_async_copy(
                        sums.at[0, behind], keep_ref.at[behind], out_sems.at[0, behind]
                    ).start()

                turn = table[peers + peers // 2 + owner // 2]
                for hop, give_ref in enumerate(give_refs):

                    @pl.when((bucket == 1) & (turn // 2 == hop))
                    def _():
                        pltpu.make_async_copy(
                            narrow.at[1, behind], give_ref.at[turn % 2], out_sems.at[1, turn]
                        ).start()

    for k in range(peers // 2):
        pltpu.make_async_copy(sums.at[0, k], keep_ref.at[k], out_sems.at[0, k]).wait()
        pltpu.make_async_copy(narrow.at[1, k], give_refs[k // 2].at[k % 2], out_sems.at[1, k]).wait()
    wait_windows(cols, out_cols, cols_sems, bricks)


GROUP = 3 * C


def start_stream(cols_ref, first, cols, weight_ref, weight, sems):
    copies = []
    planes = cols.shape[0]
    for g in range(3):
        lanes = pl.ds(g * GROUP, GROUP)
        group = [
            pltpu.make_async_copy(
                cols_ref.at[pl.ds(first, planes), :, lanes], cols.at[:, :, lanes], sems.at[g, 3]
            )
        ]
        for i in range(3):
            at = pl.ds((i * 3 + g) * GROUP, GROUP)
            group.append(pltpu.make_async_copy(weight_ref.at[at], weight.at[at], sems.at[g, i]))
        copies.append(group)
    for group in copies:
        for copy in group:
            copy.start()
    return copies


def tap_sum(copies, cols, weight):
    bricks = cols.shape[0] // 10
    totals = [None] * bricks
    for g in range(3):
        for copy in copies[g]:
            copy.wait()
        for brick in range(bricks):
            for i in range(3):
                at = brick * 10 + i
                left = cols[at : at + 8, :, g * GROUP : g * GROUP + GROUP].reshape(512, GROUP)
                right = weight[(i * 3 + g) * GROUP : (i * 3 + g + 1) * GROUP, :]
                term = jnp.dot(left, right, preferred_element_type=F32)
                totals[brick] = term if totals[brick] is None else totals[brick] + term
    return totals


def mix_body(cols_ref, weight_ref, x_ref, out_ref, cols, weight, sems):
    copies = start_stream(cols_ref, 0, cols, weight_ref, weight, sems)
    for brick, total in enumerate(tap_sum(copies, cols, weight)):
        at = slice(brick * 512, brick * 512 + 512)
        out_ref[at, :] = (x_ref[at, :].astype(F32) + total).astype(BF16)


def input_grad_body(slots, peers, count, *refs):
    served, send, table, cot_ref, x_ref, gain_ref, weight_ref = refs[:7]
    parts = refs[7 : 7 + count]
    out_ref, cells, halo, cols, share, weight, heads, more, sems, weight_sem = refs[7 + count :]
    bricks = cot_ref.shape[0] // 512
    me = table[2 * peers]
    copies = fetch(parts, share, sems)
    weight_copy = pltpu.make_async_copy(weight_ref, weight, weight_sem.at[0])
    weight_copy.start()

    def no_head(k, _):
        heads[k] = -1
        return 0

    lax.fori_loop(0, bricks * 26, no_head, 0)

    def source_of(k):
        receiver = k // slots
        at = table[receiver]
        return at, served[at, me * slots + k - receiver * slots] - 1

    def sort(k, found):
        _, entry = source_of(k)
        asked = entry >= 0
        key = send[0, k] // 6 * 26 + 25 - jnp.maximum(entry, 0) % 26
        first = asked & (heads[key] < 0)
        extra = asked & jnp.logical_not(first)

        @pl.when(first)
        def _():
            heads[key] = k

        @pl.when(extra)
        def _():
            more[found] = k

        return found + jnp.where(extra, 1, 0)

    found = lax.fori_loop(0, send.shape[1], sort, 0)
    start_padded(cot_ref, cells, halo, bricks)
    for copy in copies:
        copy.wait()
    for brick in range(bricks):
        for number, e in enumerate(DIRECTIONS):
            head = heads[brick * 26 + number]
            at, entry = source_of(jnp.maximum(head, 0))
            kind = tuple(abs(t) for t in e)
            source = jnp.maximum(entry, 0) // 26
            place(kind, e, head >= 0, at, source, brick, share, cells, halo)

    def one(n, _):
        k = more[n]
        at, entry = source_of(k)
        number = 25 - entry % 26
        tap = jnp.where(number >= 13, number + 1, number)
        e = (tap // 9 - 1, (tap // 3) % 3 - 1, tap % 3 - 1)
        on = [t != 0 for t in e]
        for kind in ((1, 0, 0), (0, 1, 0), (0, 0, 1), (1, 1, 0), (1, 0, 1), (0, 1, 1), (1, 1, 1)):
            match = functools.reduce(
                jnp.logical_and, [f if w else jnp.logical_not(f) for f, w in zip(on, kind)]
            )

            @pl.when(match)
            def _():
                place(kind, e, None, at, entry // 26, send[0, k] // 6, share, cells, halo)

        return 0

    lax.fori_loop(0, found, one, 0)
    windows(cells, halo, cols, bricks)
    weight_copy.wait()
    gain = gain_ref[...]
    for brick in range(bricks):
        rows = slice(brick * 512, brick * 512 + 512)
        grad = None
        for tap in range(27):
            i, jl = divmod(tap, 9)
            first = brick * 10 + i
            left = cols[first : first + 8, :, jl * C : jl * C + C].reshape(512, C)
            right = weight[(26 - tap) * C : (27 - tap) * C, :]
            term = lax.dot_general(left, right, (((1,), (1,)), ((), ())), preferred_element_type=F32)
            grad = term if grad is None else grad + term
        x = x_ref[rows, :].astype(F32)
        inverse = lax.rsqrt(jnp.mean(x * x, axis=-1, keepdims=True) + 1e-6)
        unit = x * inverse
        v = unit * gain
        gate = 1.0 / (1.0 + jnp.exp(-v))
        grad = grad * (gate * (1.0 + v * (1.0 - gate))) * gain
        grad = inverse * (grad - unit * jnp.mean(grad * unit, axis=-1, keepdims=True))
        out_ref[rows, :] = (cot_ref[rows, :].astype(F32) + grad).astype(BF16)


def local(features, norm_gain, conv_weight, recv_slot, send_face, cotangent):
    channels = features.shape[1]
    per_device = features.shape[0]
    bricks = per_device // 512
    peers = lax.axis_size("morton")
    slots = send_face.shape[1] // peers
    factor = 1.0 / math.sqrt(peers * per_device)
    gain = norm_gain.reshape(1, channels)
    sds = jax.ShapeDtypeStruct
    stage = pltpu.VMEM((8, 2, 64, 128), F32)

    def padded(n):
        return [
            pltpu.VMEM((n * 100, 8, channels), F32),
            pltpu.VMEM((2, n * 10, HB, channels), F32),
        ]

    def cols_shape(n):
        return (n * 10, 64, 9 * channels)


    table = jnp.asarray(ring_tables(peers))[lax.axis_index("morton")]

    hidden, share = call(
        norm_body,
        (sds((per_device, channels), BF16), sds((bricks * ROWS + NOTES, channels), BF16)),
        [SMEM, SMEM, VMEM, VMEM],
        [stage],
        name="norm",
    )(recv_slot, send_face, features, gain)
    hidden_ring = RingGather(share, peers)
    cot_share = call(
        extract_body,
        sds((bricks * ROWS, channels), BF16),
        [VMEM],
        [stage],
        name="extract",
    )(cotangent)
    hidden_ring.go(0)
    hidden_ring.go(1)
    hidden_ring.go(0, cot_share)
    hidden_ring.go(1)
    hidden_ring.go(0, table)
    hidden_ring.go(1)
    hidden_ring.go(0)
    hidden_parts = hidden_ring.places()

    cot_ring = RingGather(cot_share, peers)
    cot_ring.go(0, hidden_ring.last(1))
    cot_ring.go(1, hidden_ring.last(0))

    count = len(hidden_parts)
    rows = 27 * channels // peers
    chips = peers // 2
    keep, *give, cols, _, served = call(
        functools.partial(weight_grad_body, slots, factor, peers, count),
        (
            sds((chips, rows, channels), F32),
            *[sds((2, rows, channels), BF16)] * (chips // 2),
            sds(cols_shape(bricks), BF16),
            sds((peers, channels), jnp.int32),
            sds((peers, channels), jnp.int32),
        ),
        [SMEM] * 2 + [VMEM] * 2 + [HBM] * count,
        padded(bricks)
        + [
            pltpu.VMEM((peers, bricks * ROWS + NOTES, channels), BF16),
            pltpu.VMEM(cols_shape(bricks), BF16),
            pltpu.VMEM((2, chips, rows, channels), F32),
            pltpu.VMEM((2, chips, rows, channels), BF16),
            pltpu.VMEM((channels, per_device), BF16),
            pltpu.SMEM((peers, channels), jnp.int32),
            pltpu.SemaphoreType.DMA((count,)),
            pltpu.SemaphoreType.DMA((bricks * 10,)),
            pltpu.SemaphoreType.DMA((1,)),
            pltpu.SemaphoreType.DMA((2, chips)),
            pltpu.SemaphoreType.DMA((count,)),
        ],
        cost=9,
        name="weight_grad",
        out_specs=(*[HBM] * (2 + chips // 2), VMEM, VMEM),
    )(recv_slot, table, hidden, cotangent, *hidden_parts)

    first = (cot_ring.last(0), cot_ring.last(1))
    give = [lax.optimization_barrier((t, first))[0] for t in give]
    sums_ring = RingScatter(keep, give, peers)
    sent = sums_ring.go()
    cot_ring.go(0, cols)
    cot_ring.go(1, cols)
    second = (cot_ring.last(0), cot_ring.last(1))
    mix_cols = lax.optimization_barrier((cols, sent))[0]
    weight_scratch = [
        pltpu.VMEM((27 * channels, channels), BF16),
        pltpu.SemaphoreType.DMA((3, 4)),
    ]
    mixed = call(
        mix_body,
        sds((per_device, channels), BF16),
        [HBM, HBM, VMEM],
        [pltpu.VMEM(cols_shape(bricks), BF16)] + weight_scratch,
        cost=6,
        name="mix",
    )(mix_cols, conv_weight, features)
    sent = sums_ring.go((second, mixed))
    cot_ring.go(0)
    cot_ring.go(1)
    third = (cot_ring.last(0), cot_ring.last(1))
    sums_ring.go(third)
    cot_ring.go(0)
    sent = sums_ring.go(cot_ring.last(0))
    cot_parts = cot_ring.places(cols)
    served = lax.optimization_barrier((served, sent))[0]

    grad_features = call(
        functools.partial(input_grad_body, slots, peers, count),
        sds((per_device, channels), BF16),
        [SMEM] * 3 + [VMEM] * 3 + [HBM] * (1 + count),
        padded(bricks)
        + [
            pltpu.VMEM(cols_shape(bricks), BF16),
            pltpu.VMEM((peers, bricks * ROWS, channels), BF16),
            weight_scratch[0],
            pltpu.SMEM((bricks * 26,), jnp.int32),
            pltpu.SMEM((peers * slots,), jnp.int32),
            pltpu.SemaphoreType.DMA((count,)),
            pltpu.SemaphoreType.DMA((1,)),
        ],
        cost=13,
        name="input_grad",
    )(served, send_face, table, cotangent, features, gain, conv_weight, *cot_parts)
    for _ in range(chips // 2 - 4):
        sums_ring.go()
    return (mixed, grad_features, sums_ring.total())


def solution(mesh):
    rows = P(("groups", "morton"), None)
    return jax.shard_map(
        local,
        mesh=mesh,
        in_specs=(rows, P(), P(), rows, rows, rows),
        out_specs=(rows, rows, rows),
        check_vma=False,
    )
```

```python
import functools
import math

import jax
import jax.numpy as jnp
import numpy as np
from jax import lax
from jax.experimental import pallas as pl
from jax.experimental.pallas import tpu as pltpu
from jax.sharding import PartitionSpec as P

F32 = jnp.float32
BF16 = jnp.bfloat16
C = 256
C_LINES = 128
B_LINES = 224
ROWS = 320
NOTES = 16
HB = 24
VMEM_LIMIT = 56 * 1024 * 1024
DIRECTIONS = [
    (i, j, l)
    for i in (-1, 0, 1)
    for j in (-1, 0, 1)
    for l in (-1, 0, 1)
    if (i, j, l) != (0, 0, 0)
]

VMEM = pl.BlockSpec(memory_space=pltpu.VMEM)
SMEM = pl.BlockSpec(memory_space=pltpu.SMEM)
ANY = pl.BlockSpec(memory_space=pl.ANY)
HBM = pl.BlockSpec(memory_space=pltpu.HBM)


def ring_order(chips):
    if chips == 8:
        return [0, 2, 4, 6, 7, 5, 3, 1]
    return list(range(chips))


def ring_tables(peers):
    chips = peers // 2
    spot = np.argsort(np.array(ring_order(chips)))
    device = np.arange(peers)
    behind = (spot[device // 2][:, None] - spot[None, :]) % chips
    half = chips // 2
    turn = np.where(behind >= half, 2 * (behind - half), 2 * (half - 1 - behind) + 1)
    place_of = np.broadcast_to(device, (peers, peers)).copy()
    if chips <= 8:
        for me in range(peers):
            for other in range(peers):
                away = behind[me, other // 2] if me % 2 == 0 else -behind[me, other // 2] % chips
                same = me % 2 == other % 2
                if away == 0:
                    place = 0 if same else 1
                elif away < half or (away == half and same):
                    place = 1 + away if same else 1 + half + away
                else:
                    away = chips - away
                    place = half + (away if not same else half + away) + half
                place_of[me, other] = place
    return np.concatenate([place_of, behind, turn, device[:, None]], axis=1).astype(np.int32)


def ring_step(x, peers, step, cross=0):
    order = ring_order(peers // 2)
    pairs = [
        (2 * order[i] + (core ^ cross), 2 * order[(i + (step or 1 - 2 * core)) % len(order)] + core)
        for i in range(len(order))
        for core in range(2)
    ]
    return lax.ppermute(x, "morton", pairs)


def swap_cores(x, peers):
    return lax.ppermute(x, "morton", [(m, m ^ 1) for m in range(peers)])


class RingGather:
    def __init__(self, x, peers):
        self.x, self.peers, self.chips = x, peers, peers // 2
        self.whole = None
        if self.chips > 8:
            self.whole = lax.all_gather(x[None], "morton", axis=0, tiled=True)
            return
        self.chains = ([x], [x])

    def go(self, chain, gate=None):
        if self.whole is not None or len(self.chains[chain]) > self.chips // 2 - chain:
            return
        held = self.chains[chain][-1]
        if gate is not None:
            held = lax.optimization_barrier((held, gate))[0]
        cross = int(chain == 1 and len(self.chains[chain]) == 1)
        self.chains[chain].append(ring_step(held, self.peers, 0, cross))

    def last(self, chain):
        return self.x if self.whole is not None else self.chains[chain][-1]

    def places(self, gate=None):
        if self.whole is not None:
            return [self.whole]
        mine = self.chains[0][1:] + self.chains[1][1:]
        held = mine
        if gate is not None:
            held = [lax.optimization_barrier((t, gate))[0] for t in mine]
        others = [swap_cores(t, self.peers) for t in [self.x] + held]
        return [t[None] for t in [self.x] + others[:1] + mine + others[1:]]


class RingScatter:
    def __init__(self, keep, give, peers):
        self.keep, self.peers, self.chips = keep, peers, peers // 2
        self.other = [swap_cores(t, peers) for t in give]
        self.held = [None, None]
        self.hop = 0

    def term(self, k):
        half = self.chips // 2
        pair = self.other[k - half][0] if k >= half else self.other[half - 1 - k][1]
        return self.keep[k] + pair.astype(F32)

    def go(self, gate=None):
        sent = []
        for way, step, count in ((0, 1, self.chips // 2), (1, -1, (self.chips - 1) // 2)):
            left = count - self.hop
            if left <= 0:
                continue
            part = self.term((-step * left) % self.chips)
            if self.held[way] is not None:
                part = part + self.held[way].astype(F32)
            part = part.astype(BF16)
            if gate is not None:
                part = lax.optimization_barrier((part, gate))[0]
            sent.append(part)
            self.held[way] = ring_step(part, self.peers, step)
        self.hop += 1
        return sent

    def total(self, gate):
        held = lax.optimization_barrier((*self.held, gate))[:2]
        return sum((t.astype(F32) for t in held), self.term(0))


def call(body, out_shape, in_specs, scratch=(), cost=2, name=None, out_specs=None, aliases=None):
    return pl.pallas_call(
        body,
        out_shape=out_shape,
        in_specs=in_specs,
        out_specs=out_specs or jax.tree.map(lambda _: VMEM, out_shape),
        scratch_shapes=list(scratch),
        input_output_aliases=aliases or {},
        compiler_params=pltpu.CompilerParams(vmem_limit_bytes=VMEM_LIMIT),
        cost_estimate=pl.CostEstimate(flops=cost * 10**9, bytes_accessed=0, transcendentals=0),
        name=name,
    )


PLANES = 4


def put_boundary(rows, base, a, out_ref, stage):
    wide = rows.astype(F32)

    def put(at, value, lanes=slice(None)):
        out_ref[pl.ds(pl.multiple_of(base + at, 16), value.shape[0]), lanes] = value

    if a in (0, 7):
        put(0 if a == 0 else 64, rows)
        return
    for half in range(2):
        lanes = slice(half * 128, half * 128 + 128)
        stage[half] = wide[:, lanes]
        first = stage[half, pl.ds(0, 8, stride=8), :]
        last = stage[half, pl.ds(7, 8, stride=8), :]
        put(C_LINES - 16 + 16 * a, jnp.concatenate([first, last], axis=0).astype(BF16), lanes)
    pair = jnp.concatenate([wide[:8], wide[56:]], axis=0).astype(BF16)
    put(B_LINES - 16 + 16 * a, pair)


def each_brick(rows_of, bricks, out_ref, stage):
    def step(brick, _):
        for first in range(0, 8, PLANES):
            at = pl.multiple_of(brick * 512 + first * 64, 64)
            rows = rows_of(pl.ds(at, PLANES * 64))
            for t in range(PLANES):
                plane = rows[t * 64 : t * 64 + 64]
                put_boundary(plane, brick * ROWS, first + t, out_ref, stage.at[first + t])
        return 0

    lax.fori_loop(0, bricks, step, 0)


def norm_body(recv, send, x_ref, gain_ref, hidden_ref, out_ref, stage):
    bricks, directions = recv.shape
    gain = gain_ref[...]
    lane = lax.broadcasted_iota(jnp.int32, (1, C), 1)
    codes = jnp.zeros((1, C), jnp.int32)
    for k in range(send.shape[1]):
        codes = jnp.where(lane == k, send[0, k], codes)
    served = jnp.zeros((1, C), jnp.int32)
    for brick in range(bricks):
        for number in range(directions):
            served = jnp.where(lane == recv[brick, number], brick * directions + number + 1, served)
    row = lax.broadcasted_iota(jnp.int32, (NOTES, C), 0)
    notes = jnp.where(row == 0, codes, jnp.where(row == 1, served, 0))
    out_ref[bricks * ROWS :, :] = notes.astype(F32).astype(BF16)

    def rows_of(at):
        x = x_ref[at, :].astype(F32)
        inverse = lax.rsqrt(jnp.mean(x * x, axis=-1, keepdims=True) + 1e-6)
        v = x * inverse * gain
        rows = (v / (1.0 + jnp.exp(-v))).astype(BF16)
        hidden_ref[at, :] = rows
        return rows

    each_brick(rows_of, bricks, out_ref, stage)


def extract_body(x_ref, out_ref, stage):
    each_brick(lambda at: x_ref[at, :], x_ref.shape[0] // 512, out_ref, stage)


def start_padded(own_ref, cells, halo, bricks):
    zero = jnp.zeros((8, C), F32)

    def clear(k, _):
        for b in range(10):
            cells[k * 10 + b] = zero
        for side in range(2):
            for part in range(HB // 8):
                halo[side, k, part * 8 : part * 8 + 8, :] = zero
        return 0

    lax.fori_loop(0, bricks * 10, clear, 0)

    def fill(k, _):
        plane = (k // 8) * 10 + k % 8 + 1
        rows = own_ref[pl.ds(pl.multiple_of(k * 64, 64), 64), :].astype(F32)
        for b in range(8):
            cells[plane * 10 + b + 1] = rows[b * 8 : b * 8 + 8]
        return 0

    lax.fori_loop(0, bricks * 8, fill, 0)


def add_line(ref, index, line):
    ref[index] = ref[index] + line


def pick(flag, yes, no):
    if isinstance(flag, bool):
        return yes if flag else no
    return jnp.where(flag, yes, no)


def place(kind, e, keep, place_at, source_brick, brick, share, cells, halo):
    flags = [t == -1 for t in e]
    pads = [pick(f, 0, 9) for f in flags]
    facing = pick(flags[0], 64, 0)
    start = source_brick * ROWS

    def rows(at, size):
        got = share[place_at, pl.ds(pl.multiple_of(start + at, 16), size), :].astype(F32)
        return got if keep is None else jnp.where(keep, got, 0.0)

    def half(pair, axis):
        return pick(flags[axis], pair[8:], pair[:8])

    def line_b(at):
        plane = rows(at, 64)
        return pick(flags[1], plane[56:], plane[:8])

    def line_c(at):
        plane = rows(at, 64)
        ends = [
            pick(flags[2], plane[8 * b + 7 : 8 * b + 8], plane[8 * b : 8 * b + 1]) for b in range(8)
        ]
        return jnp.concatenate(ends, axis=0)

    def cell(at):
        line = line_b(at)
        return pick(flags[2], line[7:8], line[0:1])

    side = pick(flags[2], 0, 1)
    base = brick * 10

    def add_halo(at, line):
        halo[side, base + at, 8:16, :] = halo[side, base + at, 8:16, :] + line

    def add_cell(at, value):
        spot = pl.ds(pick(flags[1], 7, 16), 1)
        halo[side, base + at, spot, :] = halo[side, base + at, spot, :] + value

    if kind == (1, 0, 0):
        got = rows(facing, 64)
        first = (base + pads[0]) * 10 + 1
        for b in range(8):
            add_line(cells, first + b, got[b * 8 : b * 8 + 8])
    elif kind == (0, 1, 0):
        for a in range(8):
            if a in (0, 7):
                line = line_b(0 if a == 0 else 64)
            else:
                line = half(rows(B_LINES - 16 + 16 * a, 16), 1)
            add_line(cells, (base + a + 1) * 10 + pads[1], line)
    elif kind == (0, 0, 1):
        for a in range(8):
            if a in (0, 7):
                line = line_c(0 if a == 0 else 64)
            else:
                line = half(rows(C_LINES - 16 + 16 * a, 16), 2)
            add_halo(a + 1, line)
    elif kind == (1, 1, 0):
        add_line(cells, (base + pads[0]) * 10 + pads[1], line_b(facing))
    elif kind == (1, 0, 1):
        add_halo(pads[0], line_c(facing))
    elif kind == (0, 1, 1):
        for a in range(8):
            if a in (0, 7):
                value = cell(0 if a == 0 else 64)
            else:
                line = half(rows(C_LINES - 16 + 16 * a, 16), 2)
                value = pick(flags[1], line[7:8], line[0:1])
            add_cell(a + 1, value)
    else:
        add_cell(pads[0], cell(facing))


def windows(cells, halo, cols, bricks, out=None, sems=None):
    row = lax.broadcasted_iota(jnp.int32, (8, C), 0)

    def step(k, _):
        shifted = [[], [], []]
        for b in range(10):
            x = cells[k * 10 + b]
            before = halo[0, k, pl.ds(b + 7, 1), :]
            after = halo[1, k, pl.ds(b + 7, 1), :]
            shifted[0].append(jnp.where(row == 0, before, pltpu.roll(x, 1, 0)))
            shifted[1].append(x)
            shifted[2].append(jnp.where(row == 7, after, pltpu.roll(x, 7, 0)))
        for j in range(3):
            for l in range(3):
                block = jnp.concatenate(shifted[l][j : j + 8], axis=0).astype(BF16)
                at = (3 * j + l) * C
                cols[k, :, at : at + C] = block
        if out is not None:
            pltpu.make_async_copy(cols.at[k], out.at[k], sems.at[k]).start()
        return 0

    lax.fori_loop(0, bricks * 10, step, 0)


def wait_windows(cols, out, sems, bricks):
    def step(k, _):
        pltpu.make_async_copy(cols.at[k], out.at[k], sems.at[k]).wait()
        return 0

    lax.fori_loop(0, bricks * 10, step, 0)


def fetch(parts, share, sems, first=0, rows=None):
    size = parts[0].shape[0]
    lines = pl.ds(first, rows or parts[0].shape[1])
    copies = [
        pltpu.make_async_copy(part.at[:, lines], share.at[pl.ds(k * size, size), lines], sems.at[k])
        for k, part in enumerate(parts)
    ]
    for copy in copies:
        copy.start()
    return copies


def weight_grad_body(slots, factor, peers, count, *refs):
    recv, table, own_ref, cot_ref = refs[:4]
    parts = refs[4 : 4 + count]
    keep_ref = refs[4 + count]
    give_refs = refs[5 + count : 5 + count + peers // 4]
    out_cols, codes_ref, served_ref = refs[-16:-13]
    cells, halo, share, cols, sums, narrow, turned, codes = refs[-13:-5]
    sems, cols_sems, codes_sem, out_sems, notes_sems = refs[-5:]
    bricks = own_ref.shape[0] // 512
    me = table[2 * peers]
    notes_copies = fetch(parts, share, notes_sems, bricks * ROWS, NOTES)
    copies = fetch(parts, share, sems, 0, bricks * ROWS)
    for part in range(bricks * 2):
        at = slice(part * 256, part * 256 + 256)
        turned[:, at] = cot_ref[at, :].astype(F32).T.astype(BF16)
    for copy in notes_copies:
        copy.wait()
    for k in range(peers):
        notes = share[k, bricks * ROWS :, :].astype(F32).astype(jnp.int32)
        codes_ref[k : k + 1, :] = notes[0:1]
        served_ref[k : k + 1, :] = notes[1:2]
    codes_copy = pltpu.make_async_copy(codes_ref, codes, codes_sem.at[0])
    codes_copy.start()
    start_padded(own_ref, cells, halo, bricks)
    codes_copy.wait()
    for copy in copies:
        copy.wait()
    for brick in range(bricks):
        for number, e in enumerate(DIRECTIONS):
            slot = recv[brick, number]
            safe = jnp.maximum(slot, 0)
            sender = safe // slots
            at = table[sender]
            code = codes[at, me * slots + safe - sender * slots]
            kind = tuple(abs(t) for t in e)
            place(kind, e, slot >= 0, at, code // 6, brick, share, cells, halo)
    windows(cells, halo, cols, bricks, out_cols, cols_sems)

    rows = 27 * C // peers
    for tap in range(27):
        i, jl = divmod(tap, 9)
        total = None
        for brick in range(bricks):
            right = cols[brick * 10 + i : brick * 10 + i + 8, :, jl * C : jl * C + C].reshape(512, C)
            left = turned[:, brick * 512 : brick * 512 + 512]
            term = jnp.dot(left, right, preferred_element_type=F32)
            total = term if total is None else total + term
        total = (total * factor).T
        start = tap * C
        while start < (tap + 1) * C:
            owner = start // rows
            stop = min((tap + 1) * C, (owner + 1) * rows)
            piece = total[start - tap * C : stop - tap * C]
            bucket = jnp.bitwise_xor(me % 2, owner % 2)
            behind = table[peers + owner // 2]
            where = slice(start - owner * rows, stop - owner * rows)
            sums[bucket, behind, where, :] = piece
            narrow[bucket, behind, where, :] = piece.astype(BF16)
            start = stop
            if stop == (owner + 1) * rows:

                @pl.when(bucket == 0)
                def _():
                    pltpu.make_async_copy(
                        sums.at[0, behind], keep_ref.at[behind], out_sems.at[0, behind]
                    ).start()

                turn = table[peers + peers // 2 + owner // 2]
                for hop, give_ref in enumerate(give_refs):

                    @pl.when((bucket == 1) & (turn // 2 == hop))
                    def _():
                        pltpu.make_async_copy(
                            narrow.at[1, behind], give_ref.at[turn % 2], out_sems.at[1, turn]
                        ).start()

    for k in range(peers // 2):
        pltpu.make_async_copy(sums.at[0, k], keep_ref.at[k], out_sems.at[0, k]).wait()
        pltpu.make_async_copy(narrow.at[1, k], give_refs[k // 2].at[k % 2], out_sems.at[1, k]).wait()
    wait_windows(cols, out_cols, cols_sems, bricks)


GROUP = 3 * C


def start_stream(cols_ref, first, cols, weight_ref, weight, sems):
    copies = []
    planes = cols.shape[0]
    for g in range(3):
        lanes = pl.ds(g * GROUP, GROUP)
        group = [
            pltpu.make_async_copy(
                cols_ref.at[pl.ds(first, planes), :, lanes], cols.at[:, :, lanes], sems.at[g, 3]
            )
        ]
        for i in range(3):
            at = pl.ds((i * 3 + g) * GROUP, GROUP)
            group.append(pltpu.make_async_copy(weight_ref.at[at], weight.at[at], sems.at[g, i]))
        copies.append(group)
    for group in copies:
        for copy in group:
            copy.start()
    return copies


def tap_sum(copies, cols, weight):
    bricks = cols.shape[0] // 10
    totals = [None] * bricks
    for g in range(3):
        for copy in copies[g]:
            copy.wait()
        for brick in range(bricks):
            for i in range(3):
                at = brick * 10 + i
                left = cols[at : at + 8, :, g * GROUP : g * GROUP + GROUP].reshape(512, GROUP)
                right = weight[(i * 3 + g) * GROUP : (i * 3 + g + 1) * GROUP, :]
                term = jnp.dot(left, right, preferred_element_type=F32)
                totals[brick] = term if totals[brick] is None else totals[brick] + term
    return totals


def mix_body(cols_ref, weight_ref, x_ref, out_ref, cols, weight, sems):
    copies = start_stream(cols_ref, 0, cols, weight_ref, weight, sems)
    for brick, total in enumerate(tap_sum(copies, cols, weight)):
        at = slice(brick * 512, brick * 512 + 512)
        out_ref[at, :] = (x_ref[at, :].astype(F32) + total).astype(BF16)


def input_grad_body(slots, peers, count, *refs):
    served, send, table, cot_ref, x_ref, gain_ref, weight_ref = refs[:7]
    parts = refs[7 : 7 + count]
    out_ref, cells, halo, cols, share, weight, heads, more, sems, weight_sem = refs[7 + count :]
    bricks = cot_ref.shape[0] // 512
    me = table[2 * peers]
    copies = fetch(parts, share, sems)
    weight_copy = pltpu.make_async_copy(weight_ref, weight, weight_sem.at[0])
    weight_copy.start()

    def no_head(k, _):
        heads[k] = -1
        return 0

    lax.fori_loop(0, bricks * 26, no_head, 0)

    def source_of(k):
        receiver = k // slots
        at = table[receiver]
        return at, served[at, me * slots + k - receiver * slots] - 1

    def sort(k, found):
        _, entry = source_of(k)
        asked = entry >= 0
        key = send[0, k] // 6 * 26 + 25 - jnp.maximum(entry, 0) % 26
        first = asked & (heads[key] < 0)
        extra = asked & jnp.logical_not(first)

        @pl.when(first)
        def _():
            heads[key] = k

        @pl.when(extra)
        def _():
            more[found] = k

        return found + jnp.where(extra, 1, 0)

    found = lax.fori_loop(0, send.shape[1], sort, 0)
    start_padded(cot_ref, cells, halo, bricks)
    for copy in copies:
        copy.wait()
    for brick in range(bricks):
        for number, e in enumerate(DIRECTIONS):
            head = heads[brick * 26 + number]
            at, entry = source_of(jnp.maximum(head, 0))
            kind = tuple(abs(t) for t in e)
            source = jnp.maximum(entry, 0) // 26
            place(kind, e, head >= 0, at, source, brick, share, cells, halo)

    def one(n, _):
        k = more[n]
        at, entry = source_of(k)
        number = 25 - entry % 26
        tap = jnp.where(number >= 13, number + 1, number)
        e = (tap // 9 - 1, (tap // 3) % 3 - 1, tap % 3 - 1)
        on = [t != 0 for t in e]
        for kind in ((1, 0, 0), (0, 1, 0), (0, 0, 1), (1, 1, 0), (1, 0, 1), (0, 1, 1), (1, 1, 1)):
            match = functools.reduce(
                jnp.logical_and, [f if w else jnp.logical_not(f) for f, w in zip(on, kind)]
            )

            @pl.when(match)
            def _():
                place(kind, e, None, at, entry // 26, send[0, k] // 6, share, cells, halo)

        return 0

    lax.fori_loop(0, found, one, 0)
    windows(cells, halo, cols, bricks)
    weight_copy.wait()
    gain = gain_ref[...]
    for brick in range(bricks):
        rows = slice(brick * 512, brick * 512 + 512)
        grad = None
        for tap in range(27):
            i, jl = divmod(tap, 9)
            first = brick * 10 + i
            left = cols[first : first + 8, :, jl * C : jl * C + C].reshape(512, C)
            right = weight[(26 - tap) * C : (27 - tap) * C, :]
            term = lax.dot_general(left, right, (((1,), (1,)), ((), ())), preferred_element_type=F32)
            grad = term if grad is None else grad + term
        x = x_ref[rows, :].astype(F32)
        inverse = lax.rsqrt(jnp.mean(x * x, axis=-1, keepdims=True) + 1e-6)
        unit = x * inverse
        v = unit * gain
        gate = 1.0 / (1.0 + jnp.exp(-v))
        grad = grad * (gate * (1.0 + v * (1.0 - gate))) * gain
        grad = inverse * (grad - unit * jnp.mean(grad * unit, axis=-1, keepdims=True))
        out_ref[rows, :] = (cot_ref[rows, :].astype(F32) + grad).astype(BF16)


def local(features, norm_gain, conv_weight, recv_slot, send_face, cotangent):
    channels = features.shape[1]
    per_device = features.shape[0]
    bricks = per_device // 512
    peers = lax.axis_size("morton")
    slots = send_face.shape[1] // peers
    factor = 1.0 / math.sqrt(peers * per_device)
    gain = norm_gain.reshape(1, channels)
    sds = jax.ShapeDtypeStruct
    stage = pltpu.VMEM((8, 2, 64, 128), F32)

    def padded(n):
        return [
            pltpu.VMEM((n * 100, 8, channels), F32),
            pltpu.VMEM((2, n * 10, HB, channels), F32),
        ]

    def cols_shape(n):
        return (n * 10, 64, 9 * channels)


    table = jnp.asarray(ring_tables(peers))[lax.axis_index("morton")]

    hidden, share = call(
        norm_body,
        (sds((per_device, channels), BF16), sds((bricks * ROWS + NOTES, channels), BF16)),
        [SMEM, SMEM, VMEM, VMEM],
        [stage],
        name="norm",
    )(recv_slot, send_face, features, gain)
    hidden_ring = RingGather(share, peers)
    cot_share = call(
        extract_body,
        sds((bricks * ROWS, channels), BF16),
        [VMEM],
        [stage],
        name="extract",
    )(cotangent)
    hidden_ring.go(0)
    hidden_ring.go(1)
    hidden_ring.go(0, cot_share)
    hidden_ring.go(1)
    hidden_ring.go(0, table)
    hidden_ring.go(1)
    hidden_ring.go(0)
    hidden_parts = hidden_ring.places()

    cot_ring = RingGather(cot_share, peers)
    cot_ring.go(0, hidden_ring.last(1))
    cot_ring.go(1, hidden_ring.last(0))

    count = len(hidden_parts)
    rows = 27 * channels // peers
    chips = peers // 2
    keep, *give, cols, _, served = call(
        functools.partial(weight_grad_body, slots, factor, peers, count),
        (
            sds((chips, rows, channels), F32),
            *[sds((2, rows, channels), BF16)] * (chips // 2),
            sds(cols_shape(bricks), BF16),
            sds((peers, channels), jnp.int32),
            sds((peers, channels), jnp.int32),
        ),
        [SMEM] * 2 + [VMEM] * 2 + [HBM] * count,
        padded(bricks)
        + [
            pltpu.VMEM((peers, bricks * ROWS + NOTES, channels), BF16),
            pltpu.VMEM(cols_shape(bricks), BF16),
            pltpu.VMEM((2, chips, rows, channels), F32),
            pltpu.VMEM((2, chips, rows, channels), BF16),
            pltpu.VMEM((channels, per_device), BF16),
            pltpu.SMEM((peers, channels), jnp.int32),
            pltpu.SemaphoreType.DMA((count,)),
            pltpu.SemaphoreType.DMA((bricks * 10,)),
            pltpu.SemaphoreType.DMA((1,)),
            pltpu.SemaphoreType.DMA((2, chips)),
            pltpu.SemaphoreType.DMA((count,)),
        ],
        cost=9,
        name="weight_grad",
        out_specs=(*[HBM] * (2 + chips // 2), VMEM, VMEM),
    )(recv_slot, table, hidden, cotangent, *hidden_parts)

    first = (cot_ring.last(0), cot_ring.last(1))
    give = [lax.optimization_barrier((t, first))[0] for t in give]
    sums_ring = RingScatter(keep, give, peers)
    sums_ring.go()
    cot_ring.go(0, cols)
    cot_ring.go(1, cols)
    second = (cot_ring.last(0), cot_ring.last(1))
    sent = sums_ring.go(second)
    mix_cols = lax.optimization_barrier((cols, sent))[0]
    weight_scratch = pltpu.VMEM((27 * channels, channels), BF16)
    mixed = call(
        mix_body,
        sds((per_device, channels), BF16),
        [HBM, HBM, VMEM],
        [pltpu.VMEM(cols_shape(bricks), BF16), weight_scratch, pltpu.SemaphoreType.DMA((3, 4))],
        cost=6,
        name="mix",
    )(mix_cols, conv_weight, features)
    cot_ring.go(0)
    cot_ring.go(1)
    third = (cot_ring.last(0), cot_ring.last(1))
    sent = sums_ring.go((third, mixed))
    cot_ring.go(0, sent)
    cot_parts = cot_ring.places(cols)
    sent = sums_ring.go(tuple(t for k, t in enumerate(cot_parts) if k != peers // 2 + peers // 4))
    served = lax.optimization_barrier((served, sent))[0]

    grad_features = call(
        functools.partial(input_grad_body, slots, peers, count),
        sds((per_device, channels), BF16),
        [SMEM] * 3 + [VMEM] * 3 + [HBM] * (1 + count),
        padded(bricks)
        + [
            pltpu.VMEM(cols_shape(bricks), BF16),
            pltpu.VMEM((peers, bricks * ROWS, channels), BF16),
            weight_scratch,
            pltpu.SMEM((bricks * 26,), jnp.int32),
            pltpu.SMEM((peers * slots,), jnp.int32),
            pltpu.SemaphoreType.DMA((count,)),
            pltpu.SemaphoreType.DMA((1,)),
        ],
        cost=13,
        name="input_grad",
    )(served, send_face, table, cotangent, features, gain, conv_weight, *cot_parts)
    for _ in range(chips // 2 - 4):
        sums_ring.go()
    return (mixed, grad_features, sums_ring.total(grad_features))


def solution(mesh):
    rows = P(("groups", "morton"), None)
    return jax.shard_map(
        local,
        mesh=mesh,
        in_specs=(rows, P(), P(), rows, rows, rows),
        out_specs=(rows, rows, rows),
        check_vma=False,
    )
```

```python
import functools
import math

import jax
import jax.numpy as jnp
import numpy as np
from jax import lax
from jax.experimental import pallas as pl
from jax.experimental.pallas import tpu as pltpu
from jax.sharding import PartitionSpec as P

F32 = jnp.float32
BF16 = jnp.bfloat16
C = 256
C_LINES = 128
B_LINES = 224
ROWS = 320
NOTES = 16
HB = 24
VMEM_LIMIT = 56 * 1024 * 1024
DIRECTIONS = [
    (i, j, l)
    for i in (-1, 0, 1)
    for j in (-1, 0, 1)
    for l in (-1, 0, 1)
    if (i, j, l) != (0, 0, 0)
]

VMEM = pl.BlockSpec(memory_space=pltpu.VMEM)
SMEM = pl.BlockSpec(memory_space=pltpu.SMEM)
ANY = pl.BlockSpec(memory_space=pl.ANY)
HBM = pl.BlockSpec(memory_space=pltpu.HBM)


def ring_order(chips):
    if chips == 8:
        return [0, 2, 4, 6, 7, 5, 3, 1]
    return list(range(chips))


def ring_tables(peers):
    chips = peers // 2
    spot = np.argsort(np.array(ring_order(chips)))
    device = np.arange(peers)
    behind = (spot[device // 2][:, None] - spot[None, :]) % chips
    half = chips // 2
    turn = np.where(behind >= half, 2 * (behind - half), 2 * (half - 1 - behind) + 1)
    place_of = np.broadcast_to(device, (peers, peers)).copy()
    if chips <= 8:
        for me in range(peers):
            for other in range(peers):
                away = behind[me, other // 2] if me % 2 == 0 else -behind[me, other // 2] % chips
                same = me % 2 == other % 2
                if away == 0:
                    place = 0 if same else 1
                elif away < half or (away == half and same):
                    place = 1 + away if same else 1 + half + away
                else:
                    away = chips - away
                    place = half + (away if not same else half + away) + half
                place_of[me, other] = place
    return np.concatenate([place_of, behind, turn, device[:, None]], axis=1).astype(np.int32)


def ring_step(x, peers, step, cross=0):
    order = ring_order(peers // 2)
    pairs = [
        (2 * order[i] + (core ^ cross), 2 * order[(i + (step or 1 - 2 * core)) % len(order)] + core)
        for i in range(len(order))
        for core in range(2)
    ]
    return lax.ppermute(x, "morton", pairs)


def swap_cores(x, peers):
    return lax.ppermute(x, "morton", [(m, m ^ 1) for m in range(peers)])


class RingGather:
    def __init__(self, x, peers):
        self.x, self.peers, self.chips = x, peers, peers // 2
        self.whole = None
        if self.chips > 8:
            self.whole = lax.all_gather(x[None], "morton", axis=0, tiled=True)
            return
        self.chains = ([x], [x])

    def go(self, chain, gate=None):
        if self.whole is not None or len(self.chains[chain]) > self.chips // 2 - chain:
            return
        held = self.chains[chain][-1]
        if gate is not None:
            held = lax.optimization_barrier((held, gate))[0]
        cross = int(chain == 1 and len(self.chains[chain]) == 1)
        self.chains[chain].append(ring_step(held, self.peers, 0, cross))

    def last(self, chain):
        return self.x if self.whole is not None else self.chains[chain][-1]

    def places(self, gate=None):
        if self.whole is not None:
            return [self.whole]
        mine = self.chains[0][1:] + self.chains[1][1:]
        held = mine
        if gate is not None:
            held = [lax.optimization_barrier((t, gate))[0] for t in mine]
        others = [swap_cores(t, self.peers) for t in [self.x] + held]
        return [t[None] for t in [self.x] + others[:1] + mine + others[1:]]


class RingScatter:
    def __init__(self, keep, give, peers):
        self.keep, self.peers, self.chips = keep, peers, peers // 2
        self.other = [swap_cores(t, peers) for t in give]
        self.held = [None, None]
        self.hop = 0

    def term(self, k):
        half = self.chips // 2
        pair = self.other[k - half][0] if k >= half else self.other[half - 1 - k][1]
        return self.keep[k] + pair.astype(F32)

    def go(self, gate=None):
        sent = []
        for way, step, count in ((0, 1, self.chips // 2), (1, -1, (self.chips - 1) // 2)):
            left = count - self.hop
            if left <= 0:
                continue
            part = self.term((-step * left) % self.chips)
            if self.held[way] is not None:
                part = part + self.held[way].astype(F32)
            part = part.astype(BF16)
            if gate is not None:
                part = lax.optimization_barrier((part, gate))[0]
            sent.append(part)
            self.held[way] = ring_step(part, self.peers, step)
        self.hop += 1
        return sent

    def total(self, gate):
        held = lax.optimization_barrier((*self.held, gate))[:2]
        return sum((t.astype(F32) for t in held), self.term(0))


def call(body, out_shape, in_specs, scratch=(), cost=2, name=None, out_specs=None, aliases=None):
    return pl.pallas_call(
        body,
        out_shape=out_shape,
        in_specs=in_specs,
        out_specs=out_specs or jax.tree.map(lambda _: VMEM, out_shape),
        scratch_shapes=list(scratch),
        input_output_aliases=aliases or {},
        compiler_params=pltpu.CompilerParams(vmem_limit_bytes=VMEM_LIMIT),
        cost_estimate=pl.CostEstimate(flops=cost * 10**9, bytes_accessed=0, transcendentals=0),
        name=name,
    )


PLANES = 4


def put_boundary(rows, base, a, out_ref, stage):
    wide = rows.astype(F32)

    def put(at, value, lanes=slice(None)):
        out_ref[pl.ds(pl.multiple_of(base + at, 16), value.shape[0]), lanes] = value

    if a in (0, 7):
        put(0 if a == 0 else 64, rows)
        return
    for half in range(2):
        lanes = slice(half * 128, half * 128 + 128)
        stage[half] = wide[:, lanes]
        first = stage[half, pl.ds(0, 8, stride=8), :]
        last = stage[half, pl.ds(7, 8, stride=8), :]
        put(C_LINES - 16 + 16 * a, jnp.concatenate([first, last], axis=0).astype(BF16), lanes)
    pair = jnp.concatenate([wide[:8], wide[56:]], axis=0).astype(BF16)
    put(B_LINES - 16 + 16 * a, pair)


def each_brick(rows_of, bricks, out_ref, stage):
    def step(brick, _):
        for first in range(0, 8, PLANES):
            at = pl.multiple_of(brick * 512 + first * 64, 64)
            rows = rows_of(pl.ds(at, PLANES * 64))
            for t in range(PLANES):
                plane = rows[t * 64 : t * 64 + 64]
                put_boundary(plane, brick * ROWS, first + t, out_ref, stage.at[first + t])
        return 0

    lax.fori_loop(0, bricks, step, 0)


def norm_body(recv, send, x_ref, gain_ref, hidden_ref, out_ref, stage):
    bricks, directions = recv.shape
    gain = gain_ref[...]
    lane = lax.broadcasted_iota(jnp.int32, (1, C), 1)
    codes = jnp.zeros((1, C), jnp.int32)
    for k in range(send.shape[1]):
        codes = jnp.where(lane == k, send[0, k], codes)
    served = jnp.zeros((1, C), jnp.int32)
    for brick in range(bricks):
        for number in range(directions):
            served = jnp.where(lane == recv[brick, number], brick * directions + number + 1, served)
    row = lax.broadcasted_iota(jnp.int32, (NOTES, C), 0)
    notes = jnp.where(row == 0, codes, jnp.where(row == 1, served, 0))
    out_ref[bricks * ROWS :, :] = notes.astype(F32).astype(BF16)

    def rows_of(at):
        x = x_ref[at, :].astype(F32)
        inverse = lax.rsqrt(jnp.mean(x * x, axis=-1, keepdims=True) + 1e-6)
        v = x * inverse * gain
        rows = (v / (1.0 + jnp.exp(-v))).astype(BF16)
        hidden_ref[at, :] = rows
        return rows

    each_brick(rows_of, bricks, out_ref, stage)


def extract_body(x_ref, out_ref, stage):
    each_brick(lambda at: x_ref[at, :], x_ref.shape[0] // 512, out_ref, stage)


def start_padded(own_ref, cells, halo, bricks):
    zero = jnp.zeros((8, C), F32)

    def clear(k, _):
        for b in range(10):
            cells[k * 10 + b] = zero
        for side in range(2):
            for part in range(HB // 8):
                halo[side, k, part * 8 : part * 8 + 8, :] = zero
        return 0

    lax.fori_loop(0, bricks * 10, clear, 0)

    def fill(k, _):
        plane = (k // 8) * 10 + k % 8 + 1
        rows = own_ref[pl.ds(pl.multiple_of(k * 64, 64), 64), :].astype(F32)
        for b in range(8):
            cells[plane * 10 + b + 1] = rows[b * 8 : b * 8 + 8]
        return 0

    lax.fori_loop(0, bricks * 8, fill, 0)


def add_line(ref, index, line):
    ref[index] = ref[index] + line


def pick(flag, yes, no):
    if isinstance(flag, bool):
        return yes if flag else no
    return jnp.where(flag, yes, no)


def place(kind, e, keep, place_at, source_brick, brick, share, cells, halo):
    flags = [t == -1 for t in e]
    pads = [pick(f, 0, 9) for f in flags]
    facing = pick(flags[0], 64, 0)
    start = source_brick * ROWS

    def rows(at, size):
        got = share[place_at, pl.ds(pl.multiple_of(start + at, 16), size), :].astype(F32)
        return got if keep is None else jnp.where(keep, got, 0.0)

    def half(pair, axis):
        return pick(flags[axis], pair[8:], pair[:8])

    def line_b(at):
        plane = rows(at, 64)
        return pick(flags[1], plane[56:], plane[:8])

    def line_c(at):
        plane = rows(at, 64)
        ends = [
            pick(flags[2], plane[8 * b + 7 : 8 * b + 8], plane[8 * b : 8 * b + 1]) for b in range(8)
        ]
        return jnp.concatenate(ends, axis=0)

    def cell(at):
        line = line_b(at)
        return pick(flags[2], line[7:8], line[0:1])

    side = pick(flags[2], 0, 1)
    base = brick * 10

    def add_halo(at, line):
        halo[side, base + at, 8:16, :] = halo[side, base + at, 8:16, :] + line

    def add_cell(at, value):
        spot = pl.ds(pick(flags[1], 7, 16), 1)
        halo[side, base + at, spot, :] = halo[side, base + at, spot, :] + value

    if kind == (1, 0, 0):
        got = rows(facing, 64)
        first = (base + pads[0]) * 10 + 1
        for b in range(8):
            add_line(cells, first + b, got[b * 8 : b * 8 + 8])
    elif kind == (0, 1, 0):
        for a in range(8):
            if a in (0, 7):
                line = line_b(0 if a == 0 else 64)
            else:
                line = half(rows(B_LINES - 16 + 16 * a, 16), 1)
            add_line(cells, (base + a + 1) * 10 + pads[1], line)
    elif kind == (0, 0, 1):
        for a in range(8):
            if a in (0, 7):
                line = line_c(0 if a == 0 else 64)
            else:
                line = half(rows(C_LINES - 16 + 16 * a, 16), 2)
            add_halo(a + 1, line)
    elif kind == (1, 1, 0):
        add_line(cells, (base + pads[0]) * 10 + pads[1], line_b(facing))
    elif kind == (1, 0, 1):
        add_halo(pads[0], line_c(facing))
    elif kind == (0, 1, 1):
        for a in range(8):
            if a in (0, 7):
                value = cell(0 if a == 0 else 64)
            else:
                line = half(rows(C_LINES - 16 + 16 * a, 16), 2)
                value = pick(flags[1], line[7:8], line[0:1])
            add_cell(a + 1, value)
    else:
        add_cell(pads[0], cell(facing))


def windows(cells, halo, cols, bricks, out=None, sems=None):
    row = lax.broadcasted_iota(jnp.int32, (8, C), 0)

    def step(k, _):
        shifted = [[], [], []]
        for b in range(10):
            x = cells[k * 10 + b]
            before = halo[0, k, pl.ds(b + 7, 1), :]
            after = halo[1, k, pl.ds(b + 7, 1), :]
            shifted[0].append(jnp.where(row == 0, before, pltpu.roll(x, 1, 0)))
            shifted[1].append(x)
            shifted[2].append(jnp.where(row == 7, after, pltpu.roll(x, 7, 0)))
        for j in range(3):
            for l in range(3):
                block = jnp.concatenate(shifted[l][j : j + 8], axis=0).astype(BF16)
                at = (3 * j + l) * C
                cols[k, :, at : at + C] = block
        if out is not None:
            pltpu.make_async_copy(cols.at[k], out.at[k], sems.at[k]).start()
        return 0

    lax.fori_loop(0, bricks * 10, step, 0)


def wait_windows(cols, out, sems, bricks):
    def step(k, _):
        pltpu.make_async_copy(cols.at[k], out.at[k], sems.at[k]).wait()
        return 0

    lax.fori_loop(0, bricks * 10, step, 0)


def fetch(parts, share, sems, first=0, rows=None):
    size = parts[0].shape[0]
    lines = pl.ds(first, rows or parts[0].shape[1])
    copies = [
        pltpu.make_async_copy(part.at[:, lines], share.at[pl.ds(k * size, size), lines], sems.at[k])
        for k, part in enumerate(parts)
    ]
    for copy in copies:
        copy.start()
    return copies


def weight_grad_body(slots, factor, peers, count, *refs):
    recv, table, own_ref, cot_ref = refs[:4]
    parts = refs[4 : 4 + count]
    keep_ref = refs[4 + count]
    give_refs = refs[5 + count : 5 + count + peers // 4]
    out_cols, codes_ref, served_ref = refs[-16:-13]
    cells, halo, share, cols, sums, narrow, turned, codes = refs[-13:-5]
    sems, cols_sems, codes_sem, out_sems, notes_sems = refs[-5:]
    bricks = own_ref.shape[0] // 512
    me = table[2 * peers]
    notes_copies = fetch(parts, share, notes_sems, bricks * ROWS, NOTES)
    copies = fetch(parts, share, sems, 0, bricks * ROWS)
    for part in range(bricks * 2):
        at = slice(part * 256, part * 256 + 256)
        turned[:, at] = cot_ref[at, :].astype(F32).T.astype(BF16)
    for copy in notes_copies:
        copy.wait()
    for k in range(peers):
        notes = share[k, bricks * ROWS :, :].astype(F32).astype(jnp.int32)
        codes_ref[k : k + 1, :] = notes[0:1]
        served_ref[k : k + 1, :] = notes[1:2]
    codes_copy = pltpu.make_async_copy(codes_ref, codes, codes_sem.at[0])
    codes_copy.start()
    start_padded(own_ref, cells, halo, bricks)
    codes_copy.wait()
    for copy in copies:
        copy.wait()
    for brick in range(bricks):
        for number, e in enumerate(DIRECTIONS):
            slot = recv[brick, number]
            safe = jnp.maximum(slot, 0)
            sender = safe // slots
            at = table[sender]
            code = codes[at, me * slots + safe - sender * slots]
            kind = tuple(abs(t) for t in e)
            place(kind, e, slot >= 0, at, code // 6, brick, share, cells, halo)
    windows(cells, halo, cols, bricks, out_cols, cols_sems)

    rows = 27 * C // peers
    for tap in range(27):
        i, jl = divmod(tap, 9)
        total = None
        for brick in range(bricks):
            right = cols[brick * 10 + i : brick * 10 + i + 8, :, jl * C : jl * C + C].reshape(512, C)
            left = turned[:, brick * 512 : brick * 512 + 512]
            term = jnp.dot(left, right, preferred_element_type=F32)
            total = term if total is None else total + term
        total = (total * factor).T
        start = tap * C
        while start < (tap + 1) * C:
            owner = start // rows
            stop = min((tap + 1) * C, (owner + 1) * rows)
            piece = total[start - tap * C : stop - tap * C]
            bucket = jnp.bitwise_xor(me % 2, owner % 2)
            behind = table[peers + owner // 2]
            where = slice(start - owner * rows, stop - owner * rows)
            sums[bucket, behind, where, :] = piece
            narrow[bucket, behind, where, :] = piece.astype(BF16)
            start = stop
            if stop == (owner + 1) * rows:

                @pl.when(bucket == 0)
                def _():
                    pltpu.make_async_copy(
                        sums.at[0, behind], keep_ref.at[behind], out_sems.at[0, behind]
                    ).start()

                turn = table[peers + peers // 2 + owner // 2]
                for hop, give_ref in enumerate(give_refs):

                    @pl.when((bucket == 1) & (turn // 2 == hop))
                    def _():
                        pltpu.make_async_copy(
                            narrow.at[1, behind], give_ref.at[turn % 2], out_sems.at[1, turn]
                        ).start()

    for k in range(peers // 2):
        pltpu.make_async_copy(sums.at[0, k], keep_ref.at[k], out_sems.at[0, k]).wait()
        pltpu.make_async_copy(narrow.at[1, k], give_refs[k // 2].at[k % 2], out_sems.at[1, k]).wait()
    wait_windows(cols, out_cols, cols_sems, bricks)


GROUP = 3 * C


def start_stream(cols_ref, first, cols, weight_ref, weight, sems):
    copies = []
    planes = cols.shape[0]
    for g in range(3):
        lanes = pl.ds(g * GROUP, GROUP)
        group = [
            pltpu.make_async_copy(
                cols_ref.at[pl.ds(first, planes), :, lanes], cols.at[:, :, lanes], sems.at[g, 3]
            )
        ]
        for i in range(3):
            at = pl.ds((i * 3 + g) * GROUP, GROUP)
            group.append(pltpu.make_async_copy(weight_ref.at[at], weight.at[at], sems.at[g, i]))
        copies.append(group)
    for group in copies:
        for copy in group:
            copy.start()
    return copies


def tap_sum(copies, cols, weight):
    bricks = cols.shape[0] // 10
    totals = [None] * bricks
    for g in range(3):
        for copy in copies[g]:
            copy.wait()
        for brick in range(bricks):
            for i in range(3):
                at = brick * 10 + i
                left = cols[at : at + 8, :, g * GROUP : g * GROUP + GROUP].reshape(512, GROUP)
                right = weight[(i * 3 + g) * GROUP : (i * 3 + g + 1) * GROUP, :]
                term = jnp.dot(left, right, preferred_element_type=F32)
                totals[brick] = term if totals[brick] is None else totals[brick] + term
    return totals


def mix_body(here, *refs):
    cols_ref, weight_ref, x_ref = refs[:3]
    out_ref, cols, weight, rows, sems, row_sem = refs[-6:]
    copies = start_stream(cols_ref, here * 10, cols, weight_ref, weight, sems)
    (total,) = tap_sum(copies, cols, weight)
    at = pl.ds(here * 512, 512)
    rows[...] = (x_ref[at, :].astype(F32) + total).astype(BF16)
    copy = pltpu.make_async_copy(rows, out_ref.at[at], row_sem.at[0])
    copy.start()
    copy.wait()


def input_grad_body(slots, peers, count, *refs):
    served, send, table, cot_ref, x_ref, gain_ref, weight_ref = refs[:7]
    parts = refs[7 : 7 + count]
    out_ref, cells, halo, cols, share, weight, heads, more, sems, weight_sem = refs[7 + count :]
    bricks = cot_ref.shape[0] // 512
    me = table[2 * peers]
    copies = fetch(parts, share, sems)
    weight_copy = pltpu.make_async_copy(weight_ref, weight, weight_sem.at[0])
    weight_copy.start()

    def no_head(k, _):
        heads[k] = -1
        return 0

    lax.fori_loop(0, bricks * 26, no_head, 0)

    def source_of(k):
        receiver = k // slots
        at = table[receiver]
        return at, served[at, me * slots + k - receiver * slots] - 1

    def sort(k, found):
        _, entry = source_of(k)
        asked = entry >= 0
        key = send[0, k] // 6 * 26 + 25 - jnp.maximum(entry, 0) % 26
        first = asked & (heads[key] < 0)
        extra = asked & jnp.logical_not(first)

        @pl.when(first)
        def _():
            heads[key] = k

        @pl.when(extra)
        def _():
            more[found] = k

        return found + jnp.where(extra, 1, 0)

    found = lax.fori_loop(0, send.shape[1], sort, 0)
    start_padded(cot_ref, cells, halo, bricks)
    for copy in copies:
        copy.wait()
    for brick in range(bricks):
        for number, e in enumerate(DIRECTIONS):
            head = heads[brick * 26 + number]
            at, entry = source_of(jnp.maximum(head, 0))
            kind = tuple(abs(t) for t in e)
            source = jnp.maximum(entry, 0) // 26
            place(kind, e, head >= 0, at, source, brick, share, cells, halo)

    def one(n, _):
        k = more[n]
        at, entry = source_of(k)
        number = 25 - entry % 26
        tap = jnp.where(number >= 13, number + 1, number)
        e = (tap // 9 - 1, (tap // 3) % 3 - 1, tap % 3 - 1)
        on = [t != 0 for t in e]
        for kind in ((1, 0, 0), (0, 1, 0), (0, 0, 1), (1, 1, 0), (1, 0, 1), (0, 1, 1), (1, 1, 1)):
            match = functools.reduce(
                jnp.logical_and, [f if w else jnp.logical_not(f) for f, w in zip(on, kind)]
            )

            @pl.when(match)
            def _():
                place(kind, e, None, at, entry // 26, send[0, k] // 6, share, cells, halo)

        return 0

    lax.fori_loop(0, found, one, 0)
    windows(cells, halo, cols, bricks)
    weight_copy.wait()
    gain = gain_ref[...]
    for brick in range(bricks):
        rows = slice(brick * 512, brick * 512 + 512)
        grad = None
        for tap in range(27):
            i, jl = divmod(tap, 9)
            first = brick * 10 + i
            left = cols[first : first + 8, :, jl * C : jl * C + C].reshape(512, C)
            right = weight[(26 - tap) * C : (27 - tap) * C, :]
            term = lax.dot_general(left, right, (((1,), (1,)), ((), ())), preferred_element_type=F32)
            grad = term if grad is None else grad + term
        x = x_ref[rows, :].astype(F32)
        inverse = lax.rsqrt(jnp.mean(x * x, axis=-1, keepdims=True) + 1e-6)
        unit = x * inverse
        v = unit * gain
        gate = 1.0 / (1.0 + jnp.exp(-v))
        grad = grad * (gate * (1.0 + v * (1.0 - gate))) * gain
        grad = inverse * (grad - unit * jnp.mean(grad * unit, axis=-1, keepdims=True))
        out_ref[rows, :] = (cot_ref[rows, :].astype(F32) + grad).astype(BF16)


def local(features, norm_gain, conv_weight, recv_slot, send_face, cotangent):
    channels = features.shape[1]
    per_device = features.shape[0]
    bricks = per_device // 512
    peers = lax.axis_size("morton")
    slots = send_face.shape[1] // peers
    factor = 1.0 / math.sqrt(peers * per_device)
    gain = norm_gain.reshape(1, channels)
    sds = jax.ShapeDtypeStruct
    stage = pltpu.VMEM((8, 2, 64, 128), F32)

    def padded(n):
        return [
            pltpu.VMEM((n * 100, 8, channels), F32),
            pltpu.VMEM((2, n * 10, HB, channels), F32),
        ]

    def cols_shape(n):
        return (n * 10, 64, 9 * channels)


    table = jnp.asarray(ring_tables(peers))[lax.axis_index("morton")]

    hidden, share = call(
        norm_body,
        (sds((per_device, channels), BF16), sds((bricks * ROWS + NOTES, channels), BF16)),
        [SMEM, SMEM, VMEM, VMEM],
        [stage],
        name="norm",
    )(recv_slot, send_face, features, gain)
    hidden_ring = RingGather(share, peers)
    cot_share = call(
        extract_body,
        sds((bricks * ROWS, channels), BF16),
        [VMEM],
        [stage],
        name="extract",
    )(cotangent)
    hidden_ring.go(0)
    hidden_ring.go(1)
    hidden_ring.go(0, cot_share)
    hidden_ring.go(1)
    hidden_ring.go(0, table)
    hidden_ring.go(1)
    hidden_ring.go(0)
    hidden_parts = hidden_ring.places()

    cot_ring = RingGather(cot_share, peers)
    cot_ring.go(0, hidden_ring.last(1))
    cot_ring.go(1, hidden_ring.last(0))

    count = len(hidden_parts)
    rows = 27 * channels // peers
    chips = peers // 2
    keep, *give, cols, _, served = call(
        functools.partial(weight_grad_body, slots, factor, peers, count),
        (
            sds((chips, rows, channels), F32),
            *[sds((2, rows, channels), BF16)] * (chips // 2),
            sds(cols_shape(bricks), BF16),
            sds((peers, channels), jnp.int32),
            sds((peers, channels), jnp.int32),
        ),
        [SMEM] * 2 + [VMEM] * 2 + [HBM] * count,
        padded(bricks)
        + [
            pltpu.VMEM((peers, bricks * ROWS + NOTES, channels), BF16),
            pltpu.VMEM(cols_shape(bricks), BF16),
            pltpu.VMEM((2, chips, rows, channels), F32),
            pltpu.VMEM((2, chips, rows, channels), BF16),
            pltpu.VMEM((channels, per_device), BF16),
            pltpu.SMEM((peers, channels), jnp.int32),
            pltpu.SemaphoreType.DMA((count,)),
            pltpu.SemaphoreType.DMA((bricks * 10,)),
            pltpu.SemaphoreType.DMA((1,)),
            pltpu.SemaphoreType.DMA((2, chips)),
            pltpu.SemaphoreType.DMA((count,)),
        ],
        cost=9,
        name="weight_grad",
        out_specs=(*[HBM] * (2 + chips // 2), VMEM, VMEM),
    )(recv_slot, table, hidden, cotangent, *hidden_parts)

    first = (cot_ring.last(0), cot_ring.last(1))
    give = [lax.optimization_barrier((t, first))[0] for t in give]
    sums_ring = RingScatter(keep, give, peers)
    sent = sums_ring.go()
    cot_ring.go(0, cols)
    cot_ring.go(1, cols)
    ready = (cot_ring.last(0), cot_ring.last(1))
    weight_scratch = pltpu.VMEM((27 * channels, channels), BF16)
    mixed = []
    for brick in range(bricks):
        mix_cols = lax.optimization_barrier((cols, sent))[0]
        mixed.append(
            call(
                functools.partial(mix_body, brick),
                sds((per_device, channels), BF16),
                [HBM, HBM, VMEM] + [HBM] * len(mixed[-1:]),
                [
                    pltpu.VMEM(cols_shape(1), BF16),
                    weight_scratch,
                    pltpu.VMEM((512, channels), BF16),
                    pltpu.SemaphoreType.DMA((3, 4)),
                    pltpu.SemaphoreType.DMA((1,)),
                ],
                cost=3,
                name="mix_" + str(brick),
                out_specs=HBM,
                aliases={3: 0} if mixed else None,
            )(mix_cols, conv_weight, features, *mixed[-1:])
        )
        sent = sums_ring.go((ready, mixed[-1]))
        cot_ring.go(0)
        cot_ring.go(1)
        ready = (cot_ring.last(0), cot_ring.last(1))
    cot_parts = cot_ring.places(cols)
    sent = sums_ring.go(tuple(t for k, t in enumerate(cot_parts) if k != peers // 2 + peers // 4))
    served = lax.optimization_barrier((served, sent))[0]

    grad_features = call(
        functools.partial(input_grad_body, slots, peers, count),
        sds((per_device, channels), BF16),
        [SMEM] * 3 + [VMEM] * 3 + [HBM] * (1 + count),
        padded(bricks)
        + [
            pltpu.VMEM(cols_shape(bricks), BF16),
            pltpu.VMEM((peers, bricks * ROWS, channels), BF16),
            weight_scratch,
            pltpu.SMEM((bricks * 26,), jnp.int32),
            pltpu.SMEM((peers * slots,), jnp.int32),
            pltpu.SemaphoreType.DMA((count,)),
            pltpu.SemaphoreType.DMA((1,)),
        ],
        cost=13,
        name="input_grad",
    )(served, send_face, table, cotangent, features, gain, conv_weight, *cot_parts)
    for _ in range(chips // 2 - 4):
        sums_ring.go()
    return (mixed[-1], grad_features, sums_ring.total(grad_features))


def solution(mesh):
    rows = P(("groups", "morton"), None)
    return jax.shard_map(
        local,
        mesh=mesh,
        in_specs=(rows, P(), P(), rows, rows, rows),
        out_specs=(rows, rows, rows),
        check_vma=False,
    )
```

```python
import functools
import math

import jax
import jax.numpy as jnp
import numpy as np
from jax import lax
from jax.experimental import pallas as pl
from jax.experimental.pallas import tpu as pltpu
from jax.sharding import PartitionSpec as P

F32 = jnp.float32
BF16 = jnp.bfloat16
C = 256
C_LINES = 128
B_LINES = 224
ROWS = 320
NOTES = 16
HB = 24
VMEM_LIMIT = 56 * 1024 * 1024
DIRECTIONS = [
    (i, j, l)
    for i in (-1, 0, 1)
    for j in (-1, 0, 1)
    for l in (-1, 0, 1)
    if (i, j, l) != (0, 0, 0)
]

VMEM = pl.BlockSpec(memory_space=pltpu.VMEM)
SMEM = pl.BlockSpec(memory_space=pltpu.SMEM)
ANY = pl.BlockSpec(memory_space=pl.ANY)
HBM = pl.BlockSpec(memory_space=pltpu.HBM)


def ring_order(chips):
    if chips == 8:
        return [0, 2, 4, 6, 7, 5, 3, 1]
    return list(range(chips))


def ring_tables(peers):
    chips = peers // 2
    spot = np.argsort(np.array(ring_order(chips)))
    device = np.arange(peers)
    behind = (spot[device // 2][:, None] - spot[None, :]) % chips
    half = chips // 2
    turn = np.where(behind >= half, 2 * (behind - half), 2 * (half - 1 - behind) + 1)
    places = np.broadcast_to(device, (2, peers, peers)).copy()
    if chips <= 8:
        for me in range(peers):
            for other in range(peers):
                away = behind[me, other // 2] if me % 2 == 0 else -behind[me, other // 2] % chips
                same = me % 2 == other % 2
                if away == 0:
                    place = (0, 0) if same else (1, 1)
                elif away < half or (away == half and same):
                    place = (1 + away, 2 * away) if same else (1 + half + away, 2 * away + 1)
                else:
                    away = chips - away
                    place = (2 * half + away, 2 * half + 2 * away - 1)
                    if same:
                        place = (3 * half + away, 2 * half + 2 * away)
                places[:, me, other] = place
    return np.concatenate([*places, behind, turn, device[:, None]], axis=1).astype(np.int32)


def ring_step(x, peers, step, cross=0):
    order = ring_order(peers // 2)
    pairs = [
        (2 * order[i] + (core ^ cross), 2 * order[(i + (step or 1 - 2 * core)) % len(order)] + core)
        for i in range(len(order))
        for core in range(2)
    ]
    return lax.ppermute(x, "morton", pairs)


def swap_cores(x, peers):
    return lax.ppermute(x, "morton", [(m, m ^ 1) for m in range(peers)])


class RingGather:
    def __init__(self, x, peers):
        self.x, self.peers, self.chips = x, peers, peers // 2
        self.whole = None
        if self.chips > 8:
            self.whole = lax.all_gather(x[None], "morton", axis=0, tiled=True)
            return
        self.chains = ([x], [x])

    def go(self, chain, gate=None):
        if self.whole is not None or len(self.chains[chain]) > self.chips // 2 - chain:
            return
        held = self.chains[chain][-1]
        if gate is not None:
            held = lax.optimization_barrier((held, gate))[0]
        cross = int(chain == 1 and len(self.chains[chain]) == 1)
        self.chains[chain].append(ring_step(held, self.peers, 0, cross))

    def last(self, chain):
        return self.x if self.whole is not None else self.chains[chain][-1]

    def places(self, gate=None):
        if self.whole is not None:
            return [self.whole]
        mine = self.chains[0][1:] + self.chains[1][1:]
        held = mine
        if gate is not None:
            held = [lax.optimization_barrier((t, gate))[0] for t in mine]
        others = [swap_cores(t, self.peers) for t in [self.x] + held]
        return [t[None] for t in [self.x] + others[:1] + mine + others[1:]]


class PairGather:
    def __init__(self, x, peers, gate):
        self.peers, self.chips = peers, peers // 2
        self.whole = None
        if self.chips > 8:
            self.whole = lax.all_gather(x[None], "morton", axis=0, tiled=True)
            return
        self.rows = x.shape[0]
        x = lax.optimization_barrier((x, gate))[0]
        self.hops = [jnp.concatenate([x, swap_cores(x, peers)], axis=0)]

    def go(self, gate=None):
        if self.whole is not None:
            return
        held = self.hops[-1]
        if len(self.hops) == self.chips // 2:
            held = held[: self.rows]
        if gate is not None:
            held = lax.optimization_barrier((held, gate))[0]
        self.hops.append(ring_step(held, self.peers, 0))

    def last(self):
        return self.whole if self.whole is not None else self.hops[-1]

    def places(self, gate):
        if self.whole is not None:
            return [self.whole], [self.whole]
        held = [lax.optimization_barrier((t, gate))[0] for t in self.hops[1:]]
        got = self.hops + [swap_cores(t, self.peers) for t in held]
        got = [t.reshape(-1, self.rows, t.shape[1]) for t in got]
        return got, got[: self.chips // 2] + got[self.chips // 2 + 1 : -1]


class RingScatter:
    def __init__(self, keep, give, peers):
        self.keep, self.peers, self.chips = keep, peers, peers // 2
        self.other = [swap_cores(t, peers) for t in give]
        self.held = [None, None]
        self.hop = 0

    def term(self, k):
        half = self.chips // 2
        pair = self.other[k - half][0] if k >= half else self.other[half - 1 - k][1]
        return self.keep[k] + pair.astype(F32)

    def go(self, gate=None):
        sent = []
        for way, step, count in ((0, 1, self.chips // 2), (1, -1, (self.chips - 1) // 2)):
            left = count - self.hop
            if left <= 0:
                continue
            part = self.term((-step * left) % self.chips)
            if self.held[way] is not None:
                part = part + self.held[way].astype(F32)
            part = part.astype(BF16)
            if gate is not None:
                part = lax.optimization_barrier((part, gate))[0]
            sent.append(part)
            self.held[way] = ring_step(part, self.peers, step)
        self.hop += 1
        return sent

    def total(self, gate):
        held = lax.optimization_barrier((*self.held, gate))[:2]
        return sum((t.astype(F32) for t in held), self.term(0))


def call(body, out_shape, in_specs, scratch=(), cost=2, name=None, out_specs=None, aliases=None):
    return pl.pallas_call(
        body,
        out_shape=out_shape,
        in_specs=in_specs,
        out_specs=out_specs or jax.tree.map(lambda _: VMEM, out_shape),
        scratch_shapes=list(scratch),
        input_output_aliases=aliases or {},
        compiler_params=pltpu.CompilerParams(vmem_limit_bytes=VMEM_LIMIT),
        cost_estimate=pl.CostEstimate(flops=cost * 10**9, bytes_accessed=0, transcendentals=0),
        name=name,
    )


PLANES = 4


def put_boundary(rows, base, a, out_ref, stage):
    wide = rows.astype(F32)

    def put(at, value, lanes=slice(None)):
        out_ref[pl.ds(pl.multiple_of(base + at, 16), value.shape[0]), lanes] = value

    if a in (0, 7):
        put(0 if a == 0 else 64, rows)
        return
    for half in range(2):
        lanes = slice(half * 128, half * 128 + 128)
        stage[half] = wide[:, lanes]
        first = stage[half, pl.ds(0, 8, stride=8), :]
        last = stage[half, pl.ds(7, 8, stride=8), :]
        put(C_LINES - 16 + 16 * a, jnp.concatenate([first, last], axis=0).astype(BF16), lanes)
    pair = jnp.concatenate([wide[:8], wide[56:]], axis=0).astype(BF16)
    put(B_LINES - 16 + 16 * a, pair)


def each_brick(rows_of, bricks, out_ref, stage):
    def step(brick, _):
        for first in range(0, 8, PLANES):
            at = pl.multiple_of(brick * 512 + first * 64, 64)
            rows = rows_of(pl.ds(at, PLANES * 64))
            for t in range(PLANES):
                plane = rows[t * 64 : t * 64 + 64]
                put_boundary(plane, brick * ROWS, first + t, out_ref, stage.at[first + t])
        return 0

    lax.fori_loop(0, bricks, step, 0)


def norm_body(recv, send, x_ref, gain_ref, hidden_ref, out_ref, stage):
    bricks, directions = recv.shape
    gain = gain_ref[...]
    lane = lax.broadcasted_iota(jnp.int32, (1, C), 1)
    codes = jnp.zeros((1, C), jnp.int32)
    for k in range(send.shape[1]):
        codes = jnp.where(lane == k, send[0, k], codes)
    served = jnp.zeros((1, C), jnp.int32)
    for brick in range(bricks):
        for number in range(directions):
            served = jnp.where(lane == recv[brick, number], brick * directions + number + 1, served)
    row = lax.broadcasted_iota(jnp.int32, (NOTES, C), 0)
    notes = jnp.where(row == 0, codes, jnp.where(row == 1, served, 0))
    out_ref[bricks * ROWS :, :] = notes.astype(F32).astype(BF16)

    def rows_of(at):
        x = x_ref[at, :].astype(F32)
        inverse = lax.rsqrt(jnp.mean(x * x, axis=-1, keepdims=True) + 1e-6)
        v = x * inverse * gain
        rows = (v / (1.0 + jnp.exp(-v))).astype(BF16)
        hidden_ref[at, :] = rows
        return rows

    each_brick(rows_of, bricks, out_ref, stage)


def extract_body(x_ref, out_ref, stage):
    each_brick(lambda at: x_ref[at, :], x_ref.shape[0] // 512, out_ref, stage)


def start_padded(own_ref, cells, halo, bricks):
    zero = jnp.zeros((8, C), F32)

    def clear(k, _):
        for b in range(10):
            cells[k * 10 + b] = zero
        for side in range(2):
            for part in range(HB // 8):
                halo[side, k, part * 8 : part * 8 + 8, :] = zero
        return 0

    lax.fori_loop(0, bricks * 10, clear, 0)

    def fill(k, _):
        plane = (k // 8) * 10 + k % 8 + 1
        rows = own_ref[pl.ds(pl.multiple_of(k * 64, 64), 64), :].astype(F32)
        for b in range(8):
            cells[plane * 10 + b + 1] = rows[b * 8 : b * 8 + 8]
        return 0

    lax.fori_loop(0, bricks * 8, fill, 0)


def add_line(ref, index, line):
    ref[index] = ref[index] + line


def pick(flag, yes, no):
    if isinstance(flag, bool):
        return yes if flag else no
    return jnp.where(flag, yes, no)


def place(kind, e, keep, place_at, source_brick, brick, share, cells, halo):
    flags = [t == -1 for t in e]
    pads = [pick(f, 0, 9) for f in flags]
    facing = pick(flags[0], 64, 0)
    start = source_brick * ROWS

    def rows(at, size):
        got = share[place_at, pl.ds(pl.multiple_of(start + at, 16), size), :].astype(F32)
        return got if keep is None else jnp.where(keep, got, 0.0)

    def half(pair, axis):
        return pick(flags[axis], pair[8:], pair[:8])

    def line_b(at):
        plane = rows(at, 64)
        return pick(flags[1], plane[56:], plane[:8])

    def line_c(at):
        plane = rows(at, 64)
        ends = [
            pick(flags[2], plane[8 * b + 7 : 8 * b + 8], plane[8 * b : 8 * b + 1]) for b in range(8)
        ]
        return jnp.concatenate(ends, axis=0)

    def cell(at):
        line = line_b(at)
        return pick(flags[2], line[7:8], line[0:1])

    side = pick(flags[2], 0, 1)
    base = brick * 10

    def add_halo(at, line):
        halo[side, base + at, 8:16, :] = halo[side, base + at, 8:16, :] + line

    def add_cell(at, value):
        spot = pl.ds(pick(flags[1], 7, 16), 1)
        halo[side, base + at, spot, :] = halo[side, base + at, spot, :] + value

    if kind == (1, 0, 0):
        got = rows(facing, 64)
        first = (base + pads[0]) * 10 + 1
        for b in range(8):
            add_line(cells, first + b, got[b * 8 : b * 8 + 8])
    elif kind == (0, 1, 0):
        for a in range(8):
            if a in (0, 7):
                line = line_b(0 if a == 0 else 64)
            else:
                line = half(rows(B_LINES - 16 + 16 * a, 16), 1)
            add_line(cells, (base + a + 1) * 10 + pads[1], line)
    elif kind == (0, 0, 1):
        for a in range(8):
            if a in (0, 7):
                line = line_c(0 if a == 0 else 64)
            else:
                line = half(rows(C_LINES - 16 + 16 * a, 16), 2)
            add_halo(a + 1, line)
    elif kind == (1, 1, 0):
        add_line(cells, (base + pads[0]) * 10 + pads[1], line_b(facing))
    elif kind == (1, 0, 1):
        add_halo(pads[0], line_c(facing))
    elif kind == (0, 1, 1):
        for a in range(8):
            if a in (0, 7):
                value = cell(0 if a == 0 else 64)
            else:
                line = half(rows(C_LINES - 16 + 16 * a, 16), 2)
                value = pick(flags[1], line[7:8], line[0:1])
            add_cell(a + 1, value)
    else:
        add_cell(pads[0], cell(facing))


def windows(cells, halo, cols, bricks):
    row = lax.broadcasted_iota(jnp.int32, (8, C), 0)

    def step(k, _):
        shifted = [[], [], []]
        for b in range(10):
            x = cells[k * 10 + b]
            before = halo[0, k, pl.ds(b + 7, 1), :]
            after = halo[1, k, pl.ds(b + 7, 1), :]
            shifted[0].append(jnp.where(row == 0, before, pltpu.roll(x, 1, 0)))
            shifted[1].append(x)
            shifted[2].append(jnp.where(row == 7, after, pltpu.roll(x, 7, 0)))
        for j in range(3):
            for l in range(3):
                block = jnp.concatenate(shifted[l][j : j + 8], axis=0).astype(BF16)
                at = (3 * j + l) * C
                cols[k, :, at : at + C] = block
        return 0

    lax.fori_loop(0, bricks * 10, step, 0)


def fetch(parts, share, sems, first=0, rows=None):
    lines = pl.ds(first, rows or parts[0].shape[1])
    copies = []
    place = 0
    for k, part in enumerate(parts):
        size = part.shape[0]
        to = share.at[pl.ds(place, size), lines]
        copies.append(pltpu.make_async_copy(part.at[:, lines], to, sems.at[k]))
        place += size
    for copy in copies:
        copy.start()
    return copies


def weight_grad_body(slots, factor, peers, count, *refs):
    recv, table, own_ref, cot_ref, x_ref, weight_ref = refs[:6]
    parts = refs[6 : 6 + count]
    keep_ref = refs[6 + count]
    give_refs = refs[7 + count : 7 + count + peers // 4]
    mix_ref, codes_ref, served_ref = refs[-16:-13]
    cells, halo, share, cols, sums, narrow, turned, weight, codes = refs[-13:-4]
    sems, codes_sem, out_sems, notes_sems = refs[-4:]
    bricks = own_ref.shape[0] // 512
    me = table[3 * peers]
    notes_copies = fetch(parts, share, notes_sems, bricks * ROWS, NOTES)
    copies = fetch(parts, share, sems, 0, bricks * ROWS)
    weight_copy = pltpu.make_async_copy(weight_ref, weight, codes_sem.at[1])
    weight_copy.start()
    for part in range(bricks * 2):
        at = slice(part * 256, part * 256 + 256)
        turned[:, at] = cot_ref[at, :].astype(F32).T.astype(BF16)
    for copy in notes_copies:
        copy.wait()
    for k in range(peers):
        notes = share[k, bricks * ROWS :, :].astype(F32).astype(jnp.int32)
        codes_ref[k : k + 1, :] = notes[0:1]
        served_ref[k : k + 1, :] = notes[1:2]
    codes_copy = pltpu.make_async_copy(codes_ref, codes, codes_sem.at[0])
    codes_copy.start()
    start_padded(own_ref, cells, halo, bricks)
    codes_copy.wait()
    for copy in copies:
        copy.wait()
    for brick in range(bricks):
        for number, e in enumerate(DIRECTIONS):
            slot = recv[brick, number]
            safe = jnp.maximum(slot, 0)
            sender = safe // slots
            at = table[sender]
            code = codes[at, me * slots + safe - sender * slots]
            kind = tuple(abs(t) for t in e)
            place(kind, e, slot >= 0, at, code // 6, brick, share, cells, halo)
    windows(cells, halo, cols, bricks)

    rows = 27 * C // peers
    for tap in range(27):
        i, jl = divmod(tap, 9)
        total = None
        for brick in range(bricks):
            right = cols[brick * 10 + i : brick * 10 + i + 8, :, jl * C : jl * C + C].reshape(512, C)
            left = turned[:, brick * 512 : brick * 512 + 512]
            term = jnp.dot(left, right, preferred_element_type=F32)
            total = term if total is None else total + term
        total = (total * factor).T
        start = tap * C
        while start < (tap + 1) * C:
            owner = start // rows
            stop = min((tap + 1) * C, (owner + 1) * rows)
            piece = total[start - tap * C : stop - tap * C]
            bucket = jnp.bitwise_xor(me % 2, owner % 2)
            behind = table[2 * peers + owner // 2]
            where = slice(start - owner * rows, stop - owner * rows)
            sums[bucket, behind, where, :] = piece
            turn = table[2 * peers + peers // 2 + owner // 2]
            narrow[bucket, turn, where, :] = piece.astype(BF16)
            start = stop

    out_copies = []
    for k in range(peers // 2):
        give_ref = give_refs[k // 2].at[k % 2]
        out_copies.append(pltpu.make_async_copy(narrow.at[1, k], give_ref, out_sems.at[1, k]))
    for k in range(peers // 2):
        out_copies.append(pltpu.make_async_copy(sums.at[0, k], keep_ref.at[k], out_sems.at[0, k]))
    for copy in out_copies:
        copy.start()
    weight_copy.wait()
    for brick in range(bricks):
        at = slice(brick * 512, brick * 512 + 512)
        total = None
        for i in range(3):
            left = cols[brick * 10 + i : brick * 10 + i + 8].reshape(512, 9 * C)
            right = weight[i * 9 * C : (i + 1) * 9 * C, :]
            term = jnp.dot(left, right, preferred_element_type=F32)
            total = term if total is None else total + term
        mix_ref[at, :] = (x_ref[at, :].astype(F32) + total).astype(BF16)
    for copy in out_copies:
        copy.wait()


def input_grad_body(slots, peers, count, *refs):
    served, send, table, cot_ref, x_ref, gain_ref, weight_ref = refs[:7]
    parts = refs[7 : 7 + count]
    out_ref, cells, halo, cols, share, weight, heads, more, sems, weight_sem = refs[7 + count :]
    bricks = cot_ref.shape[0] // 512
    me = table[3 * peers]
    copies = fetch(parts, share, sems)
    weight_copy = pltpu.make_async_copy(weight_ref, weight, weight_sem.at[0])
    weight_copy.start()

    def no_head(k, _):
        heads[k] = -1
        return 0

    lax.fori_loop(0, bricks * 26, no_head, 0)

    def source_of(k):
        receiver = k // slots
        entry = served[table[receiver], me * slots + k - receiver * slots] - 1
        return table[peers + receiver], entry

    def sort(k, found):
        _, entry = source_of(k)
        asked = entry >= 0
        key = send[0, k] // 6 * 26 + 25 - jnp.maximum(entry, 0) % 26
        first = asked & (heads[key] < 0)
        extra = asked & jnp.logical_not(first)

        @pl.when(first)
        def _():
            heads[key] = k

        @pl.when(extra)
        def _():
            more[found] = k

        return found + jnp.where(extra, 1, 0)

    found = lax.fori_loop(0, send.shape[1], sort, 0)
    start_padded(cot_ref, cells, halo, bricks)
    for copy in copies:
        copy.wait()
    for brick in range(bricks):
        for number, e in enumerate(DIRECTIONS):
            head = heads[brick * 26 + number]
            at, entry = source_of(jnp.maximum(head, 0))
            kind = tuple(abs(t) for t in e)
            source = jnp.maximum(entry, 0) // 26
            place(kind, e, head >= 0, at, source, brick, share, cells, halo)

    def one(n, _):
        k = more[n]
        at, entry = source_of(k)
        number = 25 - entry % 26
        tap = jnp.where(number >= 13, number + 1, number)
        e = (tap // 9 - 1, (tap // 3) % 3 - 1, tap % 3 - 1)
        on = [t != 0 for t in e]
        for kind in ((1, 0, 0), (0, 1, 0), (0, 0, 1), (1, 1, 0), (1, 0, 1), (0, 1, 1), (1, 1, 1)):
            match = functools.reduce(
                jnp.logical_and, [f if w else jnp.logical_not(f) for f, w in zip(on, kind)]
            )

            @pl.when(match)
            def _():
                place(kind, e, None, at, entry // 26, send[0, k] // 6, share, cells, halo)

        return 0

    lax.fori_loop(0, found, one, 0)
    windows(cells, halo, cols, bricks)
    weight_copy.wait()
    gain = gain_ref[...]
    for brick in range(bricks):
        rows = slice(brick * 512, brick * 512 + 512)
        grad = None
        for tap in range(27):
            i, jl = divmod(tap, 9)
            first = brick * 10 + i
            left = cols[first : first + 8, :, jl * C : jl * C + C].reshape(512, C)
            right = weight[(26 - tap) * C : (27 - tap) * C, :]
            term = lax.dot_general(left, right, (((1,), (1,)), ((), ())), preferred_element_type=F32)
            grad = term if grad is None else grad + term
        x = x_ref[rows, :].astype(F32)
        inverse = lax.rsqrt(jnp.mean(x * x, axis=-1, keepdims=True) + 1e-6)
        unit = x * inverse
        v = unit * gain
        gate = 1.0 / (1.0 + jnp.exp(-v))
        grad = grad * (gate * (1.0 + v * (1.0 - gate))) * gain
        grad = inverse * (grad - unit * jnp.mean(grad * unit, axis=-1, keepdims=True))
        out_ref[rows, :] = (cot_ref[rows, :].astype(F32) + grad).astype(BF16)


def local(features, norm_gain, conv_weight, recv_slot, send_face, cotangent):
    channels = features.shape[1]
    per_device = features.shape[0]
    bricks = per_device // 512
    peers = lax.axis_size("morton")
    slots = send_face.shape[1] // peers
    factor = 1.0 / math.sqrt(peers * per_device)
    gain = norm_gain.reshape(1, channels)
    sds = jax.ShapeDtypeStruct
    stage = pltpu.VMEM((8, 2, 64, 128), F32)

    def padded(n):
        return [
            pltpu.VMEM((n * 100, 8, channels), F32),
            pltpu.VMEM((2, n * 10, HB, channels), F32),
        ]

    def cols_shape(n):
        return (n * 10, 64, 9 * channels)


    table = jnp.asarray(ring_tables(peers))[lax.axis_index("morton")]

    hidden, share = call(
        norm_body,
        (sds((per_device, channels), BF16), sds((bricks * ROWS + NOTES, channels), BF16)),
        [SMEM, SMEM, VMEM, VMEM],
        [stage],
        name="norm",
    )(recv_slot, send_face, features, gain)
    hidden_ring = RingGather(share, peers)
    cot_share = call(
        extract_body,
        sds((bricks * ROWS, channels), BF16),
        [VMEM],
        [stage],
        name="extract",
    )(cotangent)
    hidden_ring.go(0)
    hidden_ring.go(1)
    hidden_ring.go(0, cot_share)
    hidden_ring.go(1)
    cot_ring = PairGather(cot_share, peers, hidden_ring.last(0))
    hidden_ring.go(0, table)
    hidden_ring.go(1)
    hidden_ring.go(0, cot_ring.last())
    hidden_parts = hidden_ring.places()
    cot_ring.go(hidden_ring.last(0))

    count = len(hidden_parts)
    rows = 27 * channels // peers
    chips = peers // 2
    weight_scratch = pltpu.VMEM((27 * channels, channels), BF16)
    keep, *give, mixed, _, served = call(
        functools.partial(weight_grad_body, slots, factor, peers, count),
        (
            sds((chips, rows, channels), F32),
            *[sds((2, rows, channels), BF16)] * (chips // 2),
            sds((per_device, channels), BF16),
            sds((peers, channels), jnp.int32),
            sds((peers, channels), jnp.int32),
        ),
        [SMEM] * 2 + [VMEM] * 3 + [HBM] * (1 + count),
        padded(bricks)
        + [
            pltpu.VMEM((peers, bricks * ROWS + NOTES, channels), BF16),
            pltpu.VMEM(cols_shape(bricks), BF16),
            pltpu.VMEM((2, chips, rows, channels), F32),
            pltpu.VMEM((2, chips, rows, channels), BF16),
            pltpu.VMEM((channels, per_device), BF16),
            weight_scratch,
            pltpu.SMEM((peers, channels), jnp.int32),
            pltpu.SemaphoreType.DMA((count,)),
            pltpu.SemaphoreType.DMA((2,)),
            pltpu.SemaphoreType.DMA((2, chips)),
            pltpu.SemaphoreType.DMA((count,)),
        ],
        cost=13,
        name="weight_grad",
        out_specs=(*[HBM] * (1 + chips // 2), VMEM, VMEM, VMEM),
    )(recv_slot, table, hidden, cotangent, features, conv_weight, *hidden_parts)

    give = [lax.optimization_barrier((t, cot_ring.last()))[0] for t in give]
    sums_ring = RingScatter(keep, give, peers)
    cot_ring.go(served)
    sums_ring.go()
    gate = cot_ring.last()
    cot_ring.go(sums_ring.held[0])
    sums_ring.go(gate)
    sent = sums_ring.go(cot_ring.last())
    cot_ring.go(sent)
    cot_parts, early = cot_ring.places(served)
    sent = sums_ring.go(early)
    served = lax.optimization_barrier((served, sent))[0]

    grad_features = call(
        functools.partial(input_grad_body, slots, peers, len(cot_parts)),
        sds((per_device, channels), BF16),
        [SMEM] * 3 + [VMEM] * 3 + [HBM] * (1 + len(cot_parts)),
        padded(bricks)
        + [
            pltpu.VMEM(cols_shape(bricks), BF16),
            pltpu.VMEM((peers, bricks * ROWS, channels), BF16),
            weight_scratch,
            pltpu.SMEM((bricks * 26,), jnp.int32),
            pltpu.SMEM((peers * slots,), jnp.int32),
            pltpu.SemaphoreType.DMA((len(cot_parts),)),
            pltpu.SemaphoreType.DMA((1,)),
        ],
        cost=13,
        name="input_grad",
    )(served, send_face, table, cotangent, features, gain, conv_weight, *cot_parts)
    for _ in range(chips // 2 - 4):
        sums_ring.go()
    return (mixed, grad_features, sums_ring.total(grad_features))


def solution(mesh):
    rows = P(("groups", "morton"), None)
    return jax.shard_map(
        local,
        mesh=mesh,
        in_specs=(rows, P(), P(), rows, rows, rows),
        out_specs=(rows, rows, rows),
        check_vma=False,
    )
```

```python
import functools
import math

import jax
import jax.numpy as jnp
import numpy as np
from jax import lax
from jax.experimental import pallas as pl
from jax.experimental.pallas import tpu as pltpu
from jax.sharding import PartitionSpec as P

F32 = jnp.float32
BF16 = jnp.bfloat16
C = 256
C_LINES = 128
B_LINES = 224
ROWS = 320
NOTES = 16
HB = 24
VMEM_LIMIT = 56 * 1024 * 1024
DIRECTIONS = [
    (i, j, l)
    for i in (-1, 0, 1)
    for j in (-1, 0, 1)
    for l in (-1, 0, 1)
    if (i, j, l) != (0, 0, 0)
]

VMEM = pl.BlockSpec(memory_space=pltpu.VMEM)
SMEM = pl.BlockSpec(memory_space=pltpu.SMEM)
ANY = pl.BlockSpec(memory_space=pl.ANY)
HBM = pl.BlockSpec(memory_space=pltpu.HBM)


def ring_order(chips):
    if chips == 8:
        return [0, 2, 4, 6, 7, 5, 3, 1]
    return list(range(chips))


def ring_tables(peers):
    chips = peers // 2
    spot = np.argsort(np.array(ring_order(chips)))
    device = np.arange(peers)
    behind = (spot[device // 2][:, None] - spot[None, :]) % chips
    half = chips // 2
    turn = np.where(behind >= half, 2 * (behind - half), 2 * (half - 1 - behind) + 1)
    place_of = np.broadcast_to(device, (peers, peers)).copy()
    if chips <= 8:
        for me in range(peers):
            for other in range(peers):
                away = behind[me, other // 2] if me % 2 == 0 else -behind[me, other // 2] % chips
                same = me % 2 == other % 2
                if away == 0:
                    place = 0 if same else 1
                elif away < half or (away == half and same):
                    place = 1 + away if same else 1 + half + away
                else:
                    place = 3 * half + chips - away if same else 2 * half + chips - away
                place_of[me, other] = place
    return np.concatenate([place_of, behind, turn, device[:, None]], axis=1).astype(np.int32)


def ring_step(x, peers, step, cross=0):
    order = ring_order(peers // 2)
    pairs = [
        (2 * order[i] + (core ^ cross), 2 * order[(i + (step or 1 - 2 * core)) % len(order)] + core)
        for i in range(len(order))
        for core in range(2)
    ]
    return lax.ppermute(x, "morton", pairs)


def swap_cores(x, peers):
    return lax.ppermute(x, "morton", [(m, m ^ 1) for m in range(peers)])


class RingGather:
    def __init__(self, x, peers):
        self.x, self.peers, self.chips = x, peers, peers // 2
        self.whole = None
        self.swaps = {}
        if self.chips > 8:
            self.whole = lax.all_gather(x[None], "morton", axis=0, tiled=True)
            return
        self.chains = ([x], [x])

    def go(self, chain, gate=None):
        if self.whole is not None or len(self.chains[chain]) > self.chips // 2 - chain:
            return
        held = self.chains[chain][-1]
        if gate is not None:
            held = lax.optimization_barrier((held, gate))[0]
        cross = int(chain == 1 and len(self.chains[chain]) == 1)
        self.chains[chain].append(ring_step(held, self.peers, 0, cross))

    def last(self, chain):
        return self.x if self.whole is not None else self.chains[chain][-1]

    def swap(self, chain, hop, gate=None):
        if self.whole is None and (chain, hop) not in self.swaps:
            held = self.chains[chain][hop]
            if gate is not None:
                held = lax.optimization_barrier((held, gate))[0]
            self.swaps[chain, hop] = swap_cores(held, self.peers)
        return self.swaps.get((chain, hop), self.x)

    def places(self):
        if self.whole is not None:
            return [self.whole]
        keys = [(c, h) for c in (0, 1) for h in range(1, len(self.chains[c]))]
        mine = [self.x, self.swap(0, 0)] + [self.chains[c][h] for c, h in keys]
        return [t[None] for t in mine + [self.swap(c, h) for c, h in keys]]


class RingScatter:
    def __init__(self, keep, give, peers):
        self.keep, self.peers, self.chips = keep, peers, peers // 2
        self.other = [swap_cores(t, peers) for t in give]
        self.held = [None, None]
        self.hop = 0

    def term(self, k):
        half = self.chips // 2
        pair = self.other[k - half][0] if k >= half else self.other[half - 1 - k][1]
        return self.keep[k] + pair.astype(F32)

    def go(self, gate=None):
        sent = []
        for way, step, count in ((0, 1, self.chips // 2), (1, -1, (self.chips - 1) // 2)):
            left = count - self.hop
            if left <= 0:
                continue
            part = self.term((-step * left) % self.chips)
            if self.held[way] is not None:
                part = part + self.held[way].astype(F32)
            part = part.astype(BF16)
            if gate is not None:
                part = lax.optimization_barrier((part, gate))[0]
            sent.append(part)
            self.held[way] = ring_step(part, self.peers, step)
        self.hop += 1
        return sent

    def total(self, gate):
        held = lax.optimization_barrier((*self.held, gate))[:2]
        return sum((t.astype(F32) for t in held), self.term(0))


def call(body, out_shape, in_specs, scratch=(), cost=2, name=None, out_specs=None, aliases=None):
    return pl.pallas_call(
        body,
        out_shape=out_shape,
        in_specs=in_specs,
        out_specs=out_specs or jax.tree.map(lambda _: VMEM, out_shape),
        scratch_shapes=list(scratch),
        input_output_aliases=aliases or {},
        compiler_params=pltpu.CompilerParams(vmem_limit_bytes=VMEM_LIMIT),
        cost_estimate=pl.CostEstimate(flops=cost * 10**9, bytes_accessed=0, transcendentals=0),
        name=name,
    )


PLANES = 4


def put_boundary(rows, base, a, out_ref, stage):
    wide = rows.astype(F32)

    def put(at, value, lanes=slice(None)):
        out_ref[pl.ds(pl.multiple_of(base + at, 16), value.shape[0]), lanes] = value

    if a in (0, 7):
        put(0 if a == 0 else 64, rows)
        return
    for half in range(2):
        lanes = slice(half * 128, half * 128 + 128)
        stage[half] = wide[:, lanes]
        first = stage[half, pl.ds(0, 8, stride=8), :]
        last = stage[half, pl.ds(7, 8, stride=8), :]
        put(C_LINES - 16 + 16 * a, jnp.concatenate([first, last], axis=0).astype(BF16), lanes)
    pair = jnp.concatenate([wide[:8], wide[56:]], axis=0).astype(BF16)
    put(B_LINES - 16 + 16 * a, pair)


def each_brick(rows_of, bricks, out_ref, stage):
    def step(brick, _):
        for first in range(0, 8, PLANES):
            at = pl.multiple_of(brick * 512 + first * 64, 64)
            rows = rows_of(pl.ds(at, PLANES * 64))
            for t in range(PLANES):
                plane = rows[t * 64 : t * 64 + 64]
                put_boundary(plane, brick * ROWS, first + t, out_ref, stage.at[first + t])
        return 0

    lax.fori_loop(0, bricks, step, 0)


def norm_body(recv, send, x_ref, gain_ref, hidden_ref, out_ref, stage):
    bricks, directions = recv.shape
    gain = gain_ref[...]
    lane = lax.broadcasted_iota(jnp.int32, (1, C), 1)
    codes = jnp.zeros((1, C), jnp.int32)
    for k in range(send.shape[1]):
        codes = jnp.where(lane == k, send[0, k], codes)
    served = jnp.zeros((1, C), jnp.int32)
    for brick in range(bricks):
        for number in range(directions):
            served = jnp.where(lane == recv[brick, number], brick * directions + number + 1, served)
    row = lax.broadcasted_iota(jnp.int32, (NOTES, C), 0)
    notes = jnp.where(row == 0, codes, jnp.where(row == 1, served, 0))
    out_ref[bricks * ROWS :, :] = notes.astype(F32).astype(BF16)

    def rows_of(at):
        x = x_ref[at, :].astype(F32)
        inverse = lax.rsqrt(jnp.mean(x * x, axis=-1, keepdims=True) + 1e-6)
        v = x * inverse * gain
        rows = (v / (1.0 + jnp.exp(-v))).astype(BF16)
        hidden_ref[at, :] = rows
        return rows

    each_brick(rows_of, bricks, out_ref, stage)


def extract_body(x_ref, out_ref, stage):
    each_brick(lambda at: x_ref[at, :], x_ref.shape[0] // 512, out_ref, stage)


def start_padded(own_ref, cells, halo, bricks):
    zero = jnp.zeros((8, C), F32)

    def clear(k, _):
        for b in range(10):
            cells[k * 10 + b] = zero
        for side in range(2):
            for part in range(HB // 8):
                halo[side, k, part * 8 : part * 8 + 8, :] = zero
        return 0

    lax.fori_loop(0, bricks * 10, clear, 0)

    def fill(k, _):
        plane = (k // 8) * 10 + k % 8 + 1
        rows = own_ref[pl.ds(pl.multiple_of(k * 64, 64), 64), :].astype(F32)
        for b in range(8):
            cells[plane * 10 + b + 1] = rows[b * 8 : b * 8 + 8]
        return 0

    lax.fori_loop(0, bricks * 8, fill, 0)


def add_line(ref, index, line):
    ref[index] = ref[index] + line


def pick(flag, yes, no):
    if isinstance(flag, bool):
        return yes if flag else no
    return jnp.where(flag, yes, no)


def place(kind, e, keep, place_at, source_brick, brick, share, cells, halo):
    flags = [t == -1 for t in e]
    pads = [pick(f, 0, 9) for f in flags]
    facing = pick(flags[0], 64, 0)
    start = source_brick * ROWS

    def rows(at, size):
        got = share[place_at, pl.ds(pl.multiple_of(start + at, 16), size), :].astype(F32)
        return got if keep is None else jnp.where(keep, got, 0.0)

    def half(pair, axis):
        return pick(flags[axis], pair[8:], pair[:8])

    def line_b(at):
        plane = rows(at, 64)
        return pick(flags[1], plane[56:], plane[:8])

    def line_c(at):
        plane = rows(at, 64)
        ends = [
            pick(flags[2], plane[8 * b + 7 : 8 * b + 8], plane[8 * b : 8 * b + 1]) for b in range(8)
        ]
        return jnp.concatenate(ends, axis=0)

    def cell(at):
        line = line_b(at)
        return pick(flags[2], line[7:8], line[0:1])

    side = pick(flags[2], 0, 1)
    base = brick * 10

    def add_halo(at, line):
        halo[side, base + at, 8:16, :] = halo[side, base + at, 8:16, :] + line

    def add_cell(at, value):
        spot = pl.ds(pick(flags[1], 7, 16), 1)
        halo[side, base + at, spot, :] = halo[side, base + at, spot, :] + value

    if kind == (1, 0, 0):
        got = rows(facing, 64)
        first = (base + pads[0]) * 10 + 1
        for b in range(8):
            add_line(cells, first + b, got[b * 8 : b * 8 + 8])
    elif kind == (0, 1, 0):
        for a in range(8):
            if a in (0, 7):
                line = line_b(0 if a == 0 else 64)
            else:
                line = half(rows(B_LINES - 16 + 16 * a, 16), 1)
            add_line(cells, (base + a + 1) * 10 + pads[1], line)
    elif kind == (0, 0, 1):
        for a in range(8):
            if a in (0, 7):
                line = line_c(0 if a == 0 else 64)
            else:
                line = half(rows(C_LINES - 16 + 16 * a, 16), 2)
            add_halo(a + 1, line)
    elif kind == (1, 1, 0):
        add_line(cells, (base + pads[0]) * 10 + pads[1], line_b(facing))
    elif kind == (1, 0, 1):
        add_halo(pads[0], line_c(facing))
    elif kind == (0, 1, 1):
        for a in range(8):
            if a in (0, 7):
                value = cell(0 if a == 0 else 64)
            else:
                line = half(rows(C_LINES - 16 + 16 * a, 16), 2)
                value = pick(flags[1], line[7:8], line[0:1])
            add_cell(a + 1, value)
    else:
        add_cell(pads[0], cell(facing))


def windows(cells, halo, cols, bricks):
    row = lax.broadcasted_iota(jnp.int32, (8, C), 0)

    def step(k, _):
        shifted = [[], [], []]
        for b in range(10):
            x = cells[k * 10 + b]
            before = halo[0, k, pl.ds(b + 7, 1), :]
            after = halo[1, k, pl.ds(b + 7, 1), :]
            shifted[0].append(jnp.where(row == 0, before, pltpu.roll(x, 1, 0)))
            shifted[1].append(x)
            shifted[2].append(jnp.where(row == 7, after, pltpu.roll(x, 7, 0)))
        for j in range(3):
            for l in range(3):
                block = jnp.concatenate(shifted[l][j : j + 8], axis=0).astype(BF16)
                at = (3 * j + l) * C
                cols[k, :, at : at + C] = block
        return 0

    lax.fori_loop(0, bricks * 10, step, 0)


def fetch(parts, share, sems, first=0, rows=None):
    lines = pl.ds(first, rows or parts[0].shape[1])
    copies = []
    place = 0
    for k, part in enumerate(parts):
        size = part.shape[0]
        to = share.at[pl.ds(place, size), lines]
        copies.append(pltpu.make_async_copy(part.at[:, lines], to, sems.at[k]))
        place += size
    for copy in copies:
        copy.start()
    return copies


def weight_grad_body(slots, factor, peers, count, *refs):
    recv, table, own_ref, cot_ref, x_ref, weight_ref = refs[:6]
    parts = refs[6 : 6 + count]
    keep_ref = refs[6 + count]
    give_refs = refs[7 + count : 7 + count + peers // 4]
    mix_ref, codes_ref, served_ref = refs[-16:-13]
    cells, halo, share, cols, sums, narrow, turned, weight, codes = refs[-13:-4]
    sems, codes_sem, out_sems, notes_sems = refs[-4:]
    bricks = own_ref.shape[0] // 512
    me = table[2 * peers]
    notes_copies = fetch(parts, share, notes_sems, bricks * ROWS, NOTES)
    copies = fetch(parts, share, sems, 0, bricks * ROWS)
    weight_copy = pltpu.make_async_copy(weight_ref, weight, codes_sem.at[1])
    weight_copy.start()
    for part in range(bricks * 2):
        at = slice(part * 256, part * 256 + 256)
        turned[:, at] = cot_ref[at, :].astype(F32).T.astype(BF16)
    for copy in notes_copies:
        copy.wait()
    for k in range(peers):
        notes = share[k, bricks * ROWS :, :].astype(F32).astype(jnp.int32)
        codes_ref[k : k + 1, :] = notes[0:1]
        served_ref[k : k + 1, :] = notes[1:2]
    codes_copy = pltpu.make_async_copy(codes_ref, codes, codes_sem.at[0])
    codes_copy.start()
    start_padded(own_ref, cells, halo, bricks)
    codes_copy.wait()
    for copy in copies:
        copy.wait()
    for brick in range(bricks):
        for number, e in enumerate(DIRECTIONS):
            slot = recv[brick, number]
            safe = jnp.maximum(slot, 0)
            sender = safe // slots
            at = table[sender]
            code = codes[at, me * slots + safe - sender * slots]
            kind = tuple(abs(t) for t in e)
            place(kind, e, slot >= 0, at, code // 6, brick, share, cells, halo)
    windows(cells, halo, cols, bricks)

    rows = 27 * C // peers
    for tap in range(27):
        i, jl = divmod(tap, 9)
        total = None
        for brick in range(bricks):
            right = cols[brick * 10 + i : brick * 10 + i + 8, :, jl * C : jl * C + C].reshape(512, C)
            left = turned[:, brick * 512 : brick * 512 + 512]
            term = jnp.dot(left, right, preferred_element_type=F32)
            total = term if total is None else total + term
        total = (total * factor).T
        start = tap * C
        while start < (tap + 1) * C:
            owner = start // rows
            stop = min((tap + 1) * C, (owner + 1) * rows)
            piece = total[start - tap * C : stop - tap * C]
            bucket = jnp.bitwise_xor(me % 2, owner % 2)
            behind = table[peers + owner // 2]
            where = slice(start - owner * rows, stop - owner * rows)
            sums[bucket, behind, where, :] = piece
            turn = table[peers + peers // 2 + owner // 2]
            narrow[bucket, turn, where, :] = piece.astype(BF16)
            start = stop

    out_copies = []
    for k in range(peers // 2):
        give_ref = give_refs[k // 2].at[k % 2]
        out_copies.append(pltpu.make_async_copy(narrow.at[1, k], give_ref, out_sems.at[1, k]))
    for k in range(peers // 2):
        out_copies.append(pltpu.make_async_copy(sums.at[0, k], keep_ref.at[k], out_sems.at[0, k]))
    for copy in out_copies:
        copy.start()
    weight_copy.wait()
    for brick in range(bricks):
        at = slice(brick * 512, brick * 512 + 512)
        total = None
        for i in range(3):
            left = cols[brick * 10 + i : brick * 10 + i + 8].reshape(512, 9 * C)
            right = weight[i * 9 * C : (i + 1) * 9 * C, :]
            term = jnp.dot(left, right, preferred_element_type=F32)
            total = term if total is None else total + term
        mix_ref[at, :] = (x_ref[at, :].astype(F32) + total).astype(BF16)
    for copy in out_copies:
        copy.wait()


def input_grad_body(slots, peers, count, *refs):
    served, send, table, cot_ref, x_ref, gain_ref, weight_ref = refs[:7]
    parts = refs[7 : 7 + count]
    out_ref, cells, halo, cols, share, weight, heads, more, sems, weight_sem = refs[7 + count :]
    bricks = cot_ref.shape[0] // 512
    me = table[2 * peers]
    copies = fetch(parts, share, sems)
    weight_copy = pltpu.make_async_copy(weight_ref, weight, weight_sem.at[0])
    weight_copy.start()

    def no_head(k, _):
        heads[k] = -1
        return 0

    lax.fori_loop(0, bricks * 26, no_head, 0)

    def source_of(k):
        receiver = k // slots
        at = table[receiver]
        return at, served[at, me * slots + k - receiver * slots] - 1

    def sort(k, found):
        _, entry = source_of(k)
        asked = entry >= 0
        key = send[0, k] // 6 * 26 + 25 - jnp.maximum(entry, 0) % 26
        first = asked & (heads[key] < 0)
        extra = asked & jnp.logical_not(first)

        @pl.when(first)
        def _():
            heads[key] = k

        @pl.when(extra)
        def _():
            more[found] = k

        return found + jnp.where(extra, 1, 0)

    found = lax.fori_loop(0, send.shape[1], sort, 0)
    start_padded(cot_ref, cells, halo, bricks)
    for copy in copies:
        copy.wait()
    for brick in range(bricks):
        for number, e in enumerate(DIRECTIONS):
            head = heads[brick * 26 + number]
            at, entry = source_of(jnp.maximum(head, 0))
            kind = tuple(abs(t) for t in e)
            source = jnp.maximum(entry, 0) // 26
            place(kind, e, head >= 0, at, source, brick, share, cells, halo)

    def one(n, _):
        k = more[n]
        at, entry = source_of(k)
        number = 25 - entry % 26
        tap = jnp.where(number >= 13, number + 1, number)
        e = (tap // 9 - 1, (tap // 3) % 3 - 1, tap % 3 - 1)
        on = [t != 0 for t in e]
        for kind in ((1, 0, 0), (0, 1, 0), (0, 0, 1), (1, 1, 0), (1, 0, 1), (0, 1, 1), (1, 1, 1)):
            match = functools.reduce(
                jnp.logical_and, [f if w else jnp.logical_not(f) for f, w in zip(on, kind)]
            )

            @pl.when(match)
            def _():
                place(kind, e, None, at, entry // 26, send[0, k] // 6, share, cells, halo)

        return 0

    lax.fori_loop(0, found, one, 0)
    windows(cells, halo, cols, bricks)
    weight_copy.wait()
    gain = gain_ref[...]
    for brick in range(bricks):
        rows = slice(brick * 512, brick * 512 + 512)
        grad = None
        for tap in range(27):
            i, jl = divmod(tap, 9)
            first = brick * 10 + i
            left = cols[first : first + 8, :, jl * C : jl * C + C].reshape(512, C)
            right = weight[(26 - tap) * C : (27 - tap) * C, :]
            term = lax.dot_general(left, right, (((1,), (1,)), ((), ())), preferred_element_type=F32)
            grad = term if grad is None else grad + term
        x = x_ref[rows, :].astype(F32)
        inverse = lax.rsqrt(jnp.mean(x * x, axis=-1, keepdims=True) + 1e-6)
        unit = x * inverse
        v = unit * gain
        gate = 1.0 / (1.0 + jnp.exp(-v))
        grad = grad * (gate * (1.0 + v * (1.0 - gate))) * gain
        grad = inverse * (grad - unit * jnp.mean(grad * unit, axis=-1, keepdims=True))
        out_ref[rows, :] = (cot_ref[rows, :].astype(F32) + grad).astype(BF16)


def local(features, norm_gain, conv_weight, recv_slot, send_face, cotangent):
    channels = features.shape[1]
    per_device = features.shape[0]
    bricks = per_device // 512
    peers = lax.axis_size("morton")
    slots = send_face.shape[1] // peers
    factor = 1.0 / math.sqrt(peers * per_device)
    gain = norm_gain.reshape(1, channels)
    sds = jax.ShapeDtypeStruct
    stage = pltpu.VMEM((8, 2, 64, 128), F32)

    def padded(n):
        return [
            pltpu.VMEM((n * 100, 8, channels), F32),
            pltpu.VMEM((2, n * 10, HB, channels), F32),
        ]

    def cols_shape(n):
        return (n * 10, 64, 9 * channels)


    table = jnp.asarray(ring_tables(peers))[lax.axis_index("morton")]

    hidden, share = call(
        norm_body,
        (sds((per_device, channels), BF16), sds((bricks * ROWS + NOTES, channels), BF16)),
        [SMEM, SMEM, VMEM, VMEM],
        [stage],
        name="norm",
    )(recv_slot, send_face, features, gain)
    hidden_ring = RingGather(share, peers)
    cot_share = call(
        extract_body,
        sds((bricks * ROWS, channels), BF16),
        [VMEM],
        [stage],
        name="extract",
    )(cotangent)
    hidden_ring.go(0)
    hidden_ring.go(1)
    hidden_ring.go(0, cot_share)
    hidden_ring.go(1)
    hidden_ring.go(0, table)
    hidden_ring.go(1)
    hidden_ring.go(0)
    hidden_parts = hidden_ring.places()
    cot_ring = RingGather(cot_share, peers)
    cot_ring.go(0, hidden_ring.last(1))
    cot_ring.go(1, hidden_ring.last(0))

    count = len(hidden_parts)
    rows = 27 * channels // peers
    chips = peers // 2
    weight_scratch = pltpu.VMEM((27 * channels, channels), BF16)
    keep, *give, mixed, _, served = call(
        functools.partial(weight_grad_body, slots, factor, peers, count),
        (
            sds((chips, rows, channels), F32),
            *[sds((2, rows, channels), BF16)] * (chips // 2),
            sds((per_device, channels), BF16),
            sds((peers, channels), jnp.int32),
            sds((peers, channels), jnp.int32),
        ),
        [SMEM] * 2 + [VMEM] * 3 + [HBM] * (1 + count),
        padded(bricks)
        + [
            pltpu.VMEM((peers, bricks * ROWS + NOTES, channels), BF16),
            pltpu.VMEM(cols_shape(bricks), BF16),
            pltpu.VMEM((2, chips, rows, channels), F32),
            pltpu.VMEM((2, chips, rows, channels), BF16),
            pltpu.VMEM((channels, per_device), BF16),
            weight_scratch,
            pltpu.SMEM((peers, channels), jnp.int32),
            pltpu.SemaphoreType.DMA((count,)),
            pltpu.SemaphoreType.DMA((2,)),
            pltpu.SemaphoreType.DMA((2, chips)),
            pltpu.SemaphoreType.DMA((count,)),
        ],
        cost=13,
        name="weight_grad",
        out_specs=(*[HBM] * (1 + chips // 2), VMEM, VMEM, VMEM),
    )(recv_slot, table, hidden, cotangent, features, conv_weight, *hidden_parts)

    first = (cot_ring.last(0), cot_ring.last(1), cot_ring.swap(0, 0))
    give = [lax.optimization_barrier((t, first))[0] for t in give]
    sums_ring = RingScatter(keep, give, peers)
    cot_ring.go(0, served)
    cot_ring.go(1, served)
    sums_ring.go()
    gate = (cot_ring.last(0), cot_ring.last(1))
    cot_ring.go(0)
    cot_ring.go(1)
    sums_ring.go(gate)
    gate = (cot_ring.last(0), cot_ring.last(1), cot_ring.swap(0, 1), cot_ring.swap(1, 1))
    cot_ring.go(0, cot_ring.last(1))
    sums_ring.go(gate)
    cot_ring.swap(0, 4, sums_ring.held[0])
    sent = sums_ring.go(tuple(cot_ring.swap(chain, hop) for chain in (0, 1) for hop in (2, 3)))
    cot_parts = cot_ring.places()
    served = lax.optimization_barrier((served, sent))[0]

    grad_features = call(
        functools.partial(input_grad_body, slots, peers, len(cot_parts)),
        sds((per_device, channels), BF16),
        [SMEM] * 3 + [VMEM] * 3 + [HBM] * (1 + len(cot_parts)),
        padded(bricks)
        + [
            pltpu.VMEM(cols_shape(bricks), BF16),
            pltpu.VMEM((peers, bricks * ROWS, channels), BF16),
            weight_scratch,
            pltpu.SMEM((bricks * 26,), jnp.int32),
            pltpu.SMEM((peers * slots,), jnp.int32),
            pltpu.SemaphoreType.DMA((len(cot_parts),)),
            pltpu.SemaphoreType.DMA((1,)),
        ],
        cost=13,
        name="input_grad",
    )(served, send_face, table, cotangent, features, gain, conv_weight, *cot_parts)
    for _ in range(chips // 2 - 4):
        sums_ring.go()
    return (mixed, grad_features, sums_ring.total(grad_features))


def solution(mesh):
    rows = P(("groups", "morton"), None)
    return jax.shard_map(
        local,
        mesh=mesh,
        in_specs=(rows, P(), P(), rows, rows, rows),
        out_specs=(rows, rows, rows),
        check_vma=False,
    )
```

```python
import functools
import math

import jax
import jax.numpy as jnp
import numpy as np
from jax import lax
from jax.experimental import pallas as pl
from jax.experimental.pallas import tpu as pltpu
from jax.sharding import PartitionSpec as P

F32 = jnp.float32
BF16 = jnp.bfloat16
C = 256
C_LINES = 128
B_LINES = 224
ROWS = 320
NOTES = 16
HB = 24
VMEM_LIMIT = 56 * 1024 * 1024
DIRECTIONS = [
    (i, j, l)
    for i in (-1, 0, 1)
    for j in (-1, 0, 1)
    for l in (-1, 0, 1)
    if (i, j, l) != (0, 0, 0)
]

VMEM = pl.BlockSpec(memory_space=pltpu.VMEM)
SMEM = pl.BlockSpec(memory_space=pltpu.SMEM)
ANY = pl.BlockSpec(memory_space=pl.ANY)
HBM = pl.BlockSpec(memory_space=pltpu.HBM)


def ring_order(chips):
    if chips == 8:
        return [0, 2, 4, 6, 7, 5, 3, 1]
    return list(range(chips))


def ring_tables(peers):
    chips = peers // 2
    spot = np.argsort(np.array(ring_order(chips)))
    device = np.arange(peers)
    behind = (spot[device // 2][:, None] - spot[None, :]) % chips
    half = chips // 2
    turn = np.where(behind >= half, 2 * (behind - half), 2 * (half - 1 - behind) + 1)
    place_of = np.broadcast_to(device, (peers, peers)).copy()
    if chips <= 8:
        for me in range(peers):
            for other in range(peers):
                away = behind[me, other // 2] if me % 2 == 0 else -behind[me, other // 2] % chips
                same = me % 2 == other % 2
                if away == 0:
                    place = 0 if same else 1
                elif away < half or (away == half and same):
                    place = 1 + away if same else 1 + half + away
                else:
                    away = chips - away
                    place = half + (away if not same else half + away) + half
                place_of[me, other] = place
    return np.concatenate([place_of, behind, turn, device[:, None]], axis=1).astype(np.int32)


def ring_step(x, peers, step, cross=0):
    order = ring_order(peers // 2)
    pairs = [
        (2 * order[i] + (core ^ cross), 2 * order[(i + (step or 1 - 2 * core)) % len(order)] + core)
        for i in range(len(order))
        for core in range(2)
    ]
    return lax.ppermute(x, "morton", pairs)


def swap_cores(x, peers):
    return lax.ppermute(x, "morton", [(m, m ^ 1) for m in range(peers)])


class RingGather:
    def __init__(self, x, peers):
        self.x, self.peers, self.chips = x, peers, peers // 2
        self.whole = None
        self.swaps = {}
        if self.chips > 8:
            self.whole = lax.all_gather(x[None], "morton", axis=0, tiled=True)
            return
        self.chains = ([x], [x])

    def go(self, chain, gate=None):
        if self.whole is not None or len(self.chains[chain]) > self.chips // 2 - chain:
            return
        held = self.chains[chain][-1]
        if gate is not None:
            held = lax.optimization_barrier((held, gate))[0]
        cross = int(chain == 1 and len(self.chains[chain]) == 1)
        self.chains[chain].append(ring_step(held, self.peers, 0, cross))

    def last(self, chain):
        return self.x if self.whole is not None else self.chains[chain][-1]

    def swap(self, chain, hop, gate=None):
        if self.whole is None and (chain, hop) not in self.swaps:
            held = self.chains[chain][hop]
            if gate is not None:
                held = lax.optimization_barrier((held, gate))[0]
            self.swaps[chain, hop] = swap_cores(held, self.peers)
        return self.swaps.get((chain, hop), self.x)

    def places(self):
        if self.whole is not None:
            return [self.whole]
        keys = [(c, h) for c in (0, 1) for h in range(1, len(self.chains[c]))]
        mine = [self.x, self.swap(0, 0)] + [self.chains[c][h] for c, h in keys]
        return [t[None] for t in mine + [self.swap(c, h) for c, h in keys]]


class RingScatter:
    def __init__(self, keep, give, peers):
        self.keep, self.peers, self.chips = keep, peers, peers // 2
        self.other = [swap_cores(t, peers) for t in give]
        self.held = [None, None]
        self.hop = 0

    def term(self, k):
        half = self.chips // 2
        pair = self.other[k - half][0] if k >= half else self.other[half - 1 - k][1]
        return self.keep[k] + pair.astype(F32)

    def go(self, gate=None):
        sent = []
        for way, step, count in ((0, 1, self.chips // 2), (1, -1, (self.chips - 1) // 2)):
            left = count - self.hop
            if left <= 0:
                continue
            part = self.term((-step * left) % self.chips)
            if self.held[way] is not None:
                part = part + self.held[way].astype(F32)
            part = part.astype(BF16)
            if gate is not None:
                part = lax.optimization_barrier((part, gate))[0]
            sent.append(part)
            self.held[way] = ring_step(part, self.peers, step)
        self.hop += 1
        return sent

    def total(self, gate):
        held = lax.optimization_barrier((*self.held, gate))[:2]
        return sum((t.astype(F32) for t in held), self.term(0))


def call(body, out_shape, in_specs, scratch=(), cost=2, name=None, out_specs=None, aliases=None):
    return pl.pallas_call(
        body,
        out_shape=out_shape,
        in_specs=in_specs,
        out_specs=out_specs or jax.tree.map(lambda _: VMEM, out_shape),
        scratch_shapes=list(scratch),
        input_output_aliases=aliases or {},
        compiler_params=pltpu.CompilerParams(vmem_limit_bytes=VMEM_LIMIT),
        cost_estimate=pl.CostEstimate(flops=cost * 10**9, bytes_accessed=0, transcendentals=0),
        name=name,
    )


PLANES = 4


def put_boundary(rows, base, a, out_ref, stage):
    wide = rows.astype(F32)

    def put(at, value, lanes=slice(None)):
        out_ref[pl.ds(pl.multiple_of(base + at, 16), value.shape[0]), lanes] = value

    if a in (0, 7):
        put(0 if a == 0 else 64, rows)
        return
    for half in range(2):
        lanes = slice(half * 128, half * 128 + 128)
        stage[half] = wide[:, lanes]
        first = stage[half, pl.ds(0, 8, stride=8), :]
        last = stage[half, pl.ds(7, 8, stride=8), :]
        put(C_LINES - 16 + 16 * a, jnp.concatenate([first, last], axis=0).astype(BF16), lanes)
    pair = jnp.concatenate([wide[:8], wide[56:]], axis=0).astype(BF16)
    put(B_LINES - 16 + 16 * a, pair)


def each_brick(rows_of, bricks, out_ref, stage):
    def step(brick, _):
        for first in range(0, 8, PLANES):
            at = pl.multiple_of(brick * 512 + first * 64, 64)
            rows = rows_of(pl.ds(at, PLANES * 64))
            for t in range(PLANES):
                plane = rows[t * 64 : t * 64 + 64]
                put_boundary(plane, brick * ROWS, first + t, out_ref, stage.at[first + t])
        return 0

    lax.fori_loop(0, bricks, step, 0)


def norm_body(recv, send, x_ref, gain_ref, hidden_ref, out_ref, stage):
    bricks, directions = recv.shape
    gain = gain_ref[...]
    lane = lax.broadcasted_iota(jnp.int32, (1, C), 1)
    codes = jnp.zeros((1, C), jnp.int32)
    for k in range(send.shape[1]):
        codes = jnp.where(lane == k, send[0, k], codes)
    served = jnp.zeros((1, C), jnp.int32)
    for brick in range(bricks):
        for number in range(directions):
            served = jnp.where(lane == recv[brick, number], brick * directions + number + 1, served)
    row = lax.broadcasted_iota(jnp.int32, (NOTES, C), 0)
    notes = jnp.where(row == 0, codes, jnp.where(row == 1, served, 0))
    out_ref[bricks * ROWS :, :] = notes.astype(F32).astype(BF16)

    def rows_of(at):
        x = x_ref[at, :].astype(F32)
        inverse = lax.rsqrt(jnp.mean(x * x, axis=-1, keepdims=True) + 1e-6)
        v = x * inverse * gain
        rows = (v / (1.0 + jnp.exp(-v))).astype(BF16)
        hidden_ref[at, :] = rows
        return rows

    each_brick(rows_of, bricks, out_ref, stage)


def extract_body(x_ref, out_ref, stage):
    each_brick(lambda at: x_ref[at, :], x_ref.shape[0] // 512, out_ref, stage)


def start_padded(own_ref, cells, halo, bricks):
    zero = jnp.zeros((8, C), F32)

    def clear(k, _):
        for b in range(10):
            cells[k * 10 + b] = zero
        for side in range(2):
            for part in range(HB // 8):
                halo[side, k, part * 8 : part * 8 + 8, :] = zero
        return 0

    lax.fori_loop(0, bricks * 10, clear, 0)

    def fill(k, _):
        plane = (k // 8) * 10 + k % 8 + 1
        rows = own_ref[pl.ds(pl.multiple_of(k * 64, 64), 64), :].astype(F32)
        for b in range(8):
            cells[plane * 10 + b + 1] = rows[b * 8 : b * 8 + 8]
        return 0

    lax.fori_loop(0, bricks * 8, fill, 0)


def add_line(ref, index, line):
    ref[index] = ref[index] + line


def pick(flag, yes, no):
    if isinstance(flag, bool):
        return yes if flag else no
    return jnp.where(flag, yes, no)


def place(kind, e, keep, place_at, source_brick, brick, share, cells, halo):
    flags = [t == -1 for t in e]
    pads = [pick(f, 0, 9) for f in flags]
    facing = pick(flags[0], 64, 0)
    start = source_brick * ROWS

    def rows(at, size):
        got = share[place_at, pl.ds(pl.multiple_of(start + at, 16), size), :].astype(F32)
        return got if keep is None else jnp.where(keep, got, 0.0)

    def half(pair, axis):
        return pick(flags[axis], pair[8:], pair[:8])

    def line_b(at):
        plane = rows(at, 64)
        return pick(flags[1], plane[56:], plane[:8])

    def line_c(at):
        plane = rows(at, 64)
        ends = [
            pick(flags[2], plane[8 * b + 7 : 8 * b + 8], plane[8 * b : 8 * b + 1]) for b in range(8)
        ]
        return jnp.concatenate(ends, axis=0)

    def cell(at):
        line = line_b(at)
        return pick(flags[2], line[7:8], line[0:1])

    side = pick(flags[2], 0, 1)
    base = brick * 10

    def add_halo(at, line):
        halo[side, base + at, 8:16, :] = halo[side, base + at, 8:16, :] + line

    def add_cell(at, value):
        spot = pl.ds(pick(flags[1], 7, 16), 1)
        halo[side, base + at, spot, :] = halo[side, base + at, spot, :] + value

    if kind == (1, 0, 0):
        got = rows(facing, 64)
        first = (base + pads[0]) * 10 + 1
        for b in range(8):
            add_line(cells, first + b, got[b * 8 : b * 8 + 8])
    elif kind == (0, 1, 0):
        for a in range(8):
            if a in (0, 7):
                line = line_b(0 if a == 0 else 64)
            else:
                line = half(rows(B_LINES - 16 + 16 * a, 16), 1)
            add_line(cells, (base + a + 1) * 10 + pads[1], line)
    elif kind == (0, 0, 1):
        for a in range(8):
            if a in (0, 7):
                line = line_c(0 if a == 0 else 64)
            else:
                line = half(rows(C_LINES - 16 + 16 * a, 16), 2)
            add_halo(a + 1, line)
    elif kind == (1, 1, 0):
        add_line(cells, (base + pads[0]) * 10 + pads[1], line_b(facing))
    elif kind == (1, 0, 1):
        add_halo(pads[0], line_c(facing))
    elif kind == (0, 1, 1):
        for a in range(8):
            if a in (0, 7):
                value = cell(0 if a == 0 else 64)
            else:
                line = half(rows(C_LINES - 16 + 16 * a, 16), 2)
                value = pick(flags[1], line[7:8], line[0:1])
            add_cell(a + 1, value)
    else:
        add_cell(pads[0], cell(facing))


def windows(cells, halo, cols, bricks, out=None, sems=None):
    row = lax.broadcasted_iota(jnp.int32, (8, C), 0)

    def step(k, _):
        shifted = [[], [], []]
        for b in range(10):
            x = cells[k * 10 + b]
            before = halo[0, k, pl.ds(b + 7, 1), :]
            after = halo[1, k, pl.ds(b + 7, 1), :]
            shifted[0].append(jnp.where(row == 0, before, pltpu.roll(x, 1, 0)))
            shifted[1].append(x)
            shifted[2].append(jnp.where(row == 7, after, pltpu.roll(x, 7, 0)))
        for j in range(3):
            for l in range(3):
                block = jnp.concatenate(shifted[l][j : j + 8], axis=0).astype(BF16)
                at = (3 * j + l) * C
                cols[k, :, at : at + C] = block
        if out is not None:
            pltpu.make_async_copy(cols.at[k], out.at[k], sems.at[k]).start()
        return 0

    lax.fori_loop(0, bricks * 10, step, 0)


def wait_windows(cols, out, sems, bricks):
    def step(k, _):
        pltpu.make_async_copy(cols.at[k], out.at[k], sems.at[k]).wait()
        return 0

    lax.fori_loop(0, bricks * 10, step, 0)


def fetch(parts, share, sems, first=0, rows=None):
    size = parts[0].shape[0]
    lines = pl.ds(first, rows or parts[0].shape[1])
    copies = [
        pltpu.make_async_copy(part.at[:, lines], share.at[pl.ds(k * size, size), lines], sems.at[k])
        for k, part in enumerate(parts)
    ]
    for copy in copies:
        copy.start()
    return copies


def weight_grad_body(slots, factor, peers, count, *refs):
    recv, table, own_ref, cot_ref = refs[:4]
    parts = refs[4 : 4 + count]
    keep_ref = refs[4 + count]
    give_refs = refs[5 + count : 5 + count + peers // 4]
    out_cols, codes_ref, served_ref = refs[-16:-13]
    cells, halo, share, cols, sums, narrow, turned, codes = refs[-13:-5]
    sems, cols_sems, codes_sem, out_sems, notes_sems = refs[-5:]
    bricks = own_ref.shape[0] // 512
    me = table[2 * peers]
    notes_copies = fetch(parts, share, notes_sems, bricks * ROWS, NOTES)
    copies = fetch(parts, share, sems, 0, bricks * ROWS)
    for part in range(bricks * 2):
        at = slice(part * 256, part * 256 + 256)
        turned[:, at] = cot_ref[at, :].astype(F32).T.astype(BF16)
    for copy in notes_copies:
        copy.wait()
    for k in range(peers):
        notes = share[k, bricks * ROWS :, :].astype(F32).astype(jnp.int32)
        codes_ref[k : k + 1, :] = notes[0:1]
        served_ref[k : k + 1, :] = notes[1:2]
    codes_copy = pltpu.make_async_copy(codes_ref, codes, codes_sem.at[0])
    codes_copy.start()
    start_padded(own_ref, cells, halo, bricks)
    codes_copy.wait()
    for copy in copies:
        copy.wait()
    for brick in range(bricks):
        for number, e in enumerate(DIRECTIONS):
            slot = recv[brick, number]
            safe = jnp.maximum(slot, 0)
            sender = safe // slots
            at = table[sender]
            code = codes[at, me * slots + safe - sender * slots]
            kind = tuple(abs(t) for t in e)
            place(kind, e, slot >= 0, at, code // 6, brick, share, cells, halo)
    windows(cells, halo, cols, bricks, out_cols, cols_sems)

    rows = 27 * C // peers
    for tap in range(27):
        i, jl = divmod(tap, 9)
        total = None
        for brick in range(bricks):
            right = cols[brick * 10 + i : brick * 10 + i + 8, :, jl * C : jl * C + C].reshape(512, C)
            left = turned[:, brick * 512 : brick * 512 + 512]
            term = jnp.dot(left, right, preferred_element_type=F32)
            total = term if total is None else total + term
        total = (total * factor).T
        start = tap * C
        while start < (tap + 1) * C:
            owner = start // rows
            stop = min((tap + 1) * C, (owner + 1) * rows)
            piece = total[start - tap * C : stop - tap * C]
            bucket = jnp.bitwise_xor(me % 2, owner % 2)
            behind = table[peers + owner // 2]
            where = slice(start - owner * rows, stop - owner * rows)
            sums[bucket, behind, where, :] = piece
            narrow[bucket, behind, where, :] = piece.astype(BF16)
            start = stop
            if stop == (owner + 1) * rows:

                @pl.when(bucket == 0)
                def _():
                    pltpu.make_async_copy(
                        sums.at[0, behind], keep_ref.at[behind], out_sems.at[0, behind]
                    ).start()

                turn = table[peers + peers // 2 + owner // 2]
                for hop, give_ref in enumerate(give_refs):

                    @pl.when((bucket == 1) & (turn // 2 == hop))
                    def _():
                        pltpu.make_async_copy(
                            narrow.at[1, behind], give_ref.at[turn % 2], out_sems.at[1, turn]
                        ).start()

    for k in range(peers // 2):
        pltpu.make_async_copy(sums.at[0, k], keep_ref.at[k], out_sems.at[0, k]).wait()
        pltpu.make_async_copy(narrow.at[1, k], give_refs[k // 2].at[k % 2], out_sems.at[1, k]).wait()
    wait_windows(cols, out_cols, cols_sems, bricks)


GROUP = 3 * C


def start_stream(cols_ref, first, cols, weight_ref, weight, sems):
    copies = []
    planes = cols.shape[0]
    for g in range(3):
        lanes = pl.ds(g * GROUP, GROUP)
        group = [
            pltpu.make_async_copy(
                cols_ref.at[pl.ds(first, planes), :, lanes], cols.at[:, :, lanes], sems.at[g, 3]
            )
        ]
        for i in range(3):
            at = pl.ds((i * 3 + g) * GROUP, GROUP)
            group.append(pltpu.make_async_copy(weight_ref.at[at], weight.at[at], sems.at[g, i]))
        copies.append(group)
    for group in copies:
        for copy in group:
            copy.start()
    return copies


def tap_sum(copies, cols, weight):
    bricks = cols.shape[0] // 10
    totals = [None] * bricks
    for g in range(3):
        for copy in copies[g]:
            copy.wait()
        for brick in range(bricks):
            for i in range(3):
                at = brick * 10 + i
                left = cols[at : at + 8, :, g * GROUP : g * GROUP + GROUP].reshape(512, GROUP)
                right = weight[(i * 3 + g) * GROUP : (i * 3 + g + 1) * GROUP, :]
                term = jnp.dot(left, right, preferred_element_type=F32)
                totals[brick] = term if totals[brick] is None else totals[brick] + term
    return totals


def mix_body(cols_ref, weight_ref, x_ref, out_ref, cols, weight, sems):
    copies = start_stream(cols_ref, 0, cols, weight_ref, weight, sems)
    for brick, total in enumerate(tap_sum(copies, cols, weight)):
        at = slice(brick * 512, brick * 512 + 512)
        out_ref[at, :] = (x_ref[at, :].astype(F32) + total).astype(BF16)


def input_grad_body(slots, peers, count, *refs):
    served, send, table, cot_ref, x_ref, gain_ref, weight_ref = refs[:7]
    parts = refs[7 : 7 + count]
    out_ref, cells, halo, cols, share, weight, heads, more, sems, weight_sem = refs[7 + count :]
    bricks = cot_ref.shape[0] // 512
    me = table[2 * peers]
    copies = fetch(parts, share, sems)
    weight_copy = pltpu.make_async_copy(weight_ref, weight, weight_sem.at[0])
    weight_copy.start()

    def no_head(k, _):
        heads[k] = -1
        return 0

    lax.fori_loop(0, bricks * 26, no_head, 0)

    def source_of(k):
        receiver = k // slots
        at = table[receiver]
        return at, served[at, me * slots + k - receiver * slots] - 1

    def sort(k, found):
        _, entry = source_of(k)
        asked = entry >= 0
        key = send[0, k] // 6 * 26 + 25 - jnp.maximum(entry, 0) % 26
        first = asked & (heads[key] < 0)
        extra = asked & jnp.logical_not(first)

        @pl.when(first)
        def _():
            heads[key] = k

        @pl.when(extra)
        def _():
            more[found] = k

        return found + jnp.where(extra, 1, 0)

    found = lax.fori_loop(0, send.shape[1], sort, 0)
    start_padded(cot_ref, cells, halo, bricks)
    for copy in copies:
        copy.wait()
    for brick in range(bricks):
        for number, e in enumerate(DIRECTIONS):
            head = heads[brick * 26 + number]
            at, entry = source_of(jnp.maximum(head, 0))
            kind = tuple(abs(t) for t in e)
            source = jnp.maximum(entry, 0) // 26
            place(kind, e, head >= 0, at, source, brick, share, cells, halo)

    def one(n, _):
        k = more[n]
        at, entry = source_of(k)
        number = 25 - entry % 26
        tap = jnp.where(number >= 13, number + 1, number)
        e = (tap // 9 - 1, (tap // 3) % 3 - 1, tap % 3 - 1)
        on = [t != 0 for t in e]
        for kind in ((1, 0, 0), (0, 1, 0), (0, 0, 1), (1, 1, 0), (1, 0, 1), (0, 1, 1), (1, 1, 1)):
            match = functools.reduce(
                jnp.logical_and, [f if w else jnp.logical_not(f) for f, w in zip(on, kind)]
            )

            @pl.when(match)
            def _():
                place(kind, e, None, at, entry // 26, send[0, k] // 6, share, cells, halo)

        return 0

    lax.fori_loop(0, found, one, 0)
    windows(cells, halo, cols, bricks)
    weight_copy.wait()
    gain = gain_ref[...]
    for brick in range(bricks):
        rows = slice(brick * 512, brick * 512 + 512)
        grad = None
        for tap in range(27):
            i, jl = divmod(tap, 9)
            first = brick * 10 + i
            left = cols[first : first + 8, :, jl * C : jl * C + C].reshape(512, C)
            right = weight[(26 - tap) * C : (27 - tap) * C, :]
            term = lax.dot_general(left, right, (((1,), (1,)), ((), ())), preferred_element_type=F32)
            grad = term if grad is None else grad + term
        x = x_ref[rows, :].astype(F32)
        inverse = lax.rsqrt(jnp.mean(x * x, axis=-1, keepdims=True) + 1e-6)
        unit = x * inverse
        v = unit * gain
        gate = 1.0 / (1.0 + jnp.exp(-v))
        grad = grad * (gate * (1.0 + v * (1.0 - gate))) * gain
        grad = inverse * (grad - unit * jnp.mean(grad * unit, axis=-1, keepdims=True))
        out_ref[rows, :] = (cot_ref[rows, :].astype(F32) + grad).astype(BF16)


def local(features, norm_gain, conv_weight, recv_slot, send_face, cotangent):
    channels = features.shape[1]
    per_device = features.shape[0]
    bricks = per_device // 512
    peers = lax.axis_size("morton")
    slots = send_face.shape[1] // peers
    factor = 1.0 / math.sqrt(peers * per_device)
    gain = norm_gain.reshape(1, channels)
    sds = jax.ShapeDtypeStruct
    stage = pltpu.VMEM((8, 2, 64, 128), F32)

    def padded(n):
        return [
            pltpu.VMEM((n * 100, 8, channels), F32),
            pltpu.VMEM((2, n * 10, HB, channels), F32),
        ]

    def cols_shape(n):
        return (n * 10, 64, 9 * channels)


    table = jnp.asarray(ring_tables(peers))[lax.axis_index("morton")]

    hidden, share = call(
        norm_body,
        (sds((per_device, channels), BF16), sds((bricks * ROWS + NOTES, channels), BF16)),
        [SMEM, SMEM, VMEM, VMEM],
        [stage],
        name="norm",
    )(recv_slot, send_face, features, gain)
    hidden_ring = RingGather(share, peers)
    cot_share = call(
        extract_body,
        sds((bricks * ROWS, channels), BF16),
        [VMEM],
        [stage],
        name="extract",
    )(cotangent)
    hidden_ring.go(0)
    hidden_ring.go(1)
    hidden_ring.go(0, cot_share)
    hidden_ring.go(1)
    hidden_ring.go(0, table)
    hidden_ring.go(1)
    hidden_ring.go(0)
    hidden_parts = hidden_ring.places()

    cot_ring = RingGather(cot_share, peers)
    cot_ring.go(0, hidden_ring.last(1))
    cot_ring.go(1, hidden_ring.last(0))

    count = len(hidden_parts)
    rows = 27 * channels // peers
    chips = peers // 2
    keep, *give, cols, _, served = call(
        functools.partial(weight_grad_body, slots, factor, peers, count),
        (
            sds((chips, rows, channels), F32),
            *[sds((2, rows, channels), BF16)] * (chips // 2),
            sds(cols_shape(bricks), BF16),
            sds((peers, channels), jnp.int32),
            sds((peers, channels), jnp.int32),
        ),
        [SMEM] * 2 + [VMEM] * 2 + [HBM] * count,
        padded(bricks)
        + [
            pltpu.VMEM((peers, bricks * ROWS + NOTES, channels), BF16),
            pltpu.VMEM(cols_shape(bricks), BF16),
            pltpu.VMEM((2, chips, rows, channels), F32),
            pltpu.VMEM((2, chips, rows, channels), BF16),
            pltpu.VMEM((channels, per_device), BF16),
            pltpu.SMEM((peers, channels), jnp.int32),
            pltpu.SemaphoreType.DMA((count,)),
            pltpu.SemaphoreType.DMA((bricks * 10,)),
            pltpu.SemaphoreType.DMA((1,)),
            pltpu.SemaphoreType.DMA((2, chips)),
            pltpu.SemaphoreType.DMA((count,)),
        ],
        cost=9,
        name="weight_grad",
        out_specs=(*[HBM] * (2 + chips // 2), VMEM, VMEM),
    )(recv_slot, table, hidden, cotangent, *hidden_parts)

    first = (cot_ring.last(0), cot_ring.last(1), cot_ring.swap(0, 0))
    give = [lax.optimization_barrier((t, first))[0] for t in give]
    sums_ring = RingScatter(keep, give, peers)
    sent = sums_ring.go()
    cot_ring.go(0, cols)
    cot_ring.go(1, cols)
    second = (cot_ring.last(0), cot_ring.last(1))
    mix_cols = lax.optimization_barrier((cols, sent))[0]
    weight_scratch = [
        pltpu.VMEM((27 * channels, channels), BF16),
        pltpu.SemaphoreType.DMA((3, 4)),
    ]
    mixed = call(
        mix_body,
        sds((per_device, channels), BF16),
        [HBM, HBM, VMEM],
        [pltpu.VMEM(cols_shape(bricks), BF16)] + weight_scratch,
        cost=6,
        name="mix",
    )(mix_cols, conv_weight, features)
    sums_ring.go((second, mixed))
    cot_ring.go(0)
    cot_ring.go(1)
    third = (cot_ring.last(0), cot_ring.last(1), cot_ring.swap(0, 1), cot_ring.swap(1, 1))
    cot_ring.go(0, cot_ring.last(1))
    sums_ring.go(third)
    cot_ring.swap(0, 4, sums_ring.held[0])
    sent = sums_ring.go(tuple(cot_ring.swap(chain, hop) for chain in (0, 1) for hop in (2, 3)))
    cot_parts = cot_ring.places()
    served = lax.optimization_barrier((served, sent))[0]

    grad_features = call(
        functools.partial(input_grad_body, slots, peers, count),
        sds((per_device, channels), BF16),
        [SMEM] * 3 + [VMEM] * 3 + [HBM] * (1 + count),
        padded(bricks)
        + [
            pltpu.VMEM(cols_shape(bricks), BF16),
            pltpu.VMEM((peers, bricks * ROWS, channels), BF16),
            weight_scratch[0],
            pltpu.SMEM((bricks * 26,), jnp.int32),
            pltpu.SMEM((peers * slots,), jnp.int32),
            pltpu.SemaphoreType.DMA((count,)),
            pltpu.SemaphoreType.DMA((1,)),
        ],
        cost=13,
        name="input_grad",
    )(served, send_face, table, cotangent, features, gain, conv_weight, *cot_parts)
    for _ in range(chips // 2 - 4):
        sums_ring.go()
    return (mixed, grad_features, sums_ring.total(grad_features))


def solution(mesh):
    rows = P(("groups", "morton"), None)
    return jax.shard_map(
        local,
        mesh=mesh,
        in_specs=(rows, P(), P(), rows, rows, rows),
        out_specs=(rows, rows, rows),
        check_vma=False,
    )
```

```python
import functools
import math

import jax
import jax.numpy as jnp
import numpy as np
from jax import lax
from jax.experimental import pallas as pl
from jax.experimental.pallas import tpu as pltpu
from jax.sharding import PartitionSpec as P

F32 = jnp.float32
BF16 = jnp.bfloat16
C = 256
C_LINES = 128
B_LINES = 224
ROWS = 320
NOTES = 16
HB = 24
VMEM_LIMIT = 56 * 1024 * 1024
DIRECTIONS = [
    (i, j, l)
    for i in (-1, 0, 1)
    for j in (-1, 0, 1)
    for l in (-1, 0, 1)
    if (i, j, l) != (0, 0, 0)
]

VMEM = pl.BlockSpec(memory_space=pltpu.VMEM)
SMEM = pl.BlockSpec(memory_space=pltpu.SMEM)
ANY = pl.BlockSpec(memory_space=pl.ANY)
HBM = pl.BlockSpec(memory_space=pltpu.HBM)


def ring_order(chips):
    if chips == 8:
        return [0, 2, 4, 6, 7, 5, 3, 1]
    return list(range(chips))


def ring_tables(peers):
    chips = peers // 2
    spot = np.argsort(np.array(ring_order(chips)))
    device = np.arange(peers)
    behind = (spot[device // 2][:, None] - spot[None, :]) % chips
    half = chips // 2
    turn = np.where(behind >= half, 2 * (behind - half), 2 * (half - 1 - behind) + 1)
    place_of = np.broadcast_to(device, (peers, peers)).copy()
    if chips <= 8:
        for me in range(peers):
            for other in range(peers):
                away = behind[me, other // 2] if me % 2 == 0 else -behind[me, other // 2] % chips
                same = me % 2 == other % 2
                if away == 0:
                    place = 0 if same else 1
                elif away < half or (away == half and same):
                    place = 1 + away if same else 1 + half + away
                else:
                    place = 3 * half + chips - away if same else 2 * half + chips - away
                place_of[me, other] = place
    return np.concatenate([place_of, behind, turn, device[:, None]], axis=1).astype(np.int32)


def ring_step(x, peers, step, cross=0, reach=1):
    order = ring_order(peers // 2)
    chips = len(order)
    pairs = [
        (2 * order[i] + (core ^ cross), 2 * order[(i + reach * (step or 1 - 2 * core)) % chips] + core)
        for i in range(len(order))
        for core in range(2)
    ]
    return lax.ppermute(x, "morton", pairs)


def swap_cores(x, peers):
    return lax.ppermute(x, "morton", [(m, m ^ 1) for m in range(peers)])


class RingGather:
    def __init__(self, x, peers):
        self.x, self.peers, self.chips = x, peers, peers // 2
        self.whole = None
        self.swaps = {}
        if self.chips > 8:
            self.whole = lax.all_gather(x[None], "morton", axis=0, tiled=True)
            return
        self.chains = ([x], [x])

    def go(self, chain, gate=None):
        if self.whole is not None or len(self.chains[chain]) > self.chips // 2 - chain:
            return
        held = self.chains[chain][-1]
        if gate is not None:
            held = lax.optimization_barrier((held, gate))[0]
        cross = int(chain == 1 and len(self.chains[chain]) == 1)
        self.chains[chain].append(ring_step(held, self.peers, 0, cross))

    def go_far(self, chain):
        if self.whole is None and len(self.chains[chain]) == 2 <= self.chips // 2 - chain:
            self.chains[chain].append(ring_step(self.x, self.peers, 0, chain, 2))

    def last(self, chain):
        return self.x if self.whole is not None else self.chains[chain][-1]

    def swap(self, chain, hop, gate=None):
        if self.whole is None and (chain, hop) not in self.swaps:
            held = self.chains[chain][hop]
            if gate is not None:
                held = lax.optimization_barrier((held, gate))[0]
            self.swaps[chain, hop] = swap_cores(held, self.peers)
        return self.swaps.get((chain, hop), self.x)

    def places(self):
        if self.whole is not None:
            return [self.whole]
        keys = [(c, h) for c in (0, 1) for h in range(1, len(self.chains[c]))]
        mine = [self.x, self.swap(0, 0)] + [self.chains[c][h] for c, h in keys]
        return [t[None] for t in mine + [self.swap(c, h) for c, h in keys]]


class RingScatter:
    def __init__(self, keep, give, peers):
        self.keep, self.peers, self.chips = keep, peers, peers // 2
        self.other = [swap_cores(t, peers) for t in give]
        self.held = [None, None]
        self.hop = 0

    def term(self, k):
        half = self.chips // 2
        pair = self.other[k - half][0] if k >= half else self.other[half - 1 - k][1]
        return self.keep[k] + pair.astype(F32)

    def go(self, gate=None):
        sent = []
        for way, step, count in ((0, 1, self.chips // 2), (1, -1, (self.chips - 1) // 2)):
            left = count - self.hop
            if left <= 0:
                continue
            part = self.term((-step * left) % self.chips)
            if self.held[way] is not None:
                part = part + self.held[way].astype(F32)
            part = part.astype(BF16)
            if gate is not None:
                part = lax.optimization_barrier((part, gate))[0]
            sent.append(part)
            self.held[way] = ring_step(part, self.peers, step)
        self.hop += 1
        return sent

    def total(self, gate):
        held = lax.optimization_barrier((*self.held, gate))[:2]
        return sum((t.astype(F32) for t in held), self.term(0))


def call(body, out_shape, in_specs, scratch=(), cost=2, name=None, out_specs=None, aliases=None):
    return pl.pallas_call(
        body,
        out_shape=out_shape,
        in_specs=in_specs,
        out_specs=out_specs or jax.tree.map(lambda _: VMEM, out_shape),
        scratch_shapes=list(scratch),
        input_output_aliases=aliases or {},
        compiler_params=pltpu.CompilerParams(vmem_limit_bytes=VMEM_LIMIT),
        cost_estimate=pl.CostEstimate(flops=cost * 10**9, bytes_accessed=0, transcendentals=0),
        name=name,
    )


PLANES = 4


def put_boundary(rows, base, a, out_ref, stage):
    wide = rows.astype(F32)

    def put(at, value, lanes=slice(None)):
        out_ref[pl.ds(pl.multiple_of(base + at, 16), value.shape[0]), lanes] = value

    if a in (0, 7):
        put(0 if a == 0 else 64, rows)
        return
    for half in range(2):
        lanes = slice(half * 128, half * 128 + 128)
        stage[half] = wide[:, lanes]
        first = stage[half, pl.ds(0, 8, stride=8), :]
        last = stage[half, pl.ds(7, 8, stride=8), :]
        put(C_LINES - 16 + 16 * a, jnp.concatenate([first, last], axis=0).astype(BF16), lanes)
    pair = jnp.concatenate([wide[:8], wide[56:]], axis=0).astype(BF16)
    put(B_LINES - 16 + 16 * a, pair)


def each_brick(rows_of, bricks, out_ref, stage):
    def step(brick, _):
        for first in range(0, 8, PLANES):
            at = pl.multiple_of(brick * 512 + first * 64, 64)
            rows = rows_of(pl.ds(at, PLANES * 64))
            for t in range(PLANES):
                plane = rows[t * 64 : t * 64 + 64]
                put_boundary(plane, brick * ROWS, first + t, out_ref, stage.at[first + t])
        return 0

    lax.fori_loop(0, bricks, step, 0)


def norm_body(recv, send, x_ref, gain_ref, hidden_ref, out_ref, stage):
    bricks, directions = recv.shape
    gain = gain_ref[...]
    lane = lax.broadcasted_iota(jnp.int32, (1, C), 1)
    codes = jnp.zeros((1, C), jnp.int32)
    for k in range(send.shape[1]):
        codes = jnp.where(lane == k, send[0, k], codes)
    served = jnp.zeros((1, C), jnp.int32)
    for brick in range(bricks):
        for number in range(directions):
            served = jnp.where(lane == recv[brick, number], brick * directions + number + 1, served)
    row = lax.broadcasted_iota(jnp.int32, (NOTES, C), 0)
    notes = jnp.where(row == 0, codes, jnp.where(row == 1, served, 0))
    out_ref[bricks * ROWS :, :] = notes.astype(F32).astype(BF16)

    def rows_of(at):
        x = x_ref[at, :].astype(F32)
        inverse = lax.rsqrt(jnp.mean(x * x, axis=-1, keepdims=True) + 1e-6)
        v = x * inverse * gain
        rows = (v / (1.0 + jnp.exp(-v))).astype(BF16)
        hidden_ref[at, :] = rows
        return rows

    each_brick(rows_of, bricks, out_ref, stage)


def extract_body(x_ref, out_ref, stage):
    each_brick(lambda at: x_ref[at, :], x_ref.shape[0] // 512, out_ref, stage)


def start_padded(own_ref, cells, halo, bricks):
    zero = jnp.zeros((8, C), F32)

    def clear(k, _):
        for b in range(10):
            cells[k * 10 + b] = zero
        for side in range(2):
            for part in range(HB // 8):
                halo[side, k, part * 8 : part * 8 + 8, :] = zero
        return 0

    lax.fori_loop(0, bricks * 10, clear, 0)

    def fill(k, _):
        plane = (k // 8) * 10 + k % 8 + 1
        rows = own_ref[pl.ds(pl.multiple_of(k * 64, 64), 64), :].astype(F32)
        for b in range(8):
            cells[plane * 10 + b + 1] = rows[b * 8 : b * 8 + 8]
        return 0

    lax.fori_loop(0, bricks * 8, fill, 0)


def add_line(ref, index, line):
    ref[index] = ref[index] + line


def pick(flag, yes, no):
    if isinstance(flag, bool):
        return yes if flag else no
    return jnp.where(flag, yes, no)


def place(kind, e, keep, place_at, source_brick, brick, share, cells, halo):
    flags = [t == -1 for t in e]
    pads = [pick(f, 0, 9) for f in flags]
    facing = pick(flags[0], 64, 0)
    start = source_brick * ROWS

    def rows(at, size):
        got = share[place_at, pl.ds(pl.multiple_of(start + at, 16), size), :].astype(F32)
        return got if keep is None else jnp.where(keep, got, 0.0)

    def half(pair, axis):
        return pick(flags[axis], pair[8:], pair[:8])

    def line_b(at):
        plane = rows(at, 64)
        return pick(flags[1], plane[56:], plane[:8])

    def line_c(at):
        plane = rows(at, 64)
        ends = [
            pick(flags[2], plane[8 * b + 7 : 8 * b + 8], plane[8 * b : 8 * b + 1]) for b in range(8)
        ]
        return jnp.concatenate(ends, axis=0)

    def cell(at):
        line = line_b(at)
        return pick(flags[2], line[7:8], line[0:1])

    side = pick(flags[2], 0, 1)
    base = brick * 10

    def add_halo(at, line):
        halo[side, base + at, 8:16, :] = halo[side, base + at, 8:16, :] + line

    def add_cell(at, value):
        spot = pl.ds(pick(flags[1], 7, 16), 1)
        halo[side, base + at, spot, :] = halo[side, base + at, spot, :] + value

    if kind == (1, 0, 0):
        got = rows(facing, 64)
        first = (base + pads[0]) * 10 + 1
        for b in range(8):
            add_line(cells, first + b, got[b * 8 : b * 8 + 8])
    elif kind == (0, 1, 0):
        for a in range(8):
            if a in (0, 7):
                line = line_b(0 if a == 0 else 64)
            else:
                line = half(rows(B_LINES - 16 + 16 * a, 16), 1)
            add_line(cells, (base + a + 1) * 10 + pads[1], line)
    elif kind == (0, 0, 1):
        for a in range(8):
            if a in (0, 7):
                line = line_c(0 if a == 0 else 64)
            else:
                line = half(rows(C_LINES - 16 + 16 * a, 16), 2)
            add_halo(a + 1, line)
    elif kind == (1, 1, 0):
        add_line(cells, (base + pads[0]) * 10 + pads[1], line_b(facing))
    elif kind == (1, 0, 1):
        add_halo(pads[0], line_c(facing))
    elif kind == (0, 1, 1):
        for a in range(8):
            if a in (0, 7):
                value = cell(0 if a == 0 else 64)
            else:
                line = half(rows(C_LINES - 16 + 16 * a, 16), 2)
                value = pick(flags[1], line[7:8], line[0:1])
            add_cell(a + 1, value)
    else:
        add_cell(pads[0], cell(facing))


def windows(cells, halo, cols, bricks):
    row = lax.broadcasted_iota(jnp.int32, (8, C), 0)

    def step(k, _):
        shifted = [[], [], []]
        for b in range(10):
            x = cells[k * 10 + b]
            before = halo[0, k, pl.ds(b + 7, 1), :]
            after = halo[1, k, pl.ds(b + 7, 1), :]
            shifted[0].append(jnp.where(row == 0, before, pltpu.roll(x, 1, 0)))
            shifted[1].append(x)
            shifted[2].append(jnp.where(row == 7, after, pltpu.roll(x, 7, 0)))
        for j in range(3):
            for l in range(3):
                block = jnp.concatenate(shifted[l][j : j + 8], axis=0).astype(BF16)
                at = (3 * j + l) * C
                cols[k, :, at : at + C] = block
        return 0

    lax.fori_loop(0, bricks * 10, step, 0)


def fetch(parts, share, sems, first=0, rows=None):
    lines = pl.ds(first, rows or parts[0].shape[1])
    copies = []
    place = 0
    for k, part in enumerate(parts):
        size = part.shape[0]
        to = share.at[pl.ds(place, size), lines]
        copies.append(pltpu.make_async_copy(part.at[:, lines], to, sems.at[k]))
        place += size
    for copy in copies:
        copy.start()
    return copies


def weight_grad_body(slots, factor, peers, count, *refs):
    recv, table, own_ref, cot_ref, x_ref, weight_ref = refs[:6]
    parts = refs[6 : 6 + count]
    keep_ref = refs[6 + count]
    give_refs = refs[7 + count : 7 + count + peers // 4]
    mix_ref, codes_ref, served_ref = refs[-16:-13]
    cells, halo, share, cols, sums, narrow, turned, weight, codes = refs[-13:-4]
    sems, codes_sem, out_sems, notes_sems = refs[-4:]
    bricks = own_ref.shape[0] // 512
    me = table[2 * peers]
    notes_copies = fetch(parts, share, notes_sems, bricks * ROWS, NOTES)
    copies = fetch(parts, share, sems, 0, bricks * ROWS)
    weight_copy = pltpu.make_async_copy(weight_ref, weight, codes_sem.at[1])
    weight_copy.start()
    for part in range(bricks * 2):
        at = slice(part * 256, part * 256 + 256)
        turned[:, at] = cot_ref[at, :].astype(F32).T.astype(BF16)
    for copy in notes_copies:
        copy.wait()
    for k in range(peers):
        notes = share[k, bricks * ROWS :, :].astype(F32).astype(jnp.int32)
        codes_ref[k : k + 1, :] = notes[0:1]
        served_ref[k : k + 1, :] = notes[1:2]
    codes_copy = pltpu.make_async_copy(codes_ref, codes, codes_sem.at[0])
    codes_copy.start()
    start_padded(own_ref, cells, halo, bricks)
    codes_copy.wait()
    for copy in copies:
        copy.wait()
    for brick in range(bricks):
        for number, e in enumerate(DIRECTIONS):
            slot = recv[brick, number]
            safe = jnp.maximum(slot, 0)
            sender = safe // slots
            at = table[sender]
            code = codes[at, me * slots + safe - sender * slots]
            kind = tuple(abs(t) for t in e)
            place(kind, e, slot >= 0, at, code // 6, brick, share, cells, halo)
    windows(cells, halo, cols, bricks)

    rows = 27 * C // peers
    for tap in range(27):
        i, jl = divmod(tap, 9)
        total = None
        for brick in range(bricks):
            right = cols[brick * 10 + i : brick * 10 + i + 8, :, jl * C : jl * C + C].reshape(512, C)
            left = turned[:, brick * 512 : brick * 512 + 512]
            term = jnp.dot(left, right, preferred_element_type=F32)
            total = term if total is None else total + term
        total = (total * factor).T
        start = tap * C
        while start < (tap + 1) * C:
            owner = start // rows
            stop = min((tap + 1) * C, (owner + 1) * rows)
            piece = total[start - tap * C : stop - tap * C]
            bucket = jnp.bitwise_xor(me % 2, owner % 2)
            behind = table[peers + owner // 2]
            where = slice(start - owner * rows, stop - owner * rows)
            sums[bucket, behind, where, :] = piece
            turn = table[peers + peers // 2 + owner // 2]
            narrow[bucket, turn, where, :] = piece.astype(BF16)
            start = stop

    out_copies = []
    for k in range(peers // 2):
        give_ref = give_refs[k // 2].at[k % 2]
        out_copies.append(pltpu.make_async_copy(narrow.at[1, k], give_ref, out_sems.at[1, k]))
    for k in range(peers // 2):
        out_copies.append(pltpu.make_async_copy(sums.at[0, k], keep_ref.at[k], out_sems.at[0, k]))
    for copy in out_copies:
        copy.start()
    weight_copy.wait()
    for brick in range(bricks):
        at = slice(brick * 512, brick * 512 + 512)
        total = None
        for i in range(3):
            left = cols[brick * 10 + i : brick * 10 + i + 8].reshape(512, 9 * C)
            right = weight[i * 9 * C : (i + 1) * 9 * C, :]
            term = jnp.dot(left, right, preferred_element_type=F32)
            total = term if total is None else total + term
        mix_ref[at, :] = (x_ref[at, :].astype(F32) + total).astype(BF16)
    for copy in out_copies:
        copy.wait()


def input_grad_body(slots, peers, count, *refs):
    served, send, table, cot_ref, x_ref, gain_ref, weight_ref = refs[:7]
    parts = refs[7 : 7 + count]
    out_ref, cells, halo, cols, share, weight, heads, more, sems, weight_sem = refs[7 + count :]
    bricks = cot_ref.shape[0] // 512
    me = table[2 * peers]
    copies = fetch(parts, share, sems)
    weight_copy = pltpu.make_async_copy(weight_ref, weight, weight_sem.at[0])
    weight_copy.start()

    def no_head(k, _):
        heads[k] = -1
        return 0

    lax.fori_loop(0, bricks * 26, no_head, 0)

    def source_of(k):
        receiver = k // slots
        at = table[receiver]
        return at, served[at, me * slots + k - receiver * slots] - 1

    def sort(k, found):
        _, entry = source_of(k)
        asked = entry >= 0
        key = send[0, k] // 6 * 26 + 25 - jnp.maximum(entry, 0) % 26
        first = asked & (heads[key] < 0)
        extra = asked & jnp.logical_not(first)

        @pl.when(first)
        def _():
            heads[key] = k

        @pl.when(extra)
        def _():
            more[found] = k

        return found + jnp.where(extra, 1, 0)

    found = lax.fori_loop(0, send.shape[1], sort, 0)
    start_padded(cot_ref, cells, halo, bricks)
    for copy in copies:
        copy.wait()
    for brick in range(bricks):
        for number, e in enumerate(DIRECTIONS):
            head = heads[brick * 26 + number]
            at, entry = source_of(jnp.maximum(head, 0))
            kind = tuple(abs(t) for t in e)
            source = jnp.maximum(entry, 0) // 26
            place(kind, e, head >= 0, at, source, brick, share, cells, halo)

    def one(n, _):
        k = more[n]
        at, entry = source_of(k)
        number = 25 - entry % 26
        tap = jnp.where(number >= 13, number + 1, number)
        e = (tap // 9 - 1, (tap // 3) % 3 - 1, tap % 3 - 1)
        on = [t != 0 for t in e]
        for kind in ((1, 0, 0), (0, 1, 0), (0, 0, 1), (1, 1, 0), (1, 0, 1), (0, 1, 1), (1, 1, 1)):
            match = functools.reduce(
                jnp.logical_and, [f if w else jnp.logical_not(f) for f, w in zip(on, kind)]
            )

            @pl.when(match)
            def _():
                place(kind, e, None, at, entry // 26, send[0, k] // 6, share, cells, halo)

        return 0

    lax.fori_loop(0, found, one, 0)
    windows(cells, halo, cols, bricks)
    weight_copy.wait()
    gain = gain_ref[...]
    for brick in range(bricks):
        rows = slice(brick * 512, brick * 512 + 512)
        grad = None
        for tap in range(27):
            i, jl = divmod(tap, 9)
            first = brick * 10 + i
            left = cols[first : first + 8, :, jl * C : jl * C + C].reshape(512, C)
            right = weight[(26 - tap) * C : (27 - tap) * C, :]
            term = lax.dot_general(left, right, (((1,), (1,)), ((), ())), preferred_element_type=F32)
            grad = term if grad is None else grad + term
        x = x_ref[rows, :].astype(F32)
        inverse = lax.rsqrt(jnp.mean(x * x, axis=-1, keepdims=True) + 1e-6)
        unit = x * inverse
        v = unit * gain
        gate = 1.0 / (1.0 + jnp.exp(-v))
        grad = grad * (gate * (1.0 + v * (1.0 - gate))) * gain
        grad = inverse * (grad - unit * jnp.mean(grad * unit, axis=-1, keepdims=True))
        out_ref[rows, :] = (cot_ref[rows, :].astype(F32) + grad).astype(BF16)


def local(features, norm_gain, conv_weight, recv_slot, send_face, cotangent):
    channels = features.shape[1]
    per_device = features.shape[0]
    bricks = per_device // 512
    peers = lax.axis_size("morton")
    slots = send_face.shape[1] // peers
    factor = 1.0 / math.sqrt(peers * per_device)
    gain = norm_gain.reshape(1, channels)
    sds = jax.ShapeDtypeStruct
    stage = pltpu.VMEM((8, 2, 64, 128), F32)

    def padded(n):
        return [
            pltpu.VMEM((n * 100, 8, channels), F32),
            pltpu.VMEM((2, n * 10, HB, channels), F32),
        ]

    def cols_shape(n):
        return (n * 10, 64, 9 * channels)


    table = jnp.asarray(ring_tables(peers))[lax.axis_index("morton")]

    hidden, share = call(
        norm_body,
        (sds((per_device, channels), BF16), sds((bricks * ROWS + NOTES, channels), BF16)),
        [SMEM, SMEM, VMEM, VMEM],
        [stage],
        name="norm",
    )(recv_slot, send_face, features, gain)
    hidden_ring = RingGather(share, peers)
    cot_share = call(
        extract_body,
        sds((bricks * ROWS, channels), BF16),
        [VMEM],
        [stage],
        name="extract",
    )(cotangent)
    hidden_ring.go(0)
    hidden_ring.go(1)
    hidden_ring.go(0, cot_share)
    hidden_ring.go(1)
    hidden_ring.go(0, table)
    hidden_ring.go(1)
    hidden_ring.go(0)
    hidden_parts = hidden_ring.places()
    cot_ring = RingGather(cot_share, peers)
    cot_ring.go(0, hidden_ring.last(1))
    cot_ring.go(1, hidden_ring.last(0))
    cot_ring.go_far(0)
    cot_ring.go_far(1)

    count = len(hidden_parts)
    rows = 27 * channels // peers
    chips = peers // 2
    weight_scratch = pltpu.VMEM((27 * channels, channels), BF16)
    keep, *give, mixed, _, served = call(
        functools.partial(weight_grad_body, slots, factor, peers, count),
        (
            sds((chips, rows, channels), F32),
            *[sds((2, rows, channels), BF16)] * (chips // 2),
            sds((per_device, channels), BF16),
            sds((peers, channels), jnp.int32),
            sds((peers, channels), jnp.int32),
        ),
        [SMEM] * 2 + [VMEM] * 3 + [HBM] * (1 + count),
        padded(bricks)
        + [
            pltpu.VMEM((peers, bricks * ROWS + NOTES, channels), BF16),
            pltpu.VMEM(cols_shape(bricks), BF16),
            pltpu.VMEM((2, chips, rows, channels), F32),
            pltpu.VMEM((2, chips, rows, channels), BF16),
            pltpu.VMEM((channels, per_device), BF16),
            weight_scratch,
            pltpu.SMEM((peers, channels), jnp.int32),
            pltpu.SemaphoreType.DMA((count,)),
            pltpu.SemaphoreType.DMA((2,)),
            pltpu.SemaphoreType.DMA((2, chips)),
            pltpu.SemaphoreType.DMA((count,)),
        ],
        cost=13,
        name="weight_grad",
        out_specs=(*[HBM] * (1 + chips // 2), VMEM, VMEM, VMEM),
    )(recv_slot, table, hidden, cotangent, features, conv_weight, *hidden_parts)

    first = [t for chain in (0, 1) for t in cot_ring.chains[chain][1:]] if cot_ring.whole is None else []
    give = [lax.optimization_barrier((t, cot_ring.swap(0, 0), *first))[0] for t in give]
    sums_ring = RingScatter(keep, give, peers)
    cot_ring.go(0, served)
    cot_ring.go(1, served)
    sums_ring.go()
    gate = (cot_ring.last(0), cot_ring.last(1))
    cot_ring.go(0, cot_ring.last(1))
    sums_ring.go(gate)
    cot_ring.swap(0, 4, sums_ring.held[0])
    sums_ring.go(tuple(cot_ring.swap(chain, hop) for chain in (0, 1) for hop in (1, 2)))
    sent = sums_ring.go((cot_ring.swap(0, 3), cot_ring.swap(1, 3)))
    cot_parts = cot_ring.places()
    served = lax.optimization_barrier((served, sent))[0]

    grad_features = call(
        functools.partial(input_grad_body, slots, peers, len(cot_parts)),
        sds((per_device, channels), BF16),
        [SMEM] * 3 + [VMEM] * 3 + [HBM] * (1 + len(cot_parts)),
        padded(bricks)
        + [
            pltpu.VMEM(cols_shape(bricks), BF16),
            pltpu.VMEM((peers, bricks * ROWS, channels), BF16),
            weight_scratch,
            pltpu.SMEM((bricks * 26,), jnp.int32),
            pltpu.SMEM((peers * slots,), jnp.int32),
            pltpu.SemaphoreType.DMA((len(cot_parts),)),
            pltpu.SemaphoreType.DMA((1,)),
        ],
        cost=13,
        name="input_grad",
    )(served, send_face, table, cotangent, features, gain, conv_weight, *cot_parts)
    for _ in range(chips // 2 - 4):
        sums_ring.go()
    return (mixed, grad_features, sums_ring.total(grad_features))


def solution(mesh):
    rows = P(("groups", "morton"), None)
    return jax.shard_map(
        local,
        mesh=mesh,
        in_specs=(rows, P(), P(), rows, rows, rows),
        out_specs=(rows, rows, rows),
        check_vma=False,
    )
```

```python
import functools
import math

import jax
import jax.numpy as jnp
import numpy as np
from jax import lax
from jax.experimental import pallas as pl
from jax.experimental.pallas import tpu as pltpu
from jax.sharding import PartitionSpec as P

F32 = jnp.float32
BF16 = jnp.bfloat16
C = 256
B_LINES = 128
ROWS = 224
C_ROWS = 72
NOTES = 16


def payload_rows(bricks):
    return -(-bricks * (ROWS + C_ROWS) // 16) * 16


HB = 24
VMEM_LIMIT = 56 * 1024 * 1024
DIRECTIONS = [
    (i, j, l)
    for i in (-1, 0, 1)
    for j in (-1, 0, 1)
    for l in (-1, 0, 1)
    if (i, j, l) != (0, 0, 0)
]

VMEM = pl.BlockSpec(memory_space=pltpu.VMEM)
SMEM = pl.BlockSpec(memory_space=pltpu.SMEM)
ANY = pl.BlockSpec(memory_space=pl.ANY)
HBM = pl.BlockSpec(memory_space=pltpu.HBM)


def ring_order(chips):
    if chips == 8:
        return [0, 2, 4, 6, 7, 5, 3, 1]
    return list(range(chips))


def ring_tables(peers):
    chips = peers // 2
    spot = np.argsort(np.array(ring_order(chips)))
    device = np.arange(peers)
    behind = (spot[device // 2][:, None] - spot[None, :]) % chips
    half = chips // 2
    turn = np.where(behind >= half, 2 * (behind - half), 2 * (half - 1 - behind) + 1)
    place_of = np.broadcast_to(device, (peers, peers)).copy()
    if chips <= 8:
        for me in range(peers):
            for other in range(peers):
                away = behind[me, other // 2] if me % 2 == 0 else -behind[me, other // 2] % chips
                same = me % 2 == other % 2
                if away == 0:
                    place = 0 if same else 1
                elif away < half or (away == half and same):
                    place = 1 + away if same else 1 + half + away
                else:
                    away = chips - away
                    place = half + (away if not same else half + away) + half
                place_of[me, other] = place
    return np.concatenate([place_of, behind, turn, device[:, None]], axis=1).astype(np.int32)


def ring_step(x, peers, step, cross=0):
    order = ring_order(peers // 2)
    pairs = [
        (2 * order[i] + (core ^ cross), 2 * order[(i + (step or 1 - 2 * core)) % len(order)] + core)
        for i in range(len(order))
        for core in range(2)
    ]
    return lax.ppermute(x, "morton", pairs)


def swap_cores(x, peers):
    return lax.ppermute(x, "morton", [(m, m ^ 1) for m in range(peers)])


class RingGather:
    def __init__(self, x, peers):
        self.x, self.peers, self.chips = x, peers, peers // 2
        self.whole = None
        if self.chips > 8:
            self.whole = lax.all_gather(x[None], "morton", axis=0, tiled=True)
            return
        self.chains = ([x], [x])

    def go(self, chain, gate=None):
        if self.whole is not None or len(self.chains[chain]) > self.chips // 2 - chain:
            return
        held = self.chains[chain][-1]
        if gate is not None:
            held = lax.optimization_barrier((held, gate))[0]
        cross = int(chain == 1 and len(self.chains[chain]) == 1)
        self.chains[chain].append(ring_step(held, self.peers, 0, cross))

    def last(self, chain):
        return self.x if self.whole is not None else self.chains[chain][-1]

    def places(self, gate=None):
        if self.whole is not None:
            return [self.whole]
        mine = self.chains[0][1:] + self.chains[1][1:]
        held = mine
        if gate is not None:
            held = [lax.optimization_barrier((t, gate))[0] for t in mine]
        others = [swap_cores(t, self.peers) for t in [self.x] + held]
        return [t[None] for t in [self.x] + others[:1] + mine + others[1:]]


class RingScatter:
    def __init__(self, keep, give, peers):
        self.keep, self.peers, self.chips = keep, peers, peers // 2
        self.other = [swap_cores(t, peers) for t in give]
        self.held = [None, None]
        self.hop = 0

    def term(self, k):
        half = self.chips // 2
        pair = self.other[k - half][0] if k >= half else self.other[half - 1 - k][1]
        return self.keep[k] + pair.astype(F32)

    def go(self, gate=None):
        sent = []
        for way, step, count in ((0, 1, self.chips // 2), (1, -1, (self.chips - 1) // 2)):
            left = count - self.hop
            if left <= 0:
                continue
            part = self.term((-step * left) % self.chips)
            if self.held[way] is not None:
                part = part + self.held[way].astype(F32)
            part = part.astype(BF16)
            if gate is not None:
                part = lax.optimization_barrier((part, gate))[0]
            sent.append(part)
            self.held[way] = ring_step(part, self.peers, step)
        self.hop += 1
        return sent

    def total(self):
        return sum((t.astype(F32) for t in self.held if t is not None), self.term(0))


def call(body, out_shape, in_specs, scratch=(), cost=2, name=None, out_specs=None, aliases=None):
    return pl.pallas_call(
        body,
        out_shape=out_shape,
        in_specs=in_specs,
        out_specs=out_specs or jax.tree.map(lambda _: VMEM, out_shape),
        scratch_shapes=list(scratch),
        input_output_aliases=aliases or {},
        compiler_params=pltpu.CompilerParams(vmem_limit_bytes=VMEM_LIMIT),
        cost_estimate=pl.CostEstimate(flops=cost * 10**9, bytes_accessed=0, transcendentals=0),
        name=name,
    )


PLANES = 4


def put_boundary(rows, brick, a, out_ref, stage, ends):
    base = brick * ROWS
    if a in (0, 7):
        at = base if a == 0 else base + 64
        out_ref[at : at + 64, :] = rows
        return
    wide = rows.astype(F32)
    at = base + B_LINES - 16 + 16 * a
    out_ref[at : at + 16, :] = jnp.concatenate([wide[:8], wide[56:]], axis=0).astype(BF16)
    at = brick * C_ROWS + 12 * (a - 1)
    for half in range(2):
        lanes = slice(half * 128, half * 128 + 128)
        stage[half] = wide[:, lanes]
        ends[at : at + 6, lanes] = stage[half, pl.ds(8, 6, stride=8), :]
        ends[at + 6 : at + 12, lanes] = stage[half, pl.ds(15, 6, stride=8), :]


def each_brick(rows_of, bricks, out_ref, stage, ends):
    for brick in range(bricks):
        for first in range(0, 8, PLANES):
            rows = rows_of(pl.ds(brick * 512 + first * 64, PLANES * 64))
            for t in range(PLANES):
                plane = rows[t * 64 : t * 64 + 64]
                put_boundary(plane, brick, first + t, out_ref, stage.at[first + t], ends)
    out_ref[bricks * ROWS : payload_rows(bricks), :] = ends[...].astype(BF16)


def norm_body(recv, send, x_ref, gain_ref, hidden_ref, out_ref, stage, ends):
    bricks, directions = recv.shape
    gain = gain_ref[...]
    lane = lax.broadcasted_iota(jnp.int32, (1, C), 1)
    codes = jnp.zeros((1, C), jnp.int32)
    for k in range(send.shape[1]):
        codes = jnp.where(lane == k, send[0, k], codes)
    served = jnp.zeros((1, C), jnp.int32)
    for brick in range(bricks):
        for number in range(directions):
            served = jnp.where(lane == recv[brick, number], brick * directions + number + 1, served)
    row = lax.broadcasted_iota(jnp.int32, (NOTES, C), 0)
    notes = jnp.where(row == 0, codes, jnp.where(row == 1, served, 0))
    out_ref[payload_rows(bricks) :, :] = notes.astype(F32).astype(BF16)

    def rows_of(at):
        x = x_ref[at, :].astype(F32)
        inverse = lax.rsqrt(jnp.mean(x * x, axis=-1, keepdims=True) + 1e-6)
        v = x * inverse * gain
        rows = (v / (1.0 + jnp.exp(-v))).astype(BF16)
        hidden_ref[at, :] = rows
        return rows

    each_brick(rows_of, bricks, out_ref, stage, ends)


def extract_body(x_ref, out_ref, stage, ends):
    each_brick(lambda at: x_ref[at, :], x_ref.shape[0] // 512, out_ref, stage, ends)


def start_padded(own_ref, cells, halo, bricks):
    zero = jnp.zeros((8, C), F32)

    def clear(k, _):
        for b in range(10):
            cells[k * 10 + b] = zero
        for side in range(2):
            for part in range(HB // 8):
                halo[side, k, part * 8 : part * 8 + 8, :] = zero
        return 0

    lax.fori_loop(0, bricks * 10, clear, 0)

    def fill(k, _):
        plane = (k // 8) * 10 + k % 8 + 1
        rows = own_ref[pl.ds(pl.multiple_of(k * 64, 64), 64), :].astype(F32)
        for b in range(8):
            cells[plane * 10 + b + 1] = rows[b * 8 : b * 8 + 8]
        return 0

    lax.fori_loop(0, bricks * 8, fill, 0)


def add_line(ref, index, line):
    ref[index] = ref[index] + line


def pick(flag, yes, no):
    if isinstance(flag, bool):
        return yes if flag else no
    return jnp.where(flag, yes, no)


def place(kind, e, keep, place_at, source_brick, brick, share, cells, halo):
    flags = [t == -1 for t in e]
    pads = [pick(f, 0, 9) for f in flags]
    facing = pick(flags[0], 64, 0)
    start = source_brick * ROWS

    def rows(at, size):
        got = share[place_at, pl.ds(pl.multiple_of(start + at, 16), size), :].astype(F32)
        return got if keep is None else jnp.where(keep, got, 0.0)

    def half(pair, axis):
        return pick(flags[axis], pair[8:], pair[:8])

    def ends(a):
        value = None
        for number in range(cells.shape[0] // 100):
            at = cells.shape[0] // 100 * ROWS + number * C_ROWS + 12 * (a - 1)
            block = share[place_at, at // 16 * 16 : -(-(at + 12) // 16) * 16, :].astype(F32)
            block = block[at % 16 : at % 16 + 12]
            block = pick(flags[2], block[6:], block[:6])
            value = block if value is None else jnp.where(source_brick == number, block, value)
        return value if keep is None else jnp.where(keep, value, 0.0)

    def line_b(at):
        plane = rows(at, 64)
        return pick(flags[1], plane[56:], plane[:8])

    def line_c(at):
        plane = rows(at, 64)
        ends = [
            pick(flags[2], plane[8 * b + 7 : 8 * b + 8], plane[8 * b : 8 * b + 1]) for b in range(8)
        ]
        return jnp.concatenate(ends, axis=0)

    def cell(at):
        line = line_b(at)
        return pick(flags[2], line[7:8], line[0:1])

    side = pick(flags[2], 0, 1)
    base = brick * 10

    def add_halo(at, line):
        halo[side, base + at, 8:16, :] = halo[side, base + at, 8:16, :] + line

    def add_cell(at, value):
        spot = pl.ds(pick(flags[1], 7, 16), 1)
        halo[side, base + at, spot, :] = halo[side, base + at, spot, :] + value

    if kind == (1, 0, 0):
        got = rows(facing, 64)
        first = (base + pads[0]) * 10 + 1
        for b in range(8):
            add_line(cells, first + b, got[b * 8 : b * 8 + 8])
    elif kind == (0, 1, 0):
        for a in range(8):
            if a in (0, 7):
                line = line_b(0 if a == 0 else 64)
            else:
                line = half(rows(B_LINES - 16 + 16 * a, 16), 1)
            add_line(cells, (base + a + 1) * 10 + pads[1], line)
    elif kind == (0, 0, 1):
        for a in range(8):
            if a in (0, 7):
                line = line_c(0 if a == 0 else 64)
            else:
                pair = rows(B_LINES - 16 + 16 * a, 16)
                low = pick(flags[2], pair[7:8], pair[0:1])
                high = pick(flags[2], pair[15:], pair[8:9])
                line = jnp.concatenate([low, ends(a), high], axis=0)
            add_halo(a + 1, line)
    elif kind == (1, 1, 0):
        add_line(cells, (base + pads[0]) * 10 + pads[1], line_b(facing))
    elif kind == (1, 0, 1):
        add_halo(pads[0], line_c(facing))
    elif kind == (0, 1, 1):
        for a in range(8):
            if a in (0, 7):
                value = cell(0 if a == 0 else 64)
            else:
                line = half(rows(B_LINES - 16 + 16 * a, 16), 1)
                value = pick(flags[2], line[7:8], line[0:1])
            add_cell(a + 1, value)
    else:
        add_cell(pads[0], cell(facing))


def windows(cells, halo, cols, bricks, out=None, sems=None):
    row = lax.broadcasted_iota(jnp.int32, (8, C), 0)

    def step(k, _):
        shifted = [[], [], []]
        for b in range(10):
            x = cells[k * 10 + b]
            before = halo[0, k, pl.ds(b + 7, 1), :]
            after = halo[1, k, pl.ds(b + 7, 1), :]
            shifted[0].append(jnp.where(row == 0, before, pltpu.roll(x, 1, 0)))
            shifted[1].append(x)
            shifted[2].append(jnp.where(row == 7, after, pltpu.roll(x, 7, 0)))
        for j in range(3):
            for l in range(3):
                block = jnp.concatenate(shifted[l][j : j + 8], axis=0).astype(BF16)
                at = (3 * j + l) * C
                cols[k, :, at : at + C] = block
        if out is not None:
            pltpu.make_async_copy(cols.at[k], out.at[k], sems.at[k]).start()
        return 0

    lax.fori_loop(0, bricks * 10, step, 0)


def wait_windows(cols, out, sems, bricks):
    def step(k, _):
        pltpu.make_async_copy(cols.at[k], out.at[k], sems.at[k]).wait()
        return 0

    lax.fori_loop(0, bricks * 10, step, 0)


def fetch(parts, share, sems, first=0, rows=None):
    size = parts[0].shape[0]
    lines = pl.ds(first, rows or parts[0].shape[1])
    copies = [
        pltpu.make_async_copy(part.at[:, lines], share.at[pl.ds(k * size, size), lines], sems.at[k])
        for k, part in enumerate(parts)
    ]
    for copy in copies:
        copy.start()
    return copies


def weight_grad_body(slots, factor, peers, count, *refs):
    recv, table, own_ref, cot_ref = refs[:4]
    parts = refs[4 : 4 + count]
    keep_ref = refs[4 + count]
    give_refs = refs[5 + count : 5 + count + peers // 4]
    out_cols, codes_ref, served_ref = refs[-16:-13]
    cells, halo, share, cols, sums, narrow, turned, codes = refs[-13:-5]
    sems, cols_sems, codes_sem, out_sems, notes_sems = refs[-5:]
    bricks = own_ref.shape[0] // 512
    me = table[2 * peers]
    notes_copies = fetch(parts, share, notes_sems, payload_rows(bricks), NOTES)
    copies = fetch(parts, share, sems, 0, payload_rows(bricks))
    for part in range(bricks * 2):
        at = slice(part * 256, part * 256 + 256)
        turned[:, at] = cot_ref[at, :].astype(F32).T.astype(BF16)
    for copy in notes_copies:
        copy.wait()
    for k in range(peers):
        notes = share[k, payload_rows(bricks) :, :].astype(F32).astype(jnp.int32)
        codes_ref[k : k + 1, :] = notes[0:1]
        served_ref[k : k + 1, :] = notes[1:2]
    codes_copy = pltpu.make_async_copy(codes_ref, codes, codes_sem.at[0])
    codes_copy.start()
    start_padded(own_ref, cells, halo, bricks)
    codes_copy.wait()
    for copy in copies:
        copy.wait()
    for brick in range(bricks):
        for number, e in enumerate(DIRECTIONS):
            slot = recv[brick, number]
            safe = jnp.maximum(slot, 0)
            sender = safe // slots
            at = table[sender]
            code = codes[at, me * slots + safe - sender * slots]
            kind = tuple(abs(t) for t in e)
            place(kind, e, slot >= 0, at, code // 6, brick, share, cells, halo)
    windows(cells, halo, cols, bricks, out_cols, cols_sems)

    rows = 27 * C // peers
    for tap in range(27):
        i, jl = divmod(tap, 9)
        total = None
        for brick in range(bricks):
            right = cols[brick * 10 + i : brick * 10 + i + 8, :, jl * C : jl * C + C].reshape(512, C)
            left = turned[:, brick * 512 : brick * 512 + 512]
            term = jnp.dot(left, right, preferred_element_type=F32)
            total = term if total is None else total + term
        total = (total * factor).T
        start = tap * C
        while start < (tap + 1) * C:
            owner = start // rows
            stop = min((tap + 1) * C, (owner + 1) * rows)
            piece = total[start - tap * C : stop - tap * C]
            bucket = jnp.bitwise_xor(me % 2, owner % 2)
            behind = table[peers + owner // 2]
            where = slice(start - owner * rows, stop - owner * rows)
            sums[bucket, behind, where, :] = piece
            narrow[bucket, behind, where, :] = piece.astype(BF16)
            start = stop
            if stop == (owner + 1) * rows:

                @pl.when(bucket == 0)
                def _():
                    pltpu.make_async_copy(
                        sums.at[0, behind], keep_ref.at[behind], out_sems.at[0, behind]
                    ).start()

                turn = table[peers + peers // 2 + owner // 2]
                for hop, give_ref in enumerate(give_refs):

                    @pl.when((bucket == 1) & (turn // 2 == hop))
                    def _():
                        pltpu.make_async_copy(
                            narrow.at[1, behind], give_ref.at[turn % 2], out_sems.at[1, turn]
                        ).start()

    for k in range(peers // 2):
        pltpu.make_async_copy(sums.at[0, k], keep_ref.at[k], out_sems.at[0, k]).wait()
        pltpu.make_async_copy(narrow.at[1, k], give_refs[k // 2].at[k % 2], out_sems.at[1, k]).wait()
    wait_windows(cols, out_cols, cols_sems, bricks)


GROUP = 3 * C


def start_stream(cols_ref, first, cols, weight_ref, weight, sems):
    copies = []
    planes = cols.shape[0]
    for g in range(3):
        lanes = pl.ds(g * GROUP, GROUP)
        group = [
            pltpu.make_async_copy(
                cols_ref.at[pl.ds(first, planes), :, lanes], cols.at[:, :, lanes], sems.at[g, 3]
            )
        ]
        for i in range(3):
            at = pl.ds((i * 3 + g) * GROUP, GROUP)
            group.append(pltpu.make_async_copy(weight_ref.at[at], weight.at[at], sems.at[g, i]))
        copies.append(group)
    for group in copies:
        for copy in group:
            copy.start()
    return copies


def tap_sum(copies, cols, weight):
    bricks = cols.shape[0] // 10
    totals = [None] * bricks
    for g in range(3):
        for copy in copies[g]:
            copy.wait()
        for brick in range(bricks):
            for i in range(3):
                at = brick * 10 + i
                left = cols[at : at + 8, :, g * GROUP : g * GROUP + GROUP].reshape(512, GROUP)
                right = weight[(i * 3 + g) * GROUP : (i * 3 + g + 1) * GROUP, :]
                term = jnp.dot(left, right, preferred_element_type=F32)
                totals[brick] = term if totals[brick] is None else totals[brick] + term
    return totals


def mix_body(cols_ref, weight_ref, x_ref, out_ref, cols, weight, sems):
    copies = start_stream(cols_ref, 0, cols, weight_ref, weight, sems)
    for brick, total in enumerate(tap_sum(copies, cols, weight)):
        at = slice(brick * 512, brick * 512 + 512)
        out_ref[at, :] = (x_ref[at, :].astype(F32) + total).astype(BF16)


def input_grad_body(slots, peers, count, *refs):
    served, send, table, cot_ref, x_ref, gain_ref, weight_ref = refs[:7]
    parts = refs[7 : 7 + count]
    out_ref, cells, halo, cols, share, weight, heads, more, sems, weight_sem = refs[7 + count :]
    bricks = cot_ref.shape[0] // 512
    me = table[2 * peers]
    copies = fetch(parts, share, sems)
    weight_copy = pltpu.make_async_copy(weight_ref, weight, weight_sem.at[0])
    weight_copy.start()

    def no_head(k, _):
        heads[k] = -1
        return 0

    lax.fori_loop(0, bricks * 26, no_head, 0)

    def source_of(k):
        receiver = k // slots
        at = table[receiver]
        return at, served[at, me * slots + k - receiver * slots] - 1

    def sort(k, found):
        _, entry = source_of(k)
        asked = entry >= 0
        key = send[0, k] // 6 * 26 + 25 - jnp.maximum(entry, 0) % 26
        first = asked & (heads[key] < 0)
        extra = asked & jnp.logical_not(first)

        @pl.when(first)
        def _():
            heads[key] = k

        @pl.when(extra)
        def _():
            more[found] = k

        return found + jnp.where(extra, 1, 0)

    found = lax.fori_loop(0, send.shape[1], sort, 0)
    start_padded(cot_ref, cells, halo, bricks)
    for copy in copies:
        copy.wait()
    for brick in range(bricks):
        for number, e in enumerate(DIRECTIONS):
            head = heads[brick * 26 + number]
            at, entry = source_of(jnp.maximum(head, 0))
            kind = tuple(abs(t) for t in e)
            source = jnp.maximum(entry, 0) // 26
            place(kind, e, head >= 0, at, source, brick, share, cells, halo)

    def one(n, _):
        k = more[n]
        at, entry = source_of(k)
        number = 25 - entry % 26
        tap = jnp.where(number >= 13, number + 1, number)
        e = (tap // 9 - 1, (tap // 3) % 3 - 1, tap % 3 - 1)
        on = [t != 0 for t in e]
        for kind in ((1, 0, 0), (0, 1, 0), (0, 0, 1), (1, 1, 0), (1, 0, 1), (0, 1, 1), (1, 1, 1)):
            match = functools.reduce(
                jnp.logical_and, [f if w else jnp.logical_not(f) for f, w in zip(on, kind)]
            )

            @pl.when(match)
            def _():
                place(kind, e, None, at, entry // 26, send[0, k] // 6, share, cells, halo)

        return 0

    lax.fori_loop(0, found, one, 0)
    windows(cells, halo, cols, bricks)
    weight_copy.wait()
    gain = gain_ref[...]
    for brick in range(bricks):
        rows = slice(brick * 512, brick * 512 + 512)
        grad = None
        for tap in range(27):
            i, jl = divmod(tap, 9)
            first = brick * 10 + i
            left = cols[first : first + 8, :, jl * C : jl * C + C].reshape(512, C)
            right = weight[(26 - tap) * C : (27 - tap) * C, :]
            term = lax.dot_general(left, right, (((1,), (1,)), ((), ())), preferred_element_type=F32)
            grad = term if grad is None else grad + term
        x = x_ref[rows, :].astype(F32)
        inverse = lax.rsqrt(jnp.mean(x * x, axis=-1, keepdims=True) + 1e-6)
        unit = x * inverse
        v = unit * gain
        gate = 1.0 / (1.0 + jnp.exp(-v))
        grad = grad * (gate * (1.0 + v * (1.0 - gate))) * gain
        grad = inverse * (grad - unit * jnp.mean(grad * unit, axis=-1, keepdims=True))
        out_ref[rows, :] = (cot_ref[rows, :].astype(F32) + grad).astype(BF16)


def local(features, norm_gain, conv_weight, recv_slot, send_face, cotangent):
    channels = features.shape[1]
    per_device = features.shape[0]
    bricks = per_device // 512
    peers = lax.axis_size("morton")
    slots = send_face.shape[1] // peers
    factor = 1.0 / math.sqrt(peers * per_device)
    gain = norm_gain.reshape(1, channels)
    sds = jax.ShapeDtypeStruct
    share_rows = payload_rows(bricks)
    stage = [
        pltpu.VMEM((8, 2, 64, 128), F32),
        pltpu.VMEM((share_rows - bricks * ROWS, channels), F32),
    ]

    def padded(n):
        return [
            pltpu.VMEM((n * 100, 8, channels), F32),
            pltpu.VMEM((2, n * 10, HB, channels), F32),
        ]

    def cols_shape(n):
        return (n * 10, 64, 9 * channels)


    table = jnp.asarray(ring_tables(peers))[lax.axis_index("morton")]

    hidden, share = call(
        norm_body,
        (sds((per_device, channels), BF16), sds((share_rows + NOTES, channels), BF16)),
        [SMEM, SMEM, VMEM, VMEM],
        stage,
        name="norm",
    )(recv_slot, send_face, features, gain)
    hidden_ring = RingGather(share, peers)
    cot_share = call(
        extract_body,
        sds((share_rows, channels), BF16),
        [VMEM],
        stage,
        name="extract",
    )(cotangent)
    hidden_ring.go(0)
    hidden_ring.go(1)
    hidden_ring.go(0, cot_share)
    hidden_ring.go(1)
    hidden_ring.go(0, table)
    hidden_ring.go(1)
    hidden_ring.go(0)
    hidden_parts = hidden_ring.places()

    cot_ring = RingGather(cot_share, peers)
    cot_ring.go(0, hidden_ring.last(1))
    cot_ring.go(1, hidden_ring.last(0))

    count = len(hidden_parts)
    rows = 27 * channels // peers
    chips = peers // 2
    keep, *give, cols, _, served = call(
        functools.partial(weight_grad_body, slots, factor, peers, count),
        (
            sds((chips, rows, channels), F32),
            *[sds((2, rows, channels), BF16)] * (chips // 2),
            sds(cols_shape(bricks), BF16),
            sds((peers, channels), jnp.int32),
            sds((peers, channels), jnp.int32),
        ),
        [SMEM] * 2 + [VMEM] * 2 + [HBM] * count,
        padded(bricks)
        + [
            pltpu.VMEM((peers, share_rows + NOTES, channels), BF16),
            pltpu.VMEM(cols_shape(bricks), BF16),
            pltpu.VMEM((2, chips, rows, channels), F32),
            pltpu.VMEM((2, chips, rows, channels), BF16),
            pltpu.VMEM((channels, per_device), BF16),
            pltpu.SMEM((peers, channels), jnp.int32),
            pltpu.SemaphoreType.DMA((count,)),
            pltpu.SemaphoreType.DMA((bricks * 10,)),
            pltpu.SemaphoreType.DMA((1,)),
            pltpu.SemaphoreType.DMA((2, chips)),
            pltpu.SemaphoreType.DMA((count,)),
        ],
        cost=9,
        name="weight_grad",
        out_specs=(*[HBM] * (2 + chips // 2), VMEM, VMEM),
    )(recv_slot, table, hidden, cotangent, *hidden_parts)

    first = (cot_ring.last(0), cot_ring.last(1))
    give = [lax.optimization_barrier((t, first))[0] for t in give]
    sums_ring = RingScatter(keep, give, peers)
    sent = sums_ring.go()
    cot_ring.go(0, cols)
    cot_ring.go(1, cols)
    second = (cot_ring.last(0), cot_ring.last(1))
    mix_cols = lax.optimization_barrier((cols, sent))[0]
    weight_scratch = [
        pltpu.VMEM((27 * channels, channels), BF16),
        pltpu.SemaphoreType.DMA((3, 4)),
    ]
    mixed = call(
        mix_body,
        sds((per_device, channels), BF16),
        [HBM, HBM, VMEM],
        [pltpu.VMEM(cols_shape(bricks), BF16)] + weight_scratch,
        cost=6,
        name="mix",
    )(mix_cols, conv_weight, features)
    sent = sums_ring.go((second, mixed))
    cot_ring.go(0)
    cot_ring.go(1)
    third = (cot_ring.last(0), cot_ring.last(1))
    sums_ring.go(third)
    cot_ring.go(0)
    sent = sums_ring.go(cot_ring.last(0))
    cot_parts = cot_ring.places(cols)
    served = lax.optimization_barrier((served, sent))[0]

    grad_features = call(
        functools.partial(input_grad_body, slots, peers, count),
        sds((per_device, channels), BF16),
        [SMEM] * 3 + [VMEM] * 3 + [HBM] * (1 + count),
        padded(bricks)
        + [
            pltpu.VMEM(cols_shape(bricks), BF16),
            pltpu.VMEM((peers, share_rows, channels), BF16),
            weight_scratch[0],
            pltpu.SMEM((bricks * 26,), jnp.int32),
            pltpu.SMEM((peers * slots,), jnp.int32),
            pltpu.SemaphoreType.DMA((count,)),
            pltpu.SemaphoreType.DMA((1,)),
        ],
        cost=13,
        name="input_grad",
    )(served, send_face, table, cotangent, features, gain, conv_weight, *cot_parts)
    for _ in range(chips // 2 - 4):
        sums_ring.go()
    return (mixed, grad_features, sums_ring.total())


def solution(mesh):
    rows = P(("groups", "morton"), None)
    return jax.shard_map(
        local,
        mesh=mesh,
        in_specs=(rows, P(), P(), rows, rows, rows),
        out_specs=(rows, rows, rows),
        check_vma=False,
    )
```

```python
import functools
import math

import jax
import jax.numpy as jnp
import numpy as np
from jax import lax
from jax.experimental import pallas as pl
from jax.experimental.pallas import tpu as pltpu
from jax.sharding import PartitionSpec as P

F32 = jnp.float32
BF16 = jnp.bfloat16
C = 256
B_LINES = 128
ROWS = 224
C_ROWS = 72
NOTES = 16


def payload_rows(bricks):
    return -(-bricks * (ROWS + C_ROWS) // 16) * 16


HB = 24
VMEM_LIMIT = 56 * 1024 * 1024
DIRECTIONS = [
    (i, j, l)
    for i in (-1, 0, 1)
    for j in (-1, 0, 1)
    for l in (-1, 0, 1)
    if (i, j, l) != (0, 0, 0)
]

VMEM = pl.BlockSpec(memory_space=pltpu.VMEM)
SMEM = pl.BlockSpec(memory_space=pltpu.SMEM)
ANY = pl.BlockSpec(memory_space=pl.ANY)
HBM = pl.BlockSpec(memory_space=pltpu.HBM)


def ring_order(chips):
    if chips == 8:
        return [0, 2, 4, 6, 7, 5, 3, 1]
    return list(range(chips))


def ring_tables(peers):
    chips = peers // 2
    spot = np.argsort(np.array(ring_order(chips)))
    device = np.arange(peers)
    behind = (spot[device // 2][:, None] - spot[None, :]) % chips
    half = chips // 2
    turn = np.where(behind >= half, 2 * (behind - half), 2 * (half - 1 - behind) + 1)
    place_of = np.broadcast_to(device, (peers, peers)).copy()
    if chips <= 8:
        for me in range(peers):
            for other in range(peers):
                away = behind[me, other // 2] if me % 2 == 0 else -behind[me, other // 2] % chips
                same = me % 2 == other % 2
                if away == 0:
                    place = 0 if same else 1
                elif away < half or (away == half and same):
                    place = 1 + away if same else 1 + half + away
                else:
                    away = chips - away
                    place = half + (away if not same else half + away) + half
                place_of[me, other] = place
    return np.concatenate([place_of, behind, turn, device[:, None]], axis=1).astype(np.int32)


def ring_step(x, peers, step, cross=0):
    order = ring_order(peers // 2)
    pairs = [
        (2 * order[i] + (core ^ cross), 2 * order[(i + (step or 1 - 2 * core)) % len(order)] + core)
        for i in range(len(order))
        for core in range(2)
    ]
    return lax.ppermute(x, "morton", pairs)


def swap_cores(x, peers):
    return lax.ppermute(x, "morton", [(m, m ^ 1) for m in range(peers)])


class RingGather:
    def __init__(self, x, peers):
        self.x, self.peers, self.chips = x, peers, peers // 2
        self.whole = None
        if self.chips > 8:
            self.whole = lax.all_gather(x[None], "morton", axis=0, tiled=True)
            return
        self.chains = ([x], [x])

    def go(self, chain, gate=None):
        if self.whole is not None or len(self.chains[chain]) > self.chips // 2 - chain:
            return
        held = self.chains[chain][-1]
        if gate is not None:
            held = lax.optimization_barrier((held, gate))[0]
        cross = int(chain == 1 and len(self.chains[chain]) == 1)
        self.chains[chain].append(ring_step(held, self.peers, 0, cross))

    def last(self, chain):
        return self.x if self.whole is not None else self.chains[chain][-1]

    def places(self, gate=None, last_gate=None):
        if self.whole is not None:
            return [self.whole]
        mine = self.chains[0][1:] + self.chains[1][1:]
        held = mine
        if gate is not None:
            last = self.chips // 2 - 1
            gates = [last_gate if k == last else gate for k in range(len(mine))]
            held = [lax.optimization_barrier(pair)[0] for pair in zip(mine, gates)]
        others = [swap_cores(t, self.peers) for t in [self.x] + held]
        return [t[None] for t in [self.x] + others[:1] + mine + others[1:]]


class RingScatter:
    def __init__(self, keep, give, peers):
        self.keep, self.peers, self.chips = keep, peers, peers // 2
        self.other = [swap_cores(t, peers) for t in give]
        self.held = [None, None]
        self.hop = 0

    def term(self, k):
        half = self.chips // 2
        pair = self.other[k - half][0] if k >= half else self.other[half - 1 - k][1]
        return self.keep[k] + pair.astype(F32)

    def go(self, gate=None):
        sent = []
        for way, step, count in ((0, 1, self.chips // 2), (1, -1, (self.chips - 1) // 2)):
            left = count - self.hop
            if left <= 0:
                continue
            part = self.term((-step * left) % self.chips)
            if self.held[way] is not None:
                part = part + self.held[way].astype(F32)
            part = part.astype(BF16)
            if gate is not None:
                part = lax.optimization_barrier((part, gate))[0]
            sent.append(part)
            self.held[way] = ring_step(part, self.peers, step)
        self.hop += 1
        return sent

    def total(self, gate):
        held = lax.optimization_barrier((*self.held, gate))[:2]
        return sum((t.astype(F32) for t in held), self.term(0))


def call(body, out_shape, in_specs, scratch=(), cost=2, name=None, out_specs=None, aliases=None):
    return pl.pallas_call(
        body,
        out_shape=out_shape,
        in_specs=in_specs,
        out_specs=out_specs or jax.tree.map(lambda _: VMEM, out_shape),
        scratch_shapes=list(scratch),
        input_output_aliases=aliases or {},
        compiler_params=pltpu.CompilerParams(vmem_limit_bytes=VMEM_LIMIT),
        cost_estimate=pl.CostEstimate(flops=cost * 10**9, bytes_accessed=0, transcendentals=0),
        name=name,
    )


PLANES = 4


def put_boundary(rows, brick, a, out_ref, stage, ends):
    base = brick * ROWS
    if a in (0, 7):
        at = base if a == 0 else base + 64
        out_ref[at : at + 64, :] = rows
        return
    wide = rows.astype(F32)
    at = base + B_LINES - 16 + 16 * a
    out_ref[at : at + 16, :] = jnp.concatenate([wide[:8], wide[56:]], axis=0).astype(BF16)
    at = brick * C_ROWS + 12 * (a - 1)
    for half in range(2):
        lanes = slice(half * 128, half * 128 + 128)
        stage[half] = wide[:, lanes]
        ends[at : at + 6, lanes] = stage[half, pl.ds(8, 6, stride=8), :]
        ends[at + 6 : at + 12, lanes] = stage[half, pl.ds(15, 6, stride=8), :]


def each_brick(rows_of, bricks, out_ref, stage, ends):
    for brick in range(bricks):
        for first in range(0, 8, PLANES):
            rows = rows_of(pl.ds(brick * 512 + first * 64, PLANES * 64))
            for t in range(PLANES):
                plane = rows[t * 64 : t * 64 + 64]
                put_boundary(plane, brick, first + t, out_ref, stage.at[first + t], ends)
    out_ref[bricks * ROWS : payload_rows(bricks), :] = ends[...].astype(BF16)


def norm_body(recv, send, x_ref, gain_ref, hidden_ref, out_ref, stage, ends):
    bricks, directions = recv.shape
    gain = gain_ref[...]
    lane = lax.broadcasted_iota(jnp.int32, (1, C), 1)
    codes = jnp.zeros((1, C), jnp.int32)
    for k in range(send.shape[1]):
        codes = jnp.where(lane == k, send[0, k], codes)
    served = jnp.zeros((1, C), jnp.int32)
    for brick in range(bricks):
        for number in range(directions):
            served = jnp.where(lane == recv[brick, number], brick * directions + number + 1, served)
    row = lax.broadcasted_iota(jnp.int32, (NOTES, C), 0)
    notes = jnp.where(row == 0, codes, jnp.where(row == 1, served, 0))
    out_ref[payload_rows(bricks) :, :] = notes.astype(F32).astype(BF16)

    def rows_of(at):
        x = x_ref[at, :].astype(F32)
        inverse = lax.rsqrt(jnp.mean(x * x, axis=-1, keepdims=True) + 1e-6)
        v = x * inverse * gain
        rows = (v / (1.0 + jnp.exp(-v))).astype(BF16)
        hidden_ref[at, :] = rows
        return rows

    each_brick(rows_of, bricks, out_ref, stage, ends)


def extract_body(x_ref, out_ref, stage, ends):
    each_brick(lambda at: x_ref[at, :], x_ref.shape[0] // 512, out_ref, stage, ends)


def start_padded(own_ref, cells, halo, bricks):
    zero = jnp.zeros((8, C), F32)

    def clear(k, _):
        for b in range(10):
            cells[k * 10 + b] = zero
        for side in range(2):
            for part in range(HB // 8):
                halo[side, k, part * 8 : part * 8 + 8, :] = zero
        return 0

    lax.fori_loop(0, bricks * 10, clear, 0)

    def fill(k, _):
        plane = (k // 8) * 10 + k % 8 + 1
        rows = own_ref[pl.ds(pl.multiple_of(k * 64, 64), 64), :].astype(F32)
        for b in range(8):
            cells[plane * 10 + b + 1] = rows[b * 8 : b * 8 + 8]
        return 0

    lax.fori_loop(0, bricks * 8, fill, 0)


def add_line(ref, index, line):
    ref[index] = ref[index] + line


def pick(flag, yes, no):
    if isinstance(flag, bool):
        return yes if flag else no
    return jnp.where(flag, yes, no)


def place(kind, e, keep, place_at, source_brick, brick, share, cells, halo):
    flags = [t == -1 for t in e]
    pads = [pick(f, 0, 9) for f in flags]
    facing = pick(flags[0], 64, 0)
    start = source_brick * ROWS

    def rows(at, size):
        got = share[place_at, pl.ds(pl.multiple_of(start + at, 16), size), :].astype(F32)
        return got if keep is None else jnp.where(keep, got, 0.0)

    def half(pair, axis):
        return pick(flags[axis], pair[8:], pair[:8])

    def ends(a):
        value = None
        for number in range(cells.shape[0] // 100):
            at = cells.shape[0] // 100 * ROWS + number * C_ROWS + 12 * (a - 1)
            block = share[place_at, at // 16 * 16 : -(-(at + 12) // 16) * 16, :].astype(F32)
            block = block[at % 16 : at % 16 + 12]
            block = pick(flags[2], block[6:], block[:6])
            value = block if value is None else jnp.where(source_brick == number, block, value)
        return value if keep is None else jnp.where(keep, value, 0.0)

    def line_b(at):
        plane = rows(at, 64)
        return pick(flags[1], plane[56:], plane[:8])

    def line_c(at):
        plane = rows(at, 64)
        ends = [
            pick(flags[2], plane[8 * b + 7 : 8 * b + 8], plane[8 * b : 8 * b + 1]) for b in range(8)
        ]
        return jnp.concatenate(ends, axis=0)

    def cell(at):
        line = line_b(at)
        return pick(flags[2], line[7:8], line[0:1])

    side = pick(flags[2], 0, 1)
    base = brick * 10

    def add_halo(at, line):
        halo[side, base + at, 8:16, :] = halo[side, base + at, 8:16, :] + line

    def add_cell(at, value):
        spot = pl.ds(pick(flags[1], 7, 16), 1)
        halo[side, base + at, spot, :] = halo[side, base + at, spot, :] + value

    if kind == (1, 0, 0):
        got = rows(facing, 64)
        first = (base + pads[0]) * 10 + 1
        for b in range(8):
            add_line(cells, first + b, got[b * 8 : b * 8 + 8])
    elif kind == (0, 1, 0):
        for a in range(8):
            if a in (0, 7):
                line = line_b(0 if a == 0 else 64)
            else:
                line = half(rows(B_LINES - 16 + 16 * a, 16), 1)
            add_line(cells, (base + a + 1) * 10 + pads[1], line)
    elif kind == (0, 0, 1):
        for a in range(8):
            if a in (0, 7):
                line = line_c(0 if a == 0 else 64)
            else:
                pair = rows(B_LINES - 16 + 16 * a, 16)
                low = pick(flags[2], pair[7:8], pair[0:1])
                high = pick(flags[2], pair[15:], pair[8:9])
                line = jnp.concatenate([low, ends(a), high], axis=0)
            add_halo(a + 1, line)
    elif kind == (1, 1, 0):
        add_line(cells, (base + pads[0]) * 10 + pads[1], line_b(facing))
    elif kind == (1, 0, 1):
        add_halo(pads[0], line_c(facing))
    elif kind == (0, 1, 1):
        for a in range(8):
            if a in (0, 7):
                value = cell(0 if a == 0 else 64)
            else:
                line = half(rows(B_LINES - 16 + 16 * a, 16), 1)
                value = pick(flags[2], line[7:8], line[0:1])
            add_cell(a + 1, value)
    else:
        add_cell(pads[0], cell(facing))


def windows(cells, halo, cols, bricks, out=None, sems=None):
    row = lax.broadcasted_iota(jnp.int32, (8, C), 0)

    def step(k, _):
        shifted = [[], [], []]
        for b in range(10):
            x = cells[k * 10 + b]
            before = halo[0, k, pl.ds(b + 7, 1), :]
            after = halo[1, k, pl.ds(b + 7, 1), :]
            shifted[0].append(jnp.where(row == 0, before, pltpu.roll(x, 1, 0)))
            shifted[1].append(x)
            shifted[2].append(jnp.where(row == 7, after, pltpu.roll(x, 7, 0)))
        for j in range(3):
            for l in range(3):
                block = jnp.concatenate(shifted[l][j : j + 8], axis=0).astype(BF16)
                at = (3 * j + l) * C
                cols[k, :, at : at + C] = block
        if out is not None:
            pltpu.make_async_copy(cols.at[k], out.at[k], sems.at[k]).start()
        return 0

    lax.fori_loop(0, bricks * 10, step, 0)


def wait_windows(cols, out, sems, bricks):
    def step(k, _):
        pltpu.make_async_copy(cols.at[k], out.at[k], sems.at[k]).wait()
        return 0

    lax.fori_loop(0, bricks * 10, step, 0)


def fetch(parts, share, sems, first=0, rows=None):
    size = parts[0].shape[0]
    lines = pl.ds(first, rows or parts[0].shape[1])
    copies = [
        pltpu.make_async_copy(part.at[:, lines], share.at[pl.ds(k * size, size), lines], sems.at[k])
        for k, part in enumerate(parts)
    ]
    for copy in copies:
        copy.start()
    return copies


def weight_grad_body(slots, factor, peers, count, *refs):
    recv, table, own_ref, cot_ref = refs[:4]
    parts = refs[4 : 4 + count]
    keep_ref = refs[4 + count]
    give_refs = refs[5 + count : 5 + count + peers // 4]
    out_cols, codes_ref, served_ref = refs[-16:-13]
    cells, halo, share, cols, sums, narrow, turned, codes = refs[-13:-5]
    sems, cols_sems, codes_sem, out_sems, notes_sems = refs[-5:]
    bricks = own_ref.shape[0] // 512
    me = table[2 * peers]
    notes_copies = fetch(parts, share, notes_sems, payload_rows(bricks), NOTES)
    copies = fetch(parts, share, sems, 0, payload_rows(bricks))
    for part in range(bricks * 2):
        at = slice(part * 256, part * 256 + 256)
        turned[:, at] = cot_ref[at, :].astype(F32).T.astype(BF16)
    for copy in notes_copies:
        copy.wait()
    for k in range(peers):
        notes = share[k, payload_rows(bricks) :, :].astype(F32).astype(jnp.int32)
        codes_ref[k : k + 1, :] = notes[0:1]
        served_ref[k : k + 1, :] = notes[1:2]
    codes_copy = pltpu.make_async_copy(codes_ref, codes, codes_sem.at[0])
    codes_copy.start()
    start_padded(own_ref, cells, halo, bricks)
    codes_copy.wait()
    for copy in copies:
        copy.wait()
    for brick in range(bricks):
        for number, e in enumerate(DIRECTIONS):
            slot = recv[brick, number]
            safe = jnp.maximum(slot, 0)
            sender = safe // slots
            at = table[sender]
            code = codes[at, me * slots + safe - sender * slots]
            kind = tuple(abs(t) for t in e)
            place(kind, e, slot >= 0, at, code // 6, brick, share, cells, halo)
    windows(cells, halo, cols, bricks, out_cols, cols_sems)

    rows = 27 * C // peers
    for tap in range(27):
        i, jl = divmod(tap, 9)
        total = None
        for brick in range(bricks):
            right = cols[brick * 10 + i : brick * 10 + i + 8, :, jl * C : jl * C + C].reshape(512, C)
            left = turned[:, brick * 512 : brick * 512 + 512]
            term = jnp.dot(left, right, preferred_element_type=F32)
            total = term if total is None else total + term
        total = (total * factor).T
        start = tap * C
        while start < (tap + 1) * C:
            owner = start // rows
            stop = min((tap + 1) * C, (owner + 1) * rows)
            piece = total[start - tap * C : stop - tap * C]
            bucket = jnp.bitwise_xor(me % 2, owner % 2)
            behind = table[peers + owner // 2]
            where = slice(start - owner * rows, stop - owner * rows)
            sums[bucket, behind, where, :] = piece
            narrow[bucket, behind, where, :] = piece.astype(BF16)
            start = stop
            if stop == (owner + 1) * rows:

                @pl.when(bucket == 0)
                def _():
                    pltpu.make_async_copy(
                        sums.at[0, behind], keep_ref.at[behind], out_sems.at[0, behind]
                    ).start()

                turn = table[peers + peers // 2 + owner // 2]
                for hop, give_ref in enumerate(give_refs):

                    @pl.when((bucket == 1) & (turn // 2 == hop))
                    def _():
                        pltpu.make_async_copy(
                            narrow.at[1, behind], give_ref.at[turn % 2], out_sems.at[1, turn]
                        ).start()

    for k in range(peers // 2):
        pltpu.make_async_copy(sums.at[0, k], keep_ref.at[k], out_sems.at[0, k]).wait()
        pltpu.make_async_copy(narrow.at[1, k], give_refs[k // 2].at[k % 2], out_sems.at[1, k]).wait()
    wait_windows(cols, out_cols, cols_sems, bricks)


GROUP = 3 * C


def start_stream(cols_ref, first, cols, weight_ref, weight, sems):
    copies = []
    planes = cols.shape[0]
    for g in range(3):
        lanes = pl.ds(g * GROUP, GROUP)
        group = [
            pltpu.make_async_copy(
                cols_ref.at[pl.ds(first, planes), :, lanes], cols.at[:, :, lanes], sems.at[g, 3]
            )
        ]
        for i in range(3):
            at = pl.ds((i * 3 + g) * GROUP, GROUP)
            group.append(pltpu.make_async_copy(weight_ref.at[at], weight.at[at], sems.at[g, i]))
        copies.append(group)
    for group in copies:
        for copy in group:
            copy.start()
    return copies


def tap_sum(copies, cols, weight):
    bricks = cols.shape[0] // 10
    totals = [None] * bricks
    for g in range(3):
        for copy in copies[g]:
            copy.wait()
        for brick in range(bricks):
            for i in range(3):
                at = brick * 10 + i
                left = cols[at : at + 8, :, g * GROUP : g * GROUP + GROUP].reshape(512, GROUP)
                right = weight[(i * 3 + g) * GROUP : (i * 3 + g + 1) * GROUP, :]
                term = jnp.dot(left, right, preferred_element_type=F32)
                totals[brick] = term if totals[brick] is None else totals[brick] + term
    return totals


def mix_body(cols_ref, weight_ref, x_ref, out_ref, cols, weight, sems):
    copies = start_stream(cols_ref, 0, cols, weight_ref, weight, sems)
    for brick, total in enumerate(tap_sum(copies, cols, weight)):
        at = slice(brick * 512, brick * 512 + 512)
        out_ref[at, :] = (x_ref[at, :].astype(F32) + total).astype(BF16)


def input_grad_body(slots, peers, count, *refs):
    served, send, table, cot_ref, x_ref, gain_ref, weight_ref = refs[:7]
    parts = refs[7 : 7 + count]
    out_ref, cells, halo, cols, share, weight, heads, more, sems, weight_sem = refs[7 + count :]
    bricks = cot_ref.shape[0] // 512
    me = table[2 * peers]
    copies = fetch(parts, share, sems)
    weight_copy = pltpu.make_async_copy(weight_ref, weight, weight_sem.at[0])
    weight_copy.start()

    def no_head(k, _):
        heads[k] = -1
        return 0

    lax.fori_loop(0, bricks * 26, no_head, 0)

    def source_of(k):
        receiver = k // slots
        at = table[receiver]
        return at, served[at, me * slots + k - receiver * slots] - 1

    def sort(k, found):
        _, entry = source_of(k)
        asked = entry >= 0
        key = send[0, k] // 6 * 26 + 25 - jnp.maximum(entry, 0) % 26
        first = asked & (heads[key] < 0)
        extra = asked & jnp.logical_not(first)

        @pl.when(first)
        def _():
            heads[key] = k

        @pl.when(extra)
        def _():
            more[found] = k

        return found + jnp.where(extra, 1, 0)

    found = lax.fori_loop(0, send.shape[1], sort, 0)
    start_padded(cot_ref, cells, halo, bricks)
    for copy in copies:
        copy.wait()
    for brick in range(bricks):
        for number, e in enumerate(DIRECTIONS):
            head = heads[brick * 26 + number]
            at, entry = source_of(jnp.maximum(head, 0))
            kind = tuple(abs(t) for t in e)
            source = jnp.maximum(entry, 0) // 26
            place(kind, e, head >= 0, at, source, brick, share, cells, halo)

    def one(n, _):
        k = more[n]
        at, entry = source_of(k)
        number = 25 - entry % 26
        tap = jnp.where(number >= 13, number + 1, number)
        e = (tap // 9 - 1, (tap // 3) % 3 - 1, tap % 3 - 1)
        on = [t != 0 for t in e]
        for kind in ((1, 0, 0), (0, 1, 0), (0, 0, 1), (1, 1, 0), (1, 0, 1), (0, 1, 1), (1, 1, 1)):
            match = functools.reduce(
                jnp.logical_and, [f if w else jnp.logical_not(f) for f, w in zip(on, kind)]
            )

            @pl.when(match)
            def _():
                place(kind, e, None, at, entry // 26, send[0, k] // 6, share, cells, halo)

        return 0

    lax.fori_loop(0, found, one, 0)
    windows(cells, halo, cols, bricks)
    weight_copy.wait()
    gain = gain_ref[...]
    for brick in range(bricks):
        rows = slice(brick * 512, brick * 512 + 512)
        grad = None
        for tap in range(27):
            i, jl = divmod(tap, 9)
            first = brick * 10 + i
            left = cols[first : first + 8, :, jl * C : jl * C + C].reshape(512, C)
            right = weight[(26 - tap) * C : (27 - tap) * C, :]
            term = lax.dot_general(left, right, (((1,), (1,)), ((), ())), preferred_element_type=F32)
            grad = term if grad is None else grad + term
        x = x_ref[rows, :].astype(F32)
        inverse = lax.rsqrt(jnp.mean(x * x, axis=-1, keepdims=True) + 1e-6)
        unit = x * inverse
        v = unit * gain
        gate = 1.0 / (1.0 + jnp.exp(-v))
        grad = grad * (gate * (1.0 + v * (1.0 - gate))) * gain
        grad = inverse * (grad - unit * jnp.mean(grad * unit, axis=-1, keepdims=True))
        out_ref[rows, :] = (cot_ref[rows, :].astype(F32) + grad).astype(BF16)


def local(features, norm_gain, conv_weight, recv_slot, send_face, cotangent):
    channels = features.shape[1]
    per_device = features.shape[0]
    bricks = per_device // 512
    peers = lax.axis_size("morton")
    slots = send_face.shape[1] // peers
    factor = 1.0 / math.sqrt(peers * per_device)
    gain = norm_gain.reshape(1, channels)
    sds = jax.ShapeDtypeStruct
    share_rows = payload_rows(bricks)
    stage = [
        pltpu.VMEM((8, 2, 64, 128), F32),
        pltpu.VMEM((share_rows - bricks * ROWS, channels), F32),
    ]

    def padded(n):
        return [
            pltpu.VMEM((n * 100, 8, channels), F32),
            pltpu.VMEM((2, n * 10, HB, channels), F32),
        ]

    def cols_shape(n):
        return (n * 10, 64, 9 * channels)


    table = jnp.asarray(ring_tables(peers))[lax.axis_index("morton")]

    hidden, share = call(
        norm_body,
        (sds((per_device, channels), BF16), sds((share_rows + NOTES, channels), BF16)),
        [SMEM, SMEM, VMEM, VMEM],
        stage,
        name="norm",
    )(recv_slot, send_face, features, gain)
    hidden_ring = RingGather(share, peers)
    cot_share = call(
        extract_body,
        sds((share_rows, channels), BF16),
        [VMEM],
        stage,
        name="extract",
    )(cotangent)
    hidden_ring.go(0)
    hidden_ring.go(1)
    hidden_ring.go(0, cot_share)
    hidden_ring.go(1)
    hidden_ring.go(0, table)
    hidden_ring.go(1)
    hidden_ring.go(0)
    hidden_parts = hidden_ring.places()

    cot_ring = RingGather(cot_share, peers)
    cot_ring.go(0, hidden_ring.last(1))
    cot_ring.go(1, hidden_ring.last(0))

    count = len(hidden_parts)
    rows = 27 * channels // peers
    chips = peers // 2
    keep, *give, cols, _, served = call(
        functools.partial(weight_grad_body, slots, factor, peers, count),
        (
            sds((chips, rows, channels), F32),
            *[sds((2, rows, channels), BF16)] * (chips // 2),
            sds(cols_shape(bricks), BF16),
            sds((peers, channels), jnp.int32),
            sds((peers, channels), jnp.int32),
        ),
        [SMEM] * 2 + [VMEM] * 2 + [HBM] * count,
        padded(bricks)
        + [
            pltpu.VMEM((peers, share_rows + NOTES, channels), BF16),
            pltpu.VMEM(cols_shape(bricks), BF16),
            pltpu.VMEM((2, chips, rows, channels), F32),
            pltpu.VMEM((2, chips, rows, channels), BF16),
            pltpu.VMEM((channels, per_device), BF16),
            pltpu.SMEM((peers, channels), jnp.int32),
            pltpu.SemaphoreType.DMA((count,)),
            pltpu.SemaphoreType.DMA((bricks * 10,)),
            pltpu.SemaphoreType.DMA((1,)),
            pltpu.SemaphoreType.DMA((2, chips)),
            pltpu.SemaphoreType.DMA((count,)),
        ],
        cost=9,
        name="weight_grad",
        out_specs=(*[HBM] * (2 + chips // 2), VMEM, VMEM),
    )(recv_slot, table, hidden, cotangent, *hidden_parts)

    first = (cot_ring.last(0), cot_ring.last(1))
    give = [lax.optimization_barrier((t, first))[0] for t in give]
    sums_ring = RingScatter(keep, give, peers)
    sent = sums_ring.go()
    cot_ring.go(0, cols)
    cot_ring.go(1, cols)
    second = (cot_ring.last(0), cot_ring.last(1))
    mix_cols = lax.optimization_barrier((cols, sent))[0]
    weight_scratch = [
        pltpu.VMEM((27 * channels, channels), BF16),
        pltpu.SemaphoreType.DMA((3, 4)),
    ]
    mixed = call(
        mix_body,
        sds((per_device, channels), BF16),
        [HBM, HBM, VMEM],
        [pltpu.VMEM(cols_shape(bricks), BF16)] + weight_scratch,
        cost=6,
        name="mix",
    )(mix_cols, conv_weight, features)
    sent = sums_ring.go((second, mixed))
    cot_ring.go(0)
    cot_ring.go(1)
    third = (cot_ring.last(0), cot_ring.last(1))
    sums_ring.go(third)
    arrived = sums_ring.held[0]
    cot_ring.go(0)
    cot_parts = cot_ring.places(cols, arrived)
    early = [t for k, t in enumerate(cot_parts) if k != peers // 2 + peers // 4]
    sent = sums_ring.go(early)
    served = lax.optimization_barrier((served, sent))[0]

    grad_features = call(
        functools.partial(input_grad_body, slots, peers, count),
        sds((per_device, channels), BF16),
        [SMEM] * 3 + [VMEM] * 3 + [HBM] * (1 + count),
        padded(bricks)
        + [
            pltpu.VMEM(cols_shape(bricks), BF16),
            pltpu.VMEM((peers, share_rows, channels), BF16),
            weight_scratch[0],
            pltpu.SMEM((bricks * 26,), jnp.int32),
            pltpu.SMEM((peers * slots,), jnp.int32),
            pltpu.SemaphoreType.DMA((count,)),
            pltpu.SemaphoreType.DMA((1,)),
        ],
        cost=13,
        name="input_grad",
    )(served, send_face, table, cotangent, features, gain, conv_weight, *cot_parts)
    for _ in range(chips // 2 - 4):
        sums_ring.go()
    return (mixed, grad_features, sums_ring.total(grad_features))


def solution(mesh):
    rows = P(("groups", "morton"), None)
    return jax.shard_map(
        local,
        mesh=mesh,
        in_specs=(rows, P(), P(), rows, rows, rows),
        out_specs=(rows, rows, rows),
        check_vma=False,
    )
```

```python
import functools
import math

import jax
import jax.numpy as jnp
import numpy as np
from jax import lax
from jax.experimental import pallas as pl
from jax.experimental.pallas import tpu as pltpu
from jax.sharding import PartitionSpec as P

F32 = jnp.float32
BF16 = jnp.bfloat16
C = 256
B_LINES = 128
ROWS = 224
C_ROWS = 72
NOTES = 16


def payload_rows(bricks):
    return -(-bricks * (ROWS + C_ROWS) // 16) * 16


HB = 24
VMEM_LIMIT = 60 * 1024 * 1024
DIRECTIONS = [
    (i, j, l)
    for i in (-1, 0, 1)
    for j in (-1, 0, 1)
    for l in (-1, 0, 1)
    if (i, j, l) != (0, 0, 0)
]

VMEM = pl.BlockSpec(memory_space=pltpu.VMEM)
SMEM = pl.BlockSpec(memory_space=pltpu.SMEM)
ANY = pl.BlockSpec(memory_space=pl.ANY)
HBM = pl.BlockSpec(memory_space=pltpu.HBM)


def ring_order(chips):
    if chips == 8:
        return [0, 2, 4, 6, 7, 5, 3, 1]
    return list(range(chips))


def ring_tables(peers):
    chips = peers // 2
    spot = np.argsort(np.array(ring_order(chips)))
    device = np.arange(peers)
    behind = (spot[device // 2][:, None] - spot[None, :]) % chips
    half = chips // 2
    turn = np.where(behind >= half, 2 * (behind - half), 2 * (half - 1 - behind) + 1)
    place_of = np.broadcast_to(device, (peers, peers)).copy()
    if chips <= 8:
        for me in range(peers):
            for other in range(peers):
                away = behind[me, other // 2] if me % 2 == 0 else -behind[me, other // 2] % chips
                same = me % 2 == other % 2
                if away == 0:
                    place = 0 if same else 1
                elif away < half or (away == half and same):
                    place = 1 + away if same else 1 + half + away
                else:
                    away = chips - away
                    place = half + (away if not same else half + away) + half
                place_of[me, other] = place
    return np.concatenate([place_of, behind, turn, device[:, None]], axis=1).astype(np.int32)


def ring_step(x, peers, step, cross=0):
    order = ring_order(peers // 2)
    pairs = [
        (2 * order[i] + (core ^ cross), 2 * order[(i + (step or 1 - 2 * core)) % len(order)] + core)
        for i in range(len(order))
        for core in range(2)
    ]
    return lax.ppermute(x, "morton", pairs)


def swap_cores(x, peers):
    return lax.ppermute(x, "morton", [(m, m ^ 1) for m in range(peers)])


class RingGather:
    def __init__(self, x, peers):
        self.x, self.peers, self.chips = x, peers, peers // 2
        self.whole = None
        if self.chips > 8:
            self.whole = lax.all_gather(x[None], "morton", axis=0, tiled=True)
            return
        self.chains = ([x], [x])

    def go(self, chain, gate=None):
        if self.whole is not None or len(self.chains[chain]) > self.chips // 2 - chain:
            return
        held = self.chains[chain][-1]
        if gate is not None:
            held = lax.optimization_barrier((held, gate))[0]
        cross = int(chain == 1 and len(self.chains[chain]) == 1)
        self.chains[chain].append(ring_step(held, self.peers, 0, cross))

    def last(self, chain):
        return self.x if self.whole is not None else self.chains[chain][-1]

    def places(self, gate=None):
        if self.whole is not None:
            return [self.whole]
        mine = self.chains[0][1:] + self.chains[1][1:]
        held = mine
        if gate is not None:
            held = [lax.optimization_barrier((t, gate))[0] for t in mine]
        others = [swap_cores(t, self.peers) for t in [self.x] + held]
        return [t[None] for t in [self.x] + others[:1] + mine + others[1:]]


class RingScatter:
    def __init__(self, keep, give, peers):
        self.keep, self.peers, self.chips = keep, peers, peers // 2
        self.other = [swap_cores(t, peers) for t in give]
        self.held = [None, None]
        self.hop = 0

    def term(self, k):
        half = self.chips // 2
        pair = self.other[k - half][0] if k >= half else self.other[half - 1 - k][1]
        return self.keep[k] + pair.astype(F32)

    def go(self, gate=None):
        sent = []
        for way, step, count in ((0, 1, self.chips // 2), (1, -1, (self.chips - 1) // 2)):
            left = count - self.hop
            if left <= 0:
                continue
            part = self.term((-step * left) % self.chips)
            if self.held[way] is not None:
                part = part + self.held[way].astype(F32)
            part = part.astype(BF16)
            if gate is not None:
                part = lax.optimization_barrier((part, gate))[0]
            sent.append(part)
            self.held[way] = ring_step(part, self.peers, step)
        self.hop += 1
        return sent

    def total(self):
        return sum((t.astype(F32) for t in self.held if t is not None), self.term(0))


def call(body, out_shape, in_specs, scratch=(), cost=2, name=None, out_specs=None, aliases=None):
    return pl.pallas_call(
        body,
        out_shape=out_shape,
        in_specs=in_specs,
        out_specs=out_specs or jax.tree.map(lambda _: VMEM, out_shape),
        scratch_shapes=list(scratch),
        input_output_aliases=aliases or {},
        compiler_params=pltpu.CompilerParams(vmem_limit_bytes=VMEM_LIMIT),
        cost_estimate=pl.CostEstimate(flops=cost * 10**9, bytes_accessed=0, transcendentals=0),
        name=name,
    )


PLANES = 4


def put_boundary(rows, brick, a, out_ref, stage, ends):
    base = brick * ROWS
    if a in (0, 7):
        at = base if a == 0 else base + 64
        out_ref[at : at + 64, :] = rows
        return
    wide = rows.astype(F32)
    at = base + B_LINES - 16 + 16 * a
    out_ref[at : at + 16, :] = jnp.concatenate([wide[:8], wide[56:]], axis=0).astype(BF16)
    at = brick * C_ROWS + 12 * (a - 1)
    for half in range(2):
        lanes = slice(half * 128, half * 128 + 128)
        stage[half] = wide[:, lanes]
        ends[at : at + 6, lanes] = stage[half, pl.ds(8, 6, stride=8), :]
        ends[at + 6 : at + 12, lanes] = stage[half, pl.ds(15, 6, stride=8), :]


def each_brick(rows_of, bricks, out_ref, stage, ends):
    for brick in range(bricks):
        for first in range(0, 8, PLANES):
            rows = rows_of(pl.ds(brick * 512 + first * 64, PLANES * 64))
            for t in range(PLANES):
                plane = rows[t * 64 : t * 64 + 64]
                put_boundary(plane, brick, first + t, out_ref, stage.at[first + t], ends)
    out_ref[bricks * ROWS : payload_rows(bricks), :] = ends[...].astype(BF16)


def norm_body(recv, send, x_ref, gain_ref, hidden_ref, out_ref, stage, ends):
    bricks, directions = recv.shape
    gain = gain_ref[...]
    lane = lax.broadcasted_iota(jnp.int32, (1, C), 1)
    codes = jnp.zeros((1, C), jnp.int32)
    for k in range(send.shape[1]):
        codes = jnp.where(lane == k, send[0, k], codes)
    served = jnp.zeros((1, C), jnp.int32)
    for brick in range(bricks):
        for number in range(directions):
            served = jnp.where(lane == recv[brick, number], brick * directions + number + 1, served)
    row = lax.broadcasted_iota(jnp.int32, (NOTES, C), 0)
    notes = jnp.where(row == 0, codes, jnp.where(row == 1, served, 0))
    out_ref[payload_rows(bricks) :, :] = notes.astype(F32).astype(BF16)

    def rows_of(at):
        x = x_ref[at, :].astype(F32)
        inverse = lax.rsqrt(jnp.mean(x * x, axis=-1, keepdims=True) + 1e-6)
        v = x * inverse * gain
        rows = (v / (1.0 + jnp.exp(-v))).astype(BF16)
        hidden_ref[at, :] = rows
        return rows

    each_brick(rows_of, bricks, out_ref, stage, ends)


def extract_body(x_ref, out_ref, stage, ends):
    each_brick(lambda at: x_ref[at, :], x_ref.shape[0] // 512, out_ref, stage, ends)


def start_padded(own_ref, cells, halo, bricks):
    zero = jnp.zeros((8, C), F32)

    def clear(k, _):
        for b in range(10):
            cells[k * 10 + b] = zero
        for side in range(2):
            for part in range(HB // 8):
                halo[side, k, part * 8 : part * 8 + 8, :] = zero
        return 0

    lax.fori_loop(0, bricks * 10, clear, 0)

    def fill(k, _):
        plane = (k // 8) * 10 + k % 8 + 1
        rows = own_ref[pl.ds(pl.multiple_of(k * 64, 64), 64), :].astype(F32)
        for b in range(8):
            cells[plane * 10 + b + 1] = rows[b * 8 : b * 8 + 8]
        return 0

    lax.fori_loop(0, bricks * 8, fill, 0)


def add_line(ref, index, line):
    ref[index] = ref[index] + line


def pick(flag, yes, no):
    if isinstance(flag, bool):
        return yes if flag else no
    return jnp.where(flag, yes, no)


def place(kind, e, keep, place_at, source_brick, brick, share, cells, halo):
    flags = [t == -1 for t in e]
    pads = [pick(f, 0, 9) for f in flags]
    facing = pick(flags[0], 64, 0)
    start = source_brick * ROWS

    def rows(at, size):
        got = share[place_at, pl.ds(pl.multiple_of(start + at, 16), size), :].astype(F32)
        return got if keep is None else jnp.where(keep, got, 0.0)

    def half(pair, axis):
        return pick(flags[axis], pair[8:], pair[:8])

    def ends(a):
        value = None
        for number in range(cells.shape[0] // 100):
            at = cells.shape[0] // 100 * ROWS + number * C_ROWS + 12 * (a - 1)
            block = share[place_at, at // 16 * 16 : -(-(at + 12) // 16) * 16, :].astype(F32)
            block = block[at % 16 : at % 16 + 12]
            block = pick(flags[2], block[6:], block[:6])
            value = block if value is None else jnp.where(source_brick == number, block, value)
        return value if keep is None else jnp.where(keep, value, 0.0)

    def line_b(at):
        plane = rows(at, 64)
        return pick(flags[1], plane[56:], plane[:8])

    def line_c(at):
        plane = rows(at, 64)
        ends = [
            pick(flags[2], plane[8 * b + 7 : 8 * b + 8], plane[8 * b : 8 * b + 1]) for b in range(8)
        ]
        return jnp.concatenate(ends, axis=0)

    def cell(at):
        line = line_b(at)
        return pick(flags[2], line[7:8], line[0:1])

    side = pick(flags[2], 0, 1)
    base = brick * 10

    def add_halo(at, line):
        halo[side, base + at, 8:16, :] = halo[side, base + at, 8:16, :] + line

    def add_cell(at, value):
        spot = pl.ds(pick(flags[1], 7, 16), 1)
        halo[side, base + at, spot, :] = halo[side, base + at, spot, :] + value

    if kind == (1, 0, 0):
        got = rows(facing, 64)
        first = (base + pads[0]) * 10 + 1
        for b in range(8):
            add_line(cells, first + b, got[b * 8 : b * 8 + 8])
    elif kind == (0, 1, 0):
        for a in range(8):
            if a in (0, 7):
                line = line_b(0 if a == 0 else 64)
            else:
                line = half(rows(B_LINES - 16 + 16 * a, 16), 1)
            add_line(cells, (base + a + 1) * 10 + pads[1], line)
    elif kind == (0, 0, 1):
        for a in range(8):
            if a in (0, 7):
                line = line_c(0 if a == 0 else 64)
            else:
                pair = rows(B_LINES - 16 + 16 * a, 16)
                low = pick(flags[2], pair[7:8], pair[0:1])
                high = pick(flags[2], pair[15:], pair[8:9])
                line = jnp.concatenate([low, ends(a), high], axis=0)
            add_halo(a + 1, line)
    elif kind == (1, 1, 0):
        add_line(cells, (base + pads[0]) * 10 + pads[1], line_b(facing))
    elif kind == (1, 0, 1):
        add_halo(pads[0], line_c(facing))
    elif kind == (0, 1, 1):
        for a in range(8):
            if a in (0, 7):
                value = cell(0 if a == 0 else 64)
            else:
                line = half(rows(B_LINES - 16 + 16 * a, 16), 1)
                value = pick(flags[2], line[7:8], line[0:1])
            add_cell(a + 1, value)
    else:
        add_cell(pads[0], cell(facing))


def windows(cells, halo, cols, bricks, out=None, sems=None):
    row = lax.broadcasted_iota(jnp.int32, (8, C), 0)

    def step(k, _):
        shifted = [[], [], []]
        for b in range(10):
            x = cells[k * 10 + b]
            before = halo[0, k, pl.ds(b + 7, 1), :]
            after = halo[1, k, pl.ds(b + 7, 1), :]
            shifted[0].append(jnp.where(row == 0, before, pltpu.roll(x, 1, 0)))
            shifted[1].append(x)
            shifted[2].append(jnp.where(row == 7, after, pltpu.roll(x, 7, 0)))
        for j in range(3):
            for l in range(3):
                block = jnp.concatenate(shifted[l][j : j + 8], axis=0).astype(BF16)
                at = (3 * j + l) * C
                cols[k, :, at : at + C] = block
        if out is not None:
            pltpu.make_async_copy(cols.at[k], out.at[k], sems.at[k]).start()
        return 0

    lax.fori_loop(0, bricks * 10, step, 0)


def wait_windows(cols, out, sems, bricks):
    def step(k, _):
        pltpu.make_async_copy(cols.at[k], out.at[k], sems.at[k]).wait()
        return 0

    lax.fori_loop(0, bricks * 10, step, 0)


def fetch(parts, share, sems, first=0, rows=None):
    size = parts[0].shape[0]
    lines = pl.ds(first, rows or parts[0].shape[1])
    copies = [
        pltpu.make_async_copy(part.at[:, lines], share.at[pl.ds(k * size, size), lines], sems.at[k])
        for k, part in enumerate(parts)
    ]
    for copy in copies:
        copy.start()
    return copies


def weight_grad_body(slots, factor, peers, count, *refs):
    recv, table, own_ref, cot_ref = refs[:4]
    parts = refs[4 : 4 + count]
    keep_ref = refs[4 + count]
    give_refs = refs[5 + count : 5 + count + peers // 4]
    out_cols, codes_ref, served_ref = refs[-16:-13]
    cells, halo, share, cols, sums, narrow, turned, codes = refs[-13:-5]
    sems, cols_sems, codes_sem, out_sems, notes_sems = refs[-5:]
    bricks = own_ref.shape[0] // 512
    me = table[2 * peers]
    notes_copies = fetch(parts, share, notes_sems, payload_rows(bricks), NOTES)
    copies = fetch(parts, share, sems, 0, payload_rows(bricks))
    for part in range(bricks * 2):
        at = slice(part * 256, part * 256 + 256)
        turned[:, at] = cot_ref[at, :].astype(F32).T.astype(BF16)
    for copy in notes_copies:
        copy.wait()
    for k in range(peers):
        notes = share[k, payload_rows(bricks) :, :].astype(F32).astype(jnp.int32)
        codes_ref[k : k + 1, :] = notes[0:1]
        served_ref[k : k + 1, :] = notes[1:2]
    codes_copy = pltpu.make_async_copy(codes_ref, codes, codes_sem.at[0])
    codes_copy.start()
    start_padded(own_ref, cells, halo, bricks)
    codes_copy.wait()
    for copy in copies:
        copy.wait()
    for brick in range(bricks):
        for number, e in enumerate(DIRECTIONS):
            slot = recv[brick, number]
            safe = jnp.maximum(slot, 0)
            sender = safe // slots
            at = table[sender]
            code = codes[at, me * slots + safe - sender * slots]
            kind = tuple(abs(t) for t in e)
            place(kind, e, slot >= 0, at, code // 6, brick, share, cells, halo)
    windows(cells, halo, cols, bricks, out_cols, cols_sems)

    rows = 27 * C // peers
    for tap in range(27):
        i, jl = divmod(tap, 9)
        total = None
        for brick in range(bricks):
            right = cols[brick * 10 + i : brick * 10 + i + 8, :, jl * C : jl * C + C].reshape(512, C)
            left = turned[:, brick * 512 : brick * 512 + 512]
            term = jnp.dot(left, right, preferred_element_type=F32)
            total = term if total is None else total + term
        total = (total * factor).T
        start = tap * C
        while start < (tap + 1) * C:
            owner = start // rows
            stop = min((tap + 1) * C, (owner + 1) * rows)
            piece = total[start - tap * C : stop - tap * C]
            bucket = jnp.bitwise_xor(me % 2, owner % 2)
            behind = table[peers + owner // 2]
            where = slice(start - owner * rows, stop - owner * rows)
            sums[bucket, behind, where, :] = piece
            narrow[bucket, behind, where, :] = piece.astype(BF16)
            start = stop
            if stop == (owner + 1) * rows:

                @pl.when(bucket == 0)
                def _():
                    pltpu.make_async_copy(
                        sums.at[0, behind], keep_ref.at[behind], out_sems.at[0, behind]
                    ).start()

                turn = table[peers + peers // 2 + owner // 2]
                for hop, give_ref in enumerate(give_refs):

                    @pl.when((bucket == 1) & (turn // 2 == hop))
                    def _():
                        pltpu.make_async_copy(
                            narrow.at[1, behind], give_ref.at[turn % 2], out_sems.at[1, turn]
                        ).start()

    for k in range(peers // 2):
        pltpu.make_async_copy(sums.at[0, k], keep_ref.at[k], out_sems.at[0, k]).wait()
        pltpu.make_async_copy(narrow.at[1, k], give_refs[k // 2].at[k % 2], out_sems.at[1, k]).wait()
    wait_windows(cols, out_cols, cols_sems, bricks)


GROUP = 3 * C


def start_stream(cols_ref, first, cols, weight_ref, weight, sems):
    copies = []
    planes = cols.shape[0]
    for g in range(3):
        lanes = pl.ds(g * GROUP, GROUP)
        group = [
            pltpu.make_async_copy(
                cols_ref.at[pl.ds(first, planes), :, lanes], cols.at[:, :, lanes], sems.at[g, 3]
            )
        ]
        for i in range(3):
            at = pl.ds((i * 3 + g) * GROUP, GROUP)
            group.append(pltpu.make_async_copy(weight_ref.at[at], weight.at[at], sems.at[g, i]))
        copies.append(group)
    for group in copies:
        for copy in group:
            copy.start()
    return copies


def tap_sum(copies, cols, weight):
    bricks = cols.shape[0] // 10
    totals = [None] * bricks
    for g in range(3):
        for copy in copies[g]:
            copy.wait()
        for brick in range(bricks):
            for i in range(3):
                at = brick * 10 + i
                left = cols[at : at + 8, :, g * GROUP : g * GROUP + GROUP].reshape(512, GROUP)
                right = weight[(i * 3 + g) * GROUP : (i * 3 + g + 1) * GROUP, :]
                term = jnp.dot(left, right, preferred_element_type=F32)
                totals[brick] = term if totals[brick] is None else totals[brick] + term
    return totals


def mix_body(cols_ref, weight_ref, x_ref, out_ref, cols, weight, sems):
    copies = start_stream(cols_ref, 0, cols, weight_ref, weight, sems)
    for brick, total in enumerate(tap_sum(copies, cols, weight)):
        at = slice(brick * 512, brick * 512 + 512)
        out_ref[at, :] = (x_ref[at, :].astype(F32) + total).astype(BF16)


def input_grad_body(slots, peers, count, *refs):
    served, send, table, cot_ref, x_ref, gain_ref, weight_ref = refs[:7]
    parts = refs[7 : 7 + count]
    out_ref, cells, halo, cols, share, weight, heads, more, sems, weight_sem = refs[7 + count :]
    bricks = cot_ref.shape[0] // 512
    me = table[2 * peers]
    copies = fetch(parts, share, sems)
    weight_copy = pltpu.make_async_copy(weight_ref, weight, weight_sem.at[0])
    weight_copy.start()

    def no_head(k, _):
        heads[k] = -1
        return 0

    lax.fori_loop(0, bricks * 26, no_head, 0)

    def source_of(k):
        receiver = k // slots
        at = table[receiver]
        return at, served[at, me * slots + k - receiver * slots] - 1

    def sort(k, found):
        _, entry = source_of(k)
        asked = entry >= 0
        key = send[0, k] // 6 * 26 + 25 - jnp.maximum(entry, 0) % 26
        first = asked & (heads[key] < 0)
        extra = asked & jnp.logical_not(first)

        @pl.when(first)
        def _():
            heads[key] = k

        @pl.when(extra)
        def _():
            more[found] = k

        return found + jnp.where(extra, 1, 0)

    found = lax.fori_loop(0, send.shape[1], sort, 0)
    start_padded(cot_ref, cells, halo, bricks)
    for copy in copies:
        copy.wait()
    for brick in range(bricks):
        for number, e in enumerate(DIRECTIONS):
            head = heads[brick * 26 + number]
            at, entry = source_of(jnp.maximum(head, 0))
            kind = tuple(abs(t) for t in e)
            source = jnp.maximum(entry, 0) // 26
            place(kind, e, head >= 0, at, source, brick, share, cells, halo)

    def one(n, _):
        k = more[n]
        at, entry = source_of(k)
        number = 25 - entry % 26
        tap = jnp.where(number >= 13, number + 1, number)
        e = (tap // 9 - 1, (tap // 3) % 3 - 1, tap % 3 - 1)
        on = [t != 0 for t in e]
        for kind in ((1, 0, 0), (0, 1, 0), (0, 0, 1), (1, 1, 0), (1, 0, 1), (0, 1, 1), (1, 1, 1)):
            match = functools.reduce(
                jnp.logical_and, [f if w else jnp.logical_not(f) for f, w in zip(on, kind)]
            )

            @pl.when(match)
            def _():
                place(kind, e, None, at, entry // 26, send[0, k] // 6, share, cells, halo)

        return 0

    lax.fori_loop(0, found, one, 0)
    windows(cells, halo, cols, bricks)
    weight_copy.wait()
    gain = gain_ref[...]
    for brick in range(bricks):
        rows = slice(brick * 512, brick * 512 + 512)
        grad = None
        for tap in range(27):
            i, jl = divmod(tap, 9)
            first = brick * 10 + i
            left = cols[first : first + 8, :, jl * C : jl * C + C].reshape(512, C)
            right = weight[(26 - tap) * C : (27 - tap) * C, :]
            term = lax.dot_general(left, right, (((1,), (1,)), ((), ())), preferred_element_type=F32)
            grad = term if grad is None else grad + term
        x = x_ref[rows, :].astype(F32)
        inverse = lax.rsqrt(jnp.mean(x * x, axis=-1, keepdims=True) + 1e-6)
        unit = x * inverse
        v = unit * gain
        gate = 1.0 / (1.0 + jnp.exp(-v))
        grad = grad * (gate * (1.0 + v * (1.0 - gate))) * gain
        grad = inverse * (grad - unit * jnp.mean(grad * unit, axis=-1, keepdims=True))
        out_ref[rows, :] = (cot_ref[rows, :].astype(F32) + grad).astype(BF16)


def local(features, norm_gain, conv_weight, recv_slot, send_face, cotangent):
    channels = features.shape[1]
    per_device = features.shape[0]
    bricks = per_device // 512
    peers = lax.axis_size("morton")
    slots = send_face.shape[1] // peers
    factor = 1.0 / math.sqrt(peers * per_device)
    gain = norm_gain.reshape(1, channels)
    sds = jax.ShapeDtypeStruct
    share_rows = payload_rows(bricks)
    stage = [
        pltpu.VMEM((8, 2, 64, 128), F32),
        pltpu.VMEM((share_rows - bricks * ROWS, channels), F32),
    ]

    def padded(n):
        return [
            pltpu.VMEM((n * 100, 8, channels), F32),
            pltpu.VMEM((2, n * 10, HB, channels), F32),
        ]

    def cols_shape(n):
        return (n * 10, 64, 9 * channels)


    table = jnp.asarray(ring_tables(peers))[lax.axis_index("morton")]

    hidden, share = call(
        norm_body,
        (sds((per_device, channels), BF16), sds((share_rows + NOTES, channels), BF16)),
        [SMEM, SMEM, VMEM, VMEM],
        stage,
        name="norm",
    )(recv_slot, send_face, features, gain)
    hidden_ring = RingGather(share, peers)
    cot_share = call(
        extract_body,
        sds((share_rows, channels), BF16),
        [VMEM],
        stage,
        name="extract",
    )(cotangent)
    hidden_ring.go(0)
    hidden_ring.go(1)
    hidden_ring.go(0, (cot_share, table))
    hidden_ring.go(1)
    hidden_ring.go(0)
    hidden_ring.go(1)
    hidden_ring.go(0)
    hidden_parts = hidden_ring.places()

    cot_ring = RingGather(cot_share, peers)
    cot_ring.go(0, hidden_ring.last(1))
    cot_ring.go(1, hidden_ring.last(0))

    count = len(hidden_parts)
    rows = 27 * channels // peers
    chips = peers // 2
    keep, *give, cols, _, served = call(
        functools.partial(weight_grad_body, slots, factor, peers, count),
        (
            sds((chips, rows, channels), F32),
            *[sds((2, rows, channels), BF16)] * (chips // 2),
            sds(cols_shape(bricks), BF16),
            sds((peers, channels), jnp.int32),
            sds((peers, channels), jnp.int32),
        ),
        [SMEM] * 2 + [VMEM] * 2 + [HBM] * count,
        padded(bricks)
        + [
            pltpu.VMEM((peers, share_rows + NOTES, channels), BF16),
            pltpu.VMEM(cols_shape(bricks), BF16),
            pltpu.VMEM((2, chips, rows, channels), F32),
            pltpu.VMEM((2, chips, rows, channels), BF16),
            pltpu.VMEM((channels, per_device), BF16),
            pltpu.SMEM((peers, channels), jnp.int32),
            pltpu.SemaphoreType.DMA((count,)),
            pltpu.SemaphoreType.DMA((bricks * 10,)),
            pltpu.SemaphoreType.DMA((1,)),
            pltpu.SemaphoreType.DMA((2, chips)),
            pltpu.SemaphoreType.DMA((count,)),
        ],
        cost=9,
        name="weight_grad",
        out_specs=(*[HBM] * (2 + chips // 2), VMEM, VMEM),
    )(recv_slot, table, hidden, cotangent, *hidden_parts)

    first = (cot_ring.last(0), cot_ring.last(1))
    give = [lax.optimization_barrier((t, first))[0] for t in give]
    sums_ring = RingScatter(keep, give, peers)
    sent = sums_ring.go()
    cot_ring.go(0, cols)
    cot_ring.go(1, cols)
    second = (cot_ring.last(0), cot_ring.last(1))
    mix_cols = lax.optimization_barrier((cols, sent))[0]
    weight_scratch = [
        pltpu.VMEM((27 * channels, channels), BF16),
        pltpu.SemaphoreType.DMA((3, 4)),
    ]
    mixed = call(
        mix_body,
        sds((per_device, channels), BF16),
        [HBM, HBM, VMEM],
        [pltpu.VMEM(cols_shape(bricks), BF16)] + weight_scratch,
        cost=6,
        name="mix",
    )(mix_cols, conv_weight, features)
    sent = sums_ring.go((second, mixed))
    cot_ring.go(0)
    cot_ring.go(1)
    third = (cot_ring.last(0), cot_ring.last(1))
    sums_ring.go(third)
    cot_ring.go(0)
    sent = sums_ring.go(cot_ring.last(0))
    cot_parts = cot_ring.places(cols)
    served = lax.optimization_barrier((served, sent))[0]

    grad_features = call(
        functools.partial(input_grad_body, slots, peers, count),
        sds((per_device, channels), BF16),
        [SMEM] * 3 + [VMEM] * 3 + [HBM] * (1 + count),
        padded(bricks)
        + [
            pltpu.VMEM(cols_shape(bricks), BF16),
            pltpu.VMEM((peers, share_rows, channels), BF16),
            weight_scratch[0],
            pltpu.SMEM((bricks * 26,), jnp.int32),
            pltpu.SMEM((peers * slots,), jnp.int32),
            pltpu.SemaphoreType.DMA((count,)),
            pltpu.SemaphoreType.DMA((1,)),
        ],
        cost=13,
        name="input_grad",
    )(served, send_face, table, cotangent, features, gain, conv_weight, *cot_parts)
    for _ in range(chips // 2 - 4):
        sums_ring.go()
    return (mixed, grad_features, sums_ring.total())


def solution(mesh):
    rows = P(("groups", "morton"), None)
    return jax.shard_map(
        local,
        mesh=mesh,
        in_specs=(rows, P(), P(), rows, rows, rows),
        out_specs=(rows, rows, rows),
        check_vma=False,
    )
```

```python
import functools
import math

import jax
import jax.numpy as jnp
import numpy as np
from jax import lax
from jax.experimental import pallas as pl
from jax.experimental.pallas import tpu as pltpu
from jax.sharding import PartitionSpec as P

F32 = jnp.float32
BF16 = jnp.bfloat16
C = 256
B_LINES = 128
ROWS = 224
C_ROWS = 72
NOTES = 16


def payload_rows(bricks):
    return -(-bricks * (ROWS + C_ROWS) // 16) * 16


HB = 24
VMEM_LIMIT = 40 * 1024 * 1024
DIRECTIONS = [
    (i, j, l)
    for i in (-1, 0, 1)
    for j in (-1, 0, 1)
    for l in (-1, 0, 1)
    if (i, j, l) != (0, 0, 0)
]

VMEM = pl.BlockSpec(memory_space=pltpu.VMEM)
SMEM = pl.BlockSpec(memory_space=pltpu.SMEM)
ANY = pl.BlockSpec(memory_space=pl.ANY)
HBM = pl.BlockSpec(memory_space=pltpu.HBM)


def ring_order(chips):
    if chips == 8:
        return [0, 2, 4, 6, 7, 5, 3, 1]
    return list(range(chips))


def ring_tables(peers):
    chips = peers // 2
    spot = np.argsort(np.array(ring_order(chips)))
    device = np.arange(peers)
    behind = (spot[device // 2][:, None] - spot[None, :]) % chips
    half = chips // 2
    turn = np.where(behind >= half, 2 * (behind - half), 2 * (half - 1 - behind) + 1)
    place_of = np.broadcast_to(device, (peers, peers)).copy()
    if chips <= 8:
        for me in range(peers):
            for other in range(peers):
                away = behind[me, other // 2] if me % 2 == 0 else -behind[me, other // 2] % chips
                same = me % 2 == other % 2
                if away == 0:
                    place = 0 if same else 1
                elif away < half or (away == half and same):
                    place = 1 + away if same else 1 + half + away
                else:
                    away = chips - away
                    place = half + (away if not same else half + away) + half
                place_of[me, other] = place
    return np.concatenate([place_of, behind, turn, device[:, None]], axis=1).astype(np.int32)


def ring_step(x, peers, step, cross=0):
    order = ring_order(peers // 2)
    pairs = [
        (2 * order[i] + (core ^ cross), 2 * order[(i + (step or 1 - 2 * core)) % len(order)] + core)
        for i in range(len(order))
        for core in range(2)
    ]
    return lax.ppermute(x, "morton", pairs)


def swap_cores(x, peers):
    return lax.ppermute(x, "morton", [(m, m ^ 1) for m in range(peers)])


class RingGather:
    def __init__(self, x, peers):
        self.x, self.peers, self.chips = x, peers, peers // 2
        self.whole = None
        if self.chips > 8:
            self.whole = lax.all_gather(x[None], "morton", axis=0, tiled=True)
            return
        self.chains = ([x], [x])

    def go(self, chain, gate=None):
        if self.whole is not None or len(self.chains[chain]) > self.chips // 2 - chain:
            return
        held = self.chains[chain][-1]
        if gate is not None:
            held = lax.optimization_barrier((held, gate))[0]
        cross = int(chain == 1 and len(self.chains[chain]) == 1)
        self.chains[chain].append(ring_step(held, self.peers, 0, cross))

    def last(self, chain):
        return self.x if self.whole is not None else self.chains[chain][-1]

    def places(self, gate=None):
        if self.whole is not None:
            return [self.whole]
        mine = self.chains[0][1:] + self.chains[1][1:]
        held = mine
        if gate is not None:
            held = [lax.optimization_barrier((t, gate))[0] for t in mine]
        others = [swap_cores(t, self.peers) for t in [self.x] + held]
        return [t[None] for t in [self.x] + others[:1] + mine + others[1:]]


class RingScatter:
    def __init__(self, keep, give, peers):
        self.keep, self.peers, self.chips = keep, peers, peers // 2
        self.other = [swap_cores(t, peers) for t in give]
        self.held = [None, None]
        self.hop = 0

    def term(self, k):
        half = self.chips // 2
        pair = self.other[k - half][0] if k >= half else self.other[half - 1 - k][1]
        return self.keep[k] + pair.astype(F32)

    def go(self, gate=None):
        sent = []
        for way, step, count in ((0, 1, self.chips // 2), (1, -1, (self.chips - 1) // 2)):
            left = count - self.hop
            if left <= 0:
                continue
            part = self.term((-step * left) % self.chips)
            if self.held[way] is not None:
                part = part + self.held[way].astype(F32)
            part = part.astype(BF16)
            if gate is not None:
                part = lax.optimization_barrier((part, gate))[0]
            sent.append(part)
            self.held[way] = ring_step(part, self.peers, step)
        self.hop += 1
        return sent

    def total(self):
        return sum((t.astype(F32) for t in self.held if t is not None), self.term(0))


def call(body, out_shape, in_specs, scratch=(), cost=2, name=None, out_specs=None, aliases=None):
    return pl.pallas_call(
        body,
        out_shape=out_shape,
        in_specs=in_specs,
        out_specs=out_specs or jax.tree.map(lambda _: VMEM, out_shape),
        scratch_shapes=list(scratch),
        input_output_aliases=aliases or {},
        compiler_params=pltpu.CompilerParams(vmem_limit_bytes=VMEM_LIMIT),
        cost_estimate=pl.CostEstimate(flops=cost * 10**9, bytes_accessed=0, transcendentals=0),
        name=name,
    )


PLANES = 4


def put_boundary(rows, brick, a, out_ref, stage, ends):
    base = brick * ROWS
    if a in (0, 7):
        at = base if a == 0 else base + 64
        out_ref[at : at + 64, :] = rows
        return
    wide = rows.astype(F32)
    at = base + B_LINES - 16 + 16 * a
    out_ref[at : at + 16, :] = jnp.concatenate([wide[:8], wide[56:]], axis=0).astype(BF16)
    at = brick * C_ROWS + 12 * (a - 1)
    for half in range(2):
        lanes = slice(half * 128, half * 128 + 128)
        stage[half] = wide[:, lanes]
        ends[at : at + 6, lanes] = stage[half, pl.ds(8, 6, stride=8), :]
        ends[at + 6 : at + 12, lanes] = stage[half, pl.ds(15, 6, stride=8), :]


def each_brick(rows_of, bricks, out_ref, stage, ends):
    for brick in range(bricks):
        for first in range(0, 8, PLANES):
            rows = rows_of(pl.ds(brick * 512 + first * 64, PLANES * 64))
            for t in range(PLANES):
                plane = rows[t * 64 : t * 64 + 64]
                put_boundary(plane, brick, first + t, out_ref, stage.at[first + t], ends)
    out_ref[bricks * ROWS : payload_rows(bricks), :] = ends[...].astype(BF16)


def norm_body(recv, send, x_ref, gain_ref, hidden_ref, out_ref, stage, ends):
    bricks, directions = recv.shape
    gain = gain_ref[...]
    lane = lax.broadcasted_iota(jnp.int32, (1, C), 1)
    codes = jnp.zeros((1, C), jnp.int32)
    for k in range(send.shape[1]):
        codes = jnp.where(lane == k, send[0, k], codes)
    served = jnp.zeros((1, C), jnp.int32)
    for brick in range(bricks):
        for number in range(directions):
            served = jnp.where(lane == recv[brick, number], brick * directions + number + 1, served)
    row = lax.broadcasted_iota(jnp.int32, (NOTES, C), 0)
    notes = jnp.where(row == 0, codes, jnp.where(row == 1, served, 0))
    out_ref[payload_rows(bricks) :, :] = notes.astype(F32).astype(BF16)

    def rows_of(at):
        x = x_ref[at, :].astype(F32)
        inverse = lax.rsqrt(jnp.mean(x * x, axis=-1, keepdims=True) + 1e-6)
        v = x * inverse * gain
        rows = (v / (1.0 + jnp.exp(-v))).astype(BF16)
        hidden_ref[at, :] = rows
        return rows

    each_brick(rows_of, bricks, out_ref, stage, ends)


def extract_body(x_ref, out_ref, stage, ends):
    each_brick(lambda at: x_ref[at, :], x_ref.shape[0] // 512, out_ref, stage, ends)


def start_padded(own_ref, cells, halo, bricks):
    zero = jnp.zeros((8, C), F32)

    def clear(k, _):
        for b in range(10):
            cells[k * 10 + b] = zero
        for side in range(2):
            for part in range(HB // 8):
                halo[side, k, part * 8 : part * 8 + 8, :] = zero
        return 0

    lax.fori_loop(0, bricks * 10, clear, 0)

    def fill(k, _):
        plane = (k // 8) * 10 + k % 8 + 1
        rows = own_ref[pl.ds(pl.multiple_of(k * 64, 64), 64), :].astype(F32)
        for b in range(8):
            cells[plane * 10 + b + 1] = rows[b * 8 : b * 8 + 8]
        return 0

    lax.fori_loop(0, bricks * 8, fill, 0)


def add_line(ref, index, line):
    ref[index] = ref[index] + line


def pick(flag, yes, no):
    if isinstance(flag, bool):
        return yes if flag else no
    return jnp.where(flag, yes, no)


def place(kind, e, keep, place_at, source_brick, brick, share, cells, halo):
    flags = [t == -1 for t in e]
    pads = [pick(f, 0, 9) for f in flags]
    facing = pick(flags[0], 64, 0)
    start = source_brick * ROWS

    def rows(at, size):
        got = share[place_at, pl.ds(pl.multiple_of(start + at, 16), size), :].astype(F32)
        return got if keep is None else jnp.where(keep, got, 0.0)

    def half(pair, axis):
        return pick(flags[axis], pair[8:], pair[:8])

    def ends(a):
        value = None
        for number in range(cells.shape[0] // 100):
            at = cells.shape[0] // 100 * ROWS + number * C_ROWS + 12 * (a - 1)
            block = share[place_at, at // 16 * 16 : -(-(at + 12) // 16) * 16, :].astype(F32)
            block = block[at % 16 : at % 16 + 12]
            block = pick(flags[2], block[6:], block[:6])
            value = block if value is None else jnp.where(source_brick == number, block, value)
        return value if keep is None else jnp.where(keep, value, 0.0)

    def line_b(at):
        plane = rows(at, 64)
        return pick(flags[1], plane[56:], plane[:8])

    def line_c(at):
        plane = rows(at, 64)
        ends = [
            pick(flags[2], plane[8 * b + 7 : 8 * b + 8], plane[8 * b : 8 * b + 1]) for b in range(8)
        ]
        return jnp.concatenate(ends, axis=0)

    def cell(at):
        line = line_b(at)
        return pick(flags[2], line[7:8], line[0:1])

    side = pick(flags[2], 0, 1)
    base = brick * 10

    def add_halo(at, line):
        halo[side, base + at, 8:16, :] = halo[side, base + at, 8:16, :] + line

    def add_cell(at, value):
        spot = pl.ds(pick(flags[1], 7, 16), 1)
        halo[side, base + at, spot, :] = halo[side, base + at, spot, :] + value

    if kind == (1, 0, 0):
        got = rows(facing, 64)
        first = (base + pads[0]) * 10 + 1
        for b in range(8):
            add_line(cells, first + b, got[b * 8 : b * 8 + 8])
    elif kind == (0, 1, 0):
        for a in range(8):
            if a in (0, 7):
                line = line_b(0 if a == 0 else 64)
            else:
                line = half(rows(B_LINES - 16 + 16 * a, 16), 1)
            add_line(cells, (base + a + 1) * 10 + pads[1], line)
    elif kind == (0, 0, 1):
        for a in range(8):
            if a in (0, 7):
                line = line_c(0 if a == 0 else 64)
            else:
                pair = rows(B_LINES - 16 + 16 * a, 16)
                low = pick(flags[2], pair[7:8], pair[0:1])
                high = pick(flags[2], pair[15:], pair[8:9])
                line = jnp.concatenate([low, ends(a), high], axis=0)
            add_halo(a + 1, line)
    elif kind == (1, 1, 0):
        add_line(cells, (base + pads[0]) * 10 + pads[1], line_b(facing))
    elif kind == (1, 0, 1):
        add_halo(pads[0], line_c(facing))
    elif kind == (0, 1, 1):
        for a in range(8):
            if a in (0, 7):
                value = cell(0 if a == 0 else 64)
            else:
                line = half(rows(B_LINES - 16 + 16 * a, 16), 1)
                value = pick(flags[2], line[7:8], line[0:1])
            add_cell(a + 1, value)
    else:
        add_cell(pads[0], cell(facing))


def windows(cells, halo, cols, bricks, out=None, sems=None):
    row = lax.broadcasted_iota(jnp.int32, (8, C), 0)

    def step(k, _):
        shifted = [[], [], []]
        for b in range(10):
            x = cells[k * 10 + b]
            before = halo[0, k, pl.ds(b + 7, 1), :]
            after = halo[1, k, pl.ds(b + 7, 1), :]
            shifted[0].append(jnp.where(row == 0, before, pltpu.roll(x, 1, 0)))
            shifted[1].append(x)
            shifted[2].append(jnp.where(row == 7, after, pltpu.roll(x, 7, 0)))
        for j in range(3):
            for l in range(3):
                block = jnp.concatenate(shifted[l][j : j + 8], axis=0).astype(BF16)
                at = (3 * j + l) * C
                cols[k, :, at : at + C] = block
        if out is not None:
            pltpu.make_async_copy(cols.at[k], out.at[k], sems.at[k]).start()
        return 0

    lax.fori_loop(0, bricks * 10, step, 0)


def wait_windows(cols, out, sems, bricks):
    def step(k, _):
        pltpu.make_async_copy(cols.at[k], out.at[k], sems.at[k]).wait()
        return 0

    lax.fori_loop(0, bricks * 10, step, 0)


def fetch(parts, share, sems, first=0, rows=None):
    size = parts[0].shape[0]
    lines = pl.ds(first, rows or parts[0].shape[1])
    copies = [
        pltpu.make_async_copy(part.at[:, lines], share.at[pl.ds(k * size, size), lines], sems.at[k])
        for k, part in enumerate(parts)
    ]
    for copy in copies:
        copy.start()
    return copies


def weight_grad_body(slots, factor, peers, count, *refs):
    recv, table, own_ref, cot_ref = refs[:4]
    parts = refs[4 : 4 + count]
    keep_ref = refs[4 + count]
    give_refs = refs[5 + count : 5 + count + peers // 4]
    out_cols, codes_ref, served_ref = refs[-16:-13]
    cells, halo, share, cols, sums, narrow, turned, codes = refs[-13:-5]
    sems, cols_sems, codes_sem, out_sems, notes_sems = refs[-5:]
    bricks = own_ref.shape[0] // 512
    me = table[2 * peers]
    notes_copies = fetch(parts, share, notes_sems, payload_rows(bricks), NOTES)
    copies = fetch(parts, share, sems, 0, payload_rows(bricks))
    for part in range(bricks * 2):
        at = slice(part * 256, part * 256 + 256)
        turned[:, at] = cot_ref[at, :].astype(F32).T.astype(BF16)
    for copy in notes_copies:
        copy.wait()
    for k in range(peers):
        notes = share[k, payload_rows(bricks) :, :].astype(F32).astype(jnp.int32)
        codes_ref[k : k + 1, :] = notes[0:1]
        served_ref[k : k + 1, :] = notes[1:2]
    codes_copy = pltpu.make_async_copy(codes_ref, codes, codes_sem.at[0])
    codes_copy.start()
    start_padded(own_ref, cells, halo, bricks)
    codes_copy.wait()
    for copy in copies:
        copy.wait()
    for brick in range(bricks):
        for number, e in enumerate(DIRECTIONS):
            slot = recv[brick, number]
            safe = jnp.maximum(slot, 0)
            sender = safe // slots
            at = table[sender]
            code = codes[at, me * slots + safe - sender * slots]
            kind = tuple(abs(t) for t in e)
            place(kind, e, slot >= 0, at, code // 6, brick, share, cells, halo)
    windows(cells, halo, cols, bricks, out_cols, cols_sems)

    rows = 27 * C // peers
    for tap in range(27):
        i, jl = divmod(tap, 9)
        total = None
        for brick in range(bricks):
            right = cols[brick * 10 + i : brick * 10 + i + 8, :, jl * C : jl * C + C].reshape(512, C)
            left = turned[:, brick * 512 : brick * 512 + 512]
            term = jnp.dot(left, right, preferred_element_type=F32)
            total = term if total is None else total + term
        total = (total * factor).T
        start = tap * C
        while start < (tap + 1) * C:
            owner = start // rows
            stop = min((tap + 1) * C, (owner + 1) * rows)
            piece = total[start - tap * C : stop - tap * C]
            bucket = jnp.bitwise_xor(me % 2, owner % 2)
            behind = table[peers + owner // 2]
            where = slice(start - owner * rows, stop - owner * rows)
            sums[bucket, behind, where, :] = piece
            narrow[bucket, behind, where, :] = piece.astype(BF16)
            start = stop
            if stop == (owner + 1) * rows:

                @pl.when(bucket == 0)
                def _():
                    pltpu.make_async_copy(
                        sums.at[0, behind], keep_ref.at[behind], out_sems.at[0, behind]
                    ).start()

                turn = table[peers + peers // 2 + owner // 2]
                for hop, give_ref in enumerate(give_refs):

                    @pl.when((bucket == 1) & (turn // 2 == hop))
                    def _():
                        pltpu.make_async_copy(
                            narrow.at[1, behind], give_ref.at[turn % 2], out_sems.at[1, turn]
                        ).start()

    for k in range(peers // 2):
        pltpu.make_async_copy(sums.at[0, k], keep_ref.at[k], out_sems.at[0, k]).wait()
        pltpu.make_async_copy(narrow.at[1, k], give_refs[k // 2].at[k % 2], out_sems.at[1, k]).wait()
    wait_windows(cols, out_cols, cols_sems, bricks)


GROUP = 3 * C


def start_stream(cols_ref, first, cols, weight_ref, weight, sems):
    copies = []
    planes = cols.shape[0]
    for g in range(3):
        lanes = pl.ds(g * GROUP, GROUP)
        group = [
            pltpu.make_async_copy(
                cols_ref.at[pl.ds(first, planes), :, lanes], cols.at[:, :, lanes], sems.at[g, 3]
            )
        ]
        for i in range(3):
            at = pl.ds((i * 3 + g) * GROUP, GROUP)
            group.append(pltpu.make_async_copy(weight_ref.at[at], weight.at[at], sems.at[g, i]))
        copies.append(group)
    for group in copies:
        for copy in group:
            copy.start()
    return copies


def tap_sum(copies, cols, weight):
    bricks = cols.shape[0] // 10
    totals = [None] * bricks
    for g in range(3):
        for copy in copies[g]:
            copy.wait()
        for brick in range(bricks):
            for i in range(3):
                at = brick * 10 + i
                left = cols[at : at + 8, :, g * GROUP : g * GROUP + GROUP].reshape(512, GROUP)
                right = weight[(i * 3 + g) * GROUP : (i * 3 + g + 1) * GROUP, :]
                term = jnp.dot(left, right, preferred_element_type=F32)
                totals[brick] = term if totals[brick] is None else totals[brick] + term
    return totals


def mix_body(cols_ref, weight_ref, x_ref, out_ref, cols, weight, sems):
    copies = start_stream(cols_ref, 0, cols, weight_ref, weight, sems)
    for brick, total in enumerate(tap_sum(copies, cols, weight)):
        at = slice(brick * 512, brick * 512 + 512)
        out_ref[at, :] = (x_ref[at, :].astype(F32) + total).astype(BF16)


def input_grad_body(slots, peers, count, *refs):
    served, send, table, cot_ref, x_ref, gain_ref, weight_ref = refs[:7]
    parts = refs[7 : 7 + count]
    out_ref, cells, halo, cols, share, weight, heads, more, sems, weight_sem = refs[7 + count :]
    bricks = cot_ref.shape[0] // 512
    me = table[2 * peers]
    copies = fetch(parts, share, sems)
    weight_copy = pltpu.make_async_copy(weight_ref, weight, weight_sem.at[0])
    weight_copy.start()

    def no_head(k, _):
        heads[k] = -1
        return 0

    lax.fori_loop(0, bricks * 26, no_head, 0)

    def source_of(k):
        receiver = k // slots
        at = table[receiver]
        return at, served[at, me * slots + k - receiver * slots] - 1

    def sort(k, found):
        _, entry = source_of(k)
        asked = entry >= 0
        key = send[0, k] // 6 * 26 + 25 - jnp.maximum(entry, 0) % 26
        first = asked & (heads[key] < 0)
        extra = asked & jnp.logical_not(first)

        @pl.when(first)
        def _():
            heads[key] = k

        @pl.when(extra)
        def _():
            more[found] = k

        return found + jnp.where(extra, 1, 0)

    found = lax.fori_loop(0, send.shape[1], sort, 0)
    start_padded(cot_ref, cells, halo, bricks)
    for copy in copies:
        copy.wait()
    for brick in range(bricks):
        for number, e in enumerate(DIRECTIONS):
            head = heads[brick * 26 + number]
            at, entry = source_of(jnp.maximum(head, 0))
            kind = tuple(abs(t) for t in e)
            source = jnp.maximum(entry, 0) // 26
            place(kind, e, head >= 0, at, source, brick, share, cells, halo)

    def one(n, _):
        k = more[n]
        at, entry = source_of(k)
        number = 25 - entry % 26
        tap = jnp.where(number >= 13, number + 1, number)
        e = (tap // 9 - 1, (tap // 3) % 3 - 1, tap % 3 - 1)
        on = [t != 0 for t in e]
        for kind in ((1, 0, 0), (0, 1, 0), (0, 0, 1), (1, 1, 0), (1, 0, 1), (0, 1, 1), (1, 1, 1)):
            match = functools.reduce(
                jnp.logical_and, [f if w else jnp.logical_not(f) for f, w in zip(on, kind)]
            )

            @pl.when(match)
            def _():
                place(kind, e, None, at, entry // 26, send[0, k] // 6, share, cells, halo)

        return 0

    lax.fori_loop(0, found, one, 0)
    windows(cells, halo, cols, bricks)
    weight_copy.wait()
    gain = gain_ref[...]
    for brick in range(bricks):
        rows = slice(brick * 512, brick * 512 + 512)
        grad = None
        for tap in range(27):
            i, jl = divmod(tap, 9)
            first = brick * 10 + i
            left = cols[first : first + 8, :, jl * C : jl * C + C].reshape(512, C)
            right = weight[(26 - tap) * C : (27 - tap) * C, :]
            term = lax.dot_general(left, right, (((1,), (1,)), ((), ())), preferred_element_type=F32)
            grad = term if grad is None else grad + term
        x = x_ref[rows, :].astype(F32)
        inverse = lax.rsqrt(jnp.mean(x * x, axis=-1, keepdims=True) + 1e-6)
        unit = x * inverse
        v = unit * gain
        gate = 1.0 / (1.0 + jnp.exp(-v))
        grad = grad * (gate * (1.0 + v * (1.0 - gate))) * gain
        grad = inverse * (grad - unit * jnp.mean(grad * unit, axis=-1, keepdims=True))
        out_ref[rows, :] = (cot_ref[rows, :].astype(F32) + grad).astype(BF16)


def local(features, norm_gain, conv_weight, recv_slot, send_face, cotangent):
    channels = features.shape[1]
    per_device = features.shape[0]
    bricks = per_device // 512
    peers = lax.axis_size("morton")
    slots = send_face.shape[1] // peers
    factor = 1.0 / math.sqrt(peers * per_device)
    gain = norm_gain.reshape(1, channels)
    sds = jax.ShapeDtypeStruct
    share_rows = payload_rows(bricks)
    stage = [
        pltpu.VMEM((8, 2, 64, 128), F32),
        pltpu.VMEM((share_rows - bricks * ROWS, channels), F32),
    ]

    def padded(n):
        return [
            pltpu.VMEM((n * 100, 8, channels), F32),
            pltpu.VMEM((2, n * 10, HB, channels), F32),
        ]

    def cols_shape(n):
        return (n * 10, 64, 9 * channels)


    table = jnp.asarray(ring_tables(peers))[lax.axis_index("morton")]

    hidden, share = call(
        norm_body,
        (sds((per_device, channels), BF16), sds((share_rows + NOTES, channels), BF16)),
        [SMEM, SMEM, VMEM, VMEM],
        stage,
        name="norm",
    )(recv_slot, send_face, features, gain)
    hidden_ring = RingGather(share, peers)
    cot_share = call(
        extract_body,
        sds((share_rows, channels), BF16),
        [VMEM],
        stage,
        name="extract",
    )(cotangent)
    hidden_ring.go(0)
    hidden_ring.go(1)
    hidden_ring.go(0, cot_share)
    hidden_ring.go(1)
    hidden_ring.go(0, table)
    hidden_ring.go(1)
    hidden_ring.go(0)
    hidden_parts = hidden_ring.places()

    cot_ring = RingGather(cot_share, peers)
    cot_ring.go(0, hidden_ring.last(1))
    cot_ring.go(1, hidden_ring.last(0))

    count = len(hidden_parts)
    rows = 27 * channels // peers
    chips = peers // 2
    keep, *give, cols, _, served = call(
        functools.partial(weight_grad_body, slots, factor, peers, count),
        (
            sds((chips, rows, channels), F32),
            *[sds((2, rows, channels), BF16)] * (chips // 2),
            sds(cols_shape(bricks), BF16),
            sds((peers, channels), jnp.int32),
            sds((peers, channels), jnp.int32),
        ),
        [SMEM] * 2 + [VMEM] * 2 + [HBM] * count,
        padded(bricks)
        + [
            pltpu.VMEM((peers, share_rows + NOTES, channels), BF16),
            pltpu.VMEM(cols_shape(bricks), BF16),
            pltpu.VMEM((2, chips, rows, channels), F32),
            pltpu.VMEM((2, chips, rows, channels), BF16),
            pltpu.VMEM((channels, per_device), BF16),
            pltpu.SMEM((peers, channels), jnp.int32),
            pltpu.SemaphoreType.DMA((count,)),
            pltpu.SemaphoreType.DMA((bricks * 10,)),
            pltpu.SemaphoreType.DMA((1,)),
            pltpu.SemaphoreType.DMA((2, chips)),
            pltpu.SemaphoreType.DMA((count,)),
        ],
        cost=9,
        name="weight_grad",
        out_specs=(*[HBM] * (2 + chips // 2), VMEM, VMEM),
    )(recv_slot, table, hidden, cotangent, *hidden_parts)

    first = (cot_ring.last(0), cot_ring.last(1))
    give = [lax.optimization_barrier((t, first))[0] for t in give]
    sums_ring = RingScatter(keep, give, peers)
    sent = sums_ring.go()
    cot_ring.go(0, cols)
    cot_ring.go(1, cols)
    second = (cot_ring.last(0), cot_ring.last(1))
    mix_cols = lax.optimization_barrier((cols, sent))[0]
    weight_scratch = [
        pltpu.VMEM((27 * channels, channels), BF16),
        pltpu.SemaphoreType.DMA((3, 4)),
    ]
    mixed = call(
        mix_body,
        sds((per_device, channels), BF16),
        [HBM, HBM, VMEM],
        [pltpu.VMEM(cols_shape(bricks), BF16)] + weight_scratch,
        cost=6,
        name="mix",
    )(mix_cols, conv_weight, features)
    sent = sums_ring.go((second, mixed))
    cot_ring.go(0)
    cot_ring.go(1)
    third = (cot_ring.last(0), cot_ring.last(1))
    sums_ring.go(third)
    cot_ring.go(0)
    sent = sums_ring.go(cot_ring.last(0))
    cot_parts = cot_ring.places(cols)
    served = lax.optimization_barrier((served, sent))[0]

    grad_features = call(
        functools.partial(input_grad_body, slots, peers, count),
        sds((per_device, channels), BF16),
        [SMEM] * 3 + [VMEM] * 3 + [HBM] * (1 + count),
        padded(bricks)
        + [
            pltpu.VMEM(cols_shape(bricks), BF16),
            pltpu.VMEM((peers, share_rows, channels), BF16),
            weight_scratch[0],
            pltpu.SMEM((bricks * 26,), jnp.int32),
            pltpu.SMEM((peers * slots,), jnp.int32),
            pltpu.SemaphoreType.DMA((count,)),
            pltpu.SemaphoreType.DMA((1,)),
        ],
        cost=13,
        name="input_grad",
    )(served, send_face, table, cotangent, features, gain, conv_weight, *cot_parts)
    for _ in range(chips // 2 - 4):
        sums_ring.go()
    return (mixed, grad_features, sums_ring.total())


def solution(mesh):
    rows = P(("groups", "morton"), None)
    return jax.shard_map(
        local,
        mesh=mesh,
        in_specs=(rows, P(), P(), rows, rows, rows),
        out_specs=(rows, rows, rows),
        check_vma=False,
    )
```

```python
import functools
import math

import jax
import jax.numpy as jnp
import numpy as np
from jax import lax
from jax.experimental import pallas as pl
from jax.experimental.pallas import tpu as pltpu
from jax.sharding import PartitionSpec as P

F32 = jnp.float32
BF16 = jnp.bfloat16
C = 256
B_LINES = 128
ROWS = 224
C_ROWS = 72
NOTES = 16


def payload_rows(bricks):
    return -(-bricks * (ROWS + C_ROWS) // 16) * 16


HB = 24
VMEM_LIMIT = 52 * 1024 * 1024
DIRECTIONS = [
    (i, j, l)
    for i in (-1, 0, 1)
    for j in (-1, 0, 1)
    for l in (-1, 0, 1)
    if (i, j, l) != (0, 0, 0)
]

VMEM = pl.BlockSpec(memory_space=pltpu.VMEM)
SMEM = pl.BlockSpec(memory_space=pltpu.SMEM)
ANY = pl.BlockSpec(memory_space=pl.ANY)
HBM = pl.BlockSpec(memory_space=pltpu.HBM)


def ring_order(chips):
    if chips == 8:
        return [0, 2, 4, 6, 7, 5, 3, 1]
    return list(range(chips))


def ring_tables(peers):
    chips = peers // 2
    spot = np.argsort(np.array(ring_order(chips)))
    device = np.arange(peers)
    behind = (spot[device // 2][:, None] - spot[None, :]) % chips
    half = chips // 2
    turn = np.where(behind >= half, 2 * (behind - half), 2 * (half - 1 - behind) + 1)
    place_of = np.broadcast_to(device, (peers, peers)).copy()
    if chips <= 8:
        for me in range(peers):
            for other in range(peers):
                away = behind[me, other // 2] if me % 2 == 0 else -behind[me, other // 2] % chips
                same = me % 2 == other % 2
                if away == 0:
                    place = 0 if same else 1
                elif away < half or (away == half and same):
                    place = 1 + away if same else 1 + half + away
                else:
                    away = chips - away
                    place = half + (away if not same else half + away) + half
                place_of[me, other] = place
    return np.concatenate([place_of, behind, turn, device[:, None]], axis=1).astype(np.int32)


def ring_step(x, peers, step, cross=0):
    order = ring_order(peers // 2)
    pairs = [
        (2 * order[i] + (core ^ cross), 2 * order[(i + (step or 1 - 2 * core)) % len(order)] + core)
        for i in range(len(order))
        for core in range(2)
    ]
    return lax.ppermute(x, "morton", pairs)


def swap_cores(x, peers):
    return lax.ppermute(x, "morton", [(m, m ^ 1) for m in range(peers)])


class RingGather:
    def __init__(self, x, peers):
        self.x, self.peers, self.chips = x, peers, peers // 2
        self.whole = None
        if self.chips > 8:
            self.whole = lax.all_gather(x[None], "morton", axis=0, tiled=True)
            return
        self.chains = ([x], [x])

    def go(self, chain, gate=None):
        if self.whole is not None or len(self.chains[chain]) > self.chips // 2 - chain:
            return
        held = self.chains[chain][-1]
        if gate is not None:
            held = lax.optimization_barrier((held, gate))[0]
        cross = int(chain == 1 and len(self.chains[chain]) == 1)
        self.chains[chain].append(ring_step(held, self.peers, 0, cross))

    def last(self, chain):
        return self.x if self.whole is not None else self.chains[chain][-1]

    def places(self, gate=None):
        if self.whole is not None:
            return [self.whole]
        mine = self.chains[0][1:] + self.chains[1][1:]
        held = mine
        if gate is not None:
            held = [lax.optimization_barrier((t, gate))[0] for t in mine]
        others = [swap_cores(t, self.peers) for t in [self.x] + held]
        return [t[None] for t in [self.x] + others[:1] + mine + others[1:]]


class RingScatter:
    def __init__(self, keep, give, peers):
        self.keep, self.peers, self.chips = keep, peers, peers // 2
        self.other = [swap_cores(t, peers) for t in give]
        self.held = [None, None]
        self.hop = 0

    def term(self, k):
        half = self.chips // 2
        pair = self.other[k - half][0] if k >= half else self.other[half - 1 - k][1]
        return self.keep[k] + pair.astype(F32)

    def go(self, gate=None):
        sent = []
        for way, step, count in ((0, 1, self.chips // 2), (1, -1, (self.chips - 1) // 2)):
            left = count - self.hop
            if left <= 0:
                continue
            part = self.term((-step * left) % self.chips)
            if self.held[way] is not None:
                part = part + self.held[way].astype(F32)
            part = part.astype(BF16)
            if gate is not None:
                part = lax.optimization_barrier((part, gate))[0]
            sent.append(part)
            self.held[way] = ring_step(part, self.peers, step)
        self.hop += 1
        return sent

    def total(self):
        return sum((t.astype(F32) for t in self.held if t is not None), self.term(0))


def call(body, out_shape, in_specs, scratch=(), cost=2, name=None, out_specs=None, aliases=None):
    return pl.pallas_call(
        body,
        out_shape=out_shape,
        in_specs=in_specs,
        out_specs=out_specs or jax.tree.map(lambda _: VMEM, out_shape),
        scratch_shapes=list(scratch),
        input_output_aliases=aliases or {},
        compiler_params=pltpu.CompilerParams(vmem_limit_bytes=VMEM_LIMIT),
        cost_estimate=pl.CostEstimate(flops=cost * 10**9, bytes_accessed=0, transcendentals=0),
        name=name,
    )


PLANES = 4


def put_boundary(rows, brick, a, out_ref, stage, ends):
    base = brick * ROWS
    if a in (0, 7):
        at = base if a == 0 else base + 64
        out_ref[at : at + 64, :] = rows
        return
    wide = rows.astype(F32)
    at = base + B_LINES - 16 + 16 * a
    out_ref[at : at + 16, :] = jnp.concatenate([wide[:8], wide[56:]], axis=0).astype(BF16)
    at = brick * C_ROWS + 12 * (a - 1)
    for half in range(2):
        lanes = slice(half * 128, half * 128 + 128)
        stage[half] = wide[:, lanes]
        ends[at : at + 6, lanes] = stage[half, pl.ds(8, 6, stride=8), :]
        ends[at + 6 : at + 12, lanes] = stage[half, pl.ds(15, 6, stride=8), :]


def each_brick(rows_of, bricks, out_ref, stage, ends):
    for brick in range(bricks):
        for first in range(0, 8, PLANES):
            rows = rows_of(pl.ds(brick * 512 + first * 64, PLANES * 64))
            for t in range(PLANES):
                plane = rows[t * 64 : t * 64 + 64]
                put_boundary(plane, brick, first + t, out_ref, stage.at[first + t], ends)
    out_ref[bricks * ROWS : payload_rows(bricks), :] = ends[...].astype(BF16)


def norm_body(recv, send, x_ref, gain_ref, hidden_ref, out_ref, stage, ends):
    bricks, directions = recv.shape
    gain = gain_ref[...]
    lane = lax.broadcasted_iota(jnp.int32, (1, C), 1)
    codes = jnp.zeros((1, C), jnp.int32)
    for k in range(send.shape[1]):
        codes = jnp.where(lane == k, send[0, k], codes)
    served = jnp.zeros((1, C), jnp.int32)
    for brick in range(bricks):
        for number in range(directions):
            served = jnp.where(lane == recv[brick, number], brick * directions + number + 1, served)
    row = lax.broadcasted_iota(jnp.int32, (NOTES, C), 0)
    notes = jnp.where(row == 0, codes, jnp.where(row == 1, served, 0))
    out_ref[payload_rows(bricks) :, :] = notes.astype(F32).astype(BF16)

    def rows_of(at):
        x = x_ref[at, :].astype(F32)
        inverse = lax.rsqrt(jnp.mean(x * x, axis=-1, keepdims=True) + 1e-6)
        v = x * inverse * gain
        rows = (v / (1.0 + jnp.exp(-v))).astype(BF16)
        hidden_ref[at, :] = rows
        return rows

    each_brick(rows_of, bricks, out_ref, stage, ends)


def extract_body(x_ref, out_ref, stage, ends):
    each_brick(lambda at: x_ref[at, :], x_ref.shape[0] // 512, out_ref, stage, ends)


def start_padded(own_ref, cells, halo, bricks):
    zero = jnp.zeros((8, C), F32)

    def clear(k, _):
        for b in range(10):
            cells[k * 10 + b] = zero
        for side in range(2):
            for part in range(HB // 8):
                halo[side, k, part * 8 : part * 8 + 8, :] = zero
        return 0

    lax.fori_loop(0, bricks * 10, clear, 0)

    def fill(k, _):
        plane = (k // 8) * 10 + k % 8 + 1
        rows = own_ref[pl.ds(pl.multiple_of(k * 64, 64), 64), :].astype(F32)
        for b in range(8):
            cells[plane * 10 + b + 1] = rows[b * 8 : b * 8 + 8]
        return 0

    lax.fori_loop(0, bricks * 8, fill, 0)


def add_line(ref, index, line):
    ref[index] = ref[index] + line


def pick(flag, yes, no):
    if isinstance(flag, bool):
        return yes if flag else no
    return jnp.where(flag, yes, no)


def place(kind, e, keep, place_at, source_brick, brick, share, cells, halo):
    flags = [t == -1 for t in e]
    pads = [pick(f, 0, 9) for f in flags]
    facing = pick(flags[0], 64, 0)
    start = source_brick * ROWS

    def rows(at, size):
        got = share[place_at, pl.ds(pl.multiple_of(start + at, 16), size), :].astype(F32)
        return got if keep is None else jnp.where(keep, got, 0.0)

    def half(pair, axis):
        return pick(flags[axis], pair[8:], pair[:8])

    def ends(a):
        value = None
        for number in range(cells.shape[0] // 100):
            at = cells.shape[0] // 100 * ROWS + number * C_ROWS + 12 * (a - 1)
            block = share[place_at, at // 16 * 16 : -(-(at + 12) // 16) * 16, :].astype(F32)
            block = block[at % 16 : at % 16 + 12]
            block = pick(flags[2], block[6:], block[:6])
            value = block if value is None else jnp.where(source_brick == number, block, value)
        return value if keep is None else jnp.where(keep, value, 0.0)

    def line_b(at):
        plane = rows(at, 64)
        return pick(flags[1], plane[56:], plane[:8])

    def line_c(at):
        plane = rows(at, 64)
        ends = [
            pick(flags[2], plane[8 * b + 7 : 8 * b + 8], plane[8 * b : 8 * b + 1]) for b in range(8)
        ]
        return jnp.concatenate(ends, axis=0)

    def cell(at):
        line = line_b(at)
        return pick(flags[2], line[7:8], line[0:1])

    side = pick(flags[2], 0, 1)
    base = brick * 10

    def add_halo(at, line):
        halo[side, base + at, 8:16, :] = halo[side, base + at, 8:16, :] + line

    def add_cell(at, value):
        spot = pl.ds(pick(flags[1], 7, 16), 1)
        halo[side, base + at, spot, :] = halo[side, base + at, spot, :] + value

    if kind == (1, 0, 0):
        got = rows(facing, 64)
        first = (base + pads[0]) * 10 + 1
        for b in range(8):
            add_line(cells, first + b, got[b * 8 : b * 8 + 8])
    elif kind == (0, 1, 0):
        for a in range(8):
            if a in (0, 7):
                line = line_b(0 if a == 0 else 64)
            else:
                line = half(rows(B_LINES - 16 + 16 * a, 16), 1)
            add_line(cells, (base + a + 1) * 10 + pads[1], line)
    elif kind == (0, 0, 1):
        for a in range(8):
            if a in (0, 7):
                line = line_c(0 if a == 0 else 64)
            else:
                pair = rows(B_LINES - 16 + 16 * a, 16)
                low = pick(flags[2], pair[7:8], pair[0:1])
                high = pick(flags[2], pair[15:], pair[8:9])
                line = jnp.concatenate([low, ends(a), high], axis=0)
            add_halo(a + 1, line)
    elif kind == (1, 1, 0):
        add_line(cells, (base + pads[0]) * 10 + pads[1], line_b(facing))
    elif kind == (1, 0, 1):
        add_halo(pads[0], line_c(facing))
    elif kind == (0, 1, 1):
        for a in range(8):
            if a in (0, 7):
                value = cell(0 if a == 0 else 64)
            else:
                line = half(rows(B_LINES - 16 + 16 * a, 16), 1)
                value = pick(flags[2], line[7:8], line[0:1])
            add_cell(a + 1, value)
    else:
        add_cell(pads[0], cell(facing))


def windows(cells, halo, cols, bricks, out=None, sems=None):
    row = lax.broadcasted_iota(jnp.int32, (8, C), 0)

    def step(k, _):
        shifted = [[], [], []]
        for b in range(10):
            x = cells[k * 10 + b]
            before = halo[0, k, pl.ds(b + 7, 1), :]
            after = halo[1, k, pl.ds(b + 7, 1), :]
            shifted[0].append(jnp.where(row == 0, before, pltpu.roll(x, 1, 0)))
            shifted[1].append(x)
            shifted[2].append(jnp.where(row == 7, after, pltpu.roll(x, 7, 0)))
        for j in range(3):
            for l in range(3):
                block = jnp.concatenate(shifted[l][j : j + 8], axis=0).astype(BF16)
                at = (3 * j + l) * C
                cols[k, :, at : at + C] = block
        if out is not None:
            pltpu.make_async_copy(cols.at[k], out.at[k], sems.at[k]).start()
        return 0

    lax.fori_loop(0, bricks * 10, step, 0)


def wait_windows(cols, out, sems, bricks):
    def step(k, _):
        pltpu.make_async_copy(cols.at[k], out.at[k], sems.at[k]).wait()
        return 0

    lax.fori_loop(0, bricks * 10, step, 0)


def fetch(parts, share, sems, first=0, rows=None):
    size = parts[0].shape[0]
    lines = pl.ds(first, rows or parts[0].shape[1])
    copies = [
        pltpu.make_async_copy(part.at[:, lines], share.at[pl.ds(k * size, size), lines], sems.at[k])
        for k, part in enumerate(parts)
    ]
    for copy in copies:
        copy.start()
    return copies


def weight_grad_body(slots, factor, peers, count, *refs):
    recv, table, own_ref, cot_ref = refs[:4]
    parts = refs[4 : 4 + count]
    keep_ref = refs[4 + count]
    give_refs = refs[5 + count : 5 + count + peers // 4]
    out_cols, codes_ref, served_ref = refs[-16:-13]
    cells, halo, share, cols, sums, narrow, turned, codes = refs[-13:-5]
    sems, cols_sems, codes_sem, out_sems, notes_sems = refs[-5:]
    bricks = own_ref.shape[0] // 512
    me = table[2 * peers]
    notes_copies = fetch(parts, share, notes_sems, payload_rows(bricks), NOTES)
    copies = fetch(parts, share, sems, 0, payload_rows(bricks))
    for part in range(bricks * 2):
        at = slice(part * 256, part * 256 + 256)
        turned[:, at] = cot_ref[at, :].astype(F32).T.astype(BF16)
    for copy in notes_copies:
        copy.wait()
    for k in range(peers):
        notes = share[k, payload_rows(bricks) :, :].astype(F32).astype(jnp.int32)
        codes_ref[k : k + 1, :] = notes[0:1]
        served_ref[k : k + 1, :] = notes[1:2]
    codes_copy = pltpu.make_async_copy(codes_ref, codes, codes_sem.at[0])
    codes_copy.start()
    start_padded(own_ref, cells, halo, bricks)
    codes_copy.wait()
    for copy in copies:
        copy.wait()
    for brick in range(bricks):
        for number, e in enumerate(DIRECTIONS):
            slot = recv[brick, number]
            safe = jnp.maximum(slot, 0)
            sender = safe // slots
            at = table[sender]
            code = codes[at, me * slots + safe - sender * slots]
            kind = tuple(abs(t) for t in e)
            place(kind, e, slot >= 0, at, code // 6, brick, share, cells, halo)
    windows(cells, halo, cols, bricks, out_cols, cols_sems)

    rows = 27 * C // peers
    for tap in range(27):
        i, jl = divmod(tap, 9)
        total = None
        for brick in range(bricks):
            right = cols[brick * 10 + i : brick * 10 + i + 8, :, jl * C : jl * C + C].reshape(512, C)
            left = turned[:, brick * 512 : brick * 512 + 512]
            term = jnp.dot(left, right, preferred_element_type=F32)
            total = term if total is None else total + term
        total = (total * factor).T
        start = tap * C
        while start < (tap + 1) * C:
            owner = start // rows
            stop = min((tap + 1) * C, (owner + 1) * rows)
            piece = total[start - tap * C : stop - tap * C]
            bucket = jnp.bitwise_xor(me % 2, owner % 2)
            behind = table[peers + owner // 2]
            where = slice(start - owner * rows, stop - owner * rows)
            sums[bucket, behind, where, :] = piece
            narrow[bucket, behind, where, :] = piece.astype(BF16)
            start = stop
            if stop == (owner + 1) * rows:

                @pl.when(bucket == 0)
                def _():
                    pltpu.make_async_copy(
                        sums.at[0, behind], keep_ref.at[behind], out_sems.at[0, behind]
                    ).start()

                turn = table[peers + peers // 2 + owner // 2]
                for hop, give_ref in enumerate(give_refs):

                    @pl.when((bucket == 1) & (turn // 2 == hop))
                    def _():
                        pltpu.make_async_copy(
                            narrow.at[1, behind], give_ref.at[turn % 2], out_sems.at[1, turn]
                        ).start()

    for k in range(peers // 2):
        pltpu.make_async_copy(sums.at[0, k], keep_ref.at[k], out_sems.at[0, k]).wait()
        pltpu.make_async_copy(narrow.at[1, k], give_refs[k // 2].at[k % 2], out_sems.at[1, k]).wait()
    wait_windows(cols, out_cols, cols_sems, bricks)


GROUP = 3 * C


def start_stream(cols_ref, first, cols, weight_ref, weight, sems):
    copies = []
    planes = cols.shape[0]
    for g in range(3):
        lanes = pl.ds(g * GROUP, GROUP)
        group = [
            pltpu.make_async_copy(
                cols_ref.at[pl.ds(first, planes), :, lanes], cols.at[:, :, lanes], sems.at[g, 3]
            )
        ]
        for i in range(3):
            at = pl.ds((i * 3 + g) * GROUP, GROUP)
            group.append(pltpu.make_async_copy(weight_ref.at[at], weight.at[at], sems.at[g, i]))
        copies.append(group)
    for group in copies:
        for copy in group:
            copy.start()
    return copies


def tap_sum(copies, cols, weight):
    bricks = cols.shape[0] // 10
    totals = [None] * bricks
    for g in range(3):
        for copy in copies[g]:
            copy.wait()
        for brick in range(bricks):
            for i in range(3):
                at = brick * 10 + i
                left = cols[at : at + 8, :, g * GROUP : g * GROUP + GROUP].reshape(512, GROUP)
                right = weight[(i * 3 + g) * GROUP : (i * 3 + g + 1) * GROUP, :]
                term = jnp.dot(left, right, preferred_element_type=F32)
                totals[brick] = term if totals[brick] is None else totals[brick] + term
    return totals


def mix_body(cols_ref, weight_ref, x_ref, out_ref, cols, weight, sems):
    copies = start_stream(cols_ref, 0, cols, weight_ref, weight, sems)
    for brick, total in enumerate(tap_sum(copies, cols, weight)):
        at = slice(brick * 512, brick * 512 + 512)
        out_ref[at, :] = (x_ref[at, :].astype(F32) + total).astype(BF16)


def input_grad_body(slots, peers, count, *refs):
    served, send, table, cot_ref, x_ref, gain_ref, weight_ref = refs[:7]
    parts = refs[7 : 7 + count]
    out_ref, cells, halo, cols, share, weight, heads, more, sems, weight_sem = refs[7 + count :]
    bricks = cot_ref.shape[0] // 512
    me = table[2 * peers]
    copies = fetch(parts, share, sems)
    weight_copy = pltpu.make_async_copy(weight_ref, weight, weight_sem.at[0])
    weight_copy.start()

    def no_head(k, _):
        heads[k] = -1
        return 0

    lax.fori_loop(0, bricks * 26, no_head, 0)

    def source_of(k):
        receiver = k // slots
        at = table[receiver]
        return at, served[at, me * slots + k - receiver * slots] - 1

    def sort(k, found):
        _, entry = source_of(k)
        asked = entry >= 0
        key = send[0, k] // 6 * 26 + 25 - jnp.maximum(entry, 0) % 26
        first = asked & (heads[key] < 0)
        extra = asked & jnp.logical_not(first)

        @pl.when(first)
        def _():
            heads[key] = k

        @pl.when(extra)
        def _():
            more[found] = k

        return found + jnp.where(extra, 1, 0)

    found = lax.fori_loop(0, send.shape[1], sort, 0)
    start_padded(cot_ref, cells, halo, bricks)
    for copy in copies:
        copy.wait()
    for brick in range(bricks):
        for number, e in enumerate(DIRECTIONS):
            head = heads[brick * 26 + number]
            at, entry = source_of(jnp.maximum(head, 0))
            kind = tuple(abs(t) for t in e)
            source = jnp.maximum(entry, 0) // 26
            place(kind, e, head >= 0, at, source, brick, share, cells, halo)

    def one(n, _):
        k = more[n]
        at, entry = source_of(k)
        number = 25 - entry % 26
        tap = jnp.where(number >= 13, number + 1, number)
        e = (tap // 9 - 1, (tap // 3) % 3 - 1, tap % 3 - 1)
        on = [t != 0 for t in e]
        for kind in ((1, 0, 0), (0, 1, 0), (0, 0, 1), (1, 1, 0), (1, 0, 1), (0, 1, 1), (1, 1, 1)):
            match = functools.reduce(
                jnp.logical_and, [f if w else jnp.logical_not(f) for f, w in zip(on, kind)]
            )

            @pl.when(match)
            def _():
                place(kind, e, None, at, entry // 26, send[0, k] // 6, share, cells, halo)

        return 0

    lax.fori_loop(0, found, one, 0)
    windows(cells, halo, cols, bricks)
    weight_copy.wait()
    gain = gain_ref[...]
    for brick in range(bricks):
        rows = slice(brick * 512, brick * 512 + 512)
        grad = None
        for tap in range(27):
            i, jl = divmod(tap, 9)
            first = brick * 10 + i
            left = cols[first : first + 8, :, jl * C : jl * C + C].reshape(512, C)
            right = weight[(26 - tap) * C : (27 - tap) * C, :]
            term = lax.dot_general(left, right, (((1,), (1,)), ((), ())), preferred_element_type=F32)
            grad = term if grad is None else grad + term
        x = x_ref[rows, :].astype(F32)
        inverse = lax.rsqrt(jnp.mean(x * x, axis=-1, keepdims=True) + 1e-6)
        unit = x * inverse
        v = unit * gain
        gate = 1.0 / (1.0 + jnp.exp(-v))
        grad = grad * (gate * (1.0 + v * (1.0 - gate))) * gain
        grad = inverse * (grad - unit * jnp.mean(grad * unit, axis=-1, keepdims=True))
        out_ref[rows, :] = (cot_ref[rows, :].astype(F32) + grad).astype(BF16)


def local(features, norm_gain, conv_weight, recv_slot, send_face, cotangent):
    channels = features.shape[1]
    per_device = features.shape[0]
    bricks = per_device // 512
    peers = lax.axis_size("morton")
    slots = send_face.shape[1] // peers
    factor = 1.0 / math.sqrt(peers * per_device)
    gain = norm_gain.reshape(1, channels)
    sds = jax.ShapeDtypeStruct
    share_rows = payload_rows(bricks)
    stage = [
        pltpu.VMEM((8, 2, 64, 128), F32),
        pltpu.VMEM((share_rows - bricks * ROWS, channels), F32),
    ]

    def padded(n):
        return [
            pltpu.VMEM((n * 100, 8, channels), F32),
            pltpu.VMEM((2, n * 10, HB, channels), F32),
        ]

    def cols_shape(n):
        return (n * 10, 64, 9 * channels)


    table = jnp.asarray(ring_tables(peers))[lax.axis_index("morton")]

    hidden, share = call(
        norm_body,
        (sds((per_device, channels), BF16), sds((share_rows + NOTES, channels), BF16)),
        [SMEM, SMEM, VMEM, VMEM],
        stage,
        name="norm",
    )(recv_slot, send_face, features, gain)
    hidden_ring = RingGather(share, peers)
    cot_share = call(
        extract_body,
        sds((share_rows, channels), BF16),
        [VMEM],
        stage,
        name="extract",
    )(cotangent)
    hidden_ring.go(0)
    hidden_ring.go(1)
    hidden_ring.go(0, cot_share)
    hidden_ring.go(1)
    hidden_ring.go(0, table)
    hidden_ring.go(1)
    hidden_ring.go(0)
    hidden_parts = hidden_ring.places()

    cot_ring = RingGather(cot_share, peers)
    cot_ring.go(0, hidden_ring.last(1))
    cot_ring.go(1, hidden_ring.last(0))

    count = len(hidden_parts)
    rows = 27 * channels // peers
    chips = peers // 2
    keep, *give, cols, _, served = call(
        functools.partial(weight_grad_body, slots, factor, peers, count),
        (
            sds((chips, rows, channels), F32),
            *[sds((2, rows, channels), BF16)] * (chips // 2),
            sds(cols_shape(bricks), BF16),
            sds((peers, channels), jnp.int32),
            sds((peers, channels), jnp.int32),
        ),
        [SMEM] * 2 + [VMEM] * 2 + [HBM] * count,
        padded(bricks)
        + [
            pltpu.VMEM((peers, share_rows + NOTES, channels), BF16),
            pltpu.VMEM(cols_shape(bricks), BF16),
            pltpu.VMEM((2, chips, rows, channels), F32),
            pltpu.VMEM((2, chips, rows, channels), BF16),
            pltpu.VMEM((channels, per_device), BF16),
            pltpu.SMEM((peers, channels), jnp.int32),
            pltpu.SemaphoreType.DMA((count,)),
            pltpu.SemaphoreType.DMA((bricks * 10,)),
            pltpu.SemaphoreType.DMA((1,)),
            pltpu.SemaphoreType.DMA((2, chips)),
            pltpu.SemaphoreType.DMA((count,)),
        ],
        cost=9,
        name="weight_grad",
        out_specs=(*[HBM] * (2 + chips // 2), VMEM, VMEM),
    )(recv_slot, table, hidden, cotangent, *hidden_parts)

    first = (cot_ring.last(0), cot_ring.last(1))
    give = [lax.optimization_barrier((t, first))[0] for t in give]
    sums_ring = RingScatter(keep, give, peers)
    sent = sums_ring.go()
    cot_ring.go(0, cols)
    cot_ring.go(1, cols)
    second = (cot_ring.last(0), cot_ring.last(1))
    mix_cols = lax.optimization_barrier((cols, sent))[0]
    weight_scratch = [
        pltpu.VMEM((27 * channels, channels), BF16),
        pltpu.SemaphoreType.DMA((3, 4)),
    ]
    mixed = call(
        mix_body,
        sds((per_device, channels), BF16),
        [HBM, HBM, VMEM],
        [pltpu.VMEM(cols_shape(bricks), BF16)] + weight_scratch,
        cost=6,
        name="mix",
    )(mix_cols, conv_weight, features)
    sent = sums_ring.go((second, mixed))
    cot_ring.go(0)
    cot_ring.go(1)
    third = (cot_ring.last(0), cot_ring.last(1))
    sums_ring.go(third)
    cot_ring.go(0)
    sent = sums_ring.go(cot_ring.last(0))
    cot_parts = cot_ring.places(cols)
    served = lax.optimization_barrier((served, sent))[0]

    grad_features = call(
        functools.partial(input_grad_body, slots, peers, count),
        sds((per_device, channels), BF16),
        [SMEM] * 3 + [VMEM] * 3 + [HBM] * (1 + count),
        padded(bricks)
        + [
            pltpu.VMEM(cols_shape(bricks), BF16),
            pltpu.VMEM((peers, share_rows, channels), BF16),
            weight_scratch[0],
            pltpu.SMEM((bricks * 26,), jnp.int32),
            pltpu.SMEM((peers * slots,), jnp.int32),
            pltpu.SemaphoreType.DMA((count,)),
            pltpu.SemaphoreType.DMA((1,)),
        ],
        cost=13,
        name="input_grad",
    )(served, send_face, table, cotangent, features, gain, conv_weight, *cot_parts)
    for _ in range(chips // 2 - 4):
        sums_ring.go()
    return (mixed, grad_features, sums_ring.total())


def solution(mesh):
    rows = P(("groups", "morton"), None)
    return jax.shard_map(
        local,
        mesh=mesh,
        in_specs=(rows, P(), P(), rows, rows, rows),
        out_specs=(rows, rows, rows),
        check_vma=False,
    )
```
